32 devices in a mesh: dp: 4 (over z), expert: 8 (over y, x, core).
Axes of the slice: x: 2, y: 2, z: 4, core: 2. Of those that a mesh axis runs over, the one named last changes fastest.
Arguments:
- tokens: bfloat16 [2, 6144, 1024], P(None, ('dp', 'expert')), may hold values from -6 to 6
- cotangent: bfloat16 [2, 6144, 1024], P(None, ('dp', 'expert')), may hold values from -6 to 6
- lengths: int32 [2, 32], P(None, ('dp', 'expert')), may hold values from 1 to 192, as said below
- routes: int32 [2, 6144, 16], P(None, ('dp', 'expert')), may hold values from 0 to 95, all different within a row; in each aligned block of 192 rows (0 to 191, 192 to 383, ..., all dimensions but the last counted through in order) at most 40 rows name the same one
- head_choice: int32 [2, 6144, 4, 2], P(None, ('dp', 'expert')), may hold values from 0 to 4, all different within a row
- placement: int32 [96], replicated, may hold values from 0 to 95, each once
- gain_master: float32 [1024], P(('dp', 'expert')), may hold values from 0.5 to 1.5
- gain_moment: float32 [1024], P(('dp', 'expert')), may hold values from -640 to 640
- gain_average: float32 [1024], P(('dp', 'expert')), may hold values from 0.5 to 1.5
- qkv_master: float32 [1024, 3584], P(('dp', 'expert')), may hold values from -0.1875 to 0.1875
- qkv_moment: float32 [1024, 3584], P(('dp', 'expert')), may hold values from -640 to 640
- qkv_average: float32 [1024, 3584], P(('dp', 'expert')), may hold values from -0.1875 to 0.1875
- select_master: float32 [1024, 40], P(('dp', 'expert')), may hold values from -0.125 to 0.125
- select_moment: float32 [1024, 40], P(('dp', 'expert')), may hold values from -2048 to 2048
- select_average: float32 [1024, 40], P(('dp', 'expert')), may hold values from -0.125 to 0.125
- router_master: float32 [1024, 96], P(('dp', 'expert')), may hold values from -0.0625 to 0.0625
- router_moment: float32 [1024, 96], P(('dp', 'expert')), may hold values from -512 to 512
- router_average: float32 [1024, 96], P(('dp', 'expert')), may hold values from -0.0625 to 0.0625
- heads_out_master: float32 [2560, 1024], P(('dp', 'expert')), may hold values from -3 to 3
- heads_out_moment: float32 [2560, 1024], P(('dp', 'expert')), may hold values from -64 to 64
- heads_out_average: float32 [2560, 1024], P(('dp', 'expert')), may hold values from -3 to 3
- up_master: float32 [96, 1024, 128], P('expert', 'dp'), may hold values from -0.1875 to 0.1875
- up_moment: float32 [96, 1024, 128], P('expert', 'dp'), may hold values from -128 to 128
- up_average: float32 [96, 1024, 128], P('expert', 'dp'), may hold values from -0.1875 to 0.1875
- down_master: float32 [96, 1024, 128], P('expert', 'dp'), may hold values from -0.25 to 0.25
- down_moment: float32 [96, 1024, 128], P('expert', 'dp'), may hold values from -112 to 112
- down_average: float32 [96, 1024, 128], P('expert', 'dp'), may hold values from -0.25 to 0.25
Outputs:
- mixed: bfloat16 [2, 6144, 1024], P(None, ('dp', 'expert'))
- grad_input: float32 [2, 6144, 1024], P(None, ('dp', 'expert'))
- gain_moment_new: float32 [1024], P(('dp', 'expert'))
- gain_average_new: float32 [1024], P(('dp', 'expert'))
- gain_new: float32 [1024], P(('dp', 'expert'))
- gain_new_low: bfloat16 [1024], P(('dp', 'expert'))
- qkv_moment_new: float32 [1024, 3584], P(('dp', 'expert'))
- qkv_average_new: float32 [1024, 3584], P(('dp', 'expert'))
- qkv_new: float32 [1024, 3584], P(('dp', 'expert'))
- qkv_new_low: bfloat16 [1024, 3584], P(('dp', 'expert'))
- select_moment_new: float32 [1024, 40], P(('dp', 'expert'))
- select_average_new: float32 [1024, 40], P(('dp', 'expert'))
- select_new: float32 [1024, 40], P(('dp', 'expert'))
- select_new_low: bfloat16 [1024, 40], P(('dp', 'expert'))
- router_moment_new: float32 [1024, 96], P(('dp', 'expert'))
- router_average_new: float32 [1024, 96], P(('dp', 'expert'))
- router_new: float32 [1024, 96], P(('dp', 'expert'))
- router_new_low: bfloat16 [1024, 96], P(('dp', 'expert'))
- heads_out_moment_new: float32 [2560, 1024], P(('dp', 'expert'))
- heads_out_average_new: float32 [2560, 1024], P(('dp', 'expert'))
- heads_out_new: float32 [2560, 1024], P(('dp', 'expert'))
- heads_out_new_low: bfloat16 [2560, 1024], P(('dp', 'expert'))
- up_moment_new: float32 [96, 1024, 128], P('expert', 'dp')
- up_average_new: float32 [96, 1024, 128], P('expert', 'dp')
- up_new: float32 [96, 1024, 128], P('expert', 'dp')
- up_new_low: bfloat16 [96, 1024, 128], P('expert', 'dp')
- down_moment_new: float32 [96, 1024, 128], P('expert', 'dp')
- down_average_new: float32 [96, 1024, 128], P('expert', 'dp')
- down_new: float32 [96, 1024, 128], P('expert', 'dp')
- down_new_low: bfloat16 [96, 1024, 128], P('expert', 'dp')
The draws below stay inside these ranges and needn't reach their ends.
Inputs may be any that keep to these rules, and one draw needn't show every extreme that they name: `lengths`: in each micro-batch some sequence slot has all 192 rows live. `routes`: each row names 16 different experts; in each micro-batch no expert is named by more than 40 rows of one sequence slot, a bound that some block reaches. `head_choice`: each head of each row names 2 different experts. A permutation: expert r uses the weights of slot placement[r].
All inputs are finite; a program needn't handle non-finite values.
Results may differ from the reference program's by a relative error of at most 0.015.
The reference program's roundings to bfloat16 on the way count: a program that leaves them out, or rounds other values in their place, can miss the bound.
Values may be sent and summed in bfloat16 or wider, within the bound.
A program may use at most 256 MiB of HBM per device.

```python
import math
import jax
import jax.numpy as jnp
import numpy as np
from jax import lax

D = 1024
H = 4
HD = 128
NV = 5
F = 128
TOPK = 16
VTOP = 2
EXP_DEV = 12
ROWS = 192
MB = 2
SEQS = 32
TOKENS = 6144
EXPERTS = 96
MOST = 40
QKV = 3584
VALUE = 2560
SELECT = 40
N_EXPERT = 8


def draw_lengths(key, part):
    key = jax.random.fold_in(key, 11)
    key_lengths, key_longest = jax.random.split(key)
    lengths_drawn = jax.random.randint(key_lengths, (MB, SEQS), ROWS // 2, ROWS + 1)
    longest_at = jax.random.randint(key_longest, (MB, 1), 0, SEQS)
    return jnp.where(jnp.arange(SEQS)[None, :] == longest_at, ROWS, lengths_drawn).astype(jnp.int32)


def with_spikes(drawn, stream_key, source, target, blocks, factor):
    owner, partner = [(jnp.arange(drawn.shape[axis_at]) // (drawn.shape[axis_at] // blocks)).reshape([-1 if axis == axis_at else 1 for axis in range(drawn.ndim)]) for axis_at in (source, target)]
    chosen = jax.random.permutation(stream_key, blocks)[partner]
    strong = (owner == chosen) | (owner == (partner + blocks // 2) % blocks)
    return jnp.where(strong, factor * drawn, drawn)


def block_scale(own_key, dims, cuts, least, largest):
    def one(dim, shards_of):
        steps = jax.random.uniform(jax.random.fold_in(jax.random.fold_in(own_key, 6), dim), (shards_of,), jnp.float32, least / len(cuts), largest / len(cuts))
        return jnp.repeat(jnp.exp(steps), dims[dim] // shards_of).reshape((-1,) + (1,) * (len(dims) - dim - 1))

    factor_of = one(*cuts[0])
    for cut in cuts[1:]:
        factor_of = factor_of * one(*cut)
    return factor_of


def different_ones(stream_key, rows, number_of, top, lift):
    sequence = jax.random.permutation(jax.random.fold_in(stream_key, 1), number_of)
    boost = sequence
    for power in range(3):
        boost = boost * boost // number_of
    boost = boost * lift // number_of
    lots = jax.random.randint(jax.random.fold_in(stream_key, 2), (rows, number_of), 0, 4096) + boost
    fixed_rows = jax.random.permutation(jax.random.fold_in(stream_key, 3), rows)[jnp.arange(number_of) % rows]
    lots = jnp.where(jnp.arange(rows)[:, None] == fixed_rows[None, :], 1 << 14, lots)
    priority = lots * number_of + jnp.arange(number_of)
    return lax.top_k(priority.astype(jnp.int32), top)[1].astype(jnp.int32)


def deal_out(rng, own, number, rows, amount, top, bound, lean):
    sequence = jax.random.permutation(rng, amount)
    packed, ordinary = portions_of(amount, rows * top, bound, lean, True), portions_of(amount, rows * top, bound, lean, False)
    places = jnp.arange(amount)

    def named(sizes, turn):
        used = int((sizes > 0).sum())
        fixed = max(1, used // 4)
        moved = fixed + (places - fixed + turn * (used - fixed)) % max(1, amount - fixed)
        return jnp.zeros((amount,), jnp.int32).at[sequence[jnp.where(places < fixed, places, moved)]].set(jnp.asarray(sizes, jnp.int32))

    sizes = jnp.where(number % 4 == 0, named(packed, number // 4), named(ordinary, number - number // 4 - 1))
    mixed = jax.random.permutation(jax.random.fold_in(own, 3), amount)
    source_of, receiver = mixed[0:amount // 2 * 2:2], mixed[1:amount // 2 * 2:2]
    room = jnp.minimum(sizes[source_of] - 1, bound - sizes[receiver]) // 2
    room = jnp.where((source_of == sequence[0]) | (receiver == sequence[0]) | (sizes[receiver] == 0), 0, jnp.maximum(room, 0))
    moved = jax.random.randint(jax.random.fold_in(own, 4), (amount // 2,), 0, 1 << 20) % (room + 1)
    sizes = sizes.at[source_of].add(-moved).at[receiver].add(moved)
    items = jnp.searchsorted(jnp.cumsum(sizes), jnp.arange(rows * top), side="right").astype(jnp.int32)
    grid = items.reshape(top, rows).T
    grid = grid[jax.random.permutation(jax.random.fold_in(own, 1), rows)]
    turn = jax.random.randint(jax.random.fold_in(own, 2), (rows, 1), 0, top)
    return jnp.take_along_axis(grid, (jnp.arange(top)[None, :] + turn) % top, axis=1)


def portions_of(amount, total, limit, lean, full):
    loads = [(1 << 20) // math.isqrt(standing ** lean) + 1 for standing in range(1, amount + 1)]
    largest = limit if full else min(limit, max(-(-total // amount), total * loads[0] // sum(loads)))
    least = 1 if total - largest >= amount - 1 else 0
    holding, spare = [largest] + [least] * (amount - 1), total - largest - least * (amount - 1)
    while spare > 0:
        candidates = [i for i in range(1, amount) if holding[i] < largest] or [i for i in range(1, amount) if holding[i] < limit]
        whole, budget = sum([loads[i] for i in candidates]), spare
        for i in candidates:
            more = min(limit - holding[i], max(1, budget * loads[i] // whole), spare)
            holding[i] = holding[i] + more
            spare = spare - more
    return np.array(holding)


def noise(own_key, extent, deviation, most, cuts=(), kind=jnp.bfloat16):
    gain = block_scale(own_key, extent, cuts, -0.22, 0.18) if cuts else 1.0
    drawn = jax.random.normal(own_key, extent, jnp.float32) * deviation * gain
    return jnp.minimum(jnp.maximum(drawn, -most), most).astype(kind)


def heavy_noise(rng, dims, spread, limit, cuts, heavy, kind=jnp.bfloat16):
    values = spread * jax.random.normal(rng, dims, jnp.float32)
    if cuts:
        values = values * block_scale(rng, dims, cuts, -0.22, 0.18)
    return jnp.clip(with_spikes(values, jax.random.fold_in(rng, 3), *heavy), -limit, limit).astype(kind)


def setup_inputs(seed: int = 0) -> dict:
    keys = jax.random.split(jax.random.key(seed), 28)
    tokens = heavy_noise(keys[0], (MB, TOKENS, D), 1.0, 6.0, ((1, 32),), (1, 2, 32, 2.75))
    cotangent = noise(keys[1], (MB, TOKENS, D), 1.0, 6.0, ((1, 32),))
    lengths = draw_lengths(jax.random.fold_in(keys[27], 71), 0)
    routes_keys = jax.random.split(jax.random.fold_in(keys[3], 1), MB * TOKENS // ROWS)
    routes_turns = jax.random.permutation(jax.random.fold_in(keys[3], 3), MB * TOKENS // ROWS)
    routes = jax.vmap(lambda own, number: deal_out(jax.random.fold_in(keys[3], 2), own, number, ROWS, EXPERTS, TOPK, MOST, 2))(routes_keys, routes_turns).reshape((MB, TOKENS, TOPK))
    head_choice = different_ones(keys[4], MB * TOKENS * H, NV, VTOP, 0).reshape((MB, TOKENS, H, VTOP))
    placement = jax.random.permutation(keys[5], EXPERTS).astype(jnp.int32)
    gain_master = jnp.clip(1.0 + 0.1 * jax.random.normal(keys[6], (D,), jnp.float32), 0.5, 1.5)
    gain_moment = noise(keys[7], (D,), (1.0 * (MB * TOKENS) ** 0.5), 640.0, ((0, 32),), jnp.float32)
    gain_average = jnp.clip(1.0 + 0.1 * jax.random.normal(keys[8], (D,), jnp.float32), 0.5, 1.5)
    qkv_master = noise(keys[9], (D, QKV), D ** -0.5, 0.1875, ((0, 32),), jnp.float32)
    qkv_moment = noise(keys[10], (D, QKV), (1.0 * (MB * TOKENS) ** 0.5), 640.0, ((0, 32),), jnp.float32)
    qkv_average = noise(keys[11], (D, QKV), D ** -0.5, 0.1875, ((0, 32),), jnp.float32)
    select_master = noise(keys[12], (D, SELECT), (2 * D) ** -0.5, 0.125, ((0, 32),), jnp.float32)
    select_moment = noise(keys[13], (D, SELECT), (3.0 * (MB * TOKENS) ** 0.5), 2048.0, ((0, 32),), jnp.float32)
    select_average = noise(keys[14], (D, SELECT), (2 * D) ** -0.5, 0.125, ((0, 32),), jnp.float32)
    router_master = noise(keys[15], (D, EXPERTS), (9 * D) ** -0.5, 0.0625, ((0, 32),), jnp.float32)
    router_moment = noise(keys[16], (D, EXPERTS), (2.0 * (MB * TOKENS * TOPK // EXPERTS) ** 0.5), 512.0, ((0, 32),), jnp.float32)
    router_average = noise(keys[17], (D, EXPERTS), (9 * D) ** -0.5, 0.0625, ((0, 32),), jnp.float32)
    heads_out_master = noise(keys[18], (VALUE, D), 4 ** -0.5, 3.0, ((0, 32),), jnp.float32)
    heads_out_moment = noise(keys[19], (VALUE, D), (0.1 * (MB * TOKENS) ** 0.5), 64.0, ((0, 32),), jnp.float32)
    heads_out_average = noise(keys[20], (VALUE, D), 4 ** -0.5, 3.0, ((0, 32),), jnp.float32)
    up_master = noise(keys[21], (EXPERTS, D, F), D ** -0.5, 0.1875, ((0, 8), (1, 4)), jnp.float32)
    up_moment = noise(keys[22], (EXPERTS, D, F), (0.5 * (MB * TOKENS * TOPK // EXPERTS) ** 0.5), 128.0, ((0, 8), (1, 4)), jnp.float32)
    up_average = noise(keys[23], (EXPERTS, D, F), D ** -0.5, 0.1875, ((0, 8), (1, 4)), jnp.float32)
    down_master = noise(keys[24], (EXPERTS, D, F), (4 * F) ** -0.5, 0.25, ((0, 8), (1, 4)), jnp.float32)
    down_moment = noise(keys[25], (EXPERTS, D, F), (0.4 * (MB * TOKENS * TOPK // EXPERTS) ** 0.5), 112.0, ((0, 8), (1, 4)), jnp.float32)
    down_average = noise(keys[26], (EXPERTS, D, F), (4 * F) ** -0.5, 0.25, ((0, 8), (1, 4)), jnp.float32)
    return dict(tokens=tokens, cotangent=cotangent, lengths=lengths, routes=routes, head_choice=head_choice, placement=placement, gain_master=gain_master, gain_moment=gain_moment, gain_average=gain_average, qkv_master=qkv_master, qkv_moment=qkv_moment, qkv_average=qkv_average, select_master=select_master, select_moment=select_moment, select_average=select_average, router_master=router_master, router_moment=router_moment, router_average=router_average, heads_out_master=heads_out_master, heads_out_moment=heads_out_moment, heads_out_average=heads_out_average, up_master=up_master, up_moment=up_moment, up_average=up_average, down_master=down_master, down_moment=down_moment, down_average=down_average)


@jax.custom_vjp
def low(v):
    return lax.optimization_barrier(v.astype(jnp.bfloat16)).astype(jnp.float32)

@jax.custom_vjp
def low_back(v):
    return v

def low_keep(v):
    return (low(v), None)

def low_pass(kept, grad):
    return (grad,)

def back_keep(v):
    return (v, None)

def back_low(kept, grad):
    return (low(grad),)
low.defvjp(low_keep, low_pass)
low_back.defvjp(back_keep, back_low)
momentum_decay = 0.9
average_decay = 0.5
rate_factor = 0.4
epsilon = 1e-05

def product(left, right):
    return jnp.dot(left, right, precision=lax.Precision.HIGHEST, preferred_element_type=jnp.float32)

def rounded(value):
    return low_back(low(value))

def layer_normed(inputs, gain_row):
    centred = inputs - lax.optimization_barrier(jnp.mean(inputs, axis=-1, keepdims=True))
    variance = lax.optimization_barrier(jnp.mean(centred * centred, axis=-1, keepdims=True))
    return centred * lax.rsqrt(variance + epsilon) * gain_row

def picked_mask(picks, number):
    return lax.optimization_barrier(jnp.sum((picks[..., None] == jnp.arange(number, dtype=jnp.int32)).astype(jnp.float32), axis=-2))

def step_rates(total_tokens, experts):
    root_tokens = math.sqrt(total_tokens)
    expert_share = math.sqrt(TOPK / experts)
    spread_list = (0.3, D ** (-0.5), (2 * D) ** (-0.5), (9 * D) ** (-0.5), 0.5, D ** (-0.5), (4 * F) ** (-0.5))
    gradient_list = (1.0, 1.0, 3.0, 2.0 * expert_share, 0.1, 0.5 * expert_share, 0.4 * expert_share)
    return tuple((rate_factor * spread_value / (gradient_value * root_tokens) for spread_value, gradient_value in zip(spread_list, gradient_list)))

def update_weight(master, moment, average, gradient, step_size):
    new_moment = momentum_decay * moment + gradient
    new_weight = master - step_size * (gradient + momentum_decay * new_moment)
    new_average = average_decay * average + (1.0 - average_decay) * new_weight
    return (new_moment, new_average, new_weight, new_weight.astype(jnp.bfloat16))

def attend_sequence(pieces):
    queries, keys_seq, values_seq, length = pieces
    scores = jnp.einsum('ihd,jhd->hij', queries, keys_seq, precision=lax.Precision.HIGHEST) * HD ** (-0.5)
    scores = low_back(scores)
    position = jnp.arange(queries.shape[0], dtype=jnp.int32)
    allowed = (position[None, :] <= position[:, None]) & (position[None, :] < length)
    attention = low(jax.nn.softmax(jnp.where(allowed[None], scores, -1e+30), axis=-1))
    return jnp.einsum('hij,jhd->ihd', attention, values_seq, precision=lax.Precision.HIGHEST)

def micro_forward(length_row, route_rows, pick_rows, placement):
    live_rows = (jnp.arange(TOKENS, dtype=jnp.int32) % ROWS < jnp.repeat(length_row, ROWS)).astype(jnp.float32)
    value_mask = picked_mask(pick_rows, NV)
    out_mask = value_mask * live_rows[:, None, None]
    pair_count = TOKENS * TOPK
    flat_slots = placement[route_rows].reshape(-1).astype(jnp.int32)
    pair_order = jnp.argsort(flat_slots, stable=True).astype(jnp.int32)
    sorted_slots = flat_slots[pair_order]
    starts = jnp.searchsorted(sorted_slots, jnp.arange(EXPERTS, dtype=jnp.int32)).astype(jnp.int32)
    slot_ranks = jnp.arange(pair_count, dtype=jnp.int32) - starts[sorted_slots]
    capacity = SEQS * MOST
    pair_table = jnp.full((EXPERTS, capacity), pair_count, jnp.int32).at[sorted_slots, slot_ranks].set(pair_order)
    pair_table = pair_table.reshape(N_EXPERT, EXP_DEV, capacity)
    split = 2 * H * HD

    def forward(tokens, gain_row, w_qkv, w_select, w_router, w_heads_out, w_up, w_down):
        normed = low(layer_normed(tokens, gain_row))
        query_key = rounded(product(normed, w_qkv[:, :split]))
        values_all = low_back(product(tokens, w_qkv[:, split:]))
        select = low_back(product(tokens, w_select))
        value_gate = jax.nn.sigmoid(select[:, :H * NV]).reshape(TOKENS, H, NV) * value_mask
        out_gate = jax.nn.sigmoid(select[:, H * NV:]).reshape(TOKENS, H, NV) * out_mask
        values_head = rounded(lax.optimization_barrier(jnp.sum(value_gate[..., None] * values_all.reshape(TOKENS, H, NV, HD), axis=2)))
        queries = query_key[:, :H * HD].reshape(SEQS, ROWS, H, HD)
        keys_all = query_key[:, H * HD:].reshape(SEQS, ROWS, H, HD)
        attended = lax.map(jax.checkpoint(attend_sequence), (queries, keys_all, values_head.reshape(SEQS, ROWS, H, HD), length_row))
        attended = low_back(attended.reshape(TOKENS, H, HD))
        mixed_heads = low((out_gate[..., None] * attended[:, :, None, :]).reshape(TOKENS, VALUE))
        middle = tokens + low_back(product(mixed_heads, w_heads_out))
        middle_low = low(middle)
        logits = low_back(product(middle_low, w_router))
        gate_values = jax.nn.sigmoid(jnp.take_along_axis(logits, route_rows, axis=1)) * live_rows[:, None]
        gate_padded = jnp.concatenate([gate_values.reshape(-1), jnp.zeros((1,), jnp.float32)])
        rows_padded = jnp.concatenate([middle_low, jnp.zeros((1, D), jnp.float32)], axis=0)

        def owner_group(total, owner_index):
            entries = pair_table[owner_index]
            token_index = entries // TOPK
            rows_in = low_back(rows_padded[token_index])
            up_part = lax.dynamic_slice_in_dim(w_up, owner_index * EXP_DEV, EXP_DEV, 0)
            down_part = lax.dynamic_slice_in_dim(w_down, owner_index * EXP_DEV, EXP_DEV, 0)
            pre_act = low_back(jnp.einsum('ecd,edf->ecf', rows_in, up_part, precision=lax.Precision.HIGHEST))
            hidden = low(jax.nn.gelu(pre_act))
            result = rounded(jnp.einsum('ecf,edf->ecd', hidden, down_part, precision=lax.Precision.HIGHEST))
            weighted = result * gate_padded[entries][..., None]
            return (total.at[token_index.reshape(-1)].add(weighted.reshape(-1, D)), None)
        total, unused = lax.scan(jax.checkpoint(owner_group), jnp.zeros((TOKENS + 1, D), jnp.float32), jnp.arange(N_EXPERT, dtype=jnp.int32))
        return middle + total[:TOKENS]
    return forward

def reference(tokens, cotangent, lengths, routes, head_choice, placement, gain_master, gain_moment, gain_average, qkv_master, qkv_moment, qkv_average, select_master, select_moment, select_average, router_master, router_moment, router_average, heads_out_master, heads_out_moment, heads_out_average, up_master, up_moment, up_average, down_master, down_moment, down_average):
    masters = (gain_master, qkv_master, select_master, router_master, heads_out_master, up_master, down_master)
    moments = (gain_moment, qkv_moment, select_moment, router_moment, heads_out_moment, up_moment, down_moment)
    averages = (gain_average, qkv_average, select_average, router_average, heads_out_average, up_average, down_average)
    lowered = tuple((low(master) for master in masters))
    summed = None
    mixed_list = []
    input_list = []
    for micro_index in range(MB):
        forward = micro_forward(lengths[micro_index], routes[micro_index], head_choice[micro_index], placement)
        output, pullback = jax.vjp(forward, tokens[micro_index].astype(jnp.float32), *lowered)
        gradients = pullback(cotangent[micro_index].astype(jnp.float32))
        mixed_list.append(output.astype(jnp.bfloat16))
        input_list.append(gradients[0])
        weight_grads = gradients[1:]
        if summed is None:
            summed = weight_grads
        else:
            summed = tuple((first_term + second_term for first_term, second_term in zip(summed, weight_grads)))
    step_sizes = step_rates(MB * TOKENS, EXPERTS)
    gain_out = update_weight(masters[0], moments[0], averages[0], summed[0], step_sizes[0])
    qkv_out = update_weight(masters[1], moments[1], averages[1], summed[1], step_sizes[1])
    select_out = update_weight(masters[2], moments[2], averages[2], summed[2], step_sizes[2])
    router_out = update_weight(masters[3], moments[3], averages[3], summed[3], step_sizes[3])
    heads_out_out = update_weight(masters[4], moments[4], averages[4], summed[4], step_sizes[4])
    up_out = update_weight(masters[5], moments[5], averages[5], summed[5], step_sizes[5])
    down_out = update_weight(masters[6], moments[6], averages[6], summed[6], step_sizes[6])
    return (jnp.stack(mixed_list), jnp.stack(input_list), gain_out[0], gain_out[1], gain_out[2], gain_out[3], qkv_out[0], qkv_out[1], qkv_out[2], qkv_out[3], select_out[0], select_out[1], select_out[2], select_out[3], router_out[0], router_out[1], router_out[2], router_out[3], heads_out_out[0], heads_out_out[1], heads_out_out[2], heads_out_out[3], up_out[0], up_out[1], up_out[2], up_out[3], down_out[0], down_out[1], down_out[2], down_out[3])
```

```python
import functools
import math

import jax
import jax.numpy as jnp
from jax import lax
from jax.experimental import pallas as pl
from jax.experimental.pallas import tpu as pltpu
from jax.sharding import PartitionSpec as P

D = 1024
H = 4
HD = 128
NV = 5
F = 128
TOPK = 16
MB = 2
QK = 2 * H * HD
VAL = H * NV * HD
SEL = 2 * H * NV

momentum_decay = 0.9
average_decay = 0.5
rate_factor = 0.4
epsilon = 1e-05
BF = jnp.bfloat16
F32 = jnp.float32


def step_rates(total_tokens, experts):
    root_tokens = math.sqrt(total_tokens)
    expert_share = math.sqrt(TOPK / experts)
    spread_list = (
        0.3,
        D ** (-0.5),
        (2 * D) ** (-0.5),
        (9 * D) ** (-0.5),
        0.5,
        D ** (-0.5),
        (4 * F) ** (-0.5),
    )
    gradient_list = (1.0, 1.0, 3.0, 2.0 * expert_share, 0.1, 0.5 * expert_share, 0.4 * expert_share)
    return tuple(
        rate_factor * spread_value / (gradient_value * root_tokens)
        for spread_value, gradient_value in zip(spread_list, gradient_list)
    )


def update_weight(master, moment, average, gradient, step_size):
    new_moment = momentum_decay * moment + gradient
    new_weight = master - step_size * (gradient + momentum_decay * new_moment)
    new_average = average_decay * average + (1.0 - average_decay) * new_weight
    return (new_moment, new_average, new_weight, new_weight.astype(BF))


def dot_nt(a, b):
    return lax.dot_general(a, b, (((1,), (1,)), ((), ())), preferred_element_type=F32)


def dot_tn(a, b):
    return lax.dot_general(a, b, (((0,), (0,)), ((), ())), preferred_element_type=F32)


def dot_nn(a, b):
    return jnp.dot(a, b, preferred_element_type=F32)


MESH = pl.DeviceIdType.MESH


class Place:
    def __init__(self):
        self.z = lax.axis_index("dp")
        self.e = lax.axis_index("expert")
        core = self.e % 2
        x = (self.e // 2) % 2
        y = self.e // 4
        self.sib = self.e + 1 - 2 * core
        self.xnb = self.e + 2 - 4 * x
        self.ynb = self.e + 4 - 8 * y
        self.diag = self.xnb + 4 - 8 * y
        self.core, self.x, self.y = core, x, y


def greet(place, line, owners):
    barrier = pltpu.get_barrier_semaphore()
    z = place.z
    for e in (place.sib, place.xnb, place.ynb):
        pl.semaphore_signal(barrier, inc=1, device_id=(z, e), device_id_type=MESH)
    peers = 3
    if line:

        @pl.when(z > 0)
        def _():
            pl.semaphore_signal(barrier, inc=1, device_id=(z - 1, place.e), device_id_type=MESH)

        @pl.when(z < owners - 1)
        def _():
            pl.semaphore_signal(barrier, inc=1, device_id=(z + 1, place.e), device_id_type=MESH)

        peers = peers + (z + owners - 1) // owners + (2 * owners - 2 - z) // owners
    pl.semaphore_wait(barrier, peers)


XS, YS, FA, FB, S0, S1, S2, S3, UP, DOWN = range(10)

def gather_kernel(owners, group, lines, halves, *refs):
    n = len(lines)
    ins, outs, (send, recv, own) = refs[:n], refs[n : 2 * n], refs[2 * n :]
    place = Place()
    z = place.z
    copies_own = []
    for i in range(n):
        rows = ins[i].shape[0]
        slot = (z * group + place.e) if lines[i] else place.e
        cp = pltpu.make_async_copy(ins[i], outs[i].at[pl.ds(slot * rows, rows)], own.at[i])
        cp.start()
        copies_own.append(cp)
    greet(place, any(lines), owners)

    def block(i, rel, e, part=None):
        rows = ins[i].shape[0]
        slot = ((z + rel) * group + e) if lines[i] else e
        start, size = (0, rows) if part is None else part
        return outs[i].at[pl.ds(slot * rows + start, size)]

    def source(i, rel, part=None):
        if rel == 0:
            return ins[i] if part is None else ins[i].at[pl.ds(*part)]
        return block(i, rel, place.e, part)

    def sem(rel):
        return rel + owners - 1

    def go(i, rel, kind, src, dst, to_e, dz=0):
        return pltpu.make_async_remote_copy(
            src_ref=src, dst_ref=dst, send_sem=send.at[i, sem(rel), kind],
            recv_sem=recv.at[i, sem(rel - dz), min(kind, UP)],
            device_id=(z + dz, to_e), device_id_type=MESH)

    def parts(i):
        rows = ins[i].shape[0]
        return (0, halves[i]), (halves[i], rows - halves[i])

    def valid(rel):
        return (z + rel >= 0) & (z + rel < owners)

    def copies(i, rel):
        first, second = parts(i)
        e, xn, yn, dg, sb = place.e, place.xnb, place.ynb, place.diag, place.sib
        return {
            XS: lambda: go(i, rel, XS, source(i, rel), block(i, rel, e), xn),
            YS: lambda: go(i, rel, YS, source(i, rel), block(i, rel, e), yn),
            FA: lambda: go(i, rel, FA, block(i, rel, xn, first), block(i, rel, xn, first), yn),
            FB: lambda: go(i, rel, FB, block(i, rel, yn, second), block(i, rel, yn, second), xn),
            S0: lambda: go(i, rel, S0, source(i, rel), block(i, rel, e), sb),
            S1: lambda: go(i, rel, S1, block(i, rel, xn), block(i, rel, xn), sb),
            S2: lambda: go(i, rel, S2, block(i, rel, yn), block(i, rel, yn), sb),
            S3: lambda: go(i, rel, S3, block(i, rel, dg), block(i, rel, dg), sb),
        }

    def got(i, rel, kind, e, part=None):
        ref = block(i, rel, e, part)
        pltpu.make_async_remote_copy(
            src_ref=ref, dst_ref=ref, send_sem=send.at[i, sem(rel), min(kind, UP)], recv_sem=recv.at[i, sem(rel), min(kind, UP)],
            device_id=(z, place.sib), device_id_type=MESH).wait_recv()

    def stage_z(rel):
        @pl.when(valid(rel))
        def _():
            for i in range(n):
                if rel != 0 and not lines[i]:
                    continue
                if rel != 0:
                    got(i, rel, UP, place.e)
                if lines[i] and rel <= 0 and rel > 1 - owners:
                    @pl.when(z < owners - 1)
                    def _():
                        go(i, rel, UP, source(i, rel), block(i, rel, place.e), place.e, 1).start()
                if lines[i] and rel >= 0 and rel < owners - 1:
                    @pl.when(z > 0)
                    def _():
                        go(i, rel, DOWN, source(i, rel), block(i, rel, place.e), place.e, -1).start()
                c = copies(i, rel)
                c[XS]().start()
                c[YS]().start()
                c[S0]().start()

    def each(rel, fn):
        @pl.when(valid(rel))
        def _():
            for i in range(n):
                if rel == 0 or lines[i]:
                    fn(i, rel, copies(i, rel))

    def xy(i, rel, c):
        got(i, rel, XS, place.xnb)
        c[FA]().start()
        c[S1]().start()
        got(i, rel, YS, place.ynb)
        c[FB]().start()
        c[S2]().start()

    def dg(i, rel, c):
        first, second = parts(i)
        got(i, rel, FA, place.diag, first)
        got(i, rel, FB, place.diag, second)
        c[S3]().start()

    def end(i, rel, c):
        for k, e in ((S0, place.sib),):
            got(i, rel, S0, place.sib)
        got(i, rel, S1, place.xnb + place.sib - place.e)
        got(i, rel, S2, place.ynb + place.sib - place.e)
        got(i, rel, S3, place.diag + place.sib - place.e)
        for k in (XS, YS, FA, FB, S0, S1, S2, S3):
            c[k]().wait_send()
        if lines[i] and rel <= 0 and rel > 1 - owners:
            @pl.when(z < owners - 1)
            def _():
                go(i, rel, UP, source(i, rel), block(i, rel, place.e), place.e, 1).wait_send()
        if lines[i] and rel >= 0 and rel < owners - 1:
            @pl.when(z > 0)
            def _():
                go(i, rel, DOWN, source(i, rel), block(i, rel, place.e), place.e, -1).wait_send()

    rels = [0] + [s * d for d in range(1, owners) for s in (-1, 1)]
    waves = [[0]] + [[-d, d] for d in range(1, owners)]
    for w in range(owners + 3):
        if w < owners:
            for r in waves[w]:
                stage_z(r)
        if 0 <= w - 1 < owners:
            for r in waves[w - 1]:
                each(r, xy)
        if 0 <= w - 2 < owners:
            for r in waves[w - 2]:
                each(r, dg)
    for cp in copies_own:
        cp.wait()
    for r in rels:
        each(r, end)


def gather(arrays, lines, halves, owners, group, cid):
    outs = [jax.ShapeDtypeStruct((a.shape[0] * (owners if l else 1) * group,) + a.shape[1:], a.dtype) for a, l in zip(arrays, lines)]
    n = len(arrays)
    any_spec = pl.BlockSpec(memory_space=pl.ANY)
    return pl.pallas_call(
        functools.partial(gather_kernel, owners, group, lines, halves),
        out_shape=outs, in_specs=[any_spec] * n, out_specs=[any_spec] * n,
        scratch_shapes=[pltpu.SemaphoreType.DMA((n, 2 * owners - 1, 10)), pltpu.SemaphoreType.DMA((n, 2 * owners - 1, 9)), pltpu.SemaphoreType.DMA((n,))],
        compiler_params=pltpu.CompilerParams(collective_id=cid, has_side_effects=True),
    )(*arrays)


G = 16
(LOAD, SIB, Y0, Y1, X0, X1, X2, Y2, UP, DOWN) = range(10)


def scatter_kernel(owners, lines, subs, *refs):
    n = len(lines)
    ins, outs, scratch = refs[:n], refs[n : 2 * n], refs[2 * n :]
    send, recv = scratch[6 * n :]
    place = Place()
    z = place.z
    chips = {k: e // 2 for k, e in (("me", place.e), ("xn", place.xnb), ("yn", place.ynb), ("dg", place.diag))}

    class Item:
        def __init__(self, i, rel, sub):
            self.i, self.rel = i, rel
            self.line = lines[i]
            self.own, self.sib, self.first, self.second, self.up, self.down = scratch[6 * i : 6 * i + 6]
            groups, _, wide = ins[i].shape[3:]
            self.groups, self.half = groups, (groups + 1) // 2
            self.at = z + rel if self.line else 0
            width = wide // subs[i]
            self.cols = pl.ds(sub * width, width)
            self.slot = rel + owners - 1 if self.line else sub
            self.valid = (z + rel >= 0) & (z + rel < owners)

        def piece(self, ref, *lead):
            return ref.at[(*lead, slice(None), self.cols)]

        def rows(self, second):
            return pl.ds(self.half, self.groups - self.half) if second else pl.ds(0, self.half)

        def copy(self, kind, src, dst, to, dz=0):
            there = self.slot - dz if self.line else self.slot
            return pltpu.make_async_remote_copy(
                src_ref=src, dst_ref=dst,
                send_sem=send.at[self.i, self.slot, kind], recv_sem=recv.at[self.i, there, kind],
                device_id=(z + dz, to), device_id_type=MESH)

        def load(self):
            return pltpu.make_async_copy(
                self.piece(ins[self.i], self.at, slice(None), place.core, slice(None)),
                self.piece(self.own, self.at, slice(None), slice(None)),
                send.at[self.i, self.slot, LOAD])

        def to_sib(self):
            return self.copy(SIB, self.piece(ins[self.i], self.at, slice(None), 1 - place.core, slice(None)),
                             self.piece(self.sib, self.at, slice(None), slice(None)), place.sib)

        def hop1(self, axis, other):
            second = axis == 1
            to = place.xnb if axis else place.ynb
            whose = chips["dg"] if other else chips["xn" if axis else "yn"]
            size = self.groups - self.half if second else self.half
            return self.copy((X0, X1)[other] if axis else (Y0, Y1)[other],
                             self.piece(self.own, self.at, whose, self.rows(second)),
                             self.piece(self.first, self.at, axis, other, pl.ds(0, size)), to)

        def hop2(self, second):
            to = place.ynb if second else place.xnb
            whose = chips["yn" if second else "xn"]
            size = self.groups - self.half if second else self.half
            return self.copy(Y2 if second else X2,
                             self.piece(self.own, self.at, whose, self.rows(second)),
                             self.piece(self.second, self.at, int(second), pl.ds(0, size)), to)

        def along(self, up):
            return self.copy(UP if up else DOWN, self.piece(self.own, self.at, chips["me"], slice(None)),
                             self.piece(self.up if up else self.down, self.at, slice(None)), place.e, 1 if up else -1)

        def arrive_along(self, up):
            buf = self.piece(self.up if up else self.down, self.at, slice(None))
            pltpu.make_async_remote_copy(
                src_ref=buf, dst_ref=buf, send_sem=send.at[self.i, self.slot, UP if up else DOWN],
                recv_sem=recv.at[self.i, self.slot, UP if up else DOWN],
                device_id=(z, place.sib), device_id_type=MESH).wait_recv()

        def add(self, whose, start, count, terms, keep=None):
            own, cols, at = self.own, self.cols, self.at

            @pl.loop(0, count)
            def _(g):
                total = own[at, whose, start + g, :, cols].astype(F32)
                for ref, lead in terms:
                    total = total + ref[(*lead, g, slice(None), cols)].astype(F32)
                if keep is None:
                    own[at, whose, start + g, :, cols] = total.astype(BF)
                else:
                    keep[start + g, :, cols] = total

        def stage1(self):
            self.load().wait()
            self.to_sib().wait_recv()

            @pl.loop(0, 4)
            def _(chip):
                self.add(chip, 0, self.groups, [(self.sib, (self.at, chip))])
            for axis in (0, 1):
                for other in (1, 0):
                    self.hop1(axis, other).start()

        def stage2(self):
            self.hop1(0, 1).wait_recv()
            self.add(chips["xn"], 0, self.half, [(self.first, (self.at, 0, 1))])
            self.hop2(False).start()
            self.hop1(1, 1).wait_recv()
            self.add(chips["yn"], self.half, self.groups - self.half, [(self.first, (self.at, 1, 1))])
            self.hop2(True).start()

        def stage3(self):
            for axis in (0, 1):
                self.hop1(axis, 0).wait_recv()
                self.hop2(axis == 1).wait_recv()
            out = outs[self.i]
            rel = self.rel
            last = None if self.line and rel != 0 else out
            for half in (0, 1):
                start = self.half if half else 0
                size = self.groups - self.half if half else self.half
                self.add(chips["me"], start, size, [(self.first, (self.at, half, 0)), (self.second, (self.at, half))], last)
            if not self.line:
                return
            for up in (True, False):
                if (rel >= 0) if up else (rel <= 0):
                    @pl.when((z > 0) if up else (z < owners - 1))
                    def _():
                        self.arrive_along(up)
                        buf = self.up if up else self.down

                        @pl.loop(0, self.groups)
                        def _(g):
                            more = buf[self.at, g, :, self.cols].astype(F32)
                            if rel == 0:
                                out[g, :, self.cols] += more
                            else:
                                where = (self.at, chips["me"], g, slice(None), self.cols)
                                self.own[where] = (self.own[where].astype(F32) + more).astype(BF)
            if rel != 0:
                self.along(rel > 0).start()

        def end(self):
            self.to_sib().wait_send()
            for axis in (0, 1):
                for other in (0, 1):
                    self.hop1(axis, other).wait_send()
                self.hop2(axis == 1).wait_send()
            if self.line and self.rel != 0:
                self.along(self.rel > 0).wait_send()

    waves = []
    for d in range(owners - 1, 0, -1):
        waves.append([Item(i, rel, 0) for rel in (d, -d) for i in range(n) if lines[i]])
    waves.append([Item(i, 0, 0) for i in range(n) if lines[i]])
    waves = [w for w in waves if w]
    for i in range(n):
        if not lines[i]:
            waves += [[Item(i, 0, sub)] for sub in range(subs[i])]

    def run(wave, name):
        for item in wave:
            if item.line and item.rel != 0:
                pl.when(item.valid)(getattr(item, name))
            else:
                getattr(item, name)()

    def begin(item):
        item.load().start()

    for wave in waves:
        for item in wave:
            item.begin = functools.partial(begin, item)
            item.begin_sib = functools.partial(lambda it: it.to_sib().start(), item)
    for wave in waves:
        run(wave, "begin")
    greet(place, any(lines), owners)
    for wave in waves:
        run(wave, "begin_sib")
    for w in range(len(waves) + 2):
        for lag, name in enumerate(("stage1", "stage2", "stage3")):
            if 0 <= w - lag < len(waves):
                run(waves[w - lag], name)
    for wave in waves:
        run(wave, "end")


def scatter(arrays, lines, subs, owners, cid):
    n = len(arrays)
    scratch, outs = [], []
    for a, line in zip(arrays, lines):
        zs = a.shape[0]
        groups, _, wide = a.shape[3:]
        half = (groups + 1) // 2
        zl = zs if line else 1
        lg = groups if line else 1
        scratch += [
            pltpu.VMEM((zs, 4, groups, G, wide), BF),
            pltpu.VMEM((zs, 4, groups, G, wide), BF),
            pltpu.VMEM((zs, 2, 2, half, G, wide), BF),
            pltpu.VMEM((zs, 2, half, G, wide), BF),
            pltpu.VMEM((zl, lg, G, wide if line else 128), BF),
            pltpu.VMEM((zl, lg, G, wide if line else 128), BF),
        ]
        outs.append(jax.ShapeDtypeStruct((groups, G, wide), F32))
    slots = max([2 * owners - 1 if any(lines) else 1] + list(subs))
    scratch += [pltpu.SemaphoreType.DMA((n, slots, 10)), pltpu.SemaphoreType.DMA((n, slots, 10))]
    return pl.pallas_call(
        functools.partial(scatter_kernel, owners, lines, subs),
        out_shape=outs,
        in_specs=[pl.BlockSpec(memory_space=pl.ANY)] * n,
        out_specs=[pl.BlockSpec(memory_space=pltpu.VMEM)] * n,
        scratch_shapes=scratch,
        compiler_params=pltpu.CompilerParams(collective_id=cid, has_side_effects=True, vmem_limit_bytes=60 * 1024 * 1024),
    )(*arrays)


def moe_kernel(
    steps,
    slots,
    chunk,
    m_ref,
    g_ref,
    member_ref,
    router_ref,
    order_ref,
    mine_ref,
    weights_ref,
    moe_ref,
    drow_ref,
    grads_ref,
    grouter_ref,
    router_s,
    gate_s,
    hg_s,
    dpre_s,
    mt_s,
    gt_s,
    gup_s,
    gdn_s,
    gr_s,
):
    step = pl.program_id(0)
    owners, _, share, units = weights_ref.shape
    per = chunk // F

    @pl.when(step == 0)
    def _():
        gup_s[...] = jnp.zeros_like(gup_s)
        gdn_s[...] = jnp.zeros_like(gdn_s)
        gr_s[...] = jnp.zeros_like(gr_s)
        router_s[...] = dot_nn(router_ref[...], order_ref[...]).astype(BF)

    mt_s[...] = m_ref[...].T
    gt_s[...] = g_ref[...].T
    sig = jax.nn.sigmoid(dot_nn(m_ref[...], router_s[...]))
    mask = dot_nn(member_ref[...], mine_ref[...])
    gate_s[...] = sig * mask
    root = math.sqrt(2.0 / math.pi)
    cube = 0.044715
    lane = lax.broadcasted_iota(jnp.int32, (1, F), 1)
    d_gate = jnp.zeros(gate_s.shape, F32)
    for c in range(units // chunk):
        cols = pl.ds(c * chunk, chunk)
        pre_all = dot_nn(m_ref[:, :share], weights_ref[0, 0, :, cols])
        back_all = dot_nn(g_ref[:, :share], weights_ref[0, 1, :, cols])
        for o in range(1, owners):
            part = pl.ds(o * share, share)
            pre_all += dot_nn(m_ref[:, part], weights_ref[o, 0, :, cols])
            back_all += dot_nn(g_ref[:, part], weights_ref[o, 1, :, cols])
        for j in range(per):
            slot = c * per + j
            part = slice(j * F, (j + 1) * F)
            pre = pre_all[:, part]
            back = back_all[:, part]
            square = pre * pre
            th = jnp.tanh(root * pre * (1.0 + cube * square))
            half = 0.5 * (1.0 + th)
            slope = half + (0.5 * root) * pre * (1.0 - th * th) * (1.0 + (3.0 * cube) * square)
            hidden = (pre * half).astype(BF).astype(F32)
            gate = gate_s[:, slot : slot + 1]
            d_one = jnp.sum(hidden * back, axis=1, keepdims=True)
            d_gate = d_gate + d_one * (lane == slot).astype(F32)
            where = pl.ds(slot * F, F)
            hg_s[:, where] = (gate * hidden).astype(BF)
            dpre_s[:, where] = (slope * (gate * back)).astype(BF)
    dlog = (d_gate * mask * sig * (1.0 - sig)).astype(BF)
    gr_s[...] += dot_nn(mt_s[...], dot_nt(dlog, order_ref[...]).astype(BF))
    for o in range(owners):
        where = pl.ds(o * share, share)
        moe_ref[:, where] = dot_nt(hg_s[...], weights_ref[o, 1]).astype(BF)
        drow_ref[:, where] = (
            dot_nt(dpre_s[...], weights_ref[o, 0]) + dot_nt(dlog, router_s[where, :])
        ).astype(BF)
        gup_s[where, :] += dot_nn(mt_s[where, :], dpre_s[...])
        gdn_s[where, :] += dot_nn(gt_s[where, :], hg_s[...])

    @pl.when(step == steps - 1)
    def _():
        for o in range(owners):
            grads_ref[o, 0] = gup_s[pl.ds(o * share, share), :].astype(BF)
            grads_ref[o, 1] = gdn_s[pl.ds(o * share, share), :].astype(BF)
        grouter_ref[...] = gr_s[...].astype(BF)


def moe(rows, cots, member, packed, router_at, order, mine, weights):
    count = rows.shape[0]
    tile = 512
    owners, _, share, units = weights.shape
    slots = units // F
    steps = count // tile
    lanes = member.shape[1]
    row_spec = pl.BlockSpec((tile, D), lambda i: (i, 0))
    whole = pl.BlockSpec(memory_space=pltpu.VMEM)
    router_spec = pl.BlockSpec((D, lanes), lambda i: (0, router_at // lanes))
    return pl.pallas_call(
        functools.partial(moe_kernel, steps, slots, 512),
        grid=(steps,),
        in_specs=[
            row_spec,
            row_spec,
            pl.BlockSpec((tile, lanes), lambda i: (i, 0)),
            router_spec,
            whole,
            whole,
            whole,
        ],
        out_specs=[row_spec, row_spec, whole, whole],
        out_shape=[
            jax.ShapeDtypeStruct((count, D), BF),
            jax.ShapeDtypeStruct((count, D), BF),
            jax.ShapeDtypeStruct(weights.shape, BF),
            jax.ShapeDtypeStruct((D, lanes), BF),
        ],
        scratch_shapes=[
            pltpu.VMEM((D, F), BF),
            pltpu.VMEM((tile, F), F32),
            pltpu.VMEM((tile, units), BF),
            pltpu.VMEM((tile, units), BF),
            pltpu.VMEM((D, tile), BF),
            pltpu.VMEM((D, tile), BF),
            pltpu.VMEM((D, units), F32),
            pltpu.VMEM((D, units), F32),
            pltpu.VMEM((D, lanes), F32),
        ],
        compiler_params=pltpu.CompilerParams(vmem_limit_bytes=60 * 1024 * 1024),
        cost_estimate=pl.CostEstimate(
            flops=12 * count * D * units,
            bytes_accessed=count * D * 8 + D * units * 8,
            transcendentals=count * units,
        ),
    )(rows, cots, member, packed, order, mine, weights)


def picked_mask(picks, number):
    return jnp.sum(
        (picks[..., None] == jnp.arange(number, dtype=jnp.int32)).astype(F32), axis=-2
    )


def layer_normed(inputs, gain_row):
    centred = inputs - jnp.mean(inputs, axis=-1, keepdims=True)
    variance = jnp.mean(centred * centred, axis=-1, keepdims=True)
    return centred * lax.rsqrt(variance + epsilon) * gain_row


def head_gates(select, value_mask, out_mask):
    row_count = value_mask.shape[0]
    value_gate = jax.nn.sigmoid(select[:, : H * NV]).reshape(row_count, H, NV) * value_mask
    out_gate = jax.nn.sigmoid(select[:, H * NV :]).reshape(row_count, H, NV) * out_mask
    return (value_gate, out_gate)


def dense_forward(tokens, live, lengths, picks, gain, qkv, select_w, heads):
    count = tokens.shape[0]
    seq = count // MB
    xf = tokens.astype(F32)
    value_mask = picked_mask(picks, NV)
    out_mask = value_mask * live[:, None, None]
    normed, norm_back = jax.vjp(layer_normed, xf, gain.astype(F32))
    normed_low = normed.astype(BF)
    query_key = dot_nn(normed_low, qkv[:, :QK]).astype(BF)
    values_all = dot_nn(tokens, qkv[:, QK:])
    select = dot_nn(tokens, select_w)
    (value_gate, out_gate), gate_back = jax.vjp(
        lambda logits_in: head_gates(logits_in, value_mask, out_mask), select
    )
    values_split = values_all.reshape(count, H, NV, HD)
    values_low = jnp.sum(value_gate[..., None] * values_split, axis=2).astype(BF)
    values_seq = values_low.reshape(MB, seq, H, HD)
    queries = query_key[:, : H * HD].reshape(MB, seq, H, HD)
    keys_all = query_key[:, H * HD :].reshape(MB, seq, H, HD)
    position = jnp.arange(seq, dtype=jnp.int32)
    scores = jnp.einsum("bihd,bjhd->bhij", queries, keys_all, preferred_element_type=F32) * HD ** (
        -0.5
    )
    allowed = (position[None, :] <= position[:, None])[None] & (
        position[None, None, :] < lengths[:, None, None]
    )
    masked = jnp.where(allowed[:, None], scores, -1e30)
    expo = jnp.exp(masked - jnp.max(masked, axis=-1, keepdims=True))
    attention = expo / jnp.sum(expo, axis=-1, keepdims=True)
    attended = jnp.einsum(
        "bhij,bjhd->bihd", attention.astype(BF), values_seq, preferred_element_type=F32
    ).reshape(count, H, HD)
    mixed_heads = (out_gate[..., None] * attended[:, :, None, :]).reshape(count, VAL).astype(BF)
    middle = xf + dot_nn(mixed_heads, heads)

    def backward(d_middle):
        d_branch = d_middle.astype(BF)
        grad_heads = dot_tn(mixed_heads, d_branch)
        d_mixed = dot_nt(d_branch, heads).reshape(count, H, NV, HD)
        d_attended = jnp.sum(out_gate[..., None] * d_mixed, axis=2).astype(BF)
        d_out_gate = jnp.sum(d_mixed * attended[:, :, None, :], axis=-1)
        d_att_seq = d_attended.reshape(MB, seq, H, HD)
        d_attention = jnp.einsum(
            "bihd,bjhd->bhij", d_att_seq, values_seq, preferred_element_type=F32
        )
        d_scores = (
            attention * (d_attention - jnp.sum(attention * d_attention, axis=-1, keepdims=True))
        ).astype(BF)
        d_values = (
            jnp.einsum(
                "bhij,bihd->bjhd", attention.astype(BF), d_att_seq, preferred_element_type=F32
            )
            .astype(BF)
            .reshape(count, H, HD)
        )
        d_queries = jnp.einsum(
            "bhij,bjhd->bihd", d_scores, keys_all, preferred_element_type=F32
        ) * HD ** (-0.5)
        d_keys = jnp.einsum(
            "bhij,bihd->bjhd", d_scores, queries, preferred_element_type=F32
        ) * HD ** (-0.5)
        d_query_key = jnp.concatenate(
            [d_queries.reshape(count, H * HD), d_keys.reshape(count, H * HD)], axis=1
        ).astype(BF)
        d_value_gate = jnp.sum(d_values[:, :, None, :] * values_split, axis=-1)
        d_values_all = (value_gate[..., None] * d_values[:, :, None, :]).reshape(count, VAL).astype(BF)
        d_select = gate_back((d_value_gate, d_out_gate))[0].astype(BF)
        grad_qk = dot_tn(normed_low, d_query_key)
        grad_val = dot_tn(tokens, d_values_all)
        grad_select = dot_tn(tokens, d_select)
        d_normed = dot_nt(d_query_key, qkv[:, :QK])
        d_norm_in, grad_gain = norm_back(d_normed)
        d_tokens = (
            d_middle
            + d_norm_in
            + dot_nt(d_values_all, qkv[:, QK:])
            + dot_nt(d_select, select_w)
        )
        return d_tokens, grad_gain, grad_qk, grad_val, grad_select, grad_heads

    return middle, backward


def body(
    tokens,
    cotangent,
    lengths,
    routes,
    head_choice,
    placement,
    gain_master,
    gain_moment,
    gain_average,
    qkv_master,
    qkv_moment,
    qkv_average,
    select_master,
    select_moment,
    select_average,
    router_master,
    router_moment,
    router_average,
    heads_out_master,
    heads_out_moment,
    heads_out_average,
    up_master,
    up_moment,
    up_average,
    down_master,
    down_moment,
    down_average,
):
    both = ("dp", "expert")
    owners = lax.axis_size("dp")
    group = lax.axis_size("expert")
    own_kernels = group == 8
    experts = placement.shape[0]
    slots = up_master.shape[0]
    units = slots * F
    seq = tokens.shape[1]
    count = MB * seq
    share = up_master.shape[1]
    mine = lax.axis_index("expert")
    lanes = -(-experts // 128) * 128

    own_rows = qkv_master.shape[0]
    wide = QK + VAL
    packed = jnp.concatenate(
        [
            qkv_master.astype(BF),
            router_master.astype(BF),
            jnp.zeros((own_rows, lanes - experts), BF),
            select_master.astype(BF),
            gain_master.astype(BF)[:, None],
            jnp.zeros((own_rows, 127 - SEL), BF),
        ],
        axis=1,
    )
    heads_low = heads_out_master.astype(BF)

    def flat(weights):
        return weights.astype(BF).transpose(1, 0, 2).reshape(share, units)

    experts_low = jnp.concatenate([flat(up_master), flat(down_master)], axis=0)
    experts_all = lax.all_gather(experts_low, "dp", axis=0, tiled=False)
    weights = experts_all.reshape(owners, 2, share, units)

    flat_tokens = tokens.reshape(count, D)
    flat_cots = cotangent.reshape(count, D)
    live = (jnp.arange(seq, dtype=jnp.int32)[None, :] < lengths).astype(F32).reshape(count)
    lane_ids = jnp.arange(lanes, dtype=jnp.int32)
    named = jnp.sum(
        (routes.reshape(count, TOPK)[..., None] == lane_ids).astype(F32), axis=1
    ) * live[:, None]
    padded = jnp.pad(placement, (0, lanes - experts), constant_values=-1)
    perm = (padded[:, None] == lane_ids[None, :]).astype(BF)
    member = dot_nn(named.astype(BF), perm).astype(BF)
    own_lane = jnp.arange(F, dtype=jnp.int32)[None, :]
    mine_sel = (((lane_ids[:, None] - mine * slots) == own_lane) & (own_lane < slots)).astype(BF)
    order_mine = (
        ((padded[:, None] - mine * slots) == own_lane) & (own_lane < slots) & (padded[:, None] >= 0)
    ).astype(BF)

    if own_kernels:
        packed_all, heads, cots_all, member_all = gather(
            (packed, heads_low, flat_cots, member),
            (True, True, False, False),
            (own_rows // 2, 48, count // 2, count // 2),
            owners,
            group,
            0,
        )
    else:
        packed_all = lax.all_gather(packed, both, axis=0, tiled=True)
        heads = lax.all_gather(heads_low, both, axis=0, tiled=True)
        cots_all = lax.all_gather(flat_cots, "expert", axis=0, tiled=True)
        member_all = lax.all_gather(member, "expert", axis=0, tiled=True)
    qkv = packed_all[:, :wide]
    select_w = packed_all[:, wide + lanes : wide + lanes + SEL]
    gain = packed_all[:, wide + lanes + SEL]

    middle, backward = dense_forward(
        flat_tokens,
        live,
        lengths[:, 0],
        head_choice.reshape(count, H, -1),
        gain,
        qkv,
        select_w,
        heads,
    )
    middle_low = middle.astype(BF)
    if own_kernels:
        (rows_all,) = gather((middle_low,), (False,), (count // 2,), owners, group, 1)
    else:
        rows_all = lax.all_gather(middle_low, "expert", axis=0, tiled=True)
    moe_part, drow_part, expert_grads, grad_router = moe(
        rows_all, cots_all, member_all, packed_all, wide, order_mine, mine_sel, weights
    )
    expert_sum = lax.psum_scatter(
        expert_grads.reshape(owners * 2 * share, units), "dp", scatter_dimension=0, tiled=True
    ).astype(F32)
    if own_kernels:
        (d_from_rows,) = scatter((drow_part.reshape(1, 4, 2, count // G, G, D),), (False,), (4,), owners, 2)
        d_from_rows = d_from_rows.reshape(count, D)
    else:
        d_from_rows = lax.psum_scatter(drow_part, "expert", scatter_dimension=0, tiled=True).astype(F32)
    moe_sum = lax.psum_scatter(moe_part, "expert", scatter_dimension=0, tiled=True).astype(F32)
    mixed = (middle + moe_sum).astype(BF)

    d_middle = flat_cots.astype(F32) + d_from_rows
    d_tokens, grad_gain, grad_qk, grad_val, grad_select, grad_heads = backward(d_middle)
    small_grads = jnp.concatenate(
        [
            grad_router,
            grad_select.astype(BF),
            grad_gain.astype(BF)[:, None],
            jnp.zeros((D, 127 - SEL), BF),
        ],
        axis=1,
    )
    dense_grads = (grad_qk.astype(BF), grad_val.astype(BF), small_grads, grad_heads.astype(BF))
    if own_kernels:
        sums = scatter(
            tuple(g.reshape(owners, 4, 2, -1, G, g.shape[1]) for g in dense_grads),
            (True,) * 4,
            (1,) * 4,
            owners,
            3,
        )
        qk_sum, val_sum, small_sum, heads_sum = (s.reshape(-1, s.shape[2]) for s in sums)
    else:
        qk_sum, val_sum, small_sum, heads_sum = (
            lax.psum_scatter(g, both, scatter_dimension=0, tiled=True).astype(F32)
            for g in dense_grads
        )
    qkv_sum = jnp.concatenate([qk_sum, val_sum], axis=1)
    router_sum = small_sum[:, :experts]
    select_sum = small_sum[:, lanes : lanes + SEL]
    gain_sum = small_sum[:, lanes + SEL]
    up_sum = expert_sum[:share].reshape(share, slots, F).transpose(1, 0, 2)
    down_sum = expert_sum[share:].reshape(share, slots, F).transpose(1, 0, 2)

    rates = step_rates(count * owners * group, experts)
    outs = (
        update_weight(gain_master, gain_moment, gain_average, gain_sum, rates[0])
        + update_weight(qkv_master, qkv_moment, qkv_average, qkv_sum, rates[1])
        + update_weight(select_master, select_moment, select_average, select_sum, rates[2])
        + update_weight(router_master, router_moment, router_average, router_sum, rates[3])
        + update_weight(heads_out_master, heads_out_moment, heads_out_average, heads_sum, rates[4])
        + update_weight(up_master, up_moment, up_average, up_sum, rates[5])
        + update_weight(down_master, down_moment, down_average, down_sum, rates[6])
    )
    return (mixed.reshape(tokens.shape), d_tokens.reshape(tokens.shape)) + outs


def solution(mesh):
    rows = P(None, ("dp", "expert"), None)
    flat = P(("dp", "expert"))
    dense = P(("dp", "expert"), None)
    expert = P("expert", "dp", None)
    in_specs = (
        rows,
        rows,
        P(None, ("dp", "expert")),
        rows,
        P(None, ("dp", "expert"), None, None),
        P(),
        *((flat,) * 3),
        *((dense,) * 12),
        *((expert,) * 6),
    )
    out_specs = (rows, rows, *((flat,) * 4), *((dense,) * 16), *((expert,) * 8))
    return jax.shard_map(body, mesh=mesh, in_specs=in_specs, out_specs=out_specs, check_vma=False)
```

```python
import functools
import math

import jax
import jax.numpy as jnp
from jax import lax
from jax.experimental import pallas as pl
from jax.experimental.pallas import tpu as pltpu
from jax.sharding import PartitionSpec as P

D = 1024
H = 4
HD = 128
NV = 5
F = 128
TOPK = 16
MB = 2
QK = 2 * H * HD
VAL = H * NV * HD
SEL = 2 * H * NV

momentum_decay = 0.9
average_decay = 0.5
rate_factor = 0.4
epsilon = 1e-05
BF = jnp.bfloat16
F32 = jnp.float32


def step_rates(total_tokens, experts):
    root_tokens = math.sqrt(total_tokens)
    expert_share = math.sqrt(TOPK / experts)
    spread_list = (
        0.3,
        D ** (-0.5),
        (2 * D) ** (-0.5),
        (9 * D) ** (-0.5),
        0.5,
        D ** (-0.5),
        (4 * F) ** (-0.5),
    )
    gradient_list = (1.0, 1.0, 3.0, 2.0 * expert_share, 0.1, 0.5 * expert_share, 0.4 * expert_share)
    return tuple(
        rate_factor * spread_value / (gradient_value * root_tokens)
        for spread_value, gradient_value in zip(spread_list, gradient_list)
    )


def update_weight(master, moment, average, gradient, step_size):
    new_moment = momentum_decay * moment + gradient
    new_weight = master - step_size * (gradient + momentum_decay * new_moment)
    new_average = average_decay * average + (1.0 - average_decay) * new_weight
    return (new_moment, new_average, new_weight, new_weight.astype(BF))


def dot_nt(a, b):
    return lax.dot_general(a, b, (((1,), (1,)), ((), ())), preferred_element_type=F32)


def dot_tn(a, b):
    return lax.dot_general(a, b, (((0,), (0,)), ((), ())), preferred_element_type=F32)


def dot_nn(a, b):
    return jnp.dot(a, b, preferred_element_type=F32)


MESH = pl.DeviceIdType.MESH


class Place:
    def __init__(self):
        self.z = lax.axis_index("dp")
        self.e = lax.axis_index("expert")
        core = self.e % 2
        x = (self.e // 2) % 2
        y = self.e // 4
        self.sib = self.e + 1 - 2 * core
        self.xnb = self.e + 2 - 4 * x
        self.ynb = self.e + 4 - 8 * y
        self.diag = self.xnb + 4 - 8 * y
        self.core, self.x, self.y = core, x, y


def greet(place, line, owners):
    barrier = pltpu.get_barrier_semaphore()
    z = place.z
    for e in (place.sib, place.xnb, place.ynb):
        pl.semaphore_signal(barrier, inc=1, device_id=(z, e), device_id_type=MESH)
    peers = 3
    if line:

        @pl.when(z > 0)
        def _():
            pl.semaphore_signal(barrier, inc=1, device_id=(z - 1, place.e), device_id_type=MESH)

        @pl.when(z < owners - 1)
        def _():
            pl.semaphore_signal(barrier, inc=1, device_id=(z + 1, place.e), device_id_type=MESH)

        peers = peers + (z + owners - 1) // owners + (2 * owners - 2 - z) // owners
    pl.semaphore_wait(barrier, peers)


XS, YS, FA, FB, S0, S1, S2, S3, UP, DOWN = range(10)

def gather_kernel(owners, group, lines, halves, *refs):
    n = len(lines)
    ins, outs, (send, recv, own) = refs[:n], refs[n : 2 * n], refs[2 * n :]
    place = Place()
    z = place.z
    copies_own = []
    for i in range(n):
        rows = ins[i].shape[0]
        slot = (z * group + place.e) if lines[i] else place.e
        cp = pltpu.make_async_copy(ins[i], outs[i].at[pl.ds(slot * rows, rows)], own.at[i])
        cp.start()
        copies_own.append(cp)
    greet(place, any(lines), owners)

    def block(i, rel, e, part=None):
        rows = ins[i].shape[0]
        slot = ((z + rel) * group + e) if lines[i] else e
        start, size = (0, rows) if part is None else part
        return outs[i].at[pl.ds(slot * rows + start, size)]

    def source(i, rel, part=None):
        if rel == 0:
            return ins[i] if part is None else ins[i].at[pl.ds(*part)]
        return block(i, rel, place.e, part)

    def sem(rel):
        return rel + owners - 1

    def go(i, rel, kind, src, dst, to_e, dz=0):
        return pltpu.make_async_remote_copy(
            src_ref=src, dst_ref=dst, send_sem=send.at[i, sem(rel), kind],
            recv_sem=recv.at[i, sem(rel - dz), min(kind, UP)],
            device_id=(z + dz, to_e), device_id_type=MESH)

    def parts(i):
        rows = ins[i].shape[0]
        return (0, halves[i]), (halves[i], rows - halves[i])

    def valid(rel):
        return (z + rel >= 0) & (z + rel < owners)

    def copies(i, rel):
        first, second = parts(i)
        e, xn, yn, dg, sb = place.e, place.xnb, place.ynb, place.diag, place.sib
        return {
            XS: lambda: go(i, rel, XS, source(i, rel), block(i, rel, e), xn),
            YS: lambda: go(i, rel, YS, source(i, rel), block(i, rel, e), yn),
            FA: lambda: go(i, rel, FA, block(i, rel, xn, first), block(i, rel, xn, first), yn),
            FB: lambda: go(i, rel, FB, block(i, rel, yn, second), block(i, rel, yn, second), xn),
            S0: lambda: go(i, rel, S0, source(i, rel), block(i, rel, e), sb),
            S1: lambda: go(i, rel, S1, block(i, rel, xn), block(i, rel, xn), sb),
            S2: lambda: go(i, rel, S2, block(i, rel, yn), block(i, rel, yn), sb),
            S3: lambda: go(i, rel, S3, block(i, rel, dg), block(i, rel, dg), sb),
        }

    def got(i, rel, kind, e, part=None):
        ref = block(i, rel, e, part)
        pltpu.make_async_remote_copy(
            src_ref=ref, dst_ref=ref, send_sem=send.at[i, sem(rel), min(kind, UP)], recv_sem=recv.at[i, sem(rel), min(kind, UP)],
            device_id=(z, place.sib), device_id_type=MESH).wait_recv()

    def stage_z(rel):
        @pl.when(valid(rel))
        def _():
            for i in range(n):
                if rel != 0 and not lines[i]:
                    continue
                if rel != 0:
                    got(i, rel, UP, place.e)
                if lines[i] and rel <= 0 and rel > 1 - owners:
                    @pl.when(z < owners - 1)
                    def _():
                        go(i, rel, UP, source(i, rel), block(i, rel, place.e), place.e, 1).start()
                if lines[i] and rel >= 0 and rel < owners - 1:
                    @pl.when(z > 0)
                    def _():
                        go(i, rel, DOWN, source(i, rel), block(i, rel, place.e), place.e, -1).start()
                c = copies(i, rel)
                c[XS]().start()
                c[YS]().start()
                c[S0]().start()

    def each(rel, fn):
        @pl.when(valid(rel))
        def _():
            for i in range(n):
                if rel == 0 or lines[i]:
                    fn(i, rel, copies(i, rel))

    def xy(i, rel, c):
        got(i, rel, XS, place.xnb)
        c[FA]().start()
        c[S1]().start()
        got(i, rel, YS, place.ynb)
        c[FB]().start()
        c[S2]().start()

    def dg(i, rel, c):
        first, second = parts(i)
        got(i, rel, FA, place.diag, first)
        got(i, rel, FB, place.diag, second)
        c[S3]().start()

    def end(i, rel, c):
        for k, e in ((S0, place.sib),):
            got(i, rel, S0, place.sib)
        got(i, rel, S1, place.xnb + place.sib - place.e)
        got(i, rel, S2, place.ynb + place.sib - place.e)
        got(i, rel, S3, place.diag + place.sib - place.e)
        for k in (XS, YS, FA, FB, S0, S1, S2, S3):
            c[k]().wait_send()
        if lines[i] and rel <= 0 and rel > 1 - owners:
            @pl.when(z < owners - 1)
            def _():
                go(i, rel, UP, source(i, rel), block(i, rel, place.e), place.e, 1).wait_send()
        if lines[i] and rel >= 0 and rel < owners - 1:
            @pl.when(z > 0)
            def _():
                go(i, rel, DOWN, source(i, rel), block(i, rel, place.e), place.e, -1).wait_send()

    rels = [0] + [s * d for d in range(1, owners) for s in (-1, 1)]
    waves = [[0]] + [[-d, d] for d in range(1, owners)]
    for w in range(owners + 3):
        if w < owners:
            for r in waves[w]:
                stage_z(r)
        if 0 <= w - 1 < owners:
            for r in waves[w - 1]:
                each(r, xy)
        if 0 <= w - 2 < owners:
            for r in waves[w - 2]:
                each(r, dg)
    for cp in copies_own:
        cp.wait()
    for r in rels:
        each(r, end)


def gather(arrays, lines, halves, owners, group, cid):
    outs = [jax.ShapeDtypeStruct((a.shape[0] * (owners if l else 1) * group,) + a.shape[1:], a.dtype) for a, l in zip(arrays, lines)]
    n = len(arrays)
    any_spec = pl.BlockSpec(memory_space=pl.ANY)
    return pl.pallas_call(
        functools.partial(gather_kernel, owners, group, lines, halves),
        out_shape=outs, in_specs=[any_spec] * n, out_specs=[any_spec] * n,
        scratch_shapes=[pltpu.SemaphoreType.DMA((n, 2 * owners - 1, 10)), pltpu.SemaphoreType.DMA((n, 2 * owners - 1, 9)), pltpu.SemaphoreType.DMA((n,))],
        compiler_params=pltpu.CompilerParams(collective_id=cid, has_side_effects=True),
    )(*arrays)


G = 16
(LOAD, SIB, Y0, Y1, X0, X1, X2, Y2, UP, DOWN) = range(10)


def scatter_kernel(owners, lines, subs, *refs):
    n = len(lines)
    ins, outs, scratch = refs[:n], refs[n : 2 * n], refs[2 * n :]
    send, recv = scratch[6 * n :]
    place = Place()
    z = place.z
    chips = {k: e // 2 for k, e in (("me", place.e), ("xn", place.xnb), ("yn", place.ynb), ("dg", place.diag))}

    class Item:
        def __init__(self, i, rel, sub):
            self.i, self.rel = i, rel
            self.line = lines[i]
            self.own, self.sib, self.first, self.second, self.up, self.down = scratch[6 * i : 6 * i + 6]
            groups, _, wide = ins[i].shape[3:]
            self.groups, self.half = groups, (groups + 1) // 2
            self.at = z + rel if self.line else 0
            width = wide // subs[i]
            self.cols = pl.ds(sub * width, width)
            self.slot = rel + owners - 1 if self.line else sub
            self.valid = (z + rel >= 0) & (z + rel < owners)

        def piece(self, ref, *lead):
            return ref.at[(*lead, slice(None), self.cols)]

        def rows(self, second):
            return pl.ds(self.half, self.groups - self.half) if second else pl.ds(0, self.half)

        def copy(self, kind, src, dst, to, dz=0):
            there = self.slot - dz if self.line else self.slot
            return pltpu.make_async_remote_copy(
                src_ref=src, dst_ref=dst,
                send_sem=send.at[self.i, self.slot, kind], recv_sem=recv.at[self.i, there, kind],
                device_id=(z + dz, to), device_id_type=MESH)

        def load(self):
            return pltpu.make_async_copy(
                self.piece(ins[self.i], self.at, slice(None), place.core, slice(None)),
                self.piece(self.own, self.at, slice(None), slice(None)),
                send.at[self.i, self.slot, LOAD])

        def to_sib(self):
            return self.copy(SIB, self.piece(ins[self.i], self.at, slice(None), 1 - place.core, slice(None)),
                             self.piece(self.sib, self.at, slice(None), slice(None)), place.sib)

        def hop1(self, axis, other):
            second = axis == 1
            to = place.xnb if axis else place.ynb
            whose = chips["dg"] if other else chips["xn" if axis else "yn"]
            size = self.groups - self.half if second else self.half
            return self.copy((X0, X1)[other] if axis else (Y0, Y1)[other],
                             self.piece(self.own, self.at, whose, self.rows(second)),
                             self.piece(self.first, self.at, axis, other, pl.ds(0, size)), to)

        def hop2(self, second):
            to = place.ynb if second else place.xnb
            whose = chips["yn" if second else "xn"]
            size = self.groups - self.half if second else self.half
            return self.copy(Y2 if second else X2,
                             self.piece(self.own, self.at, whose, self.rows(second)),
                             self.piece(self.second, self.at, int(second), pl.ds(0, size)), to)

        def along(self, up):
            return self.copy(UP if up else DOWN, self.piece(self.own, self.at, chips["me"], slice(None)),
                             self.piece(self.up if up else self.down, self.at, slice(None)), place.e, 1 if up else -1)

        def arrive_along(self, up):
            buf = self.piece(self.up if up else self.down, self.at, slice(None))
            pltpu.make_async_remote_copy(
                src_ref=buf, dst_ref=buf, send_sem=send.at[self.i, self.slot, UP if up else DOWN],
                recv_sem=recv.at[self.i, self.slot, UP if up else DOWN],
                device_id=(z, place.sib), device_id_type=MESH).wait_recv()

        def add(self, whose, start, count, terms, keep=None):
            own, cols, at = self.own, self.cols, self.at

            @pl.loop(0, count)
            def _(g):
                total = own[at, whose, start + g, :, cols].astype(F32)
                for ref, lead in terms:
                    total = total + ref[(*lead, g, slice(None), cols)].astype(F32)
                if keep is None:
                    own[at, whose, start + g, :, cols] = total.astype(BF)
                else:
                    keep[start + g, :, cols] = total

        def stage1(self):
            self.load().wait()
            self.to_sib().wait_recv()

            @pl.loop(0, 4)
            def _(chip):
                self.add(chip, 0, self.groups, [(self.sib, (self.at, chip))])
            for axis in (0, 1):
                for other in (1, 0):
                    self.hop1(axis, other).start()

        def stage2(self):
            self.hop1(0, 1).wait_recv()
            self.add(chips["xn"], 0, self.half, [(self.first, (self.at, 0, 1))])
            self.hop2(False).start()
            self.hop1(1, 1).wait_recv()
            self.add(chips["yn"], self.half, self.groups - self.half, [(self.first, (self.at, 1, 1))])
            self.hop2(True).start()

        def stage3(self):
            for axis in (0, 1):
                self.hop1(axis, 0).wait_recv()
                self.hop2(axis == 1).wait_recv()
            out = outs[self.i]
            rel = self.rel
            last = None if self.line and rel != 0 else out
            for half in (0, 1):
                start = self.half if half else 0
                size = self.groups - self.half if half else self.half
                self.add(chips["me"], start, size, [(self.first, (self.at, half, 0)), (self.second, (self.at, half))], last)
            if not self.line:
                return
            for up in (True, False):
                if (rel >= 0) if up else (rel <= 0):
                    @pl.when((z > 0) if up else (z < owners - 1))
                    def _():
                        self.arrive_along(up)
                        buf = self.up if up else self.down

                        @pl.loop(0, self.groups)
                        def _(g):
                            more = buf[self.at, g, :, self.cols].astype(F32)
                            if rel == 0:
                                out[g, :, self.cols] += more
                            else:
                                where = (self.at, chips["me"], g, slice(None), self.cols)
                                self.own[where] = (self.own[where].astype(F32) + more).astype(BF)
            if rel != 0:
                self.along(rel > 0).start()

        def end(self):
            self.to_sib().wait_send()
            for axis in (0, 1):
                for other in (0, 1):
                    self.hop1(axis, other).wait_send()
                self.hop2(axis == 1).wait_send()
            if self.line and self.rel != 0:
                self.along(self.rel > 0).wait_send()

    waves = []
    for d in range(owners - 1, 0, -1):
        waves.append([Item(i, rel, 0) for rel in (d, -d) for i in range(n) if lines[i]])
    waves.append([Item(i, 0, 0) for i in range(n) if lines[i]])
    waves = [w for w in waves if w]
    for i in range(n):
        if not lines[i]:
            waves += [[Item(i, 0, sub)] for sub in range(subs[i])]

    def run(wave, name):
        for item in wave:
            if item.line and item.rel != 0:
                pl.when(item.valid)(getattr(item, name))
            else:
                getattr(item, name)()

    def begin(item):
        item.load().start()

    for wave in waves:
        for item in wave:
            item.begin = functools.partial(begin, item)
            item.begin_sib = functools.partial(lambda it: it.to_sib().start(), item)
    for wave in waves:
        run(wave, "begin")
    greet(place, any(lines), owners)
    for wave in waves:
        run(wave, "begin_sib")
    for w in range(len(waves) + 2):
        for lag, name in enumerate(("stage1", "stage2", "stage3")):
            if 0 <= w - lag < len(waves):
                run(waves[w - lag], name)
    for wave in waves:
        run(wave, "end")


def scatter(arrays, lines, subs, owners, cid):
    n = len(arrays)
    scratch, outs = [], []
    for a, line in zip(arrays, lines):
        zs = a.shape[0]
        groups, _, wide = a.shape[3:]
        half = (groups + 1) // 2
        zl = zs if line else 1
        lg = groups if line else 1
        scratch += [
            pltpu.VMEM((zs, 4, groups, G, wide), BF),
            pltpu.VMEM((zs, 4, groups, G, wide), BF),
            pltpu.VMEM((zs, 2, 2, half, G, wide), BF),
            pltpu.VMEM((zs, 2, half, G, wide), BF),
            pltpu.VMEM((zl, lg, G, wide if line else 128), BF),
            pltpu.VMEM((zl, lg, G, wide if line else 128), BF),
        ]
        outs.append(jax.ShapeDtypeStruct((groups, G, wide), F32))
    slots = max([2 * owners - 1 if any(lines) else 1] + list(subs))
    scratch += [pltpu.SemaphoreType.DMA((n, slots, 10)), pltpu.SemaphoreType.DMA((n, slots, 10))]
    return pl.pallas_call(
        functools.partial(scatter_kernel, owners, lines, subs),
        out_shape=outs,
        in_specs=[pl.BlockSpec(memory_space=pl.ANY)] * n,
        out_specs=[pl.BlockSpec(memory_space=pltpu.VMEM)] * n,
        scratch_shapes=scratch,
        compiler_params=pltpu.CompilerParams(collective_id=cid, has_side_effects=True, vmem_limit_bytes=60 * 1024 * 1024),
    )(*arrays)


def moe_kernel(
    steps,
    slots,
    chunk,
    m_ref,
    g_ref,
    member_ref,
    router_ref,
    order_ref,
    mine_ref,
    weights_ref,
    moe_ref,
    drow_ref,
    grads_ref,
    grouter_ref,
    router_s,
    gate_s,
    hg_s,
    dpre_s,
    mt_s,
    gt_s,
    gup_s,
    gdn_s,
    gr_s,
):
    step = pl.program_id(0)
    owners, _, share, units = weights_ref.shape
    per = chunk // F

    @pl.when(step == 0)
    def _():
        gup_s[...] = jnp.zeros_like(gup_s)
        gdn_s[...] = jnp.zeros_like(gdn_s)
        gr_s[...] = jnp.zeros_like(gr_s)
        router_s[...] = dot_nn(router_ref[...], order_ref[...]).astype(BF)

    mt_s[...] = m_ref[...].T
    gt_s[...] = g_ref[...].T
    sig = jax.nn.sigmoid(dot_nn(m_ref[...], router_s[...]))
    mask = dot_nn(member_ref[...], mine_ref[...])
    gate_s[...] = sig * mask
    root = math.sqrt(2.0 / math.pi)
    cube = 0.044715
    lane = lax.broadcasted_iota(jnp.int32, (1, F), 1)
    d_gate = jnp.zeros(gate_s.shape, F32)
    for c in range(units // chunk):
        cols = pl.ds(c * chunk, chunk)
        pre_all = dot_nn(m_ref[:, :share], weights_ref[0, 0, :, cols])
        back_all = dot_nn(g_ref[:, :share], weights_ref[0, 1, :, cols])
        for o in range(1, owners):
            part = pl.ds(o * share, share)
            pre_all += dot_nn(m_ref[:, part], weights_ref[o, 0, :, cols])
            back_all += dot_nn(g_ref[:, part], weights_ref[o, 1, :, cols])
        for j in range(per):
            slot = c * per + j
            part = slice(j * F, (j + 1) * F)
            pre = pre_all[:, part]
            back = back_all[:, part]
            square = pre * pre
            th = jnp.tanh(root * pre * (1.0 + cube * square))
            half = 0.5 * (1.0 + th)
            slope = half + (0.5 * root) * pre * (1.0 - th * th) * (1.0 + (3.0 * cube) * square)
            hidden = (pre * half).astype(BF).astype(F32)
            gate = gate_s[:, slot : slot + 1]
            d_one = jnp.sum(hidden * back, axis=1, keepdims=True)
            d_gate = d_gate + d_one * (lane == slot).astype(F32)
            where = pl.ds(slot * F, F)
            hg_s[:, where] = (gate * hidden).astype(BF)
            dpre_s[:, where] = (slope * (gate * back)).astype(BF)
    dlog = (d_gate * mask * sig * (1.0 - sig)).astype(BF)
    gr_s[...] += dot_nn(mt_s[...], dot_nt(dlog, order_ref[...]).astype(BF))
    for o in range(owners):
        where = pl.ds(o * share, share)
        moe_ref[:, where] = dot_nt(hg_s[...], weights_ref[o, 1]).astype(BF)
        drow_ref[:, where] = (
            dot_nt(dpre_s[...], weights_ref[o, 0]) + dot_nt(dlog, router_s[where, :])
        ).astype(BF)
        gup_s[where, :] += dot_nn(mt_s[where, :], dpre_s[...])
        gdn_s[where, :] += dot_nn(gt_s[where, :], hg_s[...])

    @pl.when(step == steps - 1)
    def _():
        for o in range(owners):
            grads_ref[o, 0] = gup_s[pl.ds(o * share, share), :].astype(BF)
            grads_ref[o, 1] = gdn_s[pl.ds(o * share, share), :].astype(BF)
        grouter_ref[...] = gr_s[...].astype(BF)


def moe(rows, cots, member, packed, router_at, order, mine, weights):
    count = rows.shape[0]
    tile = 512
    owners, _, share, units = weights.shape
    slots = units // F
    steps = count // tile
    lanes = member.shape[1]
    row_spec = pl.BlockSpec((tile, D), lambda i: (i, 0))
    whole = pl.BlockSpec(memory_space=pltpu.VMEM)
    router_spec = pl.BlockSpec((D, lanes), lambda i: (0, router_at // lanes))
    return pl.pallas_call(
        functools.partial(moe_kernel, steps, slots, 512),
        grid=(steps,),
        in_specs=[
            row_spec,
            row_spec,
            pl.BlockSpec((tile, lanes), lambda i: (i, 0)),
            router_spec,
            whole,
            whole,
            whole,
        ],
        out_specs=[row_spec, row_spec, whole, whole],
        out_shape=[
            jax.ShapeDtypeStruct((count, D), BF),
            jax.ShapeDtypeStruct((count, D), BF),
            jax.ShapeDtypeStruct(weights.shape, BF),
            jax.ShapeDtypeStruct((D, lanes), BF),
        ],
        scratch_shapes=[
            pltpu.VMEM((D, F), BF),
            pltpu.VMEM((tile, F), F32),
            pltpu.VMEM((tile, units), BF),
            pltpu.VMEM((tile, units), BF),
            pltpu.VMEM((D, tile), BF),
            pltpu.VMEM((D, tile), BF),
            pltpu.VMEM((D, units), F32),
            pltpu.VMEM((D, units), F32),
            pltpu.VMEM((D, lanes), F32),
        ],
        compiler_params=pltpu.CompilerParams(vmem_limit_bytes=60 * 1024 * 1024),
        cost_estimate=pl.CostEstimate(
            flops=12 * count * D * units,
            bytes_accessed=count * D * 8 + D * units * 8,
            transcendentals=count * units,
        ),
    )(rows, cots, member, packed, order, mine, weights)


def fused_kernel(owners, slots, wide, tile_cols, *refs):
    middle, cots, member, weights, packed, order_ref, mine_ref = refs[:7]
    drow_out, moe_out, grads_out, grouter_out = refs[7:11]
    (m_s, c_s, b_s, w_s, gup_s, gdn_s, gr_s, hg_s, dpre_s, mt_s, gt_s, router_in, router_s, gate_s) = refs[11:25]
    (sib_s, first_s, second_s, gsend, grecv, ssend, srecv, local, wsem) = refs[25:]
    place = Place()
    z = place.z
    count = middle.shape[0]
    half = count // 2
    lanes = b_s.shape[1]
    share = D // owners
    ins = (member, middle, cots)
    bufs = (b_s, m_s, c_s)
    sums = (m_s, c_s)
    swap = place.sib - place.e
    mine = (place.e, place.xnb, place.ynb, place.diag)

    def span(e, start=0, size=count):
        return pl.ds(pl.multiple_of(e * count + start, 16), size)

    def remote(sems, a, kind, src, dst, to):
        return pltpu.make_async_remote_copy(
            src_ref=src, dst_ref=dst, send_sem=sems[0].at[a, kind], recv_sem=sems[1].at[a, kind],
            device_id=(z, to), device_id_type=MESH)

    def passing(a, kind):
        buf = bufs[a]
        if kind in (XS, YS, S0):
            src, at = ins[a], span(place.e)
        elif kind == FA:
            at = span(place.xnb, 0, half)
            src = buf.at[at]
        elif kind == FB:
            at = span(place.ynb, half, half)
            src = buf.at[at]
        else:
            at = span(mine[kind - S0])
            src = buf.at[at]
        to = {XS: place.xnb, YS: place.ynb, FA: place.ynb, FB: place.xnb}.get(kind, place.sib)
        return remote((gsend, grecv), a, kind, src, buf.at[at], to)

    def got(a, kind):
        at = {
            XS: lambda: span(place.xnb),
            YS: lambda: span(place.ynb),
            FA: lambda: span(place.diag, 0, half),
            FB: lambda: span(place.diag, half, half),
        }.get(kind, lambda: span(mine[kind - S0] + swap))()
        ref = bufs[a].at[at]
        remote((gsend, grecv), a, kind, ref, ref, place.sib).wait_recv()

    HY0, HY1, HX0, HX1, HX2, HY2 = 4, 5, 6, 7, 8, 9

    def to_sib(a, t):
        return remote((ssend, srecv), a, t, sums[a].at[span(mine[t] + swap)], sib_s.at[a, t], place.sib)

    def hop(a, kind):
        src_e, second, dst, to = {
            HY0: (place.ynb, False, first_s.at[a, 0], place.ynb),
            HY1: (place.diag, False, first_s.at[a, 1], place.ynb),
            HX0: (place.xnb, True, first_s.at[a, 2], place.xnb),
            HX1: (place.diag, True, first_s.at[a, 3], place.xnb),
            HX2: (place.xnb, False, second_s.at[a, 0], place.xnb),
            HY2: (place.ynb, True, second_s.at[a, 1], place.ynb),
        }[kind]
        src = sums[a].at[span(src_e, half if second else 0, half)]
        return remote((ssend, srecv), a, kind, src, dst, to)

    step_rows = 32

    def add(a, e, start, size, terms, keep=None):
        buf = sums[a]

        @pl.loop(0, size // step_rows)
        def _(g):
            here = pl.ds(pl.multiple_of(e * count + start + g * step_rows, 16), step_rows)
            there = pl.ds(pl.multiple_of(g * step_rows, 16), step_rows)
            total = buf[here, :].astype(F32)
            for lead in terms:
                total = total + lead[0][(*lead[1], there, slice(None))].astype(F32)
            if keep is None:
                buf[here, :] = total.astype(BF)
            else:
                keep[pl.ds(pl.multiple_of(start + g * step_rows, 16), step_rows), :] = total

    def with_sib(t):
        for a in (0, 1):
            to_sib(a, t).wait_recv()
            add(a, mine[t], 0, count, [(sib_s, (a, t))])

    own = [
        pltpu.make_async_copy(ins[a], bufs[a].at[span(place.e)], local.at[a]) for a in range(3)
    ]
    for c in own:
        c.start()
    router_copy = pltpu.make_async_copy(packed.at[:, pl.ds(wide, lanes)], router_in, local.at[3])
    router_copy.start()

    @pl.loop(0, slots)
    def _(s):
        for o in range(owners):
            for k in (0, 1):
                pltpu.make_async_copy(
                    weights.at[o, k * slots + s],
                    w_s.at[k, pl.ds(o * share, share), pl.ds(pl.multiple_of(s * F, F), F)],
                    wsem.at[0],
                ).start()

    greet(place, False, owners)
    for a in range(3):
        for kind in (XS, YS, S0):
            passing(a, kind).start()
    gup_s[...] = jnp.zeros_like(gup_s)
    gdn_s[...] = jnp.zeros_like(gdn_s)
    gr_s[...] = jnp.zeros_like(gr_s)

    root = math.sqrt(2.0 / math.pi)
    cube = 0.044715
    tile = 2 * count
    units = slots * F
    per = tile_cols // F

    @pl.loop(0, 4)
    def _(t):
        @pl.when(t == 0)
        def _():
            for c in own:
                c.wait()
            router_copy.wait()
            router_s[...] = dot_nn(router_in[...], order_ref[...]).astype(BF)
            for a in range(3):
                got(a, S0)
            pltpu.make_async_copy(w_s, w_s, wsem.at[0]).wait()

        @pl.when(t == 1)
        def _():
            for a in range(3):
                got(a, XS)
                passing(a, FA).start()
                passing(a, S1).start()
                got(a, YS)
                passing(a, FB).start()
                passing(a, S2).start()
            for a in range(3):
                got(a, S1)

        @pl.when(t == 2)
        def _():
            for a in range(3):
                got(a, FA)
                got(a, FB)
                passing(a, S3).start()
            for a in range(3):
                got(a, S2)

        @pl.when(t == 3)
        def _():
            for a in range(3):
                got(a, S3)

        tx, ty = t % 2, t // 2
        chip_x = place.x + tx * (1 - 2 * place.x)
        chip_y = place.y + ty * (1 - 2 * place.y)
        chip = chip_y * 2 + chip_x
        here = pl.ds(pl.multiple_of(chip * tile, 16), tile)
        mt_s[...] = m_s[here, :].T
        gt_s[...] = c_s[here, :].T
        sig = jax.nn.sigmoid(dot_nn(m_s[here, :], router_s[...]))
        mask = dot_nn(b_s[here, :], mine_ref[...])
        gate_s[...] = sig * mask
        lane = lax.broadcasted_iota(jnp.int32, (1, F), 1)
        d_gate = jnp.zeros(gate_s.shape, F32)
        for c in range(units // tile_cols):
            cols = pl.ds(c * tile_cols, tile_cols)
            pre_all = dot_nn(m_s[here, :], w_s[0, :, cols])
            back_all = dot_nn(c_s[here, :], w_s[1, :, cols])
            for j in range(per):
                slot = c * per + j
                part = slice(j * F, (j + 1) * F)
                pre = pre_all[:, part]
                back = back_all[:, part]
                square = pre * pre
                th = jnp.tanh(root * pre * (1.0 + cube * square))
                halved = 0.5 * (1.0 + th)
                slope = halved + (0.5 * root) * pre * (1.0 - th * th) * (1.0 + (3.0 * cube) * square)
                hidden = (pre * halved).astype(BF).astype(F32)
                gate = gate_s[:, slot : slot + 1]
                d_one = jnp.sum(hidden * back, axis=1, keepdims=True)
                d_gate = d_gate + d_one * (lane == slot).astype(F32)
                where = pl.ds(slot * F, F)
                hg_s[:, where] = (gate * hidden).astype(BF)
                dpre_s[:, where] = (slope * (gate * back)).astype(BF)
        dlog = (d_gate * mask * sig * (1.0 - sig)).astype(BF)
        gr_s[...] += dot_nn(mt_s[...], dot_nt(dlog, order_ref[...]).astype(BF))

        @pl.when(t == 1)
        def _():
            with_sib(0)
            for a in range(3):
                passing(a, FA).wait_send()
                passing(a, S1).wait_send()

        @pl.when(t == 2)
        def _():
            with_sib(1)
            for a in (0, 1):
                hop(a, HX0).start()
            for a in range(3):
                passing(a, FB).wait_send()
                passing(a, S2).wait_send()

        @pl.when(t == 3)
        def _():
            with_sib(2)
            for a in (0, 1):
                hop(a, HY0).start()
            for a in range(3):
                passing(a, S3).wait_send()

        for n in range(D // 256):
            where = pl.ds(n * 256, 256)
            m_s[here, where] = (
                dot_nt(dpre_s[...], w_s[0, where, :]) + dot_nt(dlog, router_s[where, :])
            ).astype(BF)
        for k in range(4):

            @pl.when(t == k)
            def _():
                to_sib(0, k).start()

        for n in range(D // 256):
            where = pl.ds(n * 256, 256)
            c_s[here, where] = dot_nt(hg_s[...], w_s[1, where, :]).astype(BF)
        for k in range(4):

            @pl.when(t == k)
            def _():
                to_sib(1, k).start()

        for n in range(D // 256):
            where = pl.ds(n * 256, 256)
            gup_s[where, :] += dot_nn(mt_s[where, :], dpre_s[...])
            gdn_s[where, :] += dot_nn(gt_s[where, :], hg_s[...])

    for a in (0, 1):
        to_sib(a, 3).wait_recv()
        add(a, mine[3], 0, count, [(sib_s, (a, 3))])
        hop(a, HY1).start()
        hop(a, HX1).start()
    w_s[0] = gup_s[...].astype(BF)
    w_s[1] = gdn_s[...].astype(BF)

    @pl.loop(0, slots)
    def _(s):
        for o in range(owners):
            for k in (0, 1):
                pltpu.make_async_copy(
                    w_s.at[k, pl.ds(o * share, share), pl.ds(pl.multiple_of(s * F, F), F)],
                    grads_out.at[o, k * slots + s],
                    wsem.at[0],
                ).start()

    grouter_out[...] = gr_s[...].astype(BF)
    for a in (0, 1):
        hop(a, HY1).wait_recv()
        add(a, place.xnb, 0, half, [(first_s, (a, 1))])
        hop(a, HX2).start()
        hop(a, HX1).wait_recv()
        add(a, place.ynb, half, half, [(first_s, (a, 3))])
        hop(a, HY2).start()
    for a, out in ((0, drow_out), (1, moe_out)):
        hop(a, HY0).wait_recv()
        hop(a, HX2).wait_recv()
        add(a, place.e, 0, half, [(first_s, (a, 0)), (second_s, (a, 0))], out)
        hop(a, HX0).wait_recv()
        hop(a, HY2).wait_recv()
        add(a, place.e, half, half, [(first_s, (a, 2)), (second_s, (a, 1))], out)
    for a in range(3):
        for kind in (XS, YS, S0):
            passing(a, kind).wait_send()
    for a in (0, 1):
        for t in range(4):
            to_sib(a, t).wait_send()
        for kind in (HY0, HY1, HX0, HX1, HX2, HY2):
            hop(a, kind).wait_send()
    pltpu.make_async_copy(w_s, w_s, wsem.at[0]).wait()


def fused_experts(middle, cots, member, weights, packed, wide, order, mine, cid):
    count = middle.shape[0]
    owners = weights.shape[0]
    slots = weights.shape[1] // 2
    lanes = member.shape[1]
    units = slots * F
    tile = 2 * count
    hbm = pl.BlockSpec(memory_space=pl.ANY)
    vmem = pl.BlockSpec(memory_space=pltpu.VMEM)
    dma = pltpu.SemaphoreType.DMA
    return pl.pallas_call(
        functools.partial(fused_kernel, owners, slots, wide, 256),
        in_specs=[hbm] * 5 + [vmem] * 2,
        out_specs=[vmem, vmem, hbm, vmem],
        out_shape=[
            jax.ShapeDtypeStruct((count, D), F32),
            jax.ShapeDtypeStruct((count, D), F32),
            jax.ShapeDtypeStruct(weights.shape, BF),
            jax.ShapeDtypeStruct((D, lanes), BF),
        ],
        scratch_shapes=[
            pltpu.VMEM((8 * count, D), BF),
            pltpu.VMEM((8 * count, D), BF),
            pltpu.VMEM((8 * count, lanes), BF),
            pltpu.VMEM((2, D, units), BF),
            pltpu.VMEM((D, units), F32),
            pltpu.VMEM((D, units), F32),
            pltpu.VMEM((D, lanes), F32),
            pltpu.VMEM((tile, units), BF),
            pltpu.VMEM((tile, units), BF),
            pltpu.VMEM((D, tile), BF),
            pltpu.VMEM((D, tile), BF),
            pltpu.VMEM((D, lanes), BF),
            pltpu.VMEM((D, F), BF),
            pltpu.VMEM((tile, F), F32),
            pltpu.VMEM((2, 4, count, D), BF),
            pltpu.VMEM((2, 4, count // 2, D), BF),
            pltpu.VMEM((2, 2, count // 2, D), BF),
            dma((3, 8)),
            dma((3, 8)),
            dma((2, 10)),
            dma((2, 10)),
            dma((4,)),
            dma((1,)),
        ],
        compiler_params=pltpu.CompilerParams(
            collective_id=cid, has_side_effects=True, vmem_limit_bytes=64 * 1024 * 1024 - 65536
        ),
        cost_estimate=pl.CostEstimate(
            flops=12 * 8 * count * D * units,
            bytes_accessed=D * units * 8,
            transcendentals=8 * count * units,
        ),
    )(middle, cots, member, weights, packed, order, mine)


def picked_mask(picks, number):
    return jnp.sum(
        (picks[..., None] == jnp.arange(number, dtype=jnp.int32)).astype(F32), axis=-2
    )


def layer_normed(inputs, gain_row):
    centred = inputs - jnp.mean(inputs, axis=-1, keepdims=True)
    variance = jnp.mean(centred * centred, axis=-1, keepdims=True)
    return centred * lax.rsqrt(variance + epsilon) * gain_row


def head_gates(select, value_mask, out_mask):
    row_count = value_mask.shape[0]
    value_gate = jax.nn.sigmoid(select[:, : H * NV]).reshape(row_count, H, NV) * value_mask
    out_gate = jax.nn.sigmoid(select[:, H * NV :]).reshape(row_count, H, NV) * out_mask
    return (value_gate, out_gate)


def dense_forward(tokens, live, lengths, picks, gain, qkv, select_w, heads):
    count = tokens.shape[0]
    seq = count // MB
    xf = tokens.astype(F32)
    value_mask = picked_mask(picks, NV)
    out_mask = value_mask * live[:, None, None]
    normed, norm_back = jax.vjp(layer_normed, xf, gain.astype(F32))
    normed_low = normed.astype(BF)
    query_key = dot_nn(normed_low, qkv[:, :QK]).astype(BF)
    values_all = dot_nn(tokens, qkv[:, QK:])
    select = dot_nn(tokens, select_w)
    (value_gate, out_gate), gate_back = jax.vjp(
        lambda logits_in: head_gates(logits_in, value_mask, out_mask), select
    )
    values_split = values_all.reshape(count, H, NV, HD)
    values_low = jnp.sum(value_gate[..., None] * values_split, axis=2).astype(BF)
    values_seq = values_low.reshape(MB, seq, H, HD)
    queries = query_key[:, : H * HD].reshape(MB, seq, H, HD)
    keys_all = query_key[:, H * HD :].reshape(MB, seq, H, HD)
    position = jnp.arange(seq, dtype=jnp.int32)
    scores = jnp.einsum("bihd,bjhd->bhij", queries, keys_all, preferred_element_type=F32) * HD ** (
        -0.5
    )
    allowed = (position[None, :] <= position[:, None])[None] & (
        position[None, None, :] < lengths[:, None, None]
    )
    masked = jnp.where(allowed[:, None], scores, -1e30)
    expo = jnp.exp(masked - jnp.max(masked, axis=-1, keepdims=True))
    attention = expo / jnp.sum(expo, axis=-1, keepdims=True)
    attended = jnp.einsum(
        "bhij,bjhd->bihd", attention.astype(BF), values_seq, preferred_element_type=F32
    ).reshape(count, H, HD)
    mixed_heads = (out_gate[..., None] * attended[:, :, None, :]).reshape(count, VAL).astype(BF)
    middle = xf + dot_nn(mixed_heads, heads)

    def backward(d_middle):
        d_branch = d_middle.astype(BF)
        grad_heads = dot_tn(mixed_heads, d_branch)
        d_mixed = dot_nt(d_branch, heads).reshape(count, H, NV, HD)
        d_attended = jnp.sum(out_gate[..., None] * d_mixed, axis=2).astype(BF)
        d_out_gate = jnp.sum(d_mixed * attended[:, :, None, :], axis=-1)
        d_att_seq = d_attended.reshape(MB, seq, H, HD)
        d_attention = jnp.einsum(
            "bihd,bjhd->bhij", d_att_seq, values_seq, preferred_element_type=F32
        )
        d_scores = (
            attention * (d_attention - jnp.sum(attention * d_attention, axis=-1, keepdims=True))
        ).astype(BF)
        d_values = (
            jnp.einsum(
                "bhij,bihd->bjhd", attention.astype(BF), d_att_seq, preferred_element_type=F32
            )
            .astype(BF)
            .reshape(count, H, HD)
        )
        d_queries = jnp.einsum(
            "bhij,bjhd->bihd", d_scores, keys_all, preferred_element_type=F32
        ) * HD ** (-0.5)
        d_keys = jnp.einsum(
            "bhij,bihd->bjhd", d_scores, queries, preferred_element_type=F32
        ) * HD ** (-0.5)
        d_query_key = jnp.concatenate(
            [d_queries.reshape(count, H * HD), d_keys.reshape(count, H * HD)], axis=1
        ).astype(BF)
        d_value_gate = jnp.sum(d_values[:, :, None, :] * values_split, axis=-1)
        d_values_all = (value_gate[..., None] * d_values[:, :, None, :]).reshape(count, VAL).astype(BF)
        d_select = gate_back((d_value_gate, d_out_gate))[0].astype(BF)
        grad_qk = dot_tn(normed_low, d_query_key)
        grad_val = dot_tn(tokens, d_values_all)
        grad_select = dot_tn(tokens, d_select)
        d_normed = dot_nt(d_query_key, qkv[:, :QK])
        d_norm_in, grad_gain = norm_back(d_normed)
        d_tokens = (
            d_middle
            + d_norm_in
            + dot_nt(d_values_all, qkv[:, QK:])
            + dot_nt(d_select, select_w)
        )
        return d_tokens, grad_gain, grad_qk, grad_val, grad_select, grad_heads

    return middle, backward


def body(
    tokens,
    cotangent,
    lengths,
    routes,
    head_choice,
    placement,
    gain_master,
    gain_moment,
    gain_average,
    qkv_master,
    qkv_moment,
    qkv_average,
    select_master,
    select_moment,
    select_average,
    router_master,
    router_moment,
    router_average,
    heads_out_master,
    heads_out_moment,
    heads_out_average,
    up_master,
    up_moment,
    up_average,
    down_master,
    down_moment,
    down_average,
):
    both = ("dp", "expert")
    owners = lax.axis_size("dp")
    group = lax.axis_size("expert")
    own_kernels = group == 8
    experts = placement.shape[0]
    slots = up_master.shape[0]
    units = slots * F
    seq = tokens.shape[1]
    count = MB * seq
    share = up_master.shape[1]
    mine = lax.axis_index("expert")
    lanes = -(-experts // 128) * 128

    own_rows = qkv_master.shape[0]
    wide = QK + VAL
    packed = jnp.concatenate(
        [
            qkv_master.astype(BF),
            router_master.astype(BF),
            jnp.zeros((own_rows, lanes - experts), BF),
            select_master.astype(BF),
            gain_master.astype(BF)[:, None],
            jnp.zeros((own_rows, 127 - SEL), BF),
        ],
        axis=1,
    )
    heads_low = heads_out_master.astype(BF)

    experts_low = jnp.concatenate([up_master.astype(BF), down_master.astype(BF)], axis=0)
    weights = lax.all_gather(experts_low, "dp", axis=0, tiled=False)

    flat_tokens = tokens.reshape(count, D)
    flat_cots = cotangent.reshape(count, D)
    live = (jnp.arange(seq, dtype=jnp.int32)[None, :] < lengths).astype(F32).reshape(count)
    lane_ids = jnp.arange(lanes, dtype=jnp.int32)
    named = jnp.sum(
        (routes.reshape(count, TOPK)[..., None] == lane_ids).astype(F32), axis=1
    ) * live[:, None]
    padded = jnp.pad(placement, (0, lanes - experts), constant_values=-1)
    perm = (padded[:, None] == lane_ids[None, :]).astype(BF)
    member = dot_nn(named.astype(BF), perm).astype(BF)
    own_lane = jnp.arange(F, dtype=jnp.int32)[None, :]
    mine_sel = (((lane_ids[:, None] - mine * slots) == own_lane) & (own_lane < slots)).astype(BF)
    order_mine = (
        ((padded[:, None] - mine * slots) == own_lane) & (own_lane < slots) & (padded[:, None] >= 0)
    ).astype(BF)

    if own_kernels:
        packed_all, heads = gather(
            (packed, heads_low), (True, True), (own_rows // 2, 48), owners, group, 0
        )
    else:
        packed_all = lax.all_gather(packed, both, axis=0, tiled=True)
        heads = lax.all_gather(heads_low, both, axis=0, tiled=True)
    qkv = packed_all[:, :wide]
    select_w = packed_all[:, wide + lanes : wide + lanes + SEL]
    gain = packed_all[:, wide + lanes + SEL]

    middle, backward = dense_forward(
        flat_tokens,
        live,
        lengths[:, 0],
        head_choice.reshape(count, H, -1),
        gain,
        qkv,
        select_w,
        heads,
    )
    middle_low = middle.astype(BF)
    if own_kernels:
        d_from_rows, moe_sum, expert_grads, grad_router = fused_experts(
            middle_low, flat_cots, member, weights, packed_all, wide, order_mine, mine_sel, 1
        )
    else:
        rows_all, cots_all, member_all = (
            lax.all_gather(a, "expert", axis=0, tiled=True) for a in (middle_low, flat_cots, member)
        )
        side = weights.reshape(owners, 2, slots, share, F).transpose(0, 1, 3, 2, 4)
        moe_part, drow_part, expert_grads, grad_router = moe(
            rows_all,
            cots_all,
            member_all,
            packed_all,
            wide,
            order_mine,
            mine_sel,
            side.reshape(owners, 2, share, units),
        )
        expert_grads = expert_grads.reshape(owners, 2, share, slots, F).transpose(0, 1, 3, 2, 4)
        d_from_rows, moe_sum = (
            lax.psum_scatter(a, "expert", scatter_dimension=0, tiled=True).astype(F32)
            for a in (drow_part, moe_part)
        )
    expert_sum = lax.psum_scatter(
        expert_grads.reshape(owners * 2 * slots, share, F), "dp", scatter_dimension=0, tiled=True
    ).astype(F32)
    mixed = (middle + moe_sum).astype(BF)

    d_middle = flat_cots.astype(F32) + d_from_rows
    d_tokens, grad_gain, grad_qk, grad_val, grad_select, grad_heads = backward(d_middle)
    small_grads = jnp.concatenate(
        [
            grad_router,
            grad_select.astype(BF),
            grad_gain.astype(BF)[:, None],
            jnp.zeros((D, 127 - SEL), BF),
        ],
        axis=1,
    )
    dense_grads = (grad_qk.astype(BF), grad_val.astype(BF), small_grads, grad_heads.astype(BF))
    if own_kernels:
        sums = scatter(
            tuple(g.reshape(owners, 4, 2, -1, G, g.shape[1]) for g in dense_grads),
            (True,) * 4,
            (1,) * 4,
            owners,
            3,
        )
        qk_sum, val_sum, small_sum, heads_sum = (s.reshape(-1, s.shape[2]) for s in sums)
    else:
        qk_sum, val_sum, small_sum, heads_sum = (
            lax.psum_scatter(g, both, scatter_dimension=0, tiled=True).astype(F32)
            for g in dense_grads
        )
    qkv_sum = jnp.concatenate([qk_sum, val_sum], axis=1)
    router_sum = small_sum[:, :experts]
    select_sum = small_sum[:, lanes : lanes + SEL]
    gain_sum = small_sum[:, lanes + SEL]
    up_sum = expert_sum[:slots]
    down_sum = expert_sum[slots:]

    rates = step_rates(count * owners * group, experts)
    outs = (
        update_weight(gain_master, gain_moment, gain_average, gain_sum, rates[0])
        + update_weight(qkv_master, qkv_moment, qkv_average, qkv_sum, rates[1])
        + update_weight(select_master, select_moment, select_average, select_sum, rates[2])
        + update_weight(router_master, router_moment, router_average, router_sum, rates[3])
        + update_weight(heads_out_master, heads_out_moment, heads_out_average, heads_sum, rates[4])
        + update_weight(up_master, up_moment, up_average, up_sum, rates[5])
        + update_weight(down_master, down_moment, down_average, down_sum, rates[6])
    )
    return (mixed.reshape(tokens.shape), d_tokens.reshape(tokens.shape)) + outs


def solution(mesh):
    rows = P(None, ("dp", "expert"), None)
    flat = P(("dp", "expert"))
    dense = P(("dp", "expert"), None)
    expert = P("expert", "dp", None)
    in_specs = (
        rows,
        rows,
        P(None, ("dp", "expert")),
        rows,
        P(None, ("dp", "expert"), None, None),
        P(),
        *((flat,) * 3),
        *((dense,) * 12),
        *((expert,) * 6),
    )
    out_specs = (rows, rows, *((flat,) * 4), *((dense,) * 16), *((expert,) * 8))
    return jax.shard_map(body, mesh=mesh, in_specs=in_specs, out_specs=out_specs, check_vma=False)
```

```python
import functools
import math

import jax
import jax.numpy as jnp
from jax import lax
from jax.experimental import pallas as pl
from jax.experimental.pallas import tpu as pltpu
from jax.sharding import PartitionSpec as P

D = 1024
H = 4
HD = 128
NV = 5
F = 128
TOPK = 16
MB = 2
QK = 2 * H * HD
VAL = H * NV * HD
SEL = 2 * H * NV

momentum_decay = 0.9
average_decay = 0.5
rate_factor = 0.4
epsilon = 1e-05
BF = jnp.bfloat16
F32 = jnp.float32


def step_rates(total_tokens, experts):
    root_tokens = math.sqrt(total_tokens)
    expert_share = math.sqrt(TOPK / experts)
    spread_list = (
        0.3,
        D ** (-0.5),
        (2 * D) ** (-0.5),
        (9 * D) ** (-0.5),
        0.5,
        D ** (-0.5),
        (4 * F) ** (-0.5),
    )
    gradient_list = (1.0, 1.0, 3.0, 2.0 * expert_share, 0.1, 0.5 * expert_share, 0.4 * expert_share)
    return tuple(
        rate_factor * spread_value / (gradient_value * root_tokens)
        for spread_value, gradient_value in zip(spread_list, gradient_list)
    )


def update_weight(master, moment, average, gradient, step_size):
    new_moment = momentum_decay * moment + gradient
    new_weight = master - step_size * (gradient + momentum_decay * new_moment)
    new_average = average_decay * average + (1.0 - average_decay) * new_weight
    return (new_moment, new_average, new_weight, new_weight.astype(BF))


def dot_nt(a, b):
    return lax.dot_general(a, b, (((1,), (1,)), ((), ())), preferred_element_type=F32)


def dot_tn(a, b):
    return lax.dot_general(a, b, (((0,), (0,)), ((), ())), preferred_element_type=F32)


def dot_nn(a, b):
    return jnp.dot(a, b, preferred_element_type=F32)


MESH = pl.DeviceIdType.MESH


class Place:
    def __init__(self):
        self.z = lax.axis_index("dp")
        self.e = lax.axis_index("expert")
        core = self.e % 2
        x = (self.e // 2) % 2
        y = self.e // 4
        self.sib = self.e + 1 - 2 * core
        self.xnb = self.e + 2 - 4 * x
        self.ynb = self.e + 4 - 8 * y
        self.diag = self.xnb + 4 - 8 * y
        self.core, self.x, self.y = core, x, y


def greet(place, line, owners):
    barrier = pltpu.get_barrier_semaphore()
    z = place.z
    for e in (place.sib, place.xnb, place.ynb):
        pl.semaphore_signal(barrier, inc=1, device_id=(z, e), device_id_type=MESH)
    peers = 3
    if line:

        @pl.when(z > 0)
        def _():
            pl.semaphore_signal(barrier, inc=1, device_id=(z - 1, place.e), device_id_type=MESH)

        @pl.when(z < owners - 1)
        def _():
            pl.semaphore_signal(barrier, inc=1, device_id=(z + 1, place.e), device_id_type=MESH)

        peers = peers + (z + owners - 1) // owners + (2 * owners - 2 - z) // owners
    pl.semaphore_wait(barrier, peers)


XS, YS, FA, FB, S0, S1, S2, S3, UP, DOWN = range(10)

def gather_kernel(owners, group, lines, halves, *refs):
    n = len(lines)
    ins, outs, (send, recv, own) = refs[:n], refs[n : 2 * n], refs[2 * n :]
    place = Place()
    z = place.z
    copies_own = []
    for i in range(n):
        rows = ins[i].shape[0]
        slot = (z * group + place.e) if lines[i] else place.e
        cp = pltpu.make_async_copy(ins[i], outs[i].at[pl.ds(slot * rows, rows)], own.at[i])
        cp.start()
        copies_own.append(cp)
    greet(place, any(lines), owners)

    def block(i, rel, e, part=None):
        rows = ins[i].shape[0]
        slot = ((z + rel) * group + e) if lines[i] else e
        start, size = (0, rows) if part is None else part
        return outs[i].at[pl.ds(slot * rows + start, size)]

    def source(i, rel, part=None):
        if rel == 0:
            return ins[i] if part is None else ins[i].at[pl.ds(*part)]
        return block(i, rel, place.e, part)

    def sem(rel):
        return rel + owners - 1

    def go(i, rel, kind, src, dst, to_e, dz=0):
        return pltpu.make_async_remote_copy(
            src_ref=src, dst_ref=dst, send_sem=send.at[i, sem(rel), kind],
            recv_sem=recv.at[i, sem(rel - dz), min(kind, UP)],
            device_id=(z + dz, to_e), device_id_type=MESH)

    def parts(i):
        rows = ins[i].shape[0]
        return (0, halves[i]), (halves[i], rows - halves[i])

    def valid(rel):
        return (z + rel >= 0) & (z + rel < owners)

    def copies(i, rel):
        first, second = parts(i)
        e, xn, yn, dg, sb = place.e, place.xnb, place.ynb, place.diag, place.sib
        return {
            XS: lambda: go(i, rel, XS, source(i, rel), block(i, rel, e), xn),
            YS: lambda: go(i, rel, YS, source(i, rel), block(i, rel, e), yn),
            FA: lambda: go(i, rel, FA, block(i, rel, xn, first), block(i, rel, xn, first), yn),
            FB: lambda: go(i, rel, FB, block(i, rel, yn, second), block(i, rel, yn, second), xn),
            S0: lambda: go(i, rel, S0, source(i, rel), block(i, rel, e), sb),
            S1: lambda: go(i, rel, S1, block(i, rel, xn), block(i, rel, xn), sb),
            S2: lambda: go(i, rel, S2, block(i, rel, yn), block(i, rel, yn), sb),
            S3: lambda: go(i, rel, S3, block(i, rel, dg), block(i, rel, dg), sb),
        }

    def got(i, rel, kind, e, part=None):
        ref = block(i, rel, e, part)
        pltpu.make_async_remote_copy(
            src_ref=ref, dst_ref=ref, send_sem=send.at[i, sem(rel), min(kind, UP)], recv_sem=recv.at[i, sem(rel), min(kind, UP)],
            device_id=(z, place.sib), device_id_type=MESH).wait_recv()

    def stage_z(rel):
        @pl.when(valid(rel))
        def _():
            for i in range(n):
                if rel != 0 and not lines[i]:
                    continue
                if rel != 0:
                    got(i, rel, UP, place.e)
                if lines[i] and rel <= 0 and rel > 1 - owners:
                    @pl.when(z < owners - 1)
                    def _():
                        go(i, rel, UP, source(i, rel), block(i, rel, place.e), place.e, 1).start()
                if lines[i] and rel >= 0 and rel < owners - 1:
                    @pl.when(z > 0)
                    def _():
                        go(i, rel, DOWN, source(i, rel), block(i, rel, place.e), place.e, -1).start()
                c = copies(i, rel)
                c[XS]().start()
                c[YS]().start()
                c[S0]().start()

    def each(rel, fn):
        @pl.when(valid(rel))
        def _():
            for i in range(n):
                if rel == 0 or lines[i]:
                    fn(i, rel, copies(i, rel))

    def xy(i, rel, c):
        got(i, rel, XS, place.xnb)
        c[FA]().start()
        c[S1]().start()
        got(i, rel, YS, place.ynb)
        c[FB]().start()
        c[S2]().start()

    def dg(i, rel, c):
        first, second = parts(i)
        got(i, rel, FA, place.diag, first)
        got(i, rel, FB, place.diag, second)
        c[S3]().start()

    def end(i, rel, c):
        for k, e in ((S0, place.sib),):
            got(i, rel, S0, place.sib)
        got(i, rel, S1, place.xnb + place.sib - place.e)
        got(i, rel, S2, place.ynb + place.sib - place.e)
        got(i, rel, S3, place.diag + place.sib - place.e)
        for k in (XS, YS, FA, FB, S0, S1, S2, S3):
            c[k]().wait_send()
        if lines[i] and rel <= 0 and rel > 1 - owners:
            @pl.when(z < owners - 1)
            def _():
                go(i, rel, UP, source(i, rel), block(i, rel, place.e), place.e, 1).wait_send()
        if lines[i] and rel >= 0 and rel < owners - 1:
            @pl.when(z > 0)
            def _():
                go(i, rel, DOWN, source(i, rel), block(i, rel, place.e), place.e, -1).wait_send()

    rels = [0] + [s * d for d in range(1, owners) for s in (-1, 1)]
    waves = [[0]] + [[-d, d] for d in range(1, owners)]
    for w in range(owners + 3):
        if w < owners:
            for r in waves[w]:
                stage_z(r)
        if 0 <= w - 1 < owners:
            for r in waves[w - 1]:
                each(r, xy)
        if 0 <= w - 2 < owners:
            for r in waves[w - 2]:
                each(r, dg)
    for cp in copies_own:
        cp.wait()
    for r in rels:
        each(r, end)


def gather(arrays, lines, halves, owners, group, cid):
    outs = [jax.ShapeDtypeStruct((a.shape[0] * (owners if l else 1) * group,) + a.shape[1:], a.dtype) for a, l in zip(arrays, lines)]
    n = len(arrays)
    any_spec = pl.BlockSpec(memory_space=pl.ANY)
    return pl.pallas_call(
        functools.partial(gather_kernel, owners, group, lines, halves),
        out_shape=outs, in_specs=[any_spec] * n, out_specs=[any_spec] * n,
        scratch_shapes=[pltpu.SemaphoreType.DMA((n, 2 * owners - 1, 10)), pltpu.SemaphoreType.DMA((n, 2 * owners - 1, 9)), pltpu.SemaphoreType.DMA((n,))],
        compiler_params=pltpu.CompilerParams(collective_id=cid, has_side_effects=True),
    )(*arrays)


G = 16
(LOAD, SIB, Y0, Y1, X0, X1, X2, Y2, UP, DOWN) = range(10)


def scatter_kernel(owners, lines, subs, *refs):
    n = len(lines)
    ins, outs, scratch = refs[:n], refs[n : 2 * n], refs[2 * n :]
    send, recv = scratch[6 * n :]
    place = Place()
    z = place.z
    chips = {k: e // 2 for k, e in (("me", place.e), ("xn", place.xnb), ("yn", place.ynb), ("dg", place.diag))}

    class Item:
        def __init__(self, i, rel, sub):
            self.i, self.rel = i, rel
            self.line = lines[i]
            self.own, self.sib, self.first, self.second, self.up, self.down = scratch[6 * i : 6 * i + 6]
            groups, _, wide = ins[i].shape[3:]
            self.groups, self.half = groups, (groups + 1) // 2
            self.at = z + rel if self.line else 0
            width = wide // subs[i]
            self.cols = pl.ds(sub * width, width)
            self.slot = rel + owners - 1 if self.line else sub
            self.valid = (z + rel >= 0) & (z + rel < owners)

        def piece(self, ref, *lead):
            return ref.at[(*lead, slice(None), self.cols)]

        def rows(self, second):
            return pl.ds(self.half, self.groups - self.half) if second else pl.ds(0, self.half)

        def copy(self, kind, src, dst, to, dz=0):
            there = self.slot - dz if self.line else self.slot
            return pltpu.make_async_remote_copy(
                src_ref=src, dst_ref=dst,
                send_sem=send.at[self.i, self.slot, kind], recv_sem=recv.at[self.i, there, kind],
                device_id=(z + dz, to), device_id_type=MESH)

        def load(self):
            return pltpu.make_async_copy(
                self.piece(ins[self.i], self.at, slice(None), place.core, slice(None)),
                self.piece(self.own, self.at, slice(None), slice(None)),
                send.at[self.i, self.slot, LOAD])

        def to_sib(self):
            return self.copy(SIB, self.piece(ins[self.i], self.at, slice(None), 1 - place.core, slice(None)),
                             self.piece(self.sib, self.at, slice(None), slice(None)), place.sib)

        def hop1(self, axis, other):
            second = axis == 1
            to = place.xnb if axis else place.ynb
            whose = chips["dg"] if other else chips["xn" if axis else "yn"]
            size = self.groups - self.half if second else self.half
            return self.copy((X0, X1)[other] if axis else (Y0, Y1)[other],
                             self.piece(self.own, self.at, whose, self.rows(second)),
                             self.piece(self.first, self.at, axis, other, pl.ds(0, size)), to)

        def hop2(self, second):
            to = place.ynb if second else place.xnb
            whose = chips["yn" if second else "xn"]
            size = self.groups - self.half if second else self.half
            return self.copy(Y2 if second else X2,
                             self.piece(self.own, self.at, whose, self.rows(second)),
                             self.piece(self.second, self.at, int(second), pl.ds(0, size)), to)

        def along(self, up):
            return self.copy(UP if up else DOWN, self.piece(self.own, self.at, chips["me"], slice(None)),
                             self.piece(self.up if up else self.down, self.at, slice(None)), place.e, 1 if up else -1)

        def arrive_along(self, up):
            buf = self.piece(self.up if up else self.down, self.at, slice(None))
            pltpu.make_async_remote_copy(
                src_ref=buf, dst_ref=buf, send_sem=send.at[self.i, self.slot, UP if up else DOWN],
                recv_sem=recv.at[self.i, self.slot, UP if up else DOWN],
                device_id=(z, place.sib), device_id_type=MESH).wait_recv()

        def add(self, whose, start, count, terms, keep=None):
            own, cols, at = self.own, self.cols, self.at

            @pl.loop(0, count)
            def _(g):
                total = own[at, whose, start + g, :, cols].astype(F32)
                for ref, lead in terms:
                    total = total + ref[(*lead, g, slice(None), cols)].astype(F32)
                if keep is None:
                    own[at, whose, start + g, :, cols] = total.astype(BF)
                else:
                    keep[start + g, :, cols] = total

        def stage1(self):
            self.load().wait()
            self.to_sib().wait_recv()

            @pl.loop(0, 4)
            def _(chip):
                self.add(chip, 0, self.groups, [(self.sib, (self.at, chip))])
            for axis in (0, 1):
                for other in (1, 0):
                    self.hop1(axis, other).start()

        def stage2(self):
            self.hop1(0, 1).wait_recv()
            self.add(chips["xn"], 0, self.half, [(self.first, (self.at, 0, 1))])
            self.hop2(False).start()
            self.hop1(1, 1).wait_recv()
            self.add(chips["yn"], self.half, self.groups - self.half, [(self.first, (self.at, 1, 1))])
            self.hop2(True).start()

        def stage3(self):
            for axis in (0, 1):
                self.hop1(axis, 0).wait_recv()
                self.hop2(axis == 1).wait_recv()
            out = outs[self.i]
            rel = self.rel
            last = None if self.line and rel != 0 else out
            for half in (0, 1):
                start = self.half if half else 0
                size = self.groups - self.half if half else self.half
                self.add(chips["me"], start, size, [(self.first, (self.at, half, 0)), (self.second, (self.at, half))], last)
            if not self.line:
                return
            for up in (True, False):
                if (rel >= 0) if up else (rel <= 0):
                    @pl.when((z > 0) if up else (z < owners - 1))
                    def _():
                        self.arrive_along(up)
                        buf = self.up if up else self.down

                        @pl.loop(0, self.groups)
                        def _(g):
                            more = buf[self.at, g, :, self.cols].astype(F32)
                            if rel == 0:
                                out[g, :, self.cols] += more
                            else:
                                where = (self.at, chips["me"], g, slice(None), self.cols)
                                self.own[where] = (self.own[where].astype(F32) + more).astype(BF)
            if rel != 0:
                self.along(rel > 0).start()

        def end(self):
            self.to_sib().wait_send()
            for axis in (0, 1):
                for other in (0, 1):
                    self.hop1(axis, other).wait_send()
                self.hop2(axis == 1).wait_send()
            if self.line and self.rel != 0:
                self.along(self.rel > 0).wait_send()

    waves = []
    for d in range(owners - 1, 0, -1):
        waves.append([Item(i, rel, 0) for rel in (d, -d) for i in range(n) if lines[i]])
    waves.append([Item(i, 0, 0) for i in range(n) if lines[i]])
    waves = [w for w in waves if w]
    for i in range(n):
        if not lines[i]:
            waves += [[Item(i, 0, sub)] for sub in range(subs[i])]

    def run(wave, name):
        for item in wave:
            if item.line and item.rel != 0:
                pl.when(item.valid)(getattr(item, name))
            else:
                getattr(item, name)()

    def begin(item):
        item.load().start()

    for wave in waves:
        for item in wave:
            item.begin = functools.partial(begin, item)
            item.begin_sib = functools.partial(lambda it: it.to_sib().start(), item)
    for wave in waves:
        run(wave, "begin")
    greet(place, any(lines), owners)
    for wave in waves:
        run(wave, "begin_sib")
    for w in range(len(waves) + 2):
        for lag, name in enumerate(("stage1", "stage2", "stage3")):
            if 0 <= w - lag < len(waves):
                run(waves[w - lag], name)
    for wave in waves:
        run(wave, "end")


def scatter(arrays, lines, subs, owners, cid):
    n = len(arrays)
    scratch, outs = [], []
    for a, line in zip(arrays, lines):
        zs = a.shape[0]
        groups, _, wide = a.shape[3:]
        half = (groups + 1) // 2
        zl = zs if line else 1
        lg = groups if line else 1
        scratch += [
            pltpu.VMEM((zs, 4, groups, G, wide), BF),
            pltpu.VMEM((zs, 4, groups, G, wide), BF),
            pltpu.VMEM((zs, 2, 2, half, G, wide), BF),
            pltpu.VMEM((zs, 2, half, G, wide), BF),
            pltpu.VMEM((zl, lg, G, wide if line else 128), BF),
            pltpu.VMEM((zl, lg, G, wide if line else 128), BF),
        ]
        outs.append(jax.ShapeDtypeStruct((groups, G, wide), F32))
    slots = max([2 * owners - 1 if any(lines) else 1] + list(subs))
    scratch += [pltpu.SemaphoreType.DMA((n, slots, 10)), pltpu.SemaphoreType.DMA((n, slots, 10))]
    return pl.pallas_call(
        functools.partial(scatter_kernel, owners, lines, subs),
        out_shape=outs,
        in_specs=[pl.BlockSpec(memory_space=pl.ANY)] * n,
        out_specs=[pl.BlockSpec(memory_space=pltpu.VMEM)] * n,
        scratch_shapes=scratch,
        compiler_params=pltpu.CompilerParams(collective_id=cid, has_side_effects=True, vmem_limit_bytes=60 * 1024 * 1024),
    )(*arrays)


def moe_kernel(
    steps,
    slots,
    chunk,
    m_ref,
    g_ref,
    member_ref,
    router_ref,
    order_ref,
    mine_ref,
    weights_ref,
    moe_ref,
    drow_ref,
    grads_ref,
    grouter_ref,
    router_s,
    gate_s,
    hg_s,
    dpre_s,
    mt_s,
    gt_s,
    gup_s,
    gdn_s,
    gr_s,
):
    step = pl.program_id(0)
    owners, _, share, units = weights_ref.shape
    per = chunk // F

    @pl.when(step == 0)
    def _():
        gup_s[...] = jnp.zeros_like(gup_s)
        gdn_s[...] = jnp.zeros_like(gdn_s)
        gr_s[...] = jnp.zeros_like(gr_s)
        router_s[...] = dot_nn(router_ref[...], order_ref[...]).astype(BF)

    mt_s[...] = m_ref[...].T
    gt_s[...] = g_ref[...].T
    sig = jax.nn.sigmoid(dot_nn(m_ref[...], router_s[...]))
    mask = dot_nn(member_ref[...], mine_ref[...])
    gate_s[...] = sig * mask
    root = math.sqrt(2.0 / math.pi)
    cube = 0.044715
    lane = lax.broadcasted_iota(jnp.int32, (1, F), 1)
    d_gate = jnp.zeros(gate_s.shape, F32)
    for c in range(units // chunk):
        cols = pl.ds(c * chunk, chunk)
        pre_all = dot_nn(m_ref[:, :share], weights_ref[0, 0, :, cols])
        back_all = dot_nn(g_ref[:, :share], weights_ref[0, 1, :, cols])
        for o in range(1, owners):
            part = pl.ds(o * share, share)
            pre_all += dot_nn(m_ref[:, part], weights_ref[o, 0, :, cols])
            back_all += dot_nn(g_ref[:, part], weights_ref[o, 1, :, cols])
        for j in range(per):
            slot = c * per + j
            part = slice(j * F, (j + 1) * F)
            pre = pre_all[:, part]
            back = back_all[:, part]
            square = pre * pre
            th = jnp.tanh(root * pre * (1.0 + cube * square))
            half = 0.5 * (1.0 + th)
            slope = half + (0.5 * root) * pre * (1.0 - th * th) * (1.0 + (3.0 * cube) * square)
            hidden = (pre * half).astype(BF).astype(F32)
            gate = gate_s[:, slot : slot + 1]
            d_one = jnp.sum(hidden * back, axis=1, keepdims=True)
            d_gate = d_gate + d_one * (lane == slot).astype(F32)
            where = pl.ds(slot * F, F)
            hg_s[:, where] = (gate * hidden).astype(BF)
            dpre_s[:, where] = (slope * (gate * back)).astype(BF)
    dlog = (d_gate * mask * sig * (1.0 - sig)).astype(BF)
    gr_s[...] += dot_nn(mt_s[...], dot_nt(dlog, order_ref[...]).astype(BF))
    for o in range(owners):
        where = pl.ds(o * share, share)
        moe_ref[:, where] = dot_nt(hg_s[...], weights_ref[o, 1]).astype(BF)
        drow_ref[:, where] = (
            dot_nt(dpre_s[...], weights_ref[o, 0]) + dot_nt(dlog, router_s[where, :])
        ).astype(BF)
        gup_s[where, :] += dot_nn(mt_s[where, :], dpre_s[...])
        gdn_s[where, :] += dot_nn(gt_s[where, :], hg_s[...])

    @pl.when(step == steps - 1)
    def _():
        for o in range(owners):
            grads_ref[o, 0] = gup_s[pl.ds(o * share, share), :].astype(BF)
            grads_ref[o, 1] = gdn_s[pl.ds(o * share, share), :].astype(BF)
        grouter_ref[...] = gr_s[...].astype(BF)


def moe(rows, cots, member, packed, router_at, order, mine, weights):
    count = rows.shape[0]
    tile = 512
    owners, _, share, units = weights.shape
    slots = units // F
    steps = count // tile
    lanes = member.shape[1]
    row_spec = pl.BlockSpec((tile, D), lambda i: (i, 0))
    whole = pl.BlockSpec(memory_space=pltpu.VMEM)
    router_spec = pl.BlockSpec((D, lanes), lambda i: (0, router_at // lanes))
    return pl.pallas_call(
        functools.partial(moe_kernel, steps, slots, 512),
        grid=(steps,),
        in_specs=[
            row_spec,
            row_spec,
            pl.BlockSpec((tile, lanes), lambda i: (i, 0)),
            router_spec,
            whole,
            whole,
            whole,
        ],
        out_specs=[row_spec, row_spec, whole, whole],
        out_shape=[
            jax.ShapeDtypeStruct((count, D), BF),
            jax.ShapeDtypeStruct((count, D), BF),
            jax.ShapeDtypeStruct(weights.shape, BF),
            jax.ShapeDtypeStruct((D, lanes), BF),
        ],
        scratch_shapes=[
            pltpu.VMEM((D, F), BF),
            pltpu.VMEM((tile, F), F32),
            pltpu.VMEM((tile, units), BF),
            pltpu.VMEM((tile, units), BF),
            pltpu.VMEM((D, tile), BF),
            pltpu.VMEM((D, tile), BF),
            pltpu.VMEM((D, units), F32),
            pltpu.VMEM((D, units), F32),
            pltpu.VMEM((D, lanes), F32),
        ],
        compiler_params=pltpu.CompilerParams(vmem_limit_bytes=60 * 1024 * 1024),
        cost_estimate=pl.CostEstimate(
            flops=12 * count * D * units,
            bytes_accessed=count * D * 8 + D * units * 8,
            transcendentals=count * units,
        ),
    )(rows, cots, member, packed, order, mine, weights)


def fused_kernel(owners, slots, wide, tile_cols, *refs):
    middle, cots, member, weights, packed, order_ref, mine_ref = refs[:7]
    drow_out, moe_out, grads_out, grouter_out = refs[7:11]
    (m_s, c_s, b_s, w_s, gup_s, gdn_s, gr_s, hg_s, dpre_s, mt_s, gt_s, router_in, router_s, gate_s) = refs[11:25]
    (sib_s, first_s, second_s, gsend, grecv, ssend, srecv, local, wsem) = refs[25:]
    place = Place()
    z = place.z
    count = middle.shape[0]
    half = count // 2
    lanes = b_s.shape[1]
    share = D // owners
    ins = (middle,)
    bufs = (m_s,)
    sums = (m_s, c_s)
    swap = place.sib - place.e
    mine = (place.e, place.xnb, place.ynb, place.diag)

    def span(e, start=0, size=count):
        return pl.ds(pl.multiple_of(e * count + start, 16), size)

    def remote(sems, a, kind, src, dst, to):
        return pltpu.make_async_remote_copy(
            src_ref=src, dst_ref=dst, send_sem=sems[0].at[a, kind], recv_sem=sems[1].at[a, kind],
            device_id=(z, to), device_id_type=MESH)

    def passing(a, kind):
        buf = bufs[a]
        if kind in (XS, YS, S0):
            src, at = ins[a], span(place.e)
        elif kind == FA:
            at = span(place.xnb, 0, half)
            src = buf.at[at]
        elif kind == FB:
            at = span(place.ynb, half, half)
            src = buf.at[at]
        else:
            at = span(mine[kind - S0])
            src = buf.at[at]
        to = {XS: place.xnb, YS: place.ynb, FA: place.ynb, FB: place.xnb}.get(kind, place.sib)
        return remote((gsend, grecv), a, kind, src, buf.at[at], to)

    def got(a, kind):
        at = {
            XS: lambda: span(place.xnb),
            YS: lambda: span(place.ynb),
            FA: lambda: span(place.diag, 0, half),
            FB: lambda: span(place.diag, half, half),
        }.get(kind, lambda: span(mine[kind - S0] + swap))()
        ref = bufs[a].at[at]
        remote((gsend, grecv), a, kind, ref, ref, place.sib).wait_recv()

    HY0, HY1, HX0, HX1, HX2, HY2 = 4, 5, 6, 7, 8, 9

    def to_sib(a, t):
        return remote((ssend, srecv), a, t, sums[a].at[span(mine[t] + swap)], sib_s.at[a, t], place.sib)

    def hop(a, kind):
        src_e, second, dst, to = {
            HY0: (place.ynb, False, first_s.at[a, 0], place.ynb),
            HY1: (place.diag, False, first_s.at[a, 1], place.ynb),
            HX0: (place.xnb, True, first_s.at[a, 2], place.xnb),
            HX1: (place.diag, True, first_s.at[a, 3], place.xnb),
            HX2: (place.xnb, False, second_s.at[a, 0], place.xnb),
            HY2: (place.ynb, True, second_s.at[a, 1], place.ynb),
        }[kind]
        src = sums[a].at[span(src_e, half if second else 0, half)]
        return remote((ssend, srecv), a, kind, src, dst, to)

    step_rows = 32

    def add(a, e, start, size, terms, keep=None):
        buf = sums[a]

        @pl.loop(0, size // step_rows)
        def _(g):
            here = pl.ds(pl.multiple_of(e * count + start + g * step_rows, 16), step_rows)
            there = pl.ds(pl.multiple_of(g * step_rows, 16), step_rows)
            total = buf[here, :].astype(F32)
            for lead in terms:
                total = total + lead[0][(*lead[1], there, slice(None))].astype(F32)
            if keep is None:
                buf[here, :] = total.astype(BF)
            else:
                keep[pl.ds(pl.multiple_of(start + g * step_rows, 16), step_rows), :] = total

    def with_sib(t):
        for a in (0, 1):
            to_sib(a, t).wait_recv()
            add(a, mine[t], 0, count, [(sib_s, (a, t))])

    own = [
        pltpu.make_async_copy(ins[a], bufs[a].at[span(place.e)], local.at[a]) for a in range(1)
    ]
    own += [
        pltpu.make_async_copy(cots, c_s, local.at[1]),
        pltpu.make_async_copy(member, b_s, local.at[2]),
    ]
    for c in own:
        c.start()
    router_copy = pltpu.make_async_copy(packed.at[:, pl.ds(wide, lanes)], router_in, local.at[3])
    router_copy.start()

    @pl.loop(0, slots)
    def _(s):
        for o in range(owners):
            for k in (0, 1):
                pltpu.make_async_copy(
                    weights.at[o, k * slots + s],
                    w_s.at[k, pl.ds(o * share, share), pl.ds(pl.multiple_of(s * F, F), F)],
                    wsem.at[0],
                ).start()

    greet(place, False, owners)
    for a in range(1):
        for kind in (XS, YS, S0):
            passing(a, kind).start()
    gup_s[...] = jnp.zeros_like(gup_s)
    gdn_s[...] = jnp.zeros_like(gdn_s)
    gr_s[...] = jnp.zeros_like(gr_s)

    root = math.sqrt(2.0 / math.pi)
    cube = 0.044715
    tile = 2 * count
    units = slots * F
    per = tile_cols // F

    @pl.loop(0, 4)
    def _(t):
        @pl.when(t == 0)
        def _():
            for c in own:
                c.wait()
            router_copy.wait()
            router_s[...] = dot_nn(router_in[...], order_ref[...]).astype(BF)
            for a in range(1):
                got(a, S0)
            pltpu.make_async_copy(w_s, w_s, wsem.at[0]).wait()

        @pl.when(t == 1)
        def _():
            for a in range(1):
                got(a, XS)
                passing(a, FA).start()
                passing(a, S1).start()
                got(a, YS)
                passing(a, FB).start()
                passing(a, S2).start()
            for a in range(1):
                got(a, S1)

        @pl.when(t == 2)
        def _():
            for a in range(1):
                got(a, FA)
                got(a, FB)
                passing(a, S3).start()
            for a in range(1):
                got(a, S2)

        @pl.when(t == 3)
        def _():
            for a in range(1):
                got(a, S3)

        tx, ty = t % 2, t // 2
        chip_x = place.x + tx * (1 - 2 * place.x)
        chip_y = place.y + ty * (1 - 2 * place.y)
        chip = chip_y * 2 + chip_x
        here = pl.ds(pl.multiple_of(chip * tile, 16), tile)
        mt_s[...] = m_s[here, :].T
        gt_s[...] = c_s[here, :].T
        sig = jax.nn.sigmoid(dot_nn(m_s[here, :], router_s[...]))
        mask = dot_nn(b_s[here, :], mine_ref[...])
        gate_s[...] = sig * mask
        lane = lax.broadcasted_iota(jnp.int32, (1, F), 1)
        d_gate = jnp.zeros(gate_s.shape, F32)
        for c in range(units // tile_cols):
            cols = pl.ds(c * tile_cols, tile_cols)
            pre_all = dot_nn(m_s[here, :], w_s[0, :, cols])
            back_all = dot_nn(c_s[here, :], w_s[1, :, cols])
            for j in range(per):
                slot = c * per + j
                part = slice(j * F, (j + 1) * F)
                pre = pre_all[:, part]
                back = back_all[:, part]
                square = pre * pre
                th = jnp.tanh(root * pre * (1.0 + cube * square))
                halved = 0.5 * (1.0 + th)
                slope = halved + (0.5 * root) * pre * (1.0 - th * th) * (1.0 + (3.0 * cube) * square)
                hidden = (pre * halved).astype(BF).astype(F32)
                gate = gate_s[:, slot : slot + 1]
                d_one = jnp.sum(hidden * back, axis=1, keepdims=True)
                d_gate = d_gate + d_one * (lane == slot).astype(F32)
                where = pl.ds(slot * F, F)
                hg_s[:, where] = (gate * hidden).astype(BF)
                dpre_s[:, where] = (slope * (gate * back)).astype(BF)
        dlog = (d_gate * mask * sig * (1.0 - sig)).astype(BF)
        gr_s[...] += dot_nn(mt_s[...], dot_nt(dlog, order_ref[...]).astype(BF))

        @pl.when(t == 1)
        def _():
            with_sib(0)
            for a in range(1):
                passing(a, FA).wait_send()
                passing(a, S1).wait_send()

        @pl.when(t == 2)
        def _():
            with_sib(1)
            for a in (0, 1):
                hop(a, HX0).start()
            for a in range(1):
                passing(a, FB).wait_send()
                passing(a, S2).wait_send()

        @pl.when(t == 3)
        def _():
            with_sib(2)
            for a in (0, 1):
                hop(a, HY0).start()
            for a in range(1):
                passing(a, S3).wait_send()

        for n in range(D // 256):
            where = pl.ds(n * 256, 256)
            m_s[here, where] = (
                dot_nt(dpre_s[...], w_s[0, where, :]) + dot_nt(dlog, router_s[where, :])
            ).astype(BF)
        for k in range(4):

            @pl.when(t == k)
            def _():
                to_sib(0, k).start()

        for n in range(D // 256):
            where = pl.ds(n * 256, 256)
            c_s[here, where] = dot_nt(hg_s[...], w_s[1, where, :]).astype(BF)
        for k in range(4):

            @pl.when(t == k)
            def _():
                to_sib(1, k).start()

        def last(a):
            @pl.when(t == 3)
            def _():
                to_sib(a, 3).wait_recv()
                add(a, mine[3], 0, count, [(sib_s, (a, 3))])
                hop(a, HY1).start()
                hop(a, HX1).start()

        last(0)
        for n in range(D // 256):
            where = pl.ds(n * 256, 256)
            gup_s[where, :] += dot_nn(mt_s[where, :], dpre_s[...])
        last(1)
        for n in range(D // 256):
            where = pl.ds(n * 256, 256)
            gdn_s[where, :] += dot_nn(gt_s[where, :], hg_s[...])

    for a in (0, 1):
        hop(a, HY1).wait_recv()
        add(a, place.xnb, 0, half, [(first_s, (a, 1))])
        hop(a, HX2).start()
        hop(a, HX1).wait_recv()
        add(a, place.ynb, half, half, [(first_s, (a, 3))])
        hop(a, HY2).start()
    w_s[0] = gup_s[...].astype(BF)
    w_s[1] = gdn_s[...].astype(BF)

    @pl.loop(0, slots)
    def _(s):
        for o in range(owners):
            for k in (0, 1):
                pltpu.make_async_copy(
                    w_s.at[k, pl.ds(o * share, share), pl.ds(pl.multiple_of(s * F, F), F)],
                    grads_out.at[o, k * slots + s],
                    wsem.at[0],
                ).start()

    grouter_out[...] = gr_s[...].astype(BF)
    for a, out in ((0, drow_out), (1, moe_out)):
        hop(a, HY0).wait_recv()
        hop(a, HX2).wait_recv()
        add(a, place.e, 0, half, [(first_s, (a, 0)), (second_s, (a, 0))], out)
        hop(a, HX0).wait_recv()
        hop(a, HY2).wait_recv()
        add(a, place.e, half, half, [(first_s, (a, 2)), (second_s, (a, 1))], out)
    for a in range(1):
        for kind in (XS, YS, S0):
            passing(a, kind).wait_send()
    for a in (0, 1):
        for t in range(4):
            to_sib(a, t).wait_send()
        for kind in (HY0, HY1, HX0, HX1, HX2, HY2):
            hop(a, kind).wait_send()
    pltpu.make_async_copy(w_s, w_s, wsem.at[0]).wait()


def fused_experts(middle, cots, member, weights, packed, wide, order, mine, cid):
    count = middle.shape[0]
    owners = weights.shape[0]
    slots = weights.shape[1] // 2
    lanes = member.shape[1]
    units = slots * F
    tile = 2 * count
    hbm = pl.BlockSpec(memory_space=pl.ANY)
    vmem = pl.BlockSpec(memory_space=pltpu.VMEM)
    dma = pltpu.SemaphoreType.DMA
    return pl.pallas_call(
        functools.partial(fused_kernel, owners, slots, wide, 256),
        in_specs=[hbm] * 5 + [vmem] * 2,
        out_specs=[vmem, vmem, hbm, vmem],
        out_shape=[
            jax.ShapeDtypeStruct((count, D), F32),
            jax.ShapeDtypeStruct((count, D), F32),
            jax.ShapeDtypeStruct(weights.shape, BF),
            jax.ShapeDtypeStruct((D, lanes), BF),
        ],
        scratch_shapes=[
            pltpu.VMEM((8 * count, D), BF),
            pltpu.VMEM((8 * count, D), BF),
            pltpu.VMEM((8 * count, lanes), BF),
            pltpu.VMEM((2, D, units), BF),
            pltpu.VMEM((D, units), F32),
            pltpu.VMEM((D, units), F32),
            pltpu.VMEM((D, lanes), F32),
            pltpu.VMEM((tile, units), BF),
            pltpu.VMEM((tile, units), BF),
            pltpu.VMEM((D, tile), BF),
            pltpu.VMEM((D, tile), BF),
            pltpu.VMEM((D, lanes), BF),
            pltpu.VMEM((D, F), BF),
            pltpu.VMEM((tile, F), F32),
            pltpu.VMEM((2, 4, count, D), BF),
            pltpu.VMEM((2, 4, count // 2, D), BF),
            pltpu.VMEM((2, 2, count // 2, D), BF),
            dma((1, 8)),
            dma((1, 8)),
            dma((2, 10)),
            dma((2, 10)),
            dma((4,)),
            dma((1,)),
        ],
        compiler_params=pltpu.CompilerParams(
            collective_id=cid, has_side_effects=True, vmem_limit_bytes=64 * 1024 * 1024 - 65536
        ),
        cost_estimate=pl.CostEstimate(
            flops=12 * 8 * count * D * units,
            bytes_accessed=D * units * 8,
            transcendentals=8 * count * units,
        ),
    )(middle, cots, member, weights, packed, order, mine)


def forward_kernel(
    wide,
    lanes,
    lengths_ref,
    x_ref,
    choice_ref,
    w_ref,
    heads_ref,
    qk_ref,
    vals_ref,
    sig_ref,
    mask_ref,
    vlow_ref,
    prob_ref,
    attended_ref,
    mixed_ref,
    middle_ref,
    mlow_ref,
):
    count = x_ref.shape[0]
    seq = count // MB
    xf = x_ref[...].astype(F32)
    centred = xf - jnp.mean(xf, axis=1, keepdims=True)
    variance = jnp.mean(centred * centred, axis=1, keepdims=True)
    gain_row = w_ref[:, pl.ds(wide + lanes, 128)].astype(F32).T[SEL : SEL + 1, :]
    normed = (centred * lax.rsqrt(variance + epsilon) * gain_row).astype(BF)
    for n in range(QK // 512):
        cols = pl.ds(n * 512, 512)
        qk_ref[:, cols] = dot_nn(normed, w_ref[:, cols]).astype(BF)
    sig = jax.nn.sigmoid(dot_nn(x_ref[...], w_ref[:, pl.ds(wide + lanes, 128)]))
    row = lax.broadcasted_iota(jnp.int32, (count, 128), 0)
    lane = lax.broadcasted_iota(jnp.int32, (count, 128), 1)
    live = (row < lengths_ref[0, 0]).astype(F32)
    for b in range(1, MB):
        live = jnp.where(row < b * seq, live, (row < b * seq + lengths_ref[b, 0]).astype(F32))
    mask = jnp.zeros((count, 128), F32)
    top = choice_ref.shape[1] // H
    for v in range(H * top):
        picked = choice_ref[:, v : v + 1] + NV * (v // top)
        mask = mask + (picked == lane).astype(F32) + (picked + H * NV == lane).astype(F32) * live
    sig_ref[...] = sig
    mask_ref[...] = mask
    gates = sig * mask
    for h in range(H):
        vals = dot_nn(x_ref[...], w_ref[:, pl.ds(QK + h * NV * HD, NV * HD)])
        vals_ref[:, pl.ds(h * NV * HD, NV * HD)] = vals
        total = gates[:, h * NV : h * NV + 1] * vals[:, :HD]
        for e in range(1, NV):
            at = h * NV + e
            total = total + gates[:, at : at + 1] * vals[:, e * HD : (e + 1) * HD]
        vlow_ref[:, pl.ds(h * HD, HD)] = total.astype(BF)
    at_i = lax.broadcasted_iota(jnp.int32, (seq, seq), 0)
    at_j = lax.broadcasted_iota(jnp.int32, (seq, seq), 1)
    for b in range(MB):
        allowed = (at_j <= at_i) & (at_j < lengths_ref[b, 0])
        here = pl.ds(b * seq, seq)
        for h in range(H):
            queries = qk_ref[here, pl.ds(h * HD, HD)]
            keys_all = qk_ref[here, pl.ds((H + h) * HD, HD)]
            scores = jnp.where(allowed, dot_nt(queries, keys_all) * HD ** (-0.5), -1e30)
            expo = jnp.exp(scores - jnp.max(scores, axis=1, keepdims=True))
            prob = expo / jnp.sum(expo, axis=1, keepdims=True)
            prob_ref[b * H + h] = prob
            attended_ref[here, pl.ds(h * HD, HD)] = dot_nn(
                prob.astype(BF), vlow_ref[here, pl.ds(h * HD, HD)]
            )
    for h in range(H):
        attended = attended_ref[:, pl.ds(h * HD, HD)]
        for e in range(NV):
            at = h * NV + e
            gate = gates[:, H * NV + at : H * NV + at + 1]
            mixed_ref[:, pl.ds(at * HD, HD)] = (gate * attended).astype(BF)
    for n in range(D // 512):
        cols = pl.ds(n * 512, 512)
        middle = x_ref[:, cols].astype(F32) + dot_nn(mixed_ref[...], heads_ref[:, cols])
        middle_ref[:, cols] = middle
        mlow_ref[:, cols] = middle.astype(BF)


def forward(lengths, tokens, choice, packed, heads, wide, lanes):
    count = tokens.shape[0]
    seq = count // MB
    vmem = pl.BlockSpec(memory_space=pltpu.VMEM)
    shape = jax.ShapeDtypeStruct
    return pl.pallas_call(
        functools.partial(forward_kernel, wide, lanes),
        in_specs=[pl.BlockSpec(memory_space=pltpu.SMEM)] + [vmem] * 4,
        out_specs=[vmem] * 10,
        out_shape=[
            shape((count, QK), BF),
            shape((count, VAL), F32),
            shape((count, 128), F32),
            shape((count, 128), F32),
            shape((count, H * HD), BF),
            shape((MB * H, seq, seq), F32),
            shape((count, H * HD), F32),
            shape((count, VAL), BF),
            shape((count, D), F32),
            shape((count, D), BF),
        ],
        compiler_params=pltpu.CompilerParams(vmem_limit_bytes=56 * 1024 * 1024),
        cost_estimate=pl.CostEstimate(
            flops=2 * count * D * (wide + VAL),
            bytes_accessed=(wide + VAL) * D * 2 + count * D * 20,
            transcendentals=count * seq * H,
        ),
    )(lengths, tokens, choice, packed, heads)


def backward_kernel(
    wide,
    lanes,
    x_ref,
    cots_ref,
    drow_ref,
    moe_ref,
    middle_ref,
    qk_ref,
    vals_ref,
    sig_ref,
    mask_ref,
    vlow_ref,
    prob_ref,
    attended_ref,
    mixed_ref,
    grouter_ref,
    w_ref,
    heads_ref,
    out_ref,
    dx_ref,
    gw_ref,
    gheads_ref,
    dvals_s,
    dqk_s,
):
    count = x_ref.shape[0]
    seq = count // MB
    out_ref[...] = (middle_ref[...] + moe_ref[...]).astype(BF)
    d_middle = cots_ref[...].astype(F32) + drow_ref[...]
    d_branch = d_middle.astype(BF)
    mask = mask_ref[...]
    sig = sig_ref[...]
    gates = sig * mask
    lane = lax.broadcasted_iota(jnp.int32, (1, 128), 1)
    d_gates = jnp.zeros((count, 128), F32)
    width = NV * HD
    for h in range(H):
        where = pl.ds(h * width, width)
        gheads_ref[where, :] = dot_tn(mixed_ref[:, where], d_branch).astype(BF)
        d_mixed = dot_nt(d_branch, heads_ref[where, :])
        attended = attended_ref[:, pl.ds(h * HD, HD)]
        total = jnp.zeros((count, HD), F32)
        for e in range(NV):
            at = H * NV + h * NV + e
            part = d_mixed[:, e * HD : (e + 1) * HD]
            total = total + gates[:, at : at + 1] * part
            d_one = jnp.sum(part * attended, axis=1, keepdims=True)
            d_gates = d_gates + d_one * (lane == at).astype(F32)
        d_attended = total.astype(BF)
        d_values = []
        for b in range(MB):
            here = pl.ds(b * seq, seq)
            rows = slice(b * seq, (b + 1) * seq)
            prob = prob_ref[b * H + h]
            values = vlow_ref[here, pl.ds(h * HD, HD)]
            d_prob = dot_nt(d_attended[rows], values)
            d_scores = (
                prob * (d_prob - jnp.sum(prob * d_prob, axis=1, keepdims=True))
            ).astype(BF)
            d_values.append(dot_tn(prob.astype(BF), d_attended[rows]).astype(BF).astype(F32))
            queries = qk_ref[here, pl.ds(h * HD, HD)]
            keys_all = qk_ref[here, pl.ds((H + h) * HD, HD)]
            dqk_s[here, pl.ds(h * HD, HD)] = (dot_nn(d_scores, keys_all) * HD ** (-0.5)).astype(BF)
            dqk_s[here, pl.ds((H + h) * HD, HD)] = (
                dot_tn(d_scores, queries) * HD ** (-0.5)
            ).astype(BF)
        d_value = jnp.concatenate(d_values, axis=0)
        for e in range(NV):
            at = h * NV + e
            cols = pl.ds(at * HD, HD)
            d_one = jnp.sum(d_value * vals_ref[:, cols], axis=1, keepdims=True)
            d_gates = d_gates + d_one * (lane == at).astype(F32)
            dvals_s[:, cols] = (gates[:, at : at + 1] * d_value).astype(BF)
    d_select = (d_gates * mask * sig * (1.0 - sig)).astype(BF)
    x_t = x_ref[...].T
    for n in range(VAL // 512):
        cols = pl.ds(n * 512, 512)
        gw_ref[:, pl.ds(QK + n * 512, 512)] = dot_nn(x_t, dvals_s[:, cols]).astype(BF)
    xf = x_ref[...].astype(F32)
    centred = xf - jnp.mean(xf, axis=1, keepdims=True)
    variance = jnp.mean(centred * centred, axis=1, keepdims=True)
    rstd = lax.rsqrt(variance + epsilon)
    unit = centred * rstd
    gain_row = w_ref[:, pl.ds(wide + lanes, 128)].astype(F32).T[SEL : SEL + 1, :]
    normed_t = (unit * gain_row).astype(BF).T
    for n in range(QK // 512):
        cols = pl.ds(n * 512, 512)
        gw_ref[:, cols] = dot_nn(normed_t, dqk_s[:, cols]).astype(BF)
    d_normed = dot_nt(dqk_s[...], w_ref[:, pl.ds(0, QK)])
    grad_gain = jnp.sum(d_normed * unit, axis=0, keepdims=True)
    small = dot_tn(d_select, x_ref[...])
    which = lax.broadcasted_iota(jnp.int32, (128, 1), 0)
    gw_ref[:, pl.ds(wide + lanes, 128)] = jnp.where(which == SEL, grad_gain, small).T.astype(BF)
    gw_ref[:, pl.ds(wide, lanes)] = grouter_ref[...]
    scaled = d_normed * gain_row
    dx_ref[...] = (
        d_middle
        + (
            scaled
            - jnp.mean(scaled, axis=1, keepdims=True)
            - unit * jnp.mean(scaled * unit, axis=1, keepdims=True)
        )
        * rstd
    )
    for n in range(D // 256):
        rows = pl.ds(n * 256, 256)
        dx_ref[:, rows] += dot_nt(dvals_s[...], w_ref[rows, pl.ds(QK, VAL)]) + dot_nt(
            d_select, w_ref[rows, pl.ds(wide + lanes, 128)]
        )


def backward(tokens, cots, drow, moe_sum, saved, grouter, packed, heads, wide, lanes):
    count = tokens.shape[0]
    qk, vals, sig, mask, vlow, prob, attended, mixed, middle = saved
    vmem = pl.BlockSpec(memory_space=pltpu.VMEM)
    shape = jax.ShapeDtypeStruct
    return pl.pallas_call(
        functools.partial(backward_kernel, wide, lanes),
        in_specs=[vmem] * 16,
        out_specs=[vmem] * 4,
        out_shape=[
            shape((count, D), BF),
            shape((count, D), F32),
            shape(packed.shape, BF),
            shape(heads.shape, BF),
        ],
        scratch_shapes=[pltpu.VMEM((count, VAL), BF), pltpu.VMEM((count, QK), BF)],
        compiler_params=pltpu.CompilerParams(vmem_limit_bytes=62 * 1024 * 1024),
        cost_estimate=pl.CostEstimate(
            flops=4 * count * D * (wide + VAL),
            bytes_accessed=(wide + VAL) * D * 4 + count * D * 30,
            transcendentals=0,
        ),
    )(
        tokens,
        cots,
        drow,
        moe_sum,
        middle,
        qk,
        vals,
        sig,
        mask,
        vlow,
        prob,
        attended,
        mixed,
        grouter,
        packed,
        heads,
    )


def body(
    tokens,
    cotangent,
    lengths,
    routes,
    head_choice,
    placement,
    gain_master,
    gain_moment,
    gain_average,
    qkv_master,
    qkv_moment,
    qkv_average,
    select_master,
    select_moment,
    select_average,
    router_master,
    router_moment,
    router_average,
    heads_out_master,
    heads_out_moment,
    heads_out_average,
    up_master,
    up_moment,
    up_average,
    down_master,
    down_moment,
    down_average,
):
    both = ("dp", "expert")
    owners = lax.axis_size("dp")
    group = lax.axis_size("expert")
    own_kernels = group == 8
    experts = placement.shape[0]
    slots = up_master.shape[0]
    units = slots * F
    seq = tokens.shape[1]
    count = MB * seq
    share = up_master.shape[1]
    mine = lax.axis_index("expert")
    lanes = -(-experts // 128) * 128

    own_rows = qkv_master.shape[0]
    wide = QK + VAL
    packed = jnp.concatenate(
        [
            qkv_master.astype(BF),
            router_master.astype(BF),
            jnp.zeros((own_rows, lanes - experts), BF),
            select_master.astype(BF),
            gain_master.astype(BF)[:, None],
            jnp.zeros((own_rows, 127 - SEL), BF),
        ],
        axis=1,
    )
    heads_low = heads_out_master.astype(BF)

    experts_low = jnp.concatenate([up_master.astype(BF), down_master.astype(BF)], axis=0)
    weights = lax.all_gather(experts_low, "dp", axis=0, tiled=False)

    flat_tokens = tokens.reshape(count, D)
    flat_cots = cotangent.reshape(count, D)
    live = (jnp.arange(seq, dtype=jnp.int32)[None, :] < lengths).astype(F32).reshape(count)
    lane_ids = jnp.arange(lanes, dtype=jnp.int32)
    named = jnp.sum(
        (routes.reshape(count, TOPK)[..., None] == lane_ids).astype(F32), axis=1
    ) * live[:, None]
    padded = jnp.pad(placement, (0, lanes - experts), constant_values=-1)
    perm = (padded[:, None] == lane_ids[None, :]).astype(BF)
    member = dot_nn(named.astype(BF), perm).astype(BF)
    own_lane = jnp.arange(F, dtype=jnp.int32)[None, :]
    mine_sel = (((lane_ids[:, None] - mine * slots) == own_lane) & (own_lane < slots)).astype(BF)
    order_mine = (
        ((padded[:, None] - mine * slots) == own_lane) & (own_lane < slots) & (padded[:, None] >= 0)
    ).astype(BF)

    if own_kernels:
        packed_all, heads, cots_all, member_all = gather(
            (packed, heads_low, flat_cots, member),
            (True, True, False, False),
            (own_rows // 2, 48, count // 2, count // 2),
            owners,
            group,
            0,
        )
    else:
        packed_all = lax.all_gather(packed, both, axis=0, tiled=True)
        heads = lax.all_gather(heads_low, both, axis=0, tiled=True)
        cots_all, member_all = (
            lax.all_gather(a, "expert", axis=0, tiled=True) for a in (flat_cots, member)
        )
    choice = head_choice.reshape(count, -1)
    *saved, middle_low = forward(lengths, flat_tokens, choice, packed_all, heads, wide, lanes)
    if own_kernels:
        d_from_rows, moe_sum, expert_grads, grad_router = fused_experts(
            middle_low, cots_all, member_all, weights, packed_all, wide, order_mine, mine_sel, 1
        )
    else:
        rows_all = lax.all_gather(middle_low, "expert", axis=0, tiled=True)
        side = weights.reshape(owners, 2, slots, share, F).transpose(0, 1, 3, 2, 4)
        moe_part, drow_part, expert_grads, grad_router = moe(
            rows_all,
            cots_all,
            member_all,
            packed_all,
            wide,
            order_mine,
            mine_sel,
            side.reshape(owners, 2, share, units),
        )
        expert_grads = expert_grads.reshape(owners, 2, share, slots, F).transpose(0, 1, 3, 2, 4)
        d_from_rows, moe_sum = (
            lax.psum_scatter(a, "expert", scatter_dimension=0, tiled=True).astype(F32)
            for a in (drow_part, moe_part)
        )
    expert_sum = lax.psum_scatter(
        expert_grads.reshape(owners * 2 * slots, share, F), "dp", scatter_dimension=0, tiled=True
    ).astype(F32)
    mixed, d_tokens, grad_packed, grad_heads = backward(
        flat_tokens,
        flat_cots,
        d_from_rows,
        moe_sum,
        saved,
        grad_router,
        packed_all,
        heads,
        wide,
        lanes,
    )
    if own_kernels:
        packed_sum, heads_sum = (
            total.reshape(-1, total.shape[2])
            for total in scatter(
                tuple(g.reshape(owners, 4, 2, -1, G, g.shape[1]) for g in (grad_packed, grad_heads)),
                (True, True),
                (1, 1),
                owners,
                3,
            )
        )
    else:
        packed_sum, heads_sum = (
            lax.psum_scatter(g, both, scatter_dimension=0, tiled=True).astype(F32)
            for g in (grad_packed, grad_heads)
        )
    qkv_sum = packed_sum[:, :wide]
    router_sum = packed_sum[:, wide : wide + experts]
    select_sum = packed_sum[:, wide + lanes : wide + lanes + SEL]
    gain_sum = packed_sum[:, wide + lanes + SEL]
    up_sum = expert_sum[:slots]
    down_sum = expert_sum[slots:]

    rates = step_rates(count * owners * group, experts)
    outs = (
        update_weight(gain_master, gain_moment, gain_average, gain_sum, rates[0])
        + update_weight(qkv_master, qkv_moment, qkv_average, qkv_sum, rates[1])
        + update_weight(select_master, select_moment, select_average, select_sum, rates[2])
        + update_weight(router_master, router_moment, router_average, router_sum, rates[3])
        + update_weight(heads_out_master, heads_out_moment, heads_out_average, heads_sum, rates[4])
        + update_weight(up_master, up_moment, up_average, up_sum, rates[5])
        + update_weight(down_master, down_moment, down_average, down_sum, rates[6])
    )
    return (mixed.reshape(tokens.shape), d_tokens.reshape(tokens.shape)) + outs


def solution(mesh):
    rows = P(None, ("dp", "expert"), None)
    flat = P(("dp", "expert"))
    dense = P(("dp", "expert"), None)
    expert = P("expert", "dp", None)
    in_specs = (
        rows,
        rows,
        P(None, ("dp", "expert")),
        rows,
        P(None, ("dp", "expert"), None, None),
        P(),
        *((flat,) * 3),
        *((dense,) * 12),
        *((expert,) * 6),
    )
    out_specs = (rows, rows, *((flat,) * 4), *((dense,) * 16), *((expert,) * 8))
    return jax.shard_map(body, mesh=mesh, in_specs=in_specs, out_specs=out_specs, check_vma=False)
```

```python
import functools
import math

import jax
import jax.numpy as jnp
from jax import lax
from jax.experimental import pallas as pl
from jax.experimental.pallas import tpu as pltpu
from jax.sharding import PartitionSpec as P

D = 1024
H = 4
HD = 128
NV = 5
F = 128
TOPK = 16
MB = 2
QK = 2 * H * HD
VAL = H * NV * HD
SEL = 2 * H * NV

momentum_decay = 0.9
average_decay = 0.5
rate_factor = 0.4
epsilon = 1e-05
BF = jnp.bfloat16
F32 = jnp.float32


def step_rates(total_tokens, experts):
    root_tokens = math.sqrt(total_tokens)
    expert_share = math.sqrt(TOPK / experts)
    spread_list = (
        0.3,
        D ** (-0.5),
        (2 * D) ** (-0.5),
        (9 * D) ** (-0.5),
        0.5,
        D ** (-0.5),
        (4 * F) ** (-0.5),
    )
    gradient_list = (1.0, 1.0, 3.0, 2.0 * expert_share, 0.1, 0.5 * expert_share, 0.4 * expert_share)
    return tuple(
        rate_factor * spread_value / (gradient_value * root_tokens)
        for spread_value, gradient_value in zip(spread_list, gradient_list)
    )


def update_weight(master, moment, average, gradient, step_size):
    new_moment = momentum_decay * moment + gradient
    new_weight = master - step_size * (gradient + momentum_decay * new_moment)
    new_average = average_decay * average + (1.0 - average_decay) * new_weight
    return (new_moment, new_average, new_weight, new_weight.astype(BF))


def dot_nt(a, b):
    return lax.dot_general(a, b, (((1,), (1,)), ((), ())), preferred_element_type=F32)


def dot_tn(a, b):
    return lax.dot_general(a, b, (((0,), (0,)), ((), ())), preferred_element_type=F32)


def dot_nn(a, b):
    return jnp.dot(a, b, preferred_element_type=F32)


MESH = pl.DeviceIdType.MESH


class Place:
    def __init__(self):
        self.z = lax.axis_index("dp")
        self.e = lax.axis_index("expert")
        core = self.e % 2
        x = (self.e // 2) % 2
        y = self.e // 4
        self.sib = self.e + 1 - 2 * core
        self.xnb = self.e + 2 - 4 * x
        self.ynb = self.e + 4 - 8 * y
        self.diag = self.xnb + 4 - 8 * y
        self.core, self.x, self.y = core, x, y


def greet(place, line, owners):
    barrier = pltpu.get_barrier_semaphore()
    z = place.z
    for e in (place.sib, place.xnb, place.ynb):
        pl.semaphore_signal(barrier, inc=1, device_id=(z, e), device_id_type=MESH)
    peers = 3
    if line:

        @pl.when(z > 0)
        def _():
            pl.semaphore_signal(barrier, inc=1, device_id=(z - 1, place.e), device_id_type=MESH)

        @pl.when(z < owners - 1)
        def _():
            pl.semaphore_signal(barrier, inc=1, device_id=(z + 1, place.e), device_id_type=MESH)

        peers = peers + (z + owners - 1) // owners + (2 * owners - 2 - z) // owners
    pl.semaphore_wait(barrier, peers)


XS, YS, FA, FB, S0, S1, S2, S3, UP, DOWN = range(10)

def gather_kernel(owners, group, lines, halves, *refs):
    n = len(lines)
    ins, outs, (send, recv, own) = refs[:n], refs[n : 2 * n], refs[2 * n :]
    place = Place()
    z = place.z
    copies_own = []
    for i in range(n):
        rows = ins[i].shape[0]
        slot = (z * group + place.e) if lines[i] else place.e
        cp = pltpu.make_async_copy(ins[i], outs[i].at[pl.ds(slot * rows, rows)], own.at[i])
        cp.start()
        copies_own.append(cp)
    greet(place, any(lines), owners)

    def block(i, rel, e, part=None):
        rows = ins[i].shape[0]
        slot = ((z + rel) * group + e) if lines[i] else e
        start, size = (0, rows) if part is None else part
        return outs[i].at[pl.ds(slot * rows + start, size)]

    def source(i, rel, part=None):
        if rel == 0:
            return ins[i] if part is None else ins[i].at[pl.ds(*part)]
        return block(i, rel, place.e, part)

    def sem(rel):
        return rel + owners - 1

    def go(i, rel, kind, src, dst, to_e, dz=0):
        return pltpu.make_async_remote_copy(
            src_ref=src, dst_ref=dst, send_sem=send.at[i, sem(rel), kind],
            recv_sem=recv.at[i, sem(rel - dz), min(kind, UP)],
            device_id=(z + dz, to_e), device_id_type=MESH)

    def parts(i):
        rows = ins[i].shape[0]
        return (0, halves[i]), (halves[i], rows - halves[i])

    def valid(rel):
        return (z + rel >= 0) & (z + rel < owners)

    def copies(i, rel):
        first, second = parts(i)
        e, xn, yn, dg, sb = place.e, place.xnb, place.ynb, place.diag, place.sib
        return {
            XS: lambda: go(i, rel, XS, source(i, rel), block(i, rel, e), xn),
            YS: lambda: go(i, rel, YS, source(i, rel), block(i, rel, e), yn),
            FA: lambda: go(i, rel, FA, block(i, rel, xn, first), block(i, rel, xn, first), yn),
            FB: lambda: go(i, rel, FB, block(i, rel, yn, second), block(i, rel, yn, second), xn),
            S0: lambda: go(i, rel, S0, source(i, rel), block(i, rel, e), sb),
            S1: lambda: go(i, rel, S1, block(i, rel, xn), block(i, rel, xn), sb),
            S2: lambda: go(i, rel, S2, block(i, rel, yn), block(i, rel, yn), sb),
            S3: lambda: go(i, rel, S3, block(i, rel, dg), block(i, rel, dg), sb),
        }

    def got(i, rel, kind, e, part=None):
        ref = block(i, rel, e, part)
        pltpu.make_async_remote_copy(
            src_ref=ref, dst_ref=ref, send_sem=send.at[i, sem(rel), min(kind, UP)], recv_sem=recv.at[i, sem(rel), min(kind, UP)],
            device_id=(z, place.sib), device_id_type=MESH).wait_recv()

    def stage_z(rel):
        @pl.when(valid(rel))
        def _():
            for i in range(n):
                if rel != 0 and not lines[i]:
                    continue
                if rel != 0:
                    got(i, rel, UP, place.e)
                if lines[i] and rel <= 0 and rel > 1 - owners:
                    @pl.when(z < owners - 1)
                    def _():
                        go(i, rel, UP, source(i, rel), block(i, rel, place.e), place.e, 1).start()
                if lines[i] and rel >= 0 and rel < owners - 1:
                    @pl.when(z > 0)
                    def _():
                        go(i, rel, DOWN, source(i, rel), block(i, rel, place.e), place.e, -1).start()
                c = copies(i, rel)
                c[XS]().start()
                c[YS]().start()
                c[S0]().start()

    def each(rel, fn):
        @pl.when(valid(rel))
        def _():
            for i in range(n):
                if rel == 0 or lines[i]:
                    fn(i, rel, copies(i, rel))

    def xy(i, rel, c):
        got(i, rel, XS, place.xnb)
        c[FA]().start()
        c[S1]().start()
        got(i, rel, YS, place.ynb)
        c[FB]().start()
        c[S2]().start()

    def dg(i, rel, c):
        first, second = parts(i)
        got(i, rel, FA, place.diag, first)
        got(i, rel, FB, place.diag, second)
        c[S3]().start()

    def end(i, rel, c):
        for k, e in ((S0, place.sib),):
            got(i, rel, S0, place.sib)
        got(i, rel, S1, place.xnb + place.sib - place.e)
        got(i, rel, S2, place.ynb + place.sib - place.e)
        got(i, rel, S3, place.diag + place.sib - place.e)
        for k in (XS, YS, FA, FB, S0, S1, S2, S3):
            c[k]().wait_send()
        if lines[i] and rel <= 0 and rel > 1 - owners:
            @pl.when(z < owners - 1)
            def _():
                go(i, rel, UP, source(i, rel), block(i, rel, place.e), place.e, 1).wait_send()
        if lines[i] and rel >= 0 and rel < owners - 1:
            @pl.when(z > 0)
            def _():
                go(i, rel, DOWN, source(i, rel), block(i, rel, place.e), place.e, -1).wait_send()

    rels = [0] + [s * d for d in range(1, owners) for s in (-1, 1)]
    waves = [[0]] + [[-d, d] for d in range(1, owners)]
    for w in range(owners + 3):
        if w < owners:
            for r in waves[w]:
                stage_z(r)
        if 0 <= w - 1 < owners:
            for r in waves[w - 1]:
                each(r, xy)
        if 0 <= w - 2 < owners:
            for r in waves[w - 2]:
                each(r, dg)
    for cp in copies_own:
        cp.wait()
    for r in rels:
        each(r, end)


def gather(arrays, lines, halves, owners, group, cid):
    outs = [jax.ShapeDtypeStruct((a.shape[0] * (owners if l else 1) * group,) + a.shape[1:], a.dtype) for a, l in zip(arrays, lines)]
    n = len(arrays)
    any_spec = pl.BlockSpec(memory_space=pl.ANY)
    return pl.pallas_call(
        functools.partial(gather_kernel, owners, group, lines, halves),
        out_shape=outs, in_specs=[any_spec] * n, out_specs=[any_spec] * n,
        scratch_shapes=[pltpu.SemaphoreType.DMA((n, 2 * owners - 1, 10)), pltpu.SemaphoreType.DMA((n, 2 * owners - 1, 9)), pltpu.SemaphoreType.DMA((n,))],
        compiler_params=pltpu.CompilerParams(collective_id=cid, has_side_effects=True),
    )(*arrays)


G = 16
(LOAD, SIB, Y0, Y1, X0, X1, X2, Y2, UP, DOWN) = range(10)


def scatter_kernel(owners, lines, subs, *refs):
    n = len(lines)
    ins, outs, scratch = refs[:n], refs[n : 2 * n], refs[2 * n :]
    send, recv = scratch[6 * n :]
    place = Place()
    z = place.z
    chips = {k: e // 2 for k, e in (("me", place.e), ("xn", place.xnb), ("yn", place.ynb), ("dg", place.diag))}

    class Item:
        def __init__(self, i, rel, sub):
            self.i, self.rel = i, rel
            self.line = lines[i]
            self.own, self.sib, self.first, self.second, self.up, self.down = scratch[6 * i : 6 * i + 6]
            groups, _, wide = ins[i].shape[3:]
            self.groups, self.half = groups, (groups + 1) // 2
            self.at = z + rel if self.line else 0
            width = wide // subs[i]
            self.cols = pl.ds(sub * width, width)
            self.slot = rel + owners - 1 if self.line else sub
            self.valid = (z + rel >= 0) & (z + rel < owners)

        def piece(self, ref, *lead):
            return ref.at[(*lead, slice(None), self.cols)]

        def rows(self, second):
            return pl.ds(self.half, self.groups - self.half) if second else pl.ds(0, self.half)

        def copy(self, kind, src, dst, to, dz=0):
            there = self.slot - dz if self.line else self.slot
            return pltpu.make_async_remote_copy(
                src_ref=src, dst_ref=dst,
                send_sem=send.at[self.i, self.slot, kind], recv_sem=recv.at[self.i, there, kind],
                device_id=(z + dz, to), device_id_type=MESH)

        def load(self):
            return pltpu.make_async_copy(
                self.piece(ins[self.i], self.at, slice(None), place.core, slice(None)),
                self.piece(self.own, self.at, slice(None), slice(None)),
                send.at[self.i, self.slot, LOAD])

        def to_sib(self):
            return self.copy(SIB, self.piece(ins[self.i], self.at, slice(None), 1 - place.core, slice(None)),
                             self.piece(self.sib, self.at, slice(None), slice(None)), place.sib)

        def hop1(self, axis, other):
            second = axis == 1
            to = place.xnb if axis else place.ynb
            whose = chips["dg"] if other else chips["xn" if axis else "yn"]
            size = self.groups - self.half if second else self.half
            return self.copy((X0, X1)[other] if axis else (Y0, Y1)[other],
                             self.piece(self.own, self.at, whose, self.rows(second)),
                             self.piece(self.first, self.at, axis, other, pl.ds(0, size)), to)

        def hop2(self, second):
            to = place.ynb if second else place.xnb
            whose = chips["yn" if second else "xn"]
            size = self.groups - self.half if second else self.half
            return self.copy(Y2 if second else X2,
                             self.piece(self.own, self.at, whose, self.rows(second)),
                             self.piece(self.second, self.at, int(second), pl.ds(0, size)), to)

        def along(self, up):
            return self.copy(UP if up else DOWN, self.piece(self.own, self.at, chips["me"], slice(None)),
                             self.piece(self.up if up else self.down, self.at, slice(None)), place.e, 1 if up else -1)

        def arrive_along(self, up):
            buf = self.piece(self.up if up else self.down, self.at, slice(None))
            pltpu.make_async_remote_copy(
                src_ref=buf, dst_ref=buf, send_sem=send.at[self.i, self.slot, UP if up else DOWN],
                recv_sem=recv.at[self.i, self.slot, UP if up else DOWN],
                device_id=(z, place.sib), device_id_type=MESH).wait_recv()

        def add(self, whose, start, count, terms, keep=None):
            own, cols, at = self.own, self.cols, self.at

            @pl.loop(0, count)
            def _(g):
                total = own[at, whose, start + g, :, cols].astype(F32)
                for ref, lead in terms:
                    total = total + ref[(*lead, g, slice(None), cols)].astype(F32)
                if keep is None:
                    own[at, whose, start + g, :, cols] = total.astype(BF)
                else:
                    keep[start + g, :, cols] = total

        def stage1(self):
            self.load().wait()
            self.to_sib().wait_recv()

            @pl.loop(0, 4)
            def _(chip):
                self.add(chip, 0, self.groups, [(self.sib, (self.at, chip))])
            for axis in (0, 1):
                for other in (1, 0):
                    self.hop1(axis, other).start()

        def stage2(self):
            self.hop1(0, 1).wait_recv()
            self.add(chips["xn"], 0, self.half, [(self.first, (self.at, 0, 1))])
            self.hop2(False).start()
            self.hop1(1, 1).wait_recv()
            self.add(chips["yn"], self.half, self.groups - self.half, [(self.first, (self.at, 1, 1))])
            self.hop2(True).start()

        def stage3(self):
            for axis in (0, 1):
                self.hop1(axis, 0).wait_recv()
                self.hop2(axis == 1).wait_recv()
            out = outs[self.i]
            rel = self.rel
            last = None if self.line and rel != 0 else out
            for half in (0, 1):
                start = self.half if half else 0
                size = self.groups - self.half if half else self.half
                self.add(chips["me"], start, size, [(self.first, (self.at, half, 0)), (self.second, (self.at, half))], last)
            if not self.line:
                return
            for up in (True, False):
                if (rel >= 0) if up else (rel <= 0):
                    @pl.when((z > 0) if up else (z < owners - 1))
                    def _():
                        self.arrive_along(up)
                        buf = self.up if up else self.down

                        @pl.loop(0, self.groups)
                        def _(g):
                            more = buf[self.at, g, :, self.cols].astype(F32)
                            if rel == 0:
                                out[g, :, self.cols] += more
                            else:
                                where = (self.at, chips["me"], g, slice(None), self.cols)
                                self.own[where] = (self.own[where].astype(F32) + more).astype(BF)
            if rel != 0:
                self.along(rel > 0).start()

        def end(self):
            self.to_sib().wait_send()
            for axis in (0, 1):
                for other in (0, 1):
                    self.hop1(axis, other).wait_send()
                self.hop2(axis == 1).wait_send()
            if self.line and self.rel != 0:
                self.along(self.rel > 0).wait_send()

    waves = []
    for d in range(owners - 1, 0, -1):
        waves.append([Item(i, rel, 0) for rel in (d, -d) for i in range(n) if lines[i]])
    waves.append([Item(i, 0, 0) for i in range(n) if lines[i]])
    waves = [w for w in waves if w]
    for i in range(n):
        if not lines[i]:
            waves += [[Item(i, 0, sub)] for sub in range(subs[i])]

    def run(wave, name):
        for item in wave:
            if item.line and item.rel != 0:
                pl.when(item.valid)(getattr(item, name))
            else:
                getattr(item, name)()

    def begin(item):
        item.load().start()

    for wave in waves:
        for item in wave:
            item.begin = functools.partial(begin, item)
            item.begin_sib = functools.partial(lambda it: it.to_sib().start(), item)
    for wave in waves:
        run(wave, "begin")
    greet(place, any(lines), owners)
    for wave in waves:
        run(wave, "begin_sib")
    for w in range(len(waves) + 2):
        for lag, name in enumerate(("stage1", "stage2", "stage3")):
            if 0 <= w - lag < len(waves):
                run(waves[w - lag], name)
    for wave in waves:
        run(wave, "end")


def scatter(arrays, lines, subs, owners, cid):
    n = len(arrays)
    scratch, outs = [], []
    for a, line in zip(arrays, lines):
        zs = a.shape[0]
        groups, _, wide = a.shape[3:]
        half = (groups + 1) // 2
        zl = zs if line else 1
        lg = groups if line else 1
        scratch += [
            pltpu.VMEM((zs, 4, groups, G, wide), BF),
            pltpu.VMEM((zs, 4, groups, G, wide), BF),
            pltpu.VMEM((zs, 2, 2, half, G, wide), BF),
            pltpu.VMEM((zs, 2, half, G, wide), BF),
            pltpu.VMEM((zl, lg, G, wide if line else 128), BF),
            pltpu.VMEM((zl, lg, G, wide if line else 128), BF),
        ]
        outs.append(jax.ShapeDtypeStruct((groups, G, wide), F32))
    slots = max([2 * owners - 1 if any(lines) else 1] + list(subs))
    scratch += [pltpu.SemaphoreType.DMA((n, slots, 10)), pltpu.SemaphoreType.DMA((n, slots, 10))]
    return pl.pallas_call(
        functools.partial(scatter_kernel, owners, lines, subs),
        out_shape=outs,
        in_specs=[pl.BlockSpec(memory_space=pl.ANY)] * n,
        out_specs=[pl.BlockSpec(memory_space=pltpu.VMEM)] * n,
        scratch_shapes=scratch,
        compiler_params=pltpu.CompilerParams(collective_id=cid, has_side_effects=True, vmem_limit_bytes=60 * 1024 * 1024),
    )(*arrays)


def moe_kernel(
    steps,
    slots,
    chunk,
    m_ref,
    g_ref,
    member_ref,
    router_ref,
    order_ref,
    mine_ref,
    weights_ref,
    moe_ref,
    drow_ref,
    grads_ref,
    grouter_ref,
    router_s,
    gate_s,
    hg_s,
    dpre_s,
    mt_s,
    gt_s,
    gup_s,
    gdn_s,
    gr_s,
):
    step = pl.program_id(0)
    owners, _, share, units = weights_ref.shape
    per = chunk // F

    @pl.when(step == 0)
    def _():
        gup_s[...] = jnp.zeros_like(gup_s)
        gdn_s[...] = jnp.zeros_like(gdn_s)
        gr_s[...] = jnp.zeros_like(gr_s)
        router_s[...] = dot_nn(router_ref[...], order_ref[...]).astype(BF)

    mt_s[...] = m_ref[...].T
    gt_s[...] = g_ref[...].T
    sig = jax.nn.sigmoid(dot_nn(m_ref[...], router_s[...]))
    mask = dot_nn(member_ref[...], mine_ref[...])
    gate_s[...] = sig * mask
    root = math.sqrt(2.0 / math.pi)
    cube = 0.044715
    lane = lax.broadcasted_iota(jnp.int32, (1, F), 1)
    d_gate = jnp.zeros(gate_s.shape, F32)
    for c in range(units // chunk):
        cols = pl.ds(c * chunk, chunk)
        pre_all = dot_nn(m_ref[:, :share], weights_ref[0, 0, :, cols])
        back_all = dot_nn(g_ref[:, :share], weights_ref[0, 1, :, cols])
        for o in range(1, owners):
            part = pl.ds(o * share, share)
            pre_all += dot_nn(m_ref[:, part], weights_ref[o, 0, :, cols])
            back_all += dot_nn(g_ref[:, part], weights_ref[o, 1, :, cols])
        for j in range(per):
            slot = c * per + j
            part = slice(j * F, (j + 1) * F)
            pre = pre_all[:, part]
            back = back_all[:, part]
            square = pre * pre
            th = jnp.tanh(root * pre * (1.0 + cube * square))
            half = 0.5 * (1.0 + th)
            slope = half + (0.5 * root) * pre * (1.0 - th * th) * (1.0 + (3.0 * cube) * square)
            hidden = (pre * half).astype(BF).astype(F32)
            gate = gate_s[:, slot : slot + 1]
            d_one = jnp.sum(hidden * back, axis=1, keepdims=True)
            d_gate = d_gate + d_one * (lane == slot).astype(F32)
            where = pl.ds(slot * F, F)
            hg_s[:, where] = (gate * hidden).astype(BF)
            dpre_s[:, where] = (slope * (gate * back)).astype(BF)
    dlog = (d_gate * mask * sig * (1.0 - sig)).astype(BF)
    gr_s[...] += dot_nn(mt_s[...], dot_nt(dlog, order_ref[...]).astype(BF))
    for o in range(owners):
        where = pl.ds(o * share, share)
        moe_ref[:, where] = dot_nt(hg_s[...], weights_ref[o, 1]).astype(BF)
        drow_ref[:, where] = (
            dot_nt(dpre_s[...], weights_ref[o, 0]) + dot_nt(dlog, router_s[where, :])
        ).astype(BF)
        gup_s[where, :] += dot_nn(mt_s[where, :], dpre_s[...])
        gdn_s[where, :] += dot_nn(gt_s[where, :], hg_s[...])

    @pl.when(step == steps - 1)
    def _():
        for o in range(owners):
            grads_ref[o, 0] = gup_s[pl.ds(o * share, share), :].astype(BF)
            grads_ref[o, 1] = gdn_s[pl.ds(o * share, share), :].astype(BF)
        grouter_ref[...] = gr_s[...].astype(BF)


def moe(rows, cots, member, packed, router_at, order, mine, weights):
    count = rows.shape[0]
    tile = 512
    owners, _, share, units = weights.shape
    slots = units // F
    steps = count // tile
    lanes = member.shape[1]
    row_spec = pl.BlockSpec((tile, D), lambda i: (i, 0))
    whole = pl.BlockSpec(memory_space=pltpu.VMEM)
    router_spec = pl.BlockSpec((D, lanes), lambda i: (0, router_at // lanes))
    return pl.pallas_call(
        functools.partial(moe_kernel, steps, slots, 512),
        grid=(steps,),
        in_specs=[
            row_spec,
            row_spec,
            pl.BlockSpec((tile, lanes), lambda i: (i, 0)),
            router_spec,
            whole,
            whole,
            whole,
        ],
        out_specs=[row_spec, row_spec, whole, whole],
        out_shape=[
            jax.ShapeDtypeStruct((count, D), BF),
            jax.ShapeDtypeStruct((count, D), BF),
            jax.ShapeDtypeStruct(weights.shape, BF),
            jax.ShapeDtypeStruct((D, lanes), BF),
        ],
        scratch_shapes=[
            pltpu.VMEM((D, F), BF),
            pltpu.VMEM((tile, F), F32),
            pltpu.VMEM((tile, units), BF),
            pltpu.VMEM((tile, units), BF),
            pltpu.VMEM((D, tile), BF),
            pltpu.VMEM((D, tile), BF),
            pltpu.VMEM((D, units), F32),
            pltpu.VMEM((D, units), F32),
            pltpu.VMEM((D, lanes), F32),
        ],
        compiler_params=pltpu.CompilerParams(vmem_limit_bytes=60 * 1024 * 1024),
        cost_estimate=pl.CostEstimate(
            flops=12 * count * D * units,
            bytes_accessed=count * D * 8 + D * units * 8,
            transcendentals=count * units,
        ),
    )(rows, cots, member, packed, order, mine, weights)


def fused_kernel(first, owners, slots, wide, tile_cols, *refs):
    if first:
        middle, cots, member, weights, packed, order_ref, mine_ref = refs[:7]
        rows_out, drow_out, moe_out, grads_out, grouter_out = refs[7:12]
        refs = refs[12:]
    else:
        middle, cots, member, weights, packed, order_ref, mine_ref = refs[:7]
        drow_in, moe_in, grouter_in = refs[7:10]
        drow_out, moe_out, grads_out, grouter_out = refs[10:14]
        refs = refs[14:]
    (m_s, c_s, b_s, w_s, gup_s, gdn_s, gr_s, hg_s, dpre_s, mt_s, gt_s, router_in, router_s, gate_s) = refs[:14]
    part_d, part_m, local, wsem, tsem = refs[14:19]
    if first:
        gsend, grecv = refs[19:]
    else:
        sib_s, first_s, second_s, ssend, srecv = refs[19:]
    place = Place()
    z = place.z
    count = m_s.shape[0] // 8
    half = count // 2
    lanes = b_s.shape[1]
    share = D // owners
    ins = (middle,)
    bufs = (m_s,)
    sums = (m_s, c_s)
    swap = place.sib - place.e
    mine = (place.e, place.xnb, place.ynb, place.diag)
    if not first:
        mine = (place.diag, place.xnb, place.ynb, place.e)

    def span(e, start=0, size=count):
        return pl.ds(pl.multiple_of(e * count + start, 16), size)

    def remote(sems, a, kind, src, dst, to):
        return pltpu.make_async_remote_copy(
            src_ref=src, dst_ref=dst, send_sem=sems[0].at[a, kind], recv_sem=sems[1].at[a, kind],
            device_id=(z, to), device_id_type=MESH)

    def passing(a, kind):
        buf = bufs[a]
        if kind in (XS, YS, S0):
            src, at = ins[a], span(place.e)
        elif kind == FA:
            at = span(place.xnb, 0, half)
            src = buf.at[at]
        elif kind == FB:
            at = span(place.ynb, half, half)
            src = buf.at[at]
        else:
            at = span(mine[kind - S0])
            src = buf.at[at]
        to = {XS: place.xnb, YS: place.ynb, FA: place.ynb, FB: place.xnb}.get(kind, place.sib)
        return remote((gsend, grecv), a, kind, src, buf.at[at], to)

    def got(a, kind):
        at = {
            XS: lambda: span(place.xnb),
            YS: lambda: span(place.ynb),
            FA: lambda: span(place.diag, 0, half),
            FB: lambda: span(place.diag, half, half),
        }.get(kind, lambda: span(mine[kind - S0] + swap))()
        ref = bufs[a].at[at]
        remote((gsend, grecv), a, kind, ref, ref, place.sib).wait_recv()

    HY0, HY1, HX0, HX1, HX2, HY2 = 4, 5, 6, 7, 8, 9

    def to_sib(a, t):
        return remote((ssend, srecv), a, t, sums[a].at[span(mine[t] + swap)], sib_s.at[a, t], place.sib)

    def hop(a, kind):
        src_e, second, dst, to = {
            HY0: (place.ynb, False, first_s.at[a, 0], place.ynb),
            HY1: (place.diag, False, first_s.at[a, 1], place.ynb),
            HX0: (place.xnb, True, first_s.at[a, 2], place.xnb),
            HX1: (place.diag, True, first_s.at[a, 3], place.xnb),
            HX2: (place.xnb, False, second_s.at[a, 0], place.xnb),
            HY2: (place.ynb, True, second_s.at[a, 1], place.ynb),
        }[kind]
        src = sums[a].at[span(src_e, half if second else 0, half)]
        return remote((ssend, srecv), a, kind, src, dst, to)

    step_rows = 32

    def add(a, e, start, size, terms, keep=None):
        buf = sums[a]

        @pl.loop(0, size // step_rows)
        def _(g):
            here = pl.ds(pl.multiple_of(e * count + start + g * step_rows, 16), step_rows)
            there = pl.ds(pl.multiple_of(g * step_rows, 16), step_rows)
            total = buf[here, :].astype(F32)
            for lead in terms:
                total = total + lead[0][(*lead[1], there, slice(None))].astype(F32)
            if keep is None:
                buf[here, :] = total.astype(BF)
            else:
                keep[pl.ds(pl.multiple_of(start + g * step_rows, 16), step_rows), :] = total

    def chip_of(t):
        tx, ty = (t % 2, t // 2) if first else ((3 - t) // 2, (3 - t) % 2)
        chip_x = place.x + tx * (1 - 2 * place.x)
        chip_y = place.y + ty * (1 - 2 * place.y)
        return pl.ds(pl.multiple_of((chip_y * 2 + chip_x) * 2 * count, 16), 2 * count)

    if first:
        own = [
            pltpu.make_async_copy(middle, m_s.at[span(place.e)], local.at[0]),
            pltpu.make_async_copy(cots, c_s, local.at[1]),
        ]
    else:
        own = []
    own.append(pltpu.make_async_copy(member, b_s, local.at[2]))
    for c in own:
        c.start()

    def tile_copies(t):
        at = chip_of(t)
        if first:
            pairs = ((m_s, rows_out), (part_d, drow_out), (part_m, moe_out))
        else:
            pairs = ((middle, m_s), (cots, c_s), (drow_in, part_d), (moe_in, part_m))
        return [
            pltpu.make_async_copy(src.at[at], dst.at[at], tsem.at[t, i])
            for i, (src, dst) in enumerate(pairs)
        ]

    if not first:
        for t in range(4):
            for c in tile_copies(t)[:2]:
                c.start()
    router_copy = pltpu.make_async_copy(packed.at[:, pl.ds(wide, lanes)], router_in, local.at[3])
    router_copy.start()

    @pl.loop(0, slots)
    def _(s):
        for o in range(owners):
            for k in (0, 1):
                pltpu.make_async_copy(
                    weights.at[o, k * slots + s],
                    w_s.at[k, pl.ds(o * share, share), pl.ds(pl.multiple_of(s * F, F), F)],
                    wsem.at[0],
                ).start()

    greet(place, False, owners)
    if first:
        for kind in (XS, YS, S0):
            passing(0, kind).start()
        gr_s[...] = jnp.zeros_like(gr_s)
    else:
        for t in range(4):
            for c in tile_copies(t)[2:]:
                c.start()
        gr_s[...] = grouter_in[...]
    gup_s[...] = jnp.zeros_like(gup_s)
    gdn_s[...] = jnp.zeros_like(gdn_s)

    root = math.sqrt(2.0 / math.pi)
    cube = 0.044715
    tile = 2 * count
    units = slots * F
    per = tile_cols // F

    @pl.loop(0, 4)
    def _(t):
        @pl.when(t == 0)
        def _():
            for c in own:
                c.wait()
            router_copy.wait()
            router_s[...] = dot_nn(router_in[...], order_ref[...]).astype(BF)
            if first:
                got(0, S0)
            pltpu.make_async_copy(w_s, w_s, wsem.at[0]).wait()

        if first:

            @pl.when(t == 1)
            def _():
                got(0, XS)
                passing(0, FA).start()
                passing(0, S1).start()
                got(0, YS)
                passing(0, FB).start()
                passing(0, S2).start()
                got(0, S1)

            @pl.when(t == 2)
            def _():
                got(0, FA)
                got(0, FB)
                passing(0, S3).start()
                got(0, S2)

            @pl.when(t == 3)
            def _():
                got(0, S3)

        else:
            for k in range(4):

                @pl.when(t == k)
                def _():
                    for c in tile_copies(k)[:2]:
                        c.wait()

        here = chip_of(t)
        if first:
            tile_copies(t)[0].start()
        mt_s[...] = m_s[here, :].T
        gt_s[...] = c_s[here, :].T
        sig = jax.nn.sigmoid(dot_nn(m_s[here, :], router_s[...]))
        mask = dot_nn(b_s[here, :], mine_ref[...])
        gate_s[...] = sig * mask
        lane = lax.broadcasted_iota(jnp.int32, (1, F), 1)
        d_gate = jnp.zeros(gate_s.shape, F32)
        for c in range(units // tile_cols):
            cols = pl.ds(c * tile_cols, tile_cols)
            pre_all = dot_nn(m_s[here, :], w_s[0, :, cols])
            back_all = dot_nn(c_s[here, :], w_s[1, :, cols])
            for j in range(per):
                slot = c * per + j
                part = slice(j * F, (j + 1) * F)
                pre = pre_all[:, part]
                back = back_all[:, part]
                square = pre * pre
                th = jnp.tanh(root * pre * (1.0 + cube * square))
                halved = 0.5 * (1.0 + th)
                slope = halved + (0.5 * root) * pre * (1.0 - th * th) * (1.0 + (3.0 * cube) * square)
                hidden = (pre * halved).astype(BF).astype(F32)
                gate = gate_s[:, slot : slot + 1]
                d_one = jnp.sum(hidden * back, axis=1, keepdims=True)
                d_gate = d_gate + d_one * (lane == slot).astype(F32)
                where = pl.ds(slot * F, F)
                hg_s[:, where] = (gate * hidden).astype(BF)
                dpre_s[:, where] = (slope * (gate * back)).astype(BF)
        dlog = (d_gate * mask * sig * (1.0 - sig)).astype(BF)
        gr_s[...] += dot_nn(mt_s[...], dot_nt(dlog, order_ref[...]).astype(BF))

        if not first:

            @pl.when(t == 3)
            def _():
                for a in (0, 1):
                    hop(a, HY1).wait_recv()
                    add(a, place.xnb, 0, half, [(first_s, (a, 1))])
                    hop(a, HX2).start()
                    hop(a, HX1).wait_recv()
                    add(a, place.ynb, half, half, [(first_s, (a, 3))])
                    hop(a, HY2).start()

            for k in range(4):

                @pl.when(t == k)
                def _():
                    for c in tile_copies(k)[2:]:
                        c.wait()

        for a, (kept, dst) in enumerate(((part_d, m_s), (part_m, c_s))):
            for n in range(D // 256):
                where = pl.ds(n * 256, 256)
                if a == 0:
                    total = dot_nt(dpre_s[...], w_s[0, where, :]) + dot_nt(dlog, router_s[where, :])
                else:
                    total = dot_nt(hg_s[...], w_s[1, where, :])
                if first:
                    kept[here, where] = total.astype(BF)
                else:
                    dst[here, where] = (total + kept[here, where].astype(F32)).astype(BF)
            if first:
                tile_copies(t)[1 + a].start()
            else:
                for k in range(4):

                    @pl.when(t == k)
                    def _():
                        to_sib(a, k).start()

        def last(a):
            if first:
                return

            for k, kinds in enumerate(((HY1, HX1), (HX0,), (HY0,), ())):

                @pl.when(t == k)
                def _():
                    to_sib(a, k).wait_recv()
                    add(a, mine[k], 0, count, [(sib_s, (a, k))])
                    for kind in kinds:
                        hop(a, kind).start()

        last(0)
        for n in range(D // 256):
            where = pl.ds(n * 256, 256)
            gup_s[where, :] += dot_nn(mt_s[where, :], dpre_s[...])
        last(1)
        for n in range(D // 256):
            where = pl.ds(n * 256, 256)
            gdn_s[where, :] += dot_nn(gt_s[where, :], hg_s[...])

    w_s[0] = gup_s[...].astype(BF)
    w_s[1] = gdn_s[...].astype(BF)

    @pl.loop(0, slots)
    def _(s):
        for o in range(owners):
            for k in (0, 1):
                pltpu.make_async_copy(
                    w_s.at[k, pl.ds(o * share, share), pl.ds(pl.multiple_of(s * F, F), F)],
                    grads_out.at[o, k * slots + s],
                    wsem.at[0],
                ).start()

    grouter_out[...] = gr_s[...].astype(grouter_out.dtype)
    if first:
        for kind in range(8):
            passing(0, kind).wait_send()
        for t in range(4):
            for c in tile_copies(t):
                c.wait()
    else:
        for a, out in ((0, drow_out), (1, moe_out)):
            hop(a, HY0).wait_recv()
            hop(a, HX2).wait_recv()
            add(a, place.e, 0, half, [(first_s, (a, 0)), (second_s, (a, 0))], out)
            hop(a, HX0).wait_recv()
            hop(a, HY2).wait_recv()
            add(a, place.e, half, half, [(first_s, (a, 2)), (second_s, (a, 1))], out)
        for a in (0, 1):
            for t in range(4):
                to_sib(a, t).wait_send()
            for kind in (HY0, HY1, HX0, HX1, HX2, HY2):
                hop(a, kind).wait_send()
    pltpu.make_async_copy(w_s, w_s, wsem.at[0]).wait()


def fused_experts(first, rows, cots, member, weights, packed, wide, order, mine, more, cid):
    owners = weights.shape[0]
    slots = weights.shape[1] // 2
    total = cots.shape[0]
    count = total // 8
    lanes = member.shape[1]
    units = slots * F
    tile = 2 * count
    hbm = pl.BlockSpec(memory_space=pl.ANY)
    vmem = pl.BlockSpec(memory_space=pltpu.VMEM)
    dma = pltpu.SemaphoreType.DMA
    shape = jax.ShapeDtypeStruct
    scratch = [
        pltpu.VMEM((total, D), BF),
        pltpu.VMEM((total, D), BF),
        pltpu.VMEM((total, lanes), BF),
        pltpu.VMEM((2, D, units), BF),
        pltpu.VMEM((D, units), F32),
        pltpu.VMEM((D, units), F32),
        pltpu.VMEM((D, lanes), F32),
        pltpu.VMEM((tile, units), BF),
        pltpu.VMEM((tile, units), BF),
        pltpu.VMEM((D, tile), BF),
        pltpu.VMEM((D, tile), BF),
        pltpu.VMEM((D, lanes), BF),
        pltpu.VMEM((D, F), BF),
        pltpu.VMEM((tile, F), F32),
        pltpu.VMEM((total, D), BF),
        pltpu.VMEM((total, D), BF),
        dma((4,)),
        dma((1,)),
        dma((4, 4)),
    ]
    if first:
        out_specs = [hbm, hbm, hbm, hbm, vmem]
        out_shape = [shape((total, D), BF)] * 3
        out_shape += [shape(weights.shape, BF), shape((D, lanes), F32)]
        in_specs = [hbm] * 5 + [vmem] * 2
        scratch += [dma((1, 8)), dma((1, 8))]
    else:
        out_specs = [vmem, vmem, hbm, vmem]
        out_shape = [shape((count, D), F32)] * 2
        out_shape += [shape(weights.shape, BF), shape((D, lanes), BF)]
        in_specs = [hbm] * 5 + [vmem] * 2 + [hbm, hbm, vmem]
        scratch += [
            pltpu.VMEM((2, 4, count, D), BF),
            pltpu.VMEM((2, 4, count // 2, D), BF),
            pltpu.VMEM((2, 2, count // 2, D), BF),
            dma((2, 10)),
            dma((2, 10)),
        ]
    return pl.pallas_call(
        functools.partial(fused_kernel, first, owners, slots, wide, 256),
        in_specs=in_specs,
        out_specs=out_specs,
        out_shape=out_shape,
        scratch_shapes=scratch,
        compiler_params=pltpu.CompilerParams(
            collective_id=cid, has_side_effects=True, vmem_limit_bytes=64 * 1024 * 1024 - 65536
        ),
        cost_estimate=pl.CostEstimate(
            flops=12 * total * D * units,
            bytes_accessed=D * units * 8 + total * D * 8,
            transcendentals=total * units,
        ),
    )(rows, cots, member, weights, packed, order, mine, *more)


def forward_kernel(
    wide,
    lanes,
    lengths_ref,
    x_ref,
    choice_ref,
    w_ref,
    heads_ref,
    qk_ref,
    vals_ref,
    sig_ref,
    mask_ref,
    vlow_ref,
    prob_ref,
    attended_ref,
    mixed_ref,
    middle_ref,
    mlow_ref,
):
    count = x_ref.shape[0]
    seq = count // MB
    xf = x_ref[...].astype(F32)
    centred = xf - jnp.mean(xf, axis=1, keepdims=True)
    variance = jnp.mean(centred * centred, axis=1, keepdims=True)
    gain_row = w_ref[:, pl.ds(wide + lanes, 128)].astype(F32).T[SEL : SEL + 1, :]
    normed = (centred * lax.rsqrt(variance + epsilon) * gain_row).astype(BF)
    for n in range(QK // 512):
        cols = pl.ds(n * 512, 512)
        qk_ref[:, cols] = dot_nn(normed, w_ref[:, cols]).astype(BF)
    sig = jax.nn.sigmoid(dot_nn(x_ref[...], w_ref[:, pl.ds(wide + lanes, 128)]))
    row = lax.broadcasted_iota(jnp.int32, (count, 128), 0)
    lane = lax.broadcasted_iota(jnp.int32, (count, 128), 1)
    live = (row < lengths_ref[0, 0]).astype(F32)
    for b in range(1, MB):
        live = jnp.where(row < b * seq, live, (row < b * seq + lengths_ref[b, 0]).astype(F32))
    mask = jnp.zeros((count, 128), F32)
    top = choice_ref.shape[1] // H
    for v in range(H * top):
        picked = choice_ref[:, v : v + 1] + NV * (v // top)
        mask = mask + (picked == lane).astype(F32) + (picked + H * NV == lane).astype(F32) * live
    sig_ref[...] = sig
    mask_ref[...] = mask
    gates = sig * mask
    for h in range(H):
        vals = dot_nn(x_ref[...], w_ref[:, pl.ds(QK + h * NV * HD, NV * HD)])
        vals_ref[:, pl.ds(h * NV * HD, NV * HD)] = vals
        total = gates[:, h * NV : h * NV + 1] * vals[:, :HD]
        for e in range(1, NV):
            at = h * NV + e
            total = total + gates[:, at : at + 1] * vals[:, e * HD : (e + 1) * HD]
        vlow_ref[:, pl.ds(h * HD, HD)] = total.astype(BF)
    at_i = lax.broadcasted_iota(jnp.int32, (seq, seq), 0)
    at_j = lax.broadcasted_iota(jnp.int32, (seq, seq), 1)
    for b in range(MB):
        allowed = (at_j <= at_i) & (at_j < lengths_ref[b, 0])
        here = pl.ds(b * seq, seq)
        for h in range(H):
            queries = qk_ref[here, pl.ds(h * HD, HD)]
            keys_all = qk_ref[here, pl.ds((H + h) * HD, HD)]
            scores = jnp.where(allowed, dot_nt(queries, keys_all) * HD ** (-0.5), -1e30)
            expo = jnp.exp(scores - jnp.max(scores, axis=1, keepdims=True))
            prob = expo / jnp.sum(expo, axis=1, keepdims=True)
            prob_ref[b * H + h] = prob
            attended_ref[here, pl.ds(h * HD, HD)] = dot_nn(
                prob.astype(BF), vlow_ref[here, pl.ds(h * HD, HD)]
            )
    for h in range(H):
        attended = attended_ref[:, pl.ds(h * HD, HD)]
        for e in range(NV):
            at = h * NV + e
            gate = gates[:, H * NV + at : H * NV + at + 1]
            mixed_ref[:, pl.ds(at * HD, HD)] = (gate * attended).astype(BF)
    for n in range(D // 512):
        cols = pl.ds(n * 512, 512)
        middle = x_ref[:, cols].astype(F32) + dot_nn(mixed_ref[...], heads_ref[:, cols])
        middle_ref[:, cols] = middle
        mlow_ref[:, cols] = middle.astype(BF)


def forward(lengths, tokens, choice, packed, heads, wide, lanes):
    count = tokens.shape[0]
    seq = count // MB
    vmem = pl.BlockSpec(memory_space=pltpu.VMEM)
    shape = jax.ShapeDtypeStruct
    return pl.pallas_call(
        functools.partial(forward_kernel, wide, lanes),
        in_specs=[pl.BlockSpec(memory_space=pltpu.SMEM)] + [vmem] * 4,
        out_specs=[vmem] * 10,
        out_shape=[
            shape((count, QK), BF),
            shape((count, VAL), F32),
            shape((count, 128), F32),
            shape((count, 128), F32),
            shape((count, H * HD), BF),
            shape((MB * H, seq, seq), F32),
            shape((count, H * HD), F32),
            shape((count, VAL), BF),
            shape((count, D), F32),
            shape((count, D), BF),
        ],
        compiler_params=pltpu.CompilerParams(vmem_limit_bytes=56 * 1024 * 1024),
        cost_estimate=pl.CostEstimate(
            flops=2 * count * D * (wide + VAL),
            bytes_accessed=(wide + VAL) * D * 2 + count * D * 20,
            transcendentals=count * seq * H,
        ),
    )(lengths, tokens, choice, packed, heads)


def backward_kernel(
    wide,
    lanes,
    x_ref,
    cots_ref,
    drow_ref,
    moe_ref,
    middle_ref,
    qk_ref,
    vals_ref,
    sig_ref,
    mask_ref,
    vlow_ref,
    prob_ref,
    attended_ref,
    mixed_ref,
    grouter_ref,
    w_ref,
    heads_ref,
    ahead_ref,
    out_ref,
    dx_ref,
    gw_ref,
    gheads_ref,
    dvals_s,
    dqk_s,
):
    count = x_ref.shape[0]
    seq = count // MB
    out_ref[...] = (middle_ref[...] + moe_ref[...]).astype(BF)
    d_middle = cots_ref[...].astype(F32) + drow_ref[...]
    d_branch = d_middle.astype(BF)
    mask = mask_ref[...]
    sig = sig_ref[...]
    gates = sig * mask
    lane = lax.broadcasted_iota(jnp.int32, (1, 128), 1)
    d_gates = jnp.zeros((count, 128), F32)
    width = NV * HD
    for h in range(H):
        where = pl.ds(h * width, width)
        gheads_ref[where, :] = dot_tn(mixed_ref[:, where], d_branch).astype(BF)
        d_mixed = dot_nt(d_branch, heads_ref[where, :])
        attended = attended_ref[:, pl.ds(h * HD, HD)]
        total = jnp.zeros((count, HD), F32)
        for e in range(NV):
            at = H * NV + h * NV + e
            part = d_mixed[:, e * HD : (e + 1) * HD]
            total = total + gates[:, at : at + 1] * part
            d_one = jnp.sum(part * attended, axis=1, keepdims=True)
            d_gates = d_gates + d_one * (lane == at).astype(F32)
        d_attended = total.astype(BF)
        d_values = []
        for b in range(MB):
            here = pl.ds(b * seq, seq)
            rows = slice(b * seq, (b + 1) * seq)
            prob = prob_ref[b * H + h]
            values = vlow_ref[here, pl.ds(h * HD, HD)]
            d_prob = dot_nt(d_attended[rows], values)
            d_scores = (
                prob * (d_prob - jnp.sum(prob * d_prob, axis=1, keepdims=True))
            ).astype(BF)
            d_values.append(dot_tn(prob.astype(BF), d_attended[rows]).astype(BF).astype(F32))
            queries = qk_ref[here, pl.ds(h * HD, HD)]
            keys_all = qk_ref[here, pl.ds((H + h) * HD, HD)]
            dqk_s[here, pl.ds(h * HD, HD)] = (dot_nn(d_scores, keys_all) * HD ** (-0.5)).astype(BF)
            dqk_s[here, pl.ds((H + h) * HD, HD)] = (
                dot_tn(d_scores, queries) * HD ** (-0.5)
            ).astype(BF)
        d_value = jnp.concatenate(d_values, axis=0)
        for e in range(NV):
            at = h * NV + e
            cols = pl.ds(at * HD, HD)
            d_one = jnp.sum(d_value * vals_ref[:, cols], axis=1, keepdims=True)
            d_gates = d_gates + d_one * (lane == at).astype(F32)
            dvals_s[:, cols] = (gates[:, at : at + 1] * d_value).astype(BF)
    d_select = (d_gates * mask * sig * (1.0 - sig)).astype(BF)
    x_t = x_ref[...].T
    for n in range(VAL // 512):
        cols = pl.ds(n * 512, 512)
        gw_ref[:, pl.ds(QK + n * 512, 512)] = dot_nn(x_t, dvals_s[:, cols]).astype(BF)
    xf = x_ref[...].astype(F32)
    centred = xf - jnp.mean(xf, axis=1, keepdims=True)
    variance = jnp.mean(centred * centred, axis=1, keepdims=True)
    rstd = lax.rsqrt(variance + epsilon)
    unit = centred * rstd
    gain_row = w_ref[:, pl.ds(wide + lanes, 128)].astype(F32).T[SEL : SEL + 1, :]
    normed_t = (unit * gain_row).astype(BF).T
    for n in range(QK // 512):
        cols = pl.ds(n * 512, 512)
        gw_ref[:, cols] = dot_nn(normed_t, dqk_s[:, cols]).astype(BF)
    d_normed = dot_nt(dqk_s[...], w_ref[:, pl.ds(0, QK)])
    grad_gain = jnp.sum(d_normed * unit, axis=0, keepdims=True)
    small = dot_tn(d_select, x_ref[...])
    which = lax.broadcasted_iota(jnp.int32, (128, 1), 0)
    gw_ref[:, pl.ds(wide + lanes, 128)] = jnp.where(which == SEL, grad_gain, small).T.astype(BF)
    gw_ref[:, pl.ds(wide, lanes)] = grouter_ref[...]
    scaled = d_normed * gain_row
    dx_ref[...] = (
        d_middle
        + (
            scaled
            - jnp.mean(scaled, axis=1, keepdims=True)
            - unit * jnp.mean(scaled * unit, axis=1, keepdims=True)
        )
        * rstd
    )
    for n in range(D // 256):
        rows = pl.ds(n * 256, 256)
        dx_ref[:, rows] += dot_nt(dvals_s[...], w_ref[rows, pl.ds(QK, VAL)]) + dot_nt(
            d_select, w_ref[rows, pl.ds(wide + lanes, 128)]
        )


def backward(tokens, cots, drow, moe_sum, saved, grouter, packed, heads, ahead, wide, lanes):
    count = tokens.shape[0]
    qk, vals, sig, mask, vlow, prob, attended, mixed, middle = saved
    vmem = pl.BlockSpec(memory_space=pltpu.VMEM)
    shape = jax.ShapeDtypeStruct
    return pl.pallas_call(
        functools.partial(backward_kernel, wide, lanes),
        in_specs=[vmem] * 16 + [pl.BlockSpec(memory_space=pl.ANY)],
        out_specs=[vmem] * 4,
        out_shape=[
            shape((count, D), BF),
            shape((count, D), F32),
            shape(packed.shape, BF),
            shape(heads.shape, BF),
        ],
        scratch_shapes=[pltpu.VMEM((count, VAL), BF), pltpu.VMEM((count, QK), BF)],
        compiler_params=pltpu.CompilerParams(vmem_limit_bytes=62 * 1024 * 1024),
        cost_estimate=pl.CostEstimate(
            flops=4 * count * D * (wide + VAL),
            bytes_accessed=(wide + VAL) * D * 4 + count * D * 30,
            transcendentals=0,
        ),
    )(
        tokens,
        cots,
        drow,
        moe_sum,
        middle,
        qk,
        vals,
        sig,
        mask,
        vlow,
        prob,
        attended,
        mixed,
        grouter,
        packed,
        heads,
        ahead,
    )


def update_kernel(wide, lanes, rates, packed_ref, heads_sum_ref, first_ref, second_ref, *refs):
    ins, outs = refs[:18], refs[18:]

    def step(i, at, gradient):
        new = update_weight(*(ref[at] for ref in ins[3 * i : 3 * i + 3]), gradient, rates[i])
        for ref, value in zip(outs[4 * i : 4 * i + 4], new):
            ref[at] = value

    everything = (slice(None), slice(None))
    step(0, everything, packed_ref[:, pl.ds(0, wide)])
    step(1, everything, packed_ref[:, pl.ds(wide + lanes, SEL)])
    step(2, everything, packed_ref[:, pl.ds(wide, ins[6].shape[1])])
    step(3, everything, heads_sum_ref[...])
    part = first_ref.shape[0] // 2
    for h, ref in enumerate((first_ref, second_ref)):

        @pl.loop(0, part)
        def _(s):
            for k in (0, 1):
                step(4 + k, h * part + s, ref[k * part + s].astype(F32))


def update_all(packed_sum, heads_sum, sums_a, sums_b, weights, rates, wide, lanes):
    vmem = pl.BlockSpec(memory_space=pltpu.VMEM)
    shapes = []
    for i in range(6):
        shapes += [jax.ShapeDtypeStruct(weights[3 * i].shape, t) for t in (F32, F32, F32, BF)]
    return pl.pallas_call(
        functools.partial(update_kernel, wide, lanes, rates),
        in_specs=[vmem] * 22,
        out_specs=[vmem] * 24,
        out_shape=shapes,
        compiler_params=pltpu.CompilerParams(vmem_limit_bytes=60 * 1024 * 1024),
    )(packed_sum, heads_sum, sums_a, sums_b, *weights)


def body(
    tokens,
    cotangent,
    lengths,
    routes,
    head_choice,
    placement,
    gain_master,
    gain_moment,
    gain_average,
    qkv_master,
    qkv_moment,
    qkv_average,
    select_master,
    select_moment,
    select_average,
    router_master,
    router_moment,
    router_average,
    heads_out_master,
    heads_out_moment,
    heads_out_average,
    up_master,
    up_moment,
    up_average,
    down_master,
    down_moment,
    down_average,
):
    both = ("dp", "expert")
    owners = lax.axis_size("dp")
    group = lax.axis_size("expert")
    own_kernels = group == 8
    experts = placement.shape[0]
    slots = up_master.shape[0]
    units = slots * F
    seq = tokens.shape[1]
    count = MB * seq
    share = up_master.shape[1]
    mine = lax.axis_index("expert")
    lanes = -(-experts // 128) * 128

    own_rows = qkv_master.shape[0]
    wide = QK + VAL
    packed = jnp.concatenate(
        [
            qkv_master.astype(BF),
            router_master.astype(BF),
            jnp.zeros((own_rows, lanes - experts), BF),
            select_master.astype(BF),
            gain_master.astype(BF)[:, None],
            jnp.zeros((own_rows, 127 - SEL), BF),
        ],
        axis=1,
    )
    heads_low = heads_out_master.astype(BF)

    part = slots // 2

    def fetch(h):
        own = slice(h * part, (h + 1) * part)
        low = jnp.concatenate([up_master[own].astype(BF), down_master[own].astype(BF)], axis=0)
        return lax.all_gather(low, "dp", axis=0, tiled=False)

    weights = (fetch(0), fetch(1))

    flat_tokens = tokens.reshape(count, D)
    flat_cots = cotangent.reshape(count, D)
    live = (jnp.arange(seq, dtype=jnp.int32)[None, :] < lengths).astype(F32).reshape(count)
    lane_ids = jnp.arange(lanes, dtype=jnp.int32)
    named = jnp.sum(
        (routes.reshape(count, TOPK)[..., None] == lane_ids).astype(F32), axis=1
    ) * live[:, None]
    padded = jnp.pad(placement, (0, lanes - experts), constant_values=-1)
    perm = (padded[:, None] == lane_ids[None, :]).astype(BF)
    member = dot_nn(named.astype(BF), perm).astype(BF)
    own_lane = jnp.arange(F, dtype=jnp.int32)[None, :]

    def selects(start, number):
        slot = mine * slots + start
        inside = own_lane < number
        return (
            (((padded[:, None] - slot) == own_lane) & inside & (padded[:, None] >= 0)).astype(BF),
            (((lane_ids[:, None] - slot) == own_lane) & inside).astype(BF),
        )

    if own_kernels:
        packed_all, heads, cots_all, member_all = gather(
            (packed, heads_low, flat_cots, member),
            (True, True, False, False),
            (own_rows // 2, 48, count // 2, count // 2),
            owners,
            group,
            0,
        )
    else:
        packed_all = lax.all_gather(packed, both, axis=0, tiled=True)
        heads = lax.all_gather(heads_low, both, axis=0, tiled=True)
        cots_all, member_all = (
            lax.all_gather(a, "expert", axis=0, tiled=True) for a in (flat_cots, member)
        )
    choice = head_choice.reshape(count, -1)
    *saved, middle_low = forward(lengths, flat_tokens, choice, packed_all, heads, wide, lanes)
    if own_kernels:
        rows_all, drow_part, moe_part, grads_a, router_part = fused_experts(
            True, middle_low, cots_all, member_all, weights[0], packed_all, wide, *selects(0, part), (), 1
        )
        d_from_rows, moe_sum, grads_b, grad_router = fused_experts(
            False,
            rows_all,
            cots_all,
            member_all,
            weights[1],
            packed_all,
            wide,
            *selects(part, part),
            (drow_part, moe_part, router_part),
            2,
        )
    else:
        rows_all = lax.all_gather(middle_low, "expert", axis=0, tiled=True)
        side = jnp.stack([w.reshape(owners, 2, part, share, F) for w in weights], axis=2)
        side = side.reshape(owners, 2, slots, share, F).transpose(0, 1, 3, 2, 4)
        moe_part, drow_part, expert_grads, grad_router = moe(
            rows_all,
            cots_all,
            member_all,
            packed_all,
            wide,
            *selects(0, slots),
            side.reshape(owners, 2, share, units),
        )
        expert_grads = expert_grads.reshape(owners, 2, share, 2, part, F).transpose(3, 0, 1, 4, 2, 5)
        grads_a, grads_b = expert_grads
        d_from_rows, moe_sum = (
            lax.psum_scatter(a, "expert", scatter_dimension=0, tiled=True).astype(F32)
            for a in (drow_part, moe_part)
        )
    sums_a, sums_b = (
        lax.psum_scatter(
            g.reshape(owners * 2 * part, share, F), "dp", scatter_dimension=0, tiled=True
        )
        for g in (grads_a, grads_b)
    )
    mixed, d_tokens, grad_packed, grad_heads = backward(
        flat_tokens,
        flat_cots,
        d_from_rows,
        moe_sum,
        saved,
        grad_router,
        packed_all,
        heads,
        sums_a,
        wide,
        lanes,
    )
    if own_kernels:
        packed_sum, heads_sum = (
            total.reshape(-1, total.shape[2])
            for total in scatter(
                tuple(g.reshape(owners, 4, 2, -1, G, g.shape[1]) for g in (grad_packed, grad_heads)),
                (True, True),
                (1, 1),
                owners,
                3,
            )
        )
    else:
        packed_sum, heads_sum = (
            lax.psum_scatter(g, both, scatter_dimension=0, tiled=True).astype(F32)
            for g in (grad_packed, grad_heads)
        )
    gain_sum = packed_sum[:, wide + lanes + SEL]
    rates = step_rates(count * owners * group, experts)
    outs = update_weight(gain_master, gain_moment, gain_average, gain_sum, rates[0]) + tuple(
        update_all(
            packed_sum,
            heads_sum,
            sums_a,
            sums_b,
            (
                qkv_master,
                qkv_moment,
                qkv_average,
                select_master,
                select_moment,
                select_average,
                router_master,
                router_moment,
                router_average,
                heads_out_master,
                heads_out_moment,
                heads_out_average,
                up_master,
                up_moment,
                up_average,
                down_master,
                down_moment,
                down_average,
            ),
            rates[1:],
            wide,
            lanes,
        )
    )
    return (mixed.reshape(tokens.shape), d_tokens.reshape(tokens.shape)) + outs


def solution(mesh):
    rows = P(None, ("dp", "expert"), None)
    flat = P(("dp", "expert"))
    dense = P(("dp", "expert"), None)
    expert = P("expert", "dp", None)
    in_specs = (
        rows,
        rows,
        P(None, ("dp", "expert")),
        rows,
        P(None, ("dp", "expert"), None, None),
        P(),
        *((flat,) * 3),
        *((dense,) * 12),
        *((expert,) * 6),
    )
    out_specs = (rows, rows, *((flat,) * 4), *((dense,) * 16), *((expert,) * 8))
    return jax.shard_map(body, mesh=mesh, in_specs=in_specs, out_specs=out_specs, check_vma=False)
```

```python
import functools
import math

import jax
import jax.numpy as jnp
from jax import lax
from jax.experimental import pallas as pl
from jax.experimental.pallas import tpu as pltpu
from jax.sharding import PartitionSpec as P

D = 1024
H = 4
HD = 128
NV = 5
F = 128
TOPK = 16
MB = 2
QK = 2 * H * HD
VAL = H * NV * HD
SEL = 2 * H * NV

momentum_decay = 0.9
average_decay = 0.5
rate_factor = 0.4
epsilon = 1e-05
BF = jnp.bfloat16
F32 = jnp.float32


def step_rates(total_tokens, experts):
    root_tokens = math.sqrt(total_tokens)
    expert_share = math.sqrt(TOPK / experts)
    spread_list = (
        0.3,
        D ** (-0.5),
        (2 * D) ** (-0.5),
        (9 * D) ** (-0.5),
        0.5,
        D ** (-0.5),
        (4 * F) ** (-0.5),
    )
    gradient_list = (1.0, 1.0, 3.0, 2.0 * expert_share, 0.1, 0.5 * expert_share, 0.4 * expert_share)
    return tuple(
        rate_factor * spread_value / (gradient_value * root_tokens)
        for spread_value, gradient_value in zip(spread_list, gradient_list)
    )


def update_weight(master, moment, average, gradient, step_size):
    new_moment = momentum_decay * moment + gradient
    new_weight = master - step_size * (gradient + momentum_decay * new_moment)
    new_average = average_decay * average + (1.0 - average_decay) * new_weight
    return (new_moment, new_average, new_weight, new_weight.astype(BF))


def dot_nt(a, b):
    return lax.dot_general(a, b, (((1,), (1,)), ((), ())), preferred_element_type=F32)


def dot_tn(a, b):
    return lax.dot_general(a, b, (((0,), (0,)), ((), ())), preferred_element_type=F32)


def dot_nn(a, b):
    return jnp.dot(a, b, preferred_element_type=F32)


MESH = pl.DeviceIdType.MESH


class Place:
    def __init__(self):
        self.z = lax.axis_index("dp")
        self.e = lax.axis_index("expert")
        core = self.e % 2
        x = (self.e // 2) % 2
        y = self.e // 4
        self.sib = self.e + 1 - 2 * core
        self.xnb = self.e + 2 - 4 * x
        self.ynb = self.e + 4 - 8 * y
        self.diag = self.xnb + 4 - 8 * y
        self.core, self.x, self.y = core, x, y


def greet(place, line, owners):
    barrier = pltpu.get_barrier_semaphore()
    z = place.z
    for e in (place.sib, place.xnb, place.ynb):
        pl.semaphore_signal(barrier, inc=1, device_id=(z, e), device_id_type=MESH)
    peers = 3
    if line:

        @pl.when(z > 0)
        def _():
            pl.semaphore_signal(barrier, inc=1, device_id=(z - 1, place.e), device_id_type=MESH)

        @pl.when(z < owners - 1)
        def _():
            pl.semaphore_signal(barrier, inc=1, device_id=(z + 1, place.e), device_id_type=MESH)

        peers = peers + (z + owners - 1) // owners + (2 * owners - 2 - z) // owners
    pl.semaphore_wait(barrier, peers)


XS, YS, FA, FB, S0, S1, S2, S3, UP, DOWN = range(10)

def gather_kernel(owners, group, lines, halves, *refs):
    n = len(lines)
    ins, outs, (send, recv, own) = refs[:n], refs[n : 2 * n], refs[2 * n :]
    place = Place()
    z = place.z
    copies_own = []
    for i in range(n):
        rows = ins[i].shape[0]
        slot = (z * group + place.e) if lines[i] else place.e
        cp = pltpu.make_async_copy(ins[i], outs[i].at[pl.ds(slot * rows, rows)], own.at[i])
        cp.start()
        copies_own.append(cp)
    greet(place, any(lines), owners)

    def block(i, rel, e, part=None):
        rows = ins[i].shape[0]
        slot = ((z + rel) * group + e) if lines[i] else e
        start, size = (0, rows) if part is None else part
        return outs[i].at[pl.ds(slot * rows + start, size)]

    def source(i, rel, part=None):
        if rel == 0:
            return ins[i] if part is None else ins[i].at[pl.ds(*part)]
        return block(i, rel, place.e, part)

    def sem(rel):
        return rel + owners - 1

    def go(i, rel, kind, src, dst, to_e, dz=0):
        return pltpu.make_async_remote_copy(
            src_ref=src, dst_ref=dst, send_sem=send.at[i, sem(rel), kind],
            recv_sem=recv.at[i, sem(rel - dz), min(kind, UP)],
            device_id=(z + dz, to_e), device_id_type=MESH)

    def parts(i):
        rows = ins[i].shape[0]
        return (0, halves[i]), (halves[i], rows - halves[i])

    def valid(rel):
        return (z + rel >= 0) & (z + rel < owners)

    def copies(i, rel):
        first, second = parts(i)
        e, xn, yn, dg, sb = place.e, place.xnb, place.ynb, place.diag, place.sib
        return {
            XS: lambda: go(i, rel, XS, source(i, rel), block(i, rel, e), xn),
            YS: lambda: go(i, rel, YS, source(i, rel), block(i, rel, e), yn),
            FA: lambda: go(i, rel, FA, block(i, rel, xn, first), block(i, rel, xn, first), yn),
            FB: lambda: go(i, rel, FB, block(i, rel, yn, second), block(i, rel, yn, second), xn),
            S0: lambda: go(i, rel, S0, source(i, rel), block(i, rel, e), sb),
            S1: lambda: go(i, rel, S1, block(i, rel, xn), block(i, rel, xn), sb),
            S2: lambda: go(i, rel, S2, block(i, rel, yn), block(i, rel, yn), sb),
            S3: lambda: go(i, rel, S3, block(i, rel, dg), block(i, rel, dg), sb),
        }

    def got(i, rel, kind, e, part=None):
        ref = block(i, rel, e, part)
        pltpu.make_async_remote_copy(
            src_ref=ref, dst_ref=ref, send_sem=send.at[i, sem(rel), min(kind, UP)], recv_sem=recv.at[i, sem(rel), min(kind, UP)],
            device_id=(z, place.sib), device_id_type=MESH).wait_recv()

    def stage_z(rel):
        @pl.when(valid(rel))
        def _():
            for i in range(n):
                if rel != 0 and not lines[i]:
                    continue
                if rel != 0:
                    got(i, rel, UP, place.e)
                if lines[i] and rel <= 0 and rel > 1 - owners:
                    @pl.when(z < owners - 1)
                    def _():
                        go(i, rel, UP, source(i, rel), block(i, rel, place.e), place.e, 1).start()
                if lines[i] and rel >= 0 and rel < owners - 1:
                    @pl.when(z > 0)
                    def _():
                        go(i, rel, DOWN, source(i, rel), block(i, rel, place.e), place.e, -1).start()
                c = copies(i, rel)
                c[XS]().start()
                c[YS]().start()
                c[S0]().start()

    def each(rel, fn):
        @pl.when(valid(rel))
        def _():
            for i in range(n):
                if rel == 0 or lines[i]:
                    fn(i, rel, copies(i, rel))

    def xy(i, rel, c):
        got(i, rel, XS, place.xnb)
        c[FA]().start()
        c[S1]().start()
        got(i, rel, YS, place.ynb)
        c[FB]().start()
        c[S2]().start()

    def dg(i, rel, c):
        first, second = parts(i)
        got(i, rel, FA, place.diag, first)
        got(i, rel, FB, place.diag, second)
        c[S3]().start()

    def end(i, rel, c):
        for k, e in ((S0, place.sib),):
            got(i, rel, S0, place.sib)
        got(i, rel, S1, place.xnb + place.sib - place.e)
        got(i, rel, S2, place.ynb + place.sib - place.e)
        got(i, rel, S3, place.diag + place.sib - place.e)
        for k in (XS, YS, FA, FB, S0, S1, S2, S3):
            c[k]().wait_send()
        if lines[i] and rel <= 0 and rel > 1 - owners:
            @pl.when(z < owners - 1)
            def _():
                go(i, rel, UP, source(i, rel), block(i, rel, place.e), place.e, 1).wait_send()
        if lines[i] and rel >= 0 and rel < owners - 1:
            @pl.when(z > 0)
            def _():
                go(i, rel, DOWN, source(i, rel), block(i, rel, place.e), place.e, -1).wait_send()

    rels = [0] + [s * d for d in range(1, owners) for s in (-1, 1)]
    waves = [[0]] + [[-d, d] for d in range(1, owners)]
    for w in range(owners + 3):
        if w < owners:
            for r in waves[w]:
                stage_z(r)
        if 0 <= w - 1 < owners:
            for r in waves[w - 1]:
                each(r, xy)
        if 0 <= w - 2 < owners:
            for r in waves[w - 2]:
                each(r, dg)
    for cp in copies_own:
        cp.wait()
    for r in rels:
        each(r, end)


def gather(arrays, lines, halves, owners, group, cid):
    outs = [jax.ShapeDtypeStruct((a.shape[0] * (owners if l else 1) * group,) + a.shape[1:], a.dtype) for a, l in zip(arrays, lines)]
    n = len(arrays)
    any_spec = pl.BlockSpec(memory_space=pl.ANY)
    return pl.pallas_call(
        functools.partial(gather_kernel, owners, group, lines, halves),
        out_shape=outs, in_specs=[any_spec] * n, out_specs=[any_spec] * n,
        scratch_shapes=[pltpu.SemaphoreType.DMA((n, 2 * owners - 1, 10)), pltpu.SemaphoreType.DMA((n, 2 * owners - 1, 9)), pltpu.SemaphoreType.DMA((n,))],
        compiler_params=pltpu.CompilerParams(collective_id=cid, has_side_effects=True),
    )(*arrays)


G = 16
(LOAD, SIB, Y0, Y1, X0, X1, X2, Y2, UP, DOWN) = range(10)


def summing_steps(owners, refs):
    outs, scratch = refs[:3], refs[3:]
    send, recv = scratch[18:]
    place = Place()
    z = place.z
    chips = {k: e // 2 for k, e in (("me", place.e), ("xn", place.xnb), ("yn", place.ynb), ("dg", place.diag))}

    class Item:
        def __init__(self, i, rel):
            self.i, self.rel = i, rel
            self.own, self.sib, self.first, self.second, self.up, self.down = scratch[6 * i : 6 * i + 6]
            groups = self.own.shape[3]
            self.groups, self.half = groups, (groups + 1) // 2
            self.at = z + rel
            self.slot = rel + owners - 1
            self.valid = (z + rel >= 0) & (z + rel < owners)

        def piece(self, ref, *lead):
            return ref.at[lead]

        def rows(self, second):
            return pl.ds(self.half, self.groups - self.half) if second else pl.ds(0, self.half)

        def copy(self, kind, src, dst, to, dz=0):
            there = self.slot - dz
            return pltpu.make_async_remote_copy(
                src_ref=src, dst_ref=dst,
                send_sem=send.at[self.i, self.slot, kind], recv_sem=recv.at[self.i, there, kind],
                device_id=(z + dz, to), device_id_type=MESH)

        def to_sib(self):
            return self.copy(SIB, self.own.at[self.at, slice(None), 1 - place.core],
                             self.sib.at[self.at], place.sib)

        def hop1(self, axis, other):
            second = axis == 1
            to = place.xnb if axis else place.ynb
            whose = chips["dg"] if other else chips["xn" if axis else "yn"]
            size = self.groups - self.half if second else self.half
            return self.copy((X0, X1)[other] if axis else (Y0, Y1)[other],
                             self.own.at[self.at, whose, place.core, self.rows(second)],
                             self.piece(self.first, self.at, axis, other, pl.ds(0, size)), to)

        def hop2(self, second):
            to = place.ynb if second else place.xnb
            whose = chips["yn" if second else "xn"]
            size = self.groups - self.half if second else self.half
            return self.copy(Y2 if second else X2,
                             self.own.at[self.at, whose, place.core, self.rows(second)],
                             self.piece(self.second, self.at, int(second), pl.ds(0, size)), to)

        def along(self, up):
            return self.copy(UP if up else DOWN, self.own.at[self.at, chips["me"], place.core],
                             (self.up if up else self.down).at[self.at], place.e, 1 if up else -1)

        def arrive_along(self, up):
            buf = (self.up if up else self.down).at[self.at]
            pltpu.make_async_remote_copy(
                src_ref=buf, dst_ref=buf, send_sem=send.at[self.i, self.slot, UP if up else DOWN],
                recv_sem=recv.at[self.i, self.slot, UP if up else DOWN],
                device_id=(z, place.sib), device_id_type=MESH).wait_recv()

        def add(self, whose, start, count, terms, keep=None):
            own, at, core = self.own, self.at, place.core

            @pl.loop(0, count)
            def _(g):
                total = own[at, whose, core, start + g].astype(F32)
                for ref, lead in terms:
                    total = total + ref[(*lead, g)].astype(F32)
                if keep is None:
                    own[at, whose, core, start + g] = total.astype(BF)
                else:
                    keep[start + g] = total

        def begin(self):
            self.to_sib().start()

        def stage1(self):
            self.to_sib().wait_recv()

            @pl.loop(0, 4)
            def _(chip):
                self.add(chip, 0, self.groups, [(self.sib, (self.at, chip))])
            for axis in (0, 1):
                for other in (1, 0):
                    self.hop1(axis, other).start()

        def stage2(self):
            self.hop1(0, 1).wait_recv()
            self.add(chips["xn"], 0, self.half, [(self.first, (self.at, 0, 1))])
            self.hop2(False).start()
            self.hop1(1, 1).wait_recv()
            self.add(chips["yn"], self.half, self.groups - self.half, [(self.first, (self.at, 1, 1))])
            self.hop2(True).start()

        def stage3(self):
            for axis in (0, 1):
                self.hop1(axis, 0).wait_recv()
                self.hop2(axis == 1).wait_recv()
            out = outs[self.i]
            rel = self.rel
            last = None if rel != 0 else out
            for half in (0, 1):
                start = self.half if half else 0
                size = self.groups - self.half if half else self.half
                self.add(chips["me"], start, size, [(self.first, (self.at, half, 0)), (self.second, (self.at, half))], last)
            for up in (True, False):
                if (rel >= 0) if up else (rel <= 0):
                    @pl.when((z > 0) if up else (z < owners - 1))
                    def _():
                        self.arrive_along(up)
                        buf = self.up if up else self.down

                        @pl.loop(0, self.groups)
                        def _(g):
                            more = buf[self.at, g].astype(F32)
                            if rel == 0:
                                out[g] += more
                            else:
                                where = (self.at, chips["me"], place.core, g)
                                self.own[where] = (self.own[where].astype(F32) + more).astype(BF)
            if rel != 0:
                self.along(rel > 0).start()

        def end(self):
            self.to_sib().wait_send()
            for axis in (0, 1):
                for other in (0, 1):
                    self.hop1(axis, other).wait_send()
                self.hop2(axis == 1).wait_send()
            if self.rel != 0:
                self.along(self.rel > 0).wait_send()

    values, heads, rest = (
        [Item(i, rel) for d in range(owners - 1, 0, -1) for rel in (d, -d)] + [Item(i, 0)]
        for i in range(3)
    )

    def run(items, name):
        for item in items:
            if item.rel != 0:
                pl.when(item.valid)(getattr(item, name))
            else:
                getattr(item, name)()

    def put(i, where, value):
        shape = scratch[6 * i].shape
        scratch[6 * i][where] = value.reshape(*shape[len(shape) - 6 + (where[0] is not Ellipsis) : 5], value.shape[1])

    def put_w(start, value):
        i = 0 if QK <= start < QK + VAL else 2
        at = start if start < QK else start - (QK if i == 0 else VAL)
        put(i, (Ellipsis, pl.ds(at, value.shape[1])), value)

    def put_h(h, value):
        put(1, (h,), value)

    plan = {
        "heads": ((heads, "begin"),),
        1: ((heads, "stage1"),),
        "values": ((values, "begin"), (heads, "stage2")),
        "rest": ((rest, "begin"), (values, "stage1")),
        "end": ((rest, "stage1"),),
    }

    def wave(items, w):
        return items[2 * w : 2 * w + 2] if 0 <= w < owners else []

    def event(name):
        if name == "heads":
            greet(place, True, owners)
        for items, stage in plan.get(name, ()):
            run(items, stage)
        if name == "end":
            for w in range(owners + 1):
                run(wave(heads, w), "stage3")
                run(wave(values, w), "stage2")
                run(wave(rest, w), "stage2")
                run(wave(values, w - 1), "stage3")
                run(wave(rest, w - 1), "stage3")
            run(heads + values + rest, "end")

    return put_w, put_h, event


def scatter_space(grads, owners):
    scratch, outs = [], []
    for rows, wide in grads:
        groups = rows // (owners * 8 * G)
        half = (groups + 1) // 2
        scratch += [
            pltpu.VMEM((owners, 4, 2, groups, G, wide), BF),
            pltpu.VMEM((owners, 4, groups, G, wide), BF),
            pltpu.VMEM((owners, 2, 2, half, G, wide), BF),
            pltpu.VMEM((owners, 2, half, G, wide), BF),
            pltpu.VMEM((owners, groups, G, wide), BF),
            pltpu.VMEM((owners, groups, G, wide), BF),
        ]
        outs.append(jax.ShapeDtypeStruct((groups, G, wide), F32))
    scratch += [pltpu.SemaphoreType.DMA((3, 2 * owners - 1, 10))] * 2
    return scratch, outs


def moe_kernel(
    steps,
    slots,
    chunk,
    m_ref,
    g_ref,
    member_ref,
    router_ref,
    order_ref,
    mine_ref,
    weights_ref,
    moe_ref,
    drow_ref,
    grads_ref,
    grouter_ref,
    router_s,
    gate_s,
    hg_s,
    dpre_s,
    mt_s,
    gt_s,
    gup_s,
    gdn_s,
    gr_s,
):
    step = pl.program_id(0)
    owners, _, share, units = weights_ref.shape
    per = chunk // F

    @pl.when(step == 0)
    def _():
        gup_s[...] = jnp.zeros_like(gup_s)
        gdn_s[...] = jnp.zeros_like(gdn_s)
        gr_s[...] = jnp.zeros_like(gr_s)
        router_s[...] = dot_nn(router_ref[...], order_ref[...]).astype(BF)

    mt_s[...] = m_ref[...].T
    gt_s[...] = g_ref[...].T
    sig = jax.nn.sigmoid(dot_nn(m_ref[...], router_s[...]))
    mask = dot_nn(member_ref[...], mine_ref[...])
    gate_s[...] = sig * mask
    root = math.sqrt(2.0 / math.pi)
    cube = 0.044715
    lane = lax.broadcasted_iota(jnp.int32, (1, F), 1)
    d_gate = jnp.zeros(gate_s.shape, F32)
    for c in range(units // chunk):
        cols = pl.ds(c * chunk, chunk)
        pre_all = dot_nn(m_ref[:, :share], weights_ref[0, 0, :, cols])
        back_all = dot_nn(g_ref[:, :share], weights_ref[0, 1, :, cols])
        for o in range(1, owners):
            part = pl.ds(o * share, share)
            pre_all += dot_nn(m_ref[:, part], weights_ref[o, 0, :, cols])
            back_all += dot_nn(g_ref[:, part], weights_ref[o, 1, :, cols])
        for j in range(per):
            slot = c * per + j
            part = slice(j * F, (j + 1) * F)
            pre = pre_all[:, part]
            back = back_all[:, part]
            square = pre * pre
            th = jnp.tanh(root * pre * (1.0 + cube * square))
            half = 0.5 * (1.0 + th)
            slope = half + (0.5 * root) * pre * (1.0 - th * th) * (1.0 + (3.0 * cube) * square)
            hidden = (pre * half).astype(BF).astype(F32)
            gate = gate_s[:, slot : slot + 1]
            d_one = jnp.sum(hidden * back, axis=1, keepdims=True)
            d_gate = d_gate + d_one * (lane == slot).astype(F32)
            where = pl.ds(slot * F, F)
            hg_s[:, where] = (gate * hidden).astype(BF)
            dpre_s[:, where] = (slope * (gate * back)).astype(BF)
    dlog = (d_gate * mask * sig * (1.0 - sig)).astype(BF)
    gr_s[...] += dot_nn(mt_s[...], dot_nt(dlog, order_ref[...]).astype(BF))
    for o in range(owners):
        where = pl.ds(o * share, share)
        moe_ref[:, where] = dot_nt(hg_s[...], weights_ref[o, 1]).astype(BF)
        drow_ref[:, where] = (
            dot_nt(dpre_s[...], weights_ref[o, 0]) + dot_nt(dlog, router_s[where, :])
        ).astype(BF)
        gup_s[where, :] += dot_nn(mt_s[where, :], dpre_s[...])
        gdn_s[where, :] += dot_nn(gt_s[where, :], hg_s[...])

    @pl.when(step == steps - 1)
    def _():
        for o in range(owners):
            grads_ref[o, 0] = gup_s[pl.ds(o * share, share), :].astype(BF)
            grads_ref[o, 1] = gdn_s[pl.ds(o * share, share), :].astype(BF)
        grouter_ref[...] = gr_s[...].astype(BF)


def moe(rows, cots, member, packed, router_at, order, mine, weights):
    count = rows.shape[0]
    tile = 512
    owners, _, share, units = weights.shape
    slots = units // F
    steps = count // tile
    lanes = member.shape[1]
    row_spec = pl.BlockSpec((tile, D), lambda i: (i, 0))
    whole = pl.BlockSpec(memory_space=pltpu.VMEM)
    router_spec = pl.BlockSpec((D, lanes), lambda i: (0, router_at // lanes))
    return pl.pallas_call(
        functools.partial(moe_kernel, steps, slots, 512),
        grid=(steps,),
        in_specs=[
            row_spec,
            row_spec,
            pl.BlockSpec((tile, lanes), lambda i: (i, 0)),
            router_spec,
            whole,
            whole,
            whole,
        ],
        out_specs=[row_spec, row_spec, whole, whole],
        out_shape=[
            jax.ShapeDtypeStruct((count, D), BF),
            jax.ShapeDtypeStruct((count, D), BF),
            jax.ShapeDtypeStruct(weights.shape, BF),
            jax.ShapeDtypeStruct((D, lanes), BF),
        ],
        scratch_shapes=[
            pltpu.VMEM((D, F), BF),
            pltpu.VMEM((tile, F), F32),
            pltpu.VMEM((tile, units), BF),
            pltpu.VMEM((tile, units), BF),
            pltpu.VMEM((D, tile), BF),
            pltpu.VMEM((D, tile), BF),
            pltpu.VMEM((D, units), F32),
            pltpu.VMEM((D, units), F32),
            pltpu.VMEM((D, lanes), F32),
        ],
        compiler_params=pltpu.CompilerParams(vmem_limit_bytes=60 * 1024 * 1024),
        cost_estimate=pl.CostEstimate(
            flops=12 * count * D * units,
            bytes_accessed=count * D * 8 + D * units * 8,
            transcendentals=count * units,
        ),
    )(rows, cots, member, packed, order, mine, weights)


def fused_kernel(first, owners, slots, wide, tile_cols, *refs):
    if first:
        middle, cots, member, weights, packed, order_ref, mine_ref = refs[:7]
        rows_out, drow_out, moe_out, grads_out, grouter_out = refs[7:12]
        refs = refs[12:]
    else:
        middle, cots, member, weights, packed, order_ref, mine_ref = refs[:7]
        drow_in, moe_in, grouter_in, middle_in = refs[7:11]
        drow_out, layer_out, grads_out, grouter_out = refs[11:15]
        refs = refs[15:]
    (m_s, c_s, b_s, w_s, gup_s, gdn_s, gr_s, hg_s, dpre_s, mt_s, gt_s, router_in, router_s, gate_s) = refs[:14]
    part_d, part_m, local, wsem, tsem = refs[14:19]
    if first:
        gsend, grecv = refs[19:]
    else:
        sib_s, first_s, second_s, ssend, srecv = refs[19:]
    place = Place()
    z = place.z
    count = m_s.shape[0] // 8
    half = count // 2
    lanes = b_s.shape[1]
    share = D // owners
    ins = (middle,)
    bufs = (m_s,)
    sums = (m_s, c_s)
    swap = place.sib - place.e
    mine = (place.e, place.xnb, place.ynb, place.diag)
    if not first:
        mine = (place.diag, place.xnb, place.ynb, place.e)

    def span(e, start=0, size=count):
        return pl.ds(pl.multiple_of(e * count + start, 16), size)

    def remote(sems, a, kind, src, dst, to):
        return pltpu.make_async_remote_copy(
            src_ref=src, dst_ref=dst, send_sem=sems[0].at[a, kind], recv_sem=sems[1].at[a, kind],
            device_id=(z, to), device_id_type=MESH)

    def passing(a, kind):
        buf = bufs[a]
        if kind in (XS, YS, S0):
            src, at = ins[a], span(place.e)
        elif kind == FA:
            at = span(place.xnb, 0, half)
            src = buf.at[at]
        elif kind == FB:
            at = span(place.ynb, half, half)
            src = buf.at[at]
        else:
            at = span(mine[kind - S0])
            src = buf.at[at]
        to = {XS: place.xnb, YS: place.ynb, FA: place.ynb, FB: place.xnb}.get(kind, place.sib)
        return remote((gsend, grecv), a, kind, src, buf.at[at], to)

    def got(a, kind):
        at = {
            XS: lambda: span(place.xnb),
            YS: lambda: span(place.ynb),
            FA: lambda: span(place.diag, 0, half),
            FB: lambda: span(place.diag, half, half),
        }.get(kind, lambda: span(mine[kind - S0] + swap))()
        ref = bufs[a].at[at]
        remote((gsend, grecv), a, kind, ref, ref, place.sib).wait_recv()

    HY0, HY1, HX0, HX1, HX2, HY2 = 4, 5, 6, 7, 8, 9

    def to_sib(a, t):
        return remote((ssend, srecv), a, t, sums[a].at[span(mine[t] + swap)], sib_s.at[a, t], place.sib)

    def hop(a, kind):
        src_e, second, dst, to = {
            HY0: (place.ynb, False, first_s.at[a, 0], place.ynb),
            HY1: (place.diag, False, first_s.at[a, 1], place.ynb),
            HX0: (place.xnb, True, first_s.at[a, 2], place.xnb),
            HX1: (place.diag, True, first_s.at[a, 3], place.xnb),
            HX2: (place.xnb, False, second_s.at[a, 0], place.xnb),
            HY2: (place.ynb, True, second_s.at[a, 1], place.ynb),
        }[kind]
        src = sums[a].at[span(src_e, half if second else 0, half)]
        return remote((ssend, srecv), a, kind, src, dst, to)

    step_rows = 32

    def add(a, e, start, size, terms, keep=None):
        buf = sums[a]

        @pl.loop(0, size // step_rows)
        def _(g):
            here = pl.ds(pl.multiple_of(e * count + start + g * step_rows, 16), step_rows)
            there = pl.ds(pl.multiple_of(g * step_rows, 16), step_rows)
            total = buf[here, :].astype(F32)
            for lead in terms:
                total = total + lead[0][(*lead[1], there, slice(None))].astype(F32)
            if keep is None:
                buf[here, :] = total.astype(BF)
            else:
                own_rows = pl.ds(pl.multiple_of(start + g * step_rows, 16), step_rows)
                if a == 1:
                    total = total + middle_in[own_rows, :]
                keep[own_rows, :] = total.astype(keep.dtype)

    def chip_of(t):
        tx, ty = (t % 2, t // 2) if first else ((3 - t) // 2, (3 - t) % 2)
        chip_x = place.x + tx * (1 - 2 * place.x)
        chip_y = place.y + ty * (1 - 2 * place.y)
        return pl.ds(pl.multiple_of((chip_y * 2 + chip_x) * 2 * count, 16), 2 * count)

    if first:
        own = [
            pltpu.make_async_copy(middle, m_s.at[span(place.e)], local.at[0]),
            pltpu.make_async_copy(cots, c_s, local.at[1]),
        ]
    else:
        own = []
    own.append(pltpu.make_async_copy(member, b_s, local.at[2]))
    for c in own:
        c.start()

    def tile_copies(t):
        at = chip_of(t)
        if first:
            pairs = ((m_s, rows_out), (part_d, drow_out), (part_m, moe_out))
        else:
            pairs = ((middle, m_s), (cots, c_s), (drow_in, part_d), (moe_in, part_m))
        slot = pl.ds(pl.multiple_of((t % 2) * 2 * count, 16), 2 * count)
        return [
            pltpu.make_async_copy(
                src.at[at], dst.at[slot if dst is part_d or dst is part_m else at], tsem.at[t, i]
            )
            for i, (src, dst) in enumerate(pairs)
        ]

    if not first:
        for t in range(4):
            for c in tile_copies(t)[:2]:
                c.start()
    router_copy = pltpu.make_async_copy(packed.at[:, pl.ds(wide, lanes)], router_in, local.at[3])
    router_copy.start()

    @pl.loop(0, slots)
    def _(s):
        for o in range(owners):
            for k in (0, 1):
                pltpu.make_async_copy(
                    weights.at[o, k * slots + s],
                    w_s.at[k, pl.ds(o * share, share), pl.ds(pl.multiple_of(s * F, F), F)],
                    wsem.at[0],
                ).start()

    greet(place, False, owners)
    if first:
        for kind in (XS, YS, S0):
            passing(0, kind).start()
        gr_s[...] = jnp.zeros_like(gr_s)
    else:
        for t in (0, 1):
            for c in tile_copies(t)[2:]:
                c.start()
        gr_s[...] = grouter_in[...]
    gup_s[...] = jnp.zeros_like(gup_s)
    gdn_s[...] = jnp.zeros_like(gdn_s)

    root = math.sqrt(2.0 / math.pi)
    cube = 0.044715
    tile = 2 * count
    units = slots * F
    per = tile_cols // F

    @pl.loop(0, 4)
    def _(t):
        @pl.when(t == 0)
        def _():
            for c in own:
                c.wait()
            router_copy.wait()
            router_s[...] = dot_nn(router_in[...], order_ref[...]).astype(BF)
            if first:
                got(0, S0)
            pltpu.make_async_copy(w_s, w_s, wsem.at[0]).wait()

        if first:

            @pl.when(t == 1)
            def _():
                got(0, XS)
                passing(0, FA).start()
                passing(0, S1).start()
                got(0, YS)
                passing(0, FB).start()
                passing(0, S2).start()
                got(0, S1)

            @pl.when(t == 2)
            def _():
                got(0, FA)
                got(0, FB)
                passing(0, S3).start()
                got(0, S2)

            @pl.when(t == 3)
            def _():
                got(0, S3)

        else:
            for k in range(4):

                @pl.when(t == k)
                def _():
                    for c in tile_copies(k)[:2]:
                        c.wait()

        here = chip_of(t)
        if first:
            tile_copies(t)[0].start()
        mt_s[...] = m_s[here, :].T
        gt_s[...] = c_s[here, :].T
        sig = jax.nn.sigmoid(dot_nn(m_s[here, :], router_s[...]))
        mask = dot_nn(b_s[here, :], mine_ref[...])
        gate_s[...] = sig * mask
        lane = lax.broadcasted_iota(jnp.int32, (1, F), 1)
        d_gate = jnp.zeros(gate_s.shape, F32)
        for c in range(units // tile_cols):
            cols = pl.ds(c * tile_cols, tile_cols)
            pre_all = dot_nn(m_s[here, :], w_s[0, :, cols])
            back_all = dot_nn(c_s[here, :], w_s[1, :, cols])
            for j in range(per):
                slot = c * per + j
                part = slice(j * F, (j + 1) * F)
                pre = pre_all[:, part]
                back = back_all[:, part]
                square = pre * pre
                th = jnp.tanh(root * pre * (1.0 + cube * square))
                halved = 0.5 * (1.0 + th)
                slope = halved + (0.5 * root) * pre * (1.0 - th * th) * (1.0 + (3.0 * cube) * square)
                hidden = (pre * halved).astype(BF).astype(F32)
                gate = gate_s[:, slot : slot + 1]
                d_one = jnp.sum(hidden * back, axis=1, keepdims=True)
                d_gate = d_gate + d_one * (lane == slot).astype(F32)
                where = pl.ds(slot * F, F)
                hg_s[:, where] = (gate * hidden).astype(BF)
                dpre_s[:, where] = (slope * (gate * back)).astype(BF)
        dlog = (d_gate * mask * sig * (1.0 - sig)).astype(BF)
        gr_s[...] += dot_nn(mt_s[...], dot_nt(dlog, order_ref[...]).astype(BF))

        if not first:

            @pl.when(t == 3)
            def _():
                for a in (0, 1):
                    hop(a, HY1).wait_recv()
                    add(a, place.xnb, 0, half, [(first_s, (a, 1))])
                    hop(a, HX2).start()
                    hop(a, HX1).wait_recv()
                    add(a, place.ynb, half, half, [(first_s, (a, 3))])
                    hop(a, HY2).start()

            for k in range(4):

                @pl.when(t == k)
                def _():
                    for c in tile_copies(k)[2:]:
                        c.wait()

        for a, (kept, dst) in enumerate(((part_d, m_s), (part_m, c_s))):
            for n in range(D // 256):
                where = pl.ds(n * 256, 256)
                if a == 0:
                    total = dot_nt(dpre_s[...], w_s[0, where, :]) + dot_nt(dlog, router_s[where, :])
                else:
                    total = dot_nt(hg_s[...], w_s[1, where, :])
                if first:
                    kept[here, where] = total.astype(BF)
                else:
                    there = pl.ds(pl.multiple_of((t % 2) * tile, 16), tile)
                    dst[here, where] = (total + kept[there, where].astype(F32)).astype(BF)
            if first:
                tile_copies(t)[1 + a].start()
            else:
                for k in range(4):

                    @pl.when(t == k)
                    def _():
                        to_sib(a, k).start()
                        if k < 2:
                            tile_copies(k + 2)[2 + a].start()

        def last(a):
            if first:
                return

            for k, kinds in enumerate(((HY1, HX1), (HX0,), (HY0,), ())):

                @pl.when(t == k)
                def _():
                    to_sib(a, k).wait_recv()
                    add(a, mine[k], 0, count, [(sib_s, (a, k))])
                    for kind in kinds:
                        hop(a, kind).start()

        last(0)
        for n in range(D // 256):
            where = pl.ds(n * 256, 256)
            gup_s[where, :] += dot_nn(mt_s[where, :], dpre_s[...])
        last(1)
        for n in range(D // 256):
            where = pl.ds(n * 256, 256)
            gdn_s[where, :] += dot_nn(gt_s[where, :], hg_s[...])

    w_s[0] = gup_s[...].astype(BF)
    w_s[1] = gdn_s[...].astype(BF)

    @pl.loop(0, slots)
    def _(s):
        for o in range(owners):
            for k in (0, 1):
                pltpu.make_async_copy(
                    w_s.at[k, pl.ds(o * share, share), pl.ds(pl.multiple_of(s * F, F), F)],
                    grads_out.at[o, k * slots + s],
                    wsem.at[0],
                ).start()

    grouter_out[...] = gr_s[...].astype(grouter_out.dtype)
    if first:
        for kind in range(8):
            passing(0, kind).wait_send()
        for t in range(4):
            for c in tile_copies(t):
                c.wait()
    else:
        for a, out in ((0, drow_out), (1, layer_out)):
            hop(a, HY0).wait_recv()
            hop(a, HX2).wait_recv()
            add(a, place.e, 0, half, [(first_s, (a, 0)), (second_s, (a, 0))], out)
            hop(a, HX0).wait_recv()
            hop(a, HY2).wait_recv()
            add(a, place.e, half, half, [(first_s, (a, 2)), (second_s, (a, 1))], out)
        for a in (0, 1):
            for t in range(4):
                to_sib(a, t).wait_send()
            for kind in (HY0, HY1, HX0, HX1, HX2, HY2):
                hop(a, kind).wait_send()
    pltpu.make_async_copy(w_s, w_s, wsem.at[0]).wait()


def fused_experts(first, rows, cots, member, weights, packed, wide, order, mine, more, cid):
    owners = weights.shape[0]
    slots = weights.shape[1] // 2
    total = cots.shape[0]
    count = total // 8
    lanes = member.shape[1]
    units = slots * F
    tile = 2 * count
    hbm = pl.BlockSpec(memory_space=pl.ANY)
    vmem = pl.BlockSpec(memory_space=pltpu.VMEM)
    dma = pltpu.SemaphoreType.DMA
    shape = jax.ShapeDtypeStruct
    scratch = [
        pltpu.VMEM((total, D), BF),
        pltpu.VMEM((total, D), BF),
        pltpu.VMEM((total, lanes), BF),
        pltpu.VMEM((2, D, units), BF),
        pltpu.VMEM((D, units), F32),
        pltpu.VMEM((D, units), F32),
        pltpu.VMEM((D, lanes), F32),
        pltpu.VMEM((tile, units), BF),
        pltpu.VMEM((tile, units), BF),
        pltpu.VMEM((D, tile), BF),
        pltpu.VMEM((D, tile), BF),
        pltpu.VMEM((D, lanes), BF),
        pltpu.VMEM((D, F), BF),
        pltpu.VMEM((tile, F), F32),
        pltpu.VMEM((total if first else 2 * tile, D), BF),
        pltpu.VMEM((total if first else 2 * tile, D), BF),
        dma((4,)),
        dma((1,)),
        dma((4, 4)),
    ]
    if first:
        out_specs = [hbm, hbm, hbm, hbm, vmem]
        out_shape = [shape((total, D), BF)] * 3
        out_shape += [shape(weights.shape, BF), shape((D, lanes), F32)]
        in_specs = [hbm] * 5 + [vmem] * 2
        scratch += [dma((1, 8)), dma((1, 8))]
    else:
        out_specs = [vmem, vmem, hbm, vmem]
        out_shape = [shape((count, D), F32), shape((count, D), BF)]
        out_shape += [shape(weights.shape, BF), shape((D, lanes), BF)]
        in_specs = [hbm] * 5 + [vmem] * 2 + [hbm, hbm, vmem, vmem]
        scratch += [
            pltpu.VMEM((2, 4, count, D), BF),
            pltpu.VMEM((2, 4, count // 2, D), BF),
            pltpu.VMEM((2, 2, count // 2, D), BF),
            dma((2, 10)),
            dma((2, 10)),
        ]
    return pl.pallas_call(
        functools.partial(fused_kernel, first, owners, slots, wide, 256),
        in_specs=in_specs,
        out_specs=out_specs,
        out_shape=out_shape,
        scratch_shapes=scratch,
        compiler_params=pltpu.CompilerParams(
            collective_id=cid, has_side_effects=True, vmem_limit_bytes=64 * 1024 * 1024 - 65536
        ),
        cost_estimate=pl.CostEstimate(
            flops=12 * total * D * units,
            bytes_accessed=D * units * 8 + total * D * 8,
            transcendentals=total * units,
        ),
    )(rows, cots, member, weights, packed, order, mine, *more)


def forward_kernel(
    wide,
    lanes,
    lengths_ref,
    x_ref,
    choice_ref,
    packed_ref,
    heads_all_ref,
    qk_ref,
    vals_ref,
    sig_ref,
    mask_ref,
    vlow_ref,
    prob_ref,
    attended_ref,
    mixed_ref,
    middle_ref,
    mlow_ref,
    w_ref,
    heads_ref,
    wsem,
):
    cuts = (pl.ds(wide + lanes, 128), pl.ds(0, QK), pl.ds(QK, VAL))
    coming = [
        pltpu.make_async_copy(packed_ref.at[:, c], w_ref.at[:, c], wsem.at[i])
        for i, c in enumerate(cuts)
    ]
    coming.append(pltpu.make_async_copy(heads_all_ref, heads_ref, wsem.at[3]))
    for c in coming:
        c.start()
    count = x_ref.shape[0]
    seq = count // MB
    xf = x_ref[...].astype(F32)
    centred = xf - jnp.mean(xf, axis=1, keepdims=True)
    variance = jnp.mean(centred * centred, axis=1, keepdims=True)
    coming[0].wait()
    gain_row = w_ref[:, pl.ds(wide + lanes, 128)].astype(F32).T[SEL : SEL + 1, :]
    normed = (centred * lax.rsqrt(variance + epsilon) * gain_row).astype(BF)
    coming[1].wait()
    for n in range(QK // 512):
        cols = pl.ds(n * 512, 512)
        qk_ref[:, cols] = dot_nn(normed, w_ref[:, cols]).astype(BF)
    sig = jax.nn.sigmoid(dot_nn(x_ref[...], w_ref[:, pl.ds(wide + lanes, 128)]))
    row = lax.broadcasted_iota(jnp.int32, (count, 128), 0)
    lane = lax.broadcasted_iota(jnp.int32, (count, 128), 1)
    live = (row < lengths_ref[0, 0]).astype(F32)
    for b in range(1, MB):
        live = jnp.where(row < b * seq, live, (row < b * seq + lengths_ref[b, 0]).astype(F32))
    mask = jnp.zeros((count, 128), F32)
    top = choice_ref.shape[1] // H
    for v in range(H * top):
        picked = choice_ref[:, v : v + 1] + NV * (v // top)
        mask = mask + (picked == lane).astype(F32) + (picked + H * NV == lane).astype(F32) * live
    sig_ref[...] = sig
    mask_ref[...] = mask
    gates = sig * mask
    coming[2].wait()
    for h in range(H):
        vals = dot_nn(x_ref[...], w_ref[:, pl.ds(QK + h * NV * HD, NV * HD)])
        vals_ref[:, pl.ds(h * NV * HD, NV * HD)] = vals.astype(BF)
        total = gates[:, h * NV : h * NV + 1] * vals[:, :HD]
        for e in range(1, NV):
            at = h * NV + e
            total = total + gates[:, at : at + 1] * vals[:, e * HD : (e + 1) * HD]
        vlow_ref[:, pl.ds(h * HD, HD)] = total.astype(BF)
    at_i = lax.broadcasted_iota(jnp.int32, (seq, seq), 0)
    at_j = lax.broadcasted_iota(jnp.int32, (seq, seq), 1)
    for b in range(MB):
        allowed = (at_j <= at_i) & (at_j < lengths_ref[b, 0])
        here = pl.ds(b * seq, seq)
        for h in range(H):
            queries = qk_ref[here, pl.ds(h * HD, HD)]
            keys_all = qk_ref[here, pl.ds((H + h) * HD, HD)]
            scores = jnp.where(allowed, dot_nt(queries, keys_all) * HD ** (-0.5), -1e30)
            expo = jnp.exp(scores - jnp.max(scores, axis=1, keepdims=True))
            prob = expo / jnp.sum(expo, axis=1, keepdims=True)
            prob_ref[b * H + h] = prob
            attended_ref[here, pl.ds(h * HD, HD)] = dot_nn(
                prob.astype(BF), vlow_ref[here, pl.ds(h * HD, HD)]
            )
    for h in range(H):
        attended = attended_ref[:, pl.ds(h * HD, HD)]
        for e in range(NV):
            at = h * NV + e
            gate = gates[:, H * NV + at : H * NV + at + 1]
            mixed_ref[:, pl.ds(at * HD, HD)] = (gate * attended).astype(BF)
    coming[3].wait()
    for n in range(D // 512):
        cols = pl.ds(n * 512, 512)
        middle = x_ref[:, cols].astype(F32) + dot_nn(mixed_ref[...], heads_ref[:, cols])
        middle_ref[:, cols] = middle
        mlow_ref[:, cols] = middle.astype(BF)


def forward(lengths, tokens, choice, packed, heads, wide, lanes):
    count = tokens.shape[0]
    seq = count // MB
    vmem = pl.BlockSpec(memory_space=pltpu.VMEM)
    shape = jax.ShapeDtypeStruct
    return pl.pallas_call(
        functools.partial(forward_kernel, wide, lanes),
        in_specs=[pl.BlockSpec(memory_space=pltpu.SMEM)]
        + [vmem] * 2
        + [pl.BlockSpec(memory_space=pl.ANY)] * 2,
        out_specs=[vmem] * 10,
        scratch_shapes=[
            pltpu.VMEM(packed.shape, BF),
            pltpu.VMEM(heads.shape, BF),
            pltpu.SemaphoreType.DMA((4,)),
        ],
        out_shape=[
            shape((count, QK), BF),
            shape((count, VAL), BF),
            shape((count, 128), F32),
            shape((count, 128), F32),
            shape((count, H * HD), BF),
            shape((MB * H, seq, seq), F32),
            shape((count, H * HD), F32),
            shape((count, VAL), BF),
            shape((count, D), F32),
            shape((count, D), BF),
        ],
        compiler_params=pltpu.CompilerParams(vmem_limit_bytes=56 * 1024 * 1024),
        cost_estimate=pl.CostEstimate(
            flops=2 * count * D * (wide + VAL),
            bytes_accessed=(wide + VAL) * D * 2 + count * D * 20,
            transcendentals=count * seq * H,
        ),
    )(lengths, tokens, choice, packed, heads)


def backward_kernel(wide, lanes, steps, *refs):
    (
        x_ref,
        cots_ref,
        drow_ref,
        qk_ref,
        vals_ref,
        sig_ref,
        mask_ref,
        vlow_ref,
        prob_ref,
        attended_ref,
        mixed_ref,
        grouter_ref,
        packed_ref,
        heads_all_ref,
        _,
        dx_ref,
    ) = refs[:16]
    dvals_s, dqk_s, w_ref, heads_ref, wsem = refs[16:21]
    put_w, put_h, event = steps(refs[21:])
    coming = [
        pltpu.make_async_copy(src, dst, wsem.at[i])
        for i, (src, dst) in enumerate(((heads_all_ref, heads_ref), (packed_ref, w_ref)))
    ]
    for c in coming:
        c.start()
    count = x_ref.shape[0]
    seq = count // MB
    d_branch = (cots_ref[...].astype(F32) + drow_ref[...]).astype(BF)
    width = NV * HD
    for h in range(H):
        where = pl.ds(h * width, width)
        put_h(h, dot_tn(mixed_ref[:, where], d_branch).astype(BF))
    event("heads")
    for c in coming:
        c.wait()
    mask = mask_ref[...]
    sig = sig_ref[...]
    gates = sig * mask
    lane = lax.broadcasted_iota(jnp.int32, (1, 128), 1)
    d_gates = jnp.zeros((count, 128), F32)
    for h in range(H):
        where = pl.ds(h * width, width)
        d_mixed = dot_nt(d_branch, heads_ref[where, :])
        attended = attended_ref[:, pl.ds(h * HD, HD)]
        total = jnp.zeros((count, HD), F32)
        for e in range(NV):
            at = H * NV + h * NV + e
            part = d_mixed[:, e * HD : (e + 1) * HD]
            total = total + gates[:, at : at + 1] * part
            d_one = jnp.sum(part * attended, axis=1, keepdims=True)
            d_gates = d_gates + d_one * (lane == at).astype(F32)
        d_attended = total.astype(BF)
        d_values = []
        for b in range(MB):
            here = pl.ds(b * seq, seq)
            rows = slice(b * seq, (b + 1) * seq)
            prob = prob_ref[b * H + h]
            values = vlow_ref[here, pl.ds(h * HD, HD)]
            d_prob = dot_nt(d_attended[rows], values)
            d_scores = (
                prob * (d_prob - jnp.sum(prob * d_prob, axis=1, keepdims=True))
            ).astype(BF)
            d_values.append(dot_tn(prob.astype(BF), d_attended[rows]).astype(BF).astype(F32))
            queries = qk_ref[here, pl.ds(h * HD, HD)]
            keys_all = qk_ref[here, pl.ds((H + h) * HD, HD)]
            dqk_s[here, pl.ds(h * HD, HD)] = (dot_nn(d_scores, keys_all) * HD ** (-0.5)).astype(BF)
            dqk_s[here, pl.ds((H + h) * HD, HD)] = (
                dot_tn(d_scores, queries) * HD ** (-0.5)
            ).astype(BF)
        d_value = jnp.concatenate(d_values, axis=0)
        for e in range(NV):
            at = h * NV + e
            cols = pl.ds(at * HD, HD)
            d_one = jnp.sum(d_value * vals_ref[:, cols].astype(F32), axis=1, keepdims=True)
            d_gates = d_gates + d_one * (lane == at).astype(F32)
            dvals_s[:, cols] = (gates[:, at : at + 1] * d_value).astype(BF)
        event(h)
    d_select = (d_gates * mask * sig * (1.0 - sig)).astype(BF)
    x_t = x_ref[...].T
    for n in range(VAL // 512):
        put_w(QK + n * 512, dot_nn(x_t, dvals_s[:, pl.ds(n * 512, 512)]).astype(BF))
    event("values")
    xf = x_ref[...].astype(F32)
    centred = xf - jnp.mean(xf, axis=1, keepdims=True)
    variance = jnp.mean(centred * centred, axis=1, keepdims=True)
    rstd = lax.rsqrt(variance + epsilon)
    unit = centred * rstd
    gain_row = w_ref[:, pl.ds(wide + lanes, 128)].astype(F32).T[SEL : SEL + 1, :]
    normed_t = (unit * gain_row).astype(BF).T
    for n in range(QK // 512):
        put_w(n * 512, dot_nn(normed_t, dqk_s[:, pl.ds(n * 512, 512)]).astype(BF))
    d_normed = dot_nt(dqk_s[...], w_ref[:, pl.ds(0, QK)])
    grad_gain = jnp.sum(d_normed * unit, axis=0, keepdims=True)
    small = dot_tn(d_select, x_ref[...])
    which = lax.broadcasted_iota(jnp.int32, (128, 1), 0)
    put_w(wide + lanes, jnp.where(which == SEL, grad_gain, small).T.astype(BF))
    put_w(wide, grouter_ref[...])
    event("rest")
    scaled = d_normed * gain_row
    dx_ref[...] = (
        cots_ref[...].astype(F32)
        + drow_ref[...]
        + (
            scaled
            - jnp.mean(scaled, axis=1, keepdims=True)
            - unit * jnp.mean(scaled * unit, axis=1, keepdims=True)
        )
        * rstd
    )
    for n in range(D // 256):
        rows = pl.ds(n * 256, 256)
        dx_ref[:, rows] += dot_nt(dvals_s[...], w_ref[rows, pl.ds(QK, VAL)]) + dot_nt(
            d_select, w_ref[rows, pl.ds(wide + lanes, 128)]
        )
    event("end")


def plain_steps(wide, refs):
    gw_ref, gheads_ref = refs

    def put_w(start, value):
        gw_ref[:, pl.ds(start, value.shape[1])] = value

    def put_h(h, value):
        gheads_ref[pl.ds(h * value.shape[0], value.shape[0]), :] = value

    def nothing(*_):
        pass

    return put_w, put_h, nothing


def backward(tokens, cots, drow, saved, grouter, packed, heads, ahead, wide, lanes, owners, cid):
    count = tokens.shape[0]
    vmem = pl.BlockSpec(memory_space=pltpu.VMEM)
    shape = jax.ShapeDtypeStruct
    scratch = [
        pltpu.VMEM((count, VAL), BF),
        pltpu.VMEM((count, QK), BF),
        pltpu.VMEM(packed.shape, BF),
        pltpu.VMEM(heads.shape, BF),
        pltpu.SemaphoreType.DMA((2,)),
    ]
    grads = (packed.shape, heads.shape)
    summed = ((D, VAL), heads.shape, (D, packed.shape[1] - VAL))
    if cid is None:
        kernel = lambda *refs: backward_kernel(
            wide, lanes, functools.partial(plain_steps, wide), *refs[:16], *refs[18:23], *refs[16:18]
        )
        out_shape = [shape((count, D), F32)] + [shape(g, BF) for g in grads]
        more = {}
    else:
        kernel = lambda *refs: backward_kernel(
            wide,
            lanes,
            functools.partial(summing_steps, owners),
            *refs[:16],
            *refs[19:24],
            *refs[16:19],
            *refs[24:],
        )
        more_scratch, sums = scatter_space(summed, owners)
        scratch += more_scratch
        out_shape = [shape((count, D), F32)] + sums
        more = dict(collective_id=cid, has_side_effects=True)
    return pl.pallas_call(
        kernel,
        in_specs=[vmem] * 12 + [pl.BlockSpec(memory_space=pl.ANY)] * 3,
        out_specs=[vmem] * len(out_shape),
        out_shape=out_shape,
        scratch_shapes=scratch,
        compiler_params=pltpu.CompilerParams(vmem_limit_bytes=64 * 1024 * 1024 - 65536, **more),
        cost_estimate=pl.CostEstimate(
            flops=4 * count * D * (wide + VAL),
            bytes_accessed=(wide + VAL) * D * 4 + count * D * 30,
            transcendentals=0,
        ),
    )(tokens, cots, drow, *saved, grouter, packed, heads, ahead)


def update_kernel(lanes, rates, values_ref, heads_sum_ref, rest_ref, first_ref, second_ref, *refs):
    ins, outs = refs[:18], refs[18:]

    def step(i, at, gradient):
        new = update_weight(*(ref[at] for ref in ins[3 * i : 3 * i + 3]), gradient, rates[i])
        for ref, value in zip(outs[4 * i : 4 * i + 4], new):
            ref[at] = value

    everything = (slice(None), slice(None))
    step(0, (slice(None), pl.ds(0, QK)), rest_ref[:, pl.ds(0, QK)])
    step(0, (slice(None), pl.ds(QK, VAL)), values_ref[...])
    step(1, everything, rest_ref[:, pl.ds(QK + lanes, SEL)])
    step(2, everything, rest_ref[:, pl.ds(QK, ins[6].shape[1])])
    step(3, everything, heads_sum_ref[...])
    start = 0
    for ref in (first_ref, second_ref):
        part = ref.shape[0] // 2

        @pl.loop(0, part)
        def _(s):
            for k in (0, 1):
                step(4 + k, start + s, ref[k * part + s].astype(F32))

        start += part


def update_all(sums, sums_a, sums_b, weights, rates, lanes):
    vmem = pl.BlockSpec(memory_space=pltpu.VMEM)
    shapes = []
    for i in range(6):
        shapes += [jax.ShapeDtypeStruct(weights[3 * i].shape, t) for t in (F32, F32, F32, BF)]
    return pl.pallas_call(
        functools.partial(update_kernel, lanes, rates),
        in_specs=[vmem] * 23,
        out_specs=[vmem] * 24,
        out_shape=shapes,
        compiler_params=pltpu.CompilerParams(vmem_limit_bytes=60 * 1024 * 1024),
    )(*sums, sums_a, sums_b, *weights)


def body(
    tokens,
    cotangent,
    lengths,
    routes,
    head_choice,
    placement,
    gain_master,
    gain_moment,
    gain_average,
    qkv_master,
    qkv_moment,
    qkv_average,
    select_master,
    select_moment,
    select_average,
    router_master,
    router_moment,
    router_average,
    heads_out_master,
    heads_out_moment,
    heads_out_average,
    up_master,
    up_moment,
    up_average,
    down_master,
    down_moment,
    down_average,
):
    both = ("dp", "expert")
    owners = lax.axis_size("dp")
    group = lax.axis_size("expert")
    own_kernels = group == 8
    experts = placement.shape[0]
    slots = up_master.shape[0]
    units = slots * F
    seq = tokens.shape[1]
    count = MB * seq
    share = up_master.shape[1]
    mine = lax.axis_index("expert")
    lanes = -(-experts // 128) * 128

    own_rows = qkv_master.shape[0]
    wide = QK + VAL
    packed = jnp.concatenate(
        [
            qkv_master.astype(BF),
            router_master.astype(BF),
            jnp.zeros((own_rows, lanes - experts), BF),
            select_master.astype(BF),
            gain_master.astype(BF)[:, None],
            jnp.zeros((own_rows, 127 - SEL), BF),
        ],
        axis=1,
    )
    heads_low = heads_out_master.astype(BF)

    part = slots // 2

    def fetch(own):
        low = jnp.concatenate([up_master[own].astype(BF), down_master[own].astype(BF)], axis=0)
        return lax.all_gather(low, "dp", axis=0, tiled=False)

    weights = (fetch(slice(0, part)), fetch(slice(part, slots)))

    flat_tokens = tokens.reshape(count, D)
    flat_cots = cotangent.reshape(count, D)
    live = (jnp.arange(seq, dtype=jnp.int32)[None, :] < lengths).astype(F32).reshape(count)
    lane_ids = jnp.arange(lanes, dtype=jnp.int32)
    named = jnp.sum(
        (routes.reshape(count, TOPK)[..., None] == lane_ids).astype(F32), axis=1
    ) * live[:, None]
    padded = jnp.pad(placement, (0, lanes - experts), constant_values=-1)
    perm = (padded[:, None] == lane_ids[None, :]).astype(BF)
    member = dot_nn(named.astype(BF), perm).astype(BF)
    own_lane = jnp.arange(F, dtype=jnp.int32)[None, :]

    def selects(start, number):
        slot = mine * slots + start
        inside = own_lane < number
        return (
            (((padded[:, None] - slot) == own_lane) & inside & (padded[:, None] >= 0)).astype(BF),
            (((lane_ids[:, None] - slot) == own_lane) & inside).astype(BF),
        )

    if own_kernels:
        packed_all, heads, cots_all, member_all = gather(
            (packed, heads_low, flat_cots, member),
            (True, True, False, False),
            (own_rows // 2, 48, count // 2, count // 2),
            owners,
            group,
            0,
        )
    else:
        packed_all = lax.all_gather(packed, both, axis=0, tiled=True)
        heads = lax.all_gather(heads_low, both, axis=0, tiled=True)
        cots_all, member_all = (
            lax.all_gather(a, "expert", axis=0, tiled=True) for a in (flat_cots, member)
        )
    choice = head_choice.reshape(count, -1)
    *saved, middle, middle_low = forward(lengths, flat_tokens, choice, packed_all, heads, wide, lanes)
    if own_kernels:
        rows_all, drow_part, moe_part, grads_a, router_part = fused_experts(
            True, middle_low, cots_all, member_all, weights[0], packed_all, wide, *selects(0, part), (), 1
        )
        d_from_rows, mixed, grads_b, grad_router = fused_experts(
            False,
            rows_all,
            cots_all,
            member_all,
            weights[1],
            packed_all,
            wide,
            *selects(part, slots - part),
            (drow_part, moe_part, router_part, middle),
            2,
        )
    else:
        rows_all = lax.all_gather(middle_low, "expert", axis=0, tiled=True)
        side = jnp.concatenate([w.reshape(owners, 2, -1, share, F) for w in weights], axis=2)
        side = side.transpose(0, 1, 3, 2, 4)
        moe_part, drow_part, expert_grads, grad_router = moe(
            rows_all,
            cots_all,
            member_all,
            packed_all,
            wide,
            *selects(0, slots),
            side.reshape(owners, 2, share, units),
        )
        expert_grads = expert_grads.reshape(owners, 2, share, slots, F).transpose(0, 1, 3, 2, 4)
        grads_a, grads_b = expert_grads[:, :, :part], expert_grads[:, :, part:]
        d_from_rows, moe_sum = (
            lax.psum_scatter(a, "expert", scatter_dimension=0, tiled=True).astype(F32)
            for a in (drow_part, moe_part)
        )
        mixed = (middle + moe_sum).astype(BF)
    sums_a, sums_b = (
        lax.psum_scatter(
            g.reshape(-1, share, F), "dp", scatter_dimension=0, tiled=True
        )
        for g in (grads_a, grads_b)
    )
    d_tokens, *grads = backward(
        flat_tokens,
        flat_cots,
        d_from_rows,
        saved,
        grad_router,
        packed_all,
        heads,
        sums_a,
        wide,
        lanes,
        owners,
        3 if own_kernels else None,
    )
    if own_kernels:
        sums = tuple(total.reshape(-1, total.shape[2]) for total in grads)
    else:
        packed_sum, heads_sum = (
            lax.psum_scatter(g, both, scatter_dimension=0, tiled=True).astype(F32) for g in grads
        )
        rest_sum = jnp.concatenate([packed_sum[:, :QK], packed_sum[:, wide:]], axis=1)
        sums = (packed_sum[:, QK:wide], heads_sum, rest_sum)
    gain_sum = sums[2][:, QK + lanes + SEL]
    rates = step_rates(count * owners * group, experts)
    outs = update_weight(gain_master, gain_moment, gain_average, gain_sum, rates[0]) + tuple(
        update_all(
            sums,
            sums_a,
            sums_b,
            (
                qkv_master,
                qkv_moment,
                qkv_average,
                select_master,
                select_moment,
                select_average,
                router_master,
                router_moment,
                router_average,
                heads_out_master,
                heads_out_moment,
                heads_out_average,
                up_master,
                up_moment,
                up_average,
                down_master,
                down_moment,
                down_average,
            ),
            rates[1:],
            lanes,
        )
    )
    return (mixed.reshape(tokens.shape), d_tokens.reshape(tokens.shape)) + outs


def solution(mesh):
    rows = P(None, ("dp", "expert"), None)
    flat = P(("dp", "expert"))
    dense = P(("dp", "expert"), None)
    expert = P("expert", "dp", None)
    in_specs = (
        rows,
        rows,
        P(None, ("dp", "expert")),
        rows,
        P(None, ("dp", "expert"), None, None),
        P(),
        *((flat,) * 3),
        *((dense,) * 12),
        *((expert,) * 6),
    )
    out_specs = (rows, rows, *((flat,) * 4), *((dense,) * 16), *((expert,) * 8))
    return jax.shard_map(body, mesh=mesh, in_specs=in_specs, out_specs=out_specs, check_vma=False)
```

```python
import functools
import math

import jax
import jax.numpy as jnp
from jax import lax
from jax.experimental import pallas as pl
from jax.experimental.pallas import tpu as pltpu
from jax.sharding import PartitionSpec as P

D = 1024
H = 4
HD = 128
NV = 5
F = 128
TOPK = 16
MB = 2
QK = 2 * H * HD
VAL = H * NV * HD
SEL = 2 * H * NV

momentum_decay = 0.9
average_decay = 0.5
rate_factor = 0.4
epsilon = 1e-05
BF = jnp.bfloat16
F32 = jnp.float32


def step_rates(total_tokens, experts):
    root_tokens = math.sqrt(total_tokens)
    expert_share = math.sqrt(TOPK / experts)
    spread_list = (
        0.3,
        D ** (-0.5),
        (2 * D) ** (-0.5),
        (9 * D) ** (-0.5),
        0.5,
        D ** (-0.5),
        (4 * F) ** (-0.5),
    )
    gradient_list = (1.0, 1.0, 3.0, 2.0 * expert_share, 0.1, 0.5 * expert_share, 0.4 * expert_share)
    return tuple(
        rate_factor * spread_value / (gradient_value * root_tokens)
        for spread_value, gradient_value in zip(spread_list, gradient_list)
    )


def update_weight(master, moment, average, gradient, step_size):
    new_moment = momentum_decay * moment + gradient
    new_weight = master - step_size * (gradient + momentum_decay * new_moment)
    new_average = average_decay * average + (1.0 - average_decay) * new_weight
    return (new_moment, new_average, new_weight, new_weight.astype(BF))


def dot_nt(a, b):
    return lax.dot_general(a, b, (((1,), (1,)), ((), ())), preferred_element_type=F32)


def dot_tn(a, b):
    return lax.dot_general(a, b, (((0,), (0,)), ((), ())), preferred_element_type=F32)


def dot_nn(a, b):
    return jnp.dot(a, b, preferred_element_type=F32)


MESH = pl.DeviceIdType.MESH


class Place:
    def __init__(self):
        self.z = lax.axis_index("dp")
        self.e = lax.axis_index("expert")
        core = self.e % 2
        x = (self.e // 2) % 2
        y = self.e // 4
        self.sib = self.e + 1 - 2 * core
        self.xnb = self.e + 2 - 4 * x
        self.ynb = self.e + 4 - 8 * y
        self.diag = self.xnb + 4 - 8 * y
        self.core, self.x, self.y = core, x, y


def greet(place, line, owners):
    barrier = pltpu.get_barrier_semaphore()
    z = place.z
    for e in (place.sib, place.xnb, place.ynb):
        pl.semaphore_signal(barrier, inc=1, device_id=(z, e), device_id_type=MESH)
    peers = 3
    if line:

        @pl.when(z > 0)
        def _():
            pl.semaphore_signal(barrier, inc=1, device_id=(z - 1, place.e), device_id_type=MESH)

        @pl.when(z < owners - 1)
        def _():
            pl.semaphore_signal(barrier, inc=1, device_id=(z + 1, place.e), device_id_type=MESH)

        peers = peers + (z + owners - 1) // owners + (2 * owners - 2 - z) // owners
    pl.semaphore_wait(barrier, peers)


XS, YS, FA, FB, S0, S1, S2, S3, UP, DOWN = range(10)

def gather_kernel(owners, group, lines, halves, *refs):
    n = len(lines)
    ins, outs, (send, recv, own) = refs[:n], refs[n : 2 * n], refs[2 * n :]
    place = Place()
    z = place.z
    copies_own = []
    for i in range(n):
        rows = ins[i].shape[0]
        slot = (z * group + place.e) if lines[i] else place.e
        cp = pltpu.make_async_copy(ins[i], outs[i].at[pl.ds(slot * rows, rows)], own.at[i])
        cp.start()
        copies_own.append(cp)
    greet(place, any(lines), owners)

    def block(i, rel, e, part=None):
        rows = ins[i].shape[0]
        slot = ((z + rel) * group + e) if lines[i] else e
        start, size = (0, rows) if part is None else part
        return outs[i].at[pl.ds(slot * rows + start, size)]

    def source(i, rel, part=None):
        if rel == 0:
            return ins[i] if part is None else ins[i].at[pl.ds(*part)]
        return block(i, rel, place.e, part)

    def sem(rel):
        return rel + owners - 1

    def go(i, rel, kind, src, dst, to_e, dz=0):
        return pltpu.make_async_remote_copy(
            src_ref=src, dst_ref=dst, send_sem=send.at[i, sem(rel), kind],
            recv_sem=recv.at[i, sem(rel - dz), min(kind, UP)],
            device_id=(z + dz, to_e), device_id_type=MESH)

    def parts(i):
        rows = ins[i].shape[0]
        return (0, halves[i]), (halves[i], rows - halves[i])

    def valid(rel):
        return (z + rel >= 0) & (z + rel < owners)

    def copies(i, rel):
        first, second = parts(i)
        e, xn, yn, dg, sb = place.e, place.xnb, place.ynb, place.diag, place.sib
        return {
            XS: lambda: go(i, rel, XS, source(i, rel), block(i, rel, e), xn),
            YS: lambda: go(i, rel, YS, source(i, rel), block(i, rel, e), yn),
            FA: lambda: go(i, rel, FA, block(i, rel, xn, first), block(i, rel, xn, first), yn),
            FB: lambda: go(i, rel, FB, block(i, rel, yn, second), block(i, rel, yn, second), xn),
            S0: lambda: go(i, rel, S0, source(i, rel), block(i, rel, e), sb),
            S1: lambda: go(i, rel, S1, block(i, rel, xn), block(i, rel, xn), sb),
            S2: lambda: go(i, rel, S2, block(i, rel, yn), block(i, rel, yn), sb),
            S3: lambda: go(i, rel, S3, block(i, rel, dg), block(i, rel, dg), sb),
        }

    def got(i, rel, kind, e, part=None):
        ref = block(i, rel, e, part)
        pltpu.make_async_remote_copy(
            src_ref=ref, dst_ref=ref, send_sem=send.at[i, sem(rel), min(kind, UP)], recv_sem=recv.at[i, sem(rel), min(kind, UP)],
            device_id=(z, place.sib), device_id_type=MESH).wait_recv()

    def stage_z(rel):
        @pl.when(valid(rel))
        def _():
            for i in range(n):
                if rel != 0 and not lines[i]:
                    continue
                if rel != 0:
                    got(i, rel, UP, place.e)
                if lines[i] and rel <= 0 and rel > 1 - owners:
                    @pl.when(z < owners - 1)
                    def _():
                        go(i, rel, UP, source(i, rel), block(i, rel, place.e), place.e, 1).start()
                if lines[i] and rel >= 0 and rel < owners - 1:
                    @pl.when(z > 0)
                    def _():
                        go(i, rel, DOWN, source(i, rel), block(i, rel, place.e), place.e, -1).start()
                c = copies(i, rel)
                c[XS]().start()
                c[YS]().start()
                c[S0]().start()

    def each(rel, fn):
        @pl.when(valid(rel))
        def _():
            for i in range(n):
                if rel == 0 or lines[i]:
                    fn(i, rel, copies(i, rel))

    def xy(i, rel, c):
        got(i, rel, XS, place.xnb)
        c[FA]().start()
        c[S1]().start()
        got(i, rel, YS, place.ynb)
        c[FB]().start()
        c[S2]().start()

    def dg(i, rel, c):
        first, second = parts(i)
        got(i, rel, FA, place.diag, first)
        got(i, rel, FB, place.diag, second)
        c[S3]().start()

    def end(i, rel, c):
        for k, e in ((S0, place.sib),):
            got(i, rel, S0, place.sib)
        got(i, rel, S1, place.xnb + place.sib - place.e)
        got(i, rel, S2, place.ynb + place.sib - place.e)
        got(i, rel, S3, place.diag + place.sib - place.e)
        for k in (XS, YS, FA, FB, S0, S1, S2, S3):
            c[k]().wait_send()
        if lines[i] and rel <= 0 and rel > 1 - owners:
            @pl.when(z < owners - 1)
            def _():
                go(i, rel, UP, source(i, rel), block(i, rel, place.e), place.e, 1).wait_send()
        if lines[i] and rel >= 0 and rel < owners - 1:
            @pl.when(z > 0)
            def _():
                go(i, rel, DOWN, source(i, rel), block(i, rel, place.e), place.e, -1).wait_send()

    rels = [0] + [s * d for d in range(1, owners) for s in (-1, 1)]
    waves = [[0]] + [[-d, d] for d in range(1, owners)]
    for w in range(owners + 3):
        if w < owners:
            for r in waves[w]:
                stage_z(r)
        if 0 <= w - 1 < owners:
            for r in waves[w - 1]:
                each(r, xy)
        if 0 <= w - 2 < owners:
            for r in waves[w - 2]:
                each(r, dg)
    for cp in copies_own:
        cp.wait()
    for r in rels:
        each(r, end)


def gather(arrays, lines, halves, owners, group, cid):
    outs = [jax.ShapeDtypeStruct((a.shape[0] * (owners if l else 1) * group,) + a.shape[1:], a.dtype) for a, l in zip(arrays, lines)]
    n = len(arrays)
    any_spec = pl.BlockSpec(memory_space=pl.ANY)
    return pl.pallas_call(
        functools.partial(gather_kernel, owners, group, lines, halves),
        out_shape=outs, in_specs=[any_spec] * n, out_specs=[any_spec] * n,
        scratch_shapes=[pltpu.SemaphoreType.DMA((n, 2 * owners - 1, 10)), pltpu.SemaphoreType.DMA((n, 2 * owners - 1, 9)), pltpu.SemaphoreType.DMA((n,))],
        compiler_params=pltpu.CompilerParams(collective_id=cid, has_side_effects=True),
    )(*arrays)


G = 16
(LOAD, SIB, Y0, Y1, X0, X1, X2, Y2, UP, DOWN) = range(10)


def summing_steps(owners, refs):
    outs, scratch = refs[:3], refs[3:]
    send, recv = scratch[18:]
    place = Place()
    z = place.z
    chips = {k: e // 2 for k, e in (("me", place.e), ("xn", place.xnb), ("yn", place.ynb), ("dg", place.diag))}

    class Item:
        def __init__(self, i, rel):
            self.i, self.rel = i, rel
            self.own, self.sib, self.first, self.second, self.up, self.down = scratch[6 * i : 6 * i + 6]
            groups = self.own.shape[3]
            self.groups, self.half = groups, (groups + 1) // 2
            self.at = z + rel
            self.slot = rel + owners - 1
            self.valid = (z + rel >= 0) & (z + rel < owners)

        def piece(self, ref, *lead):
            return ref.at[lead]

        def rows(self, second):
            return pl.ds(self.half, self.groups - self.half) if second else pl.ds(0, self.half)

        def copy(self, kind, src, dst, to, dz=0):
            there = self.slot - dz
            return pltpu.make_async_remote_copy(
                src_ref=src, dst_ref=dst,
                send_sem=send.at[self.i, self.slot, kind], recv_sem=recv.at[self.i, there, kind],
                device_id=(z + dz, to), device_id_type=MESH)

        def to_sib(self):
            return self.copy(SIB, self.own.at[self.at, slice(None), 1 - place.core],
                             self.sib.at[self.at], place.sib)

        def hop1(self, axis, other):
            second = axis == 1
            to = place.xnb if axis else place.ynb
            whose = chips["dg"] if other else chips["xn" if axis else "yn"]
            size = self.groups - self.half if second else self.half
            return self.copy((X0, X1)[other] if axis else (Y0, Y1)[other],
                             self.own.at[self.at, whose, place.core, self.rows(second)],
                             self.piece(self.first, self.at, axis, other, pl.ds(0, size)), to)

        def hop2(self, second):
            to = place.ynb if second else place.xnb
            whose = chips["yn" if second else "xn"]
            size = self.groups - self.half if second else self.half
            return self.copy(Y2 if second else X2,
                             self.own.at[self.at, whose, place.core, self.rows(second)],
                             self.piece(self.second, self.at, int(second), pl.ds(0, size)), to)

        def along(self, up):
            return self.copy(UP if up else DOWN, self.own.at[self.at, chips["me"], place.core],
                             (self.up if up else self.down).at[self.at], place.e, 1 if up else -1)

        def arrive_along(self, up):
            buf = (self.up if up else self.down).at[self.at]
            pltpu.make_async_remote_copy(
                src_ref=buf, dst_ref=buf, send_sem=send.at[self.i, self.slot, UP if up else DOWN],
                recv_sem=recv.at[self.i, self.slot, UP if up else DOWN],
                device_id=(z, place.sib), device_id_type=MESH).wait_recv()

        def add(self, whose, start, count, terms, keep=None):
            own, at, core = self.own, self.at, place.core

            @pl.loop(0, count)
            def _(g):
                total = own[at, whose, core, start + g].astype(F32)
                for ref, lead in terms:
                    total = total + ref[(*lead, g)].astype(F32)
                if keep is None:
                    own[at, whose, core, start + g] = total.astype(BF)
                else:
                    keep[start + g] = total

        def begin(self):
            self.to_sib().start()

        def stage1(self):
            self.to_sib().wait_recv()

            @pl.loop(0, 4)
            def _(chip):
                self.add(chip, 0, self.groups, [(self.sib, (self.at, chip))])
            for axis in (0, 1):
                for other in (1, 0):
                    self.hop1(axis, other).start()

        def stage2(self):
            self.hop1(0, 1).wait_recv()
            self.add(chips["xn"], 0, self.half, [(self.first, (self.at, 0, 1))])
            self.hop2(False).start()
            self.hop1(1, 1).wait_recv()
            self.add(chips["yn"], self.half, self.groups - self.half, [(self.first, (self.at, 1, 1))])
            self.hop2(True).start()

        def stage3(self):
            for axis in (0, 1):
                self.hop1(axis, 0).wait_recv()
                self.hop2(axis == 1).wait_recv()
            out = outs[self.i]
            rel = self.rel
            last = None if rel != 0 else out
            for half in (0, 1):
                start = self.half if half else 0
                size = self.groups - self.half if half else self.half
                self.add(chips["me"], start, size, [(self.first, (self.at, half, 0)), (self.second, (self.at, half))], last)
            for up in (True, False):
                if (rel >= 0) if up else (rel <= 0):
                    @pl.when((z > 0) if up else (z < owners - 1))
                    def _():
                        self.arrive_along(up)
                        buf = self.up if up else self.down

                        @pl.loop(0, self.groups)
                        def _(g):
                            more = buf[self.at, g].astype(F32)
                            if rel == 0:
                                out[g] += more
                            else:
                                where = (self.at, chips["me"], place.core, g)
                                self.own[where] = (self.own[where].astype(F32) + more).astype(BF)
            if rel != 0:
                self.along(rel > 0).start()

        def end(self):
            self.to_sib().wait_send()
            for axis in (0, 1):
                for other in (0, 1):
                    self.hop1(axis, other).wait_send()
                self.hop2(axis == 1).wait_send()
            if self.rel != 0:
                self.along(self.rel > 0).wait_send()

    values, heads, rest = (
        [Item(i, rel) for d in range(owners - 1, 0, -1) for rel in (d, -d)] + [Item(i, 0)]
        for i in range(3)
    )

    def run(items, name):
        for item in items:
            if item.rel != 0:
                pl.when(item.valid)(getattr(item, name))
            else:
                getattr(item, name)()

    def put(i, where, value):
        shape = scratch[6 * i].shape
        scratch[6 * i][where] = value.reshape(*shape[len(shape) - 6 + (where[0] is not Ellipsis) : 5], value.shape[1])

    def put_w(start, value):
        i = 0 if QK <= start < QK + VAL else 2
        at = start if start < QK else start - (QK if i == 0 else VAL)
        put(i, (Ellipsis, pl.ds(at, value.shape[1])), value)

    def put_h(h, value):
        put(1, (h,), value)

    plan = {
        "heads": ((heads, "begin"),),
        1: ((heads, "stage1"),),
        "values": ((values, "begin"), (heads, "stage2")),
        "rest": ((rest, "begin"), (values, "stage1")),
        "end": ((rest, "stage1"),),
    }

    def wave(items, w):
        return items[2 * w : 2 * w + 2] if 0 <= w < owners else []

    def event(name):
        if name == "heads":
            greet(place, True, owners)
        for items, stage in plan.get(name, ()):
            run(items, stage)
        if name == "end":
            for w in range(owners + 1):
                run(wave(heads, w), "stage3")
                run(wave(values, w), "stage2")
                run(wave(rest, w), "stage2")
                run(wave(values, w - 1), "stage3")
                run(wave(rest, w - 1), "stage3")
            run(heads + values + rest, "end")

    return put_w, put_h, event


def scatter_space(grads, owners):
    scratch, outs = [], []
    for rows, wide in grads:
        groups = rows // (owners * 8 * G)
        half = (groups + 1) // 2
        scratch += [
            pltpu.VMEM((owners, 4, 2, groups, G, wide), BF),
            pltpu.VMEM((owners, 4, groups, G, wide), BF),
            pltpu.VMEM((owners, 2, 2, half, G, wide), BF),
            pltpu.VMEM((owners, 2, half, G, wide), BF),
            pltpu.VMEM((owners, groups, G, wide), BF),
            pltpu.VMEM((owners, groups, G, wide), BF),
        ]
        outs.append(jax.ShapeDtypeStruct((groups, G, wide), F32))
    scratch += [pltpu.SemaphoreType.DMA((3, 2 * owners - 1, 10))] * 2
    return scratch, outs


def moe_kernel(
    steps,
    slots,
    chunk,
    m_ref,
    g_ref,
    member_ref,
    router_ref,
    order_ref,
    mine_ref,
    weights_ref,
    moe_ref,
    drow_ref,
    grads_ref,
    grouter_ref,
    router_s,
    gate_s,
    hg_s,
    dpre_s,
    mt_s,
    gt_s,
    gup_s,
    gdn_s,
    gr_s,
):
    step = pl.program_id(0)
    owners, _, share, units = weights_ref.shape
    per = chunk // F

    @pl.when(step == 0)
    def _():
        gup_s[...] = jnp.zeros_like(gup_s)
        gdn_s[...] = jnp.zeros_like(gdn_s)
        gr_s[...] = jnp.zeros_like(gr_s)
        router_s[...] = dot_nn(router_ref[...], order_ref[...]).astype(BF)

    mt_s[...] = m_ref[...].T
    gt_s[...] = g_ref[...].T
    sig = jax.nn.sigmoid(dot_nn(m_ref[...], router_s[...]))
    mask = dot_nn(member_ref[...], mine_ref[...])
    gate_s[...] = sig * mask
    root = math.sqrt(2.0 / math.pi)
    cube = 0.044715
    lane = lax.broadcasted_iota(jnp.int32, (1, F), 1)
    d_gate = jnp.zeros(gate_s.shape, F32)
    for c in range(units // chunk):
        cols = pl.ds(c * chunk, chunk)
        pre_all = dot_nn(m_ref[:, :share], weights_ref[0, 0, :, cols])
        back_all = dot_nn(g_ref[:, :share], weights_ref[0, 1, :, cols])
        for o in range(1, owners):
            part = pl.ds(o * share, share)
            pre_all += dot_nn(m_ref[:, part], weights_ref[o, 0, :, cols])
            back_all += dot_nn(g_ref[:, part], weights_ref[o, 1, :, cols])
        for j in range(per):
            slot = c * per + j
            part = slice(j * F, (j + 1) * F)
            pre = pre_all[:, part]
            back = back_all[:, part]
            square = pre * pre
            th = jnp.tanh(root * pre * (1.0 + cube * square))
            half = 0.5 * (1.0 + th)
            slope = half + (0.5 * root) * pre * (1.0 - th * th) * (1.0 + (3.0 * cube) * square)
            hidden = (pre * half).astype(BF).astype(F32)
            gate = gate_s[:, slot : slot + 1]
            d_one = jnp.sum(hidden * back, axis=1, keepdims=True)
            d_gate = d_gate + d_one * (lane == slot).astype(F32)
            where = pl.ds(slot * F, F)
            hg_s[:, where] = (gate * hidden).astype(BF)
            dpre_s[:, where] = (slope * (gate * back)).astype(BF)
    dlog = (d_gate * mask * sig * (1.0 - sig)).astype(BF)
    gr_s[...] += dot_nn(mt_s[...], dot_nt(dlog, order_ref[...]).astype(BF))
    for o in range(owners):
        where = pl.ds(o * share, share)
        moe_ref[:, where] = dot_nt(hg_s[...], weights_ref[o, 1]).astype(BF)
        drow_ref[:, where] = (
            dot_nt(dpre_s[...], weights_ref[o, 0]) + dot_nt(dlog, router_s[where, :])
        ).astype(BF)
        gup_s[where, :] += dot_nn(mt_s[where, :], dpre_s[...])
        gdn_s[where, :] += dot_nn(gt_s[where, :], hg_s[...])

    @pl.when(step == steps - 1)
    def _():
        for o in range(owners):
            grads_ref[o, 0] = gup_s[pl.ds(o * share, share), :].astype(BF)
            grads_ref[o, 1] = gdn_s[pl.ds(o * share, share), :].astype(BF)
        grouter_ref[...] = gr_s[...].astype(BF)


def moe(rows, cots, member, packed, router_at, order, mine, weights):
    count = rows.shape[0]
    tile = 512
    owners, _, share, units = weights.shape
    slots = units // F
    steps = count // tile
    lanes = member.shape[1]
    row_spec = pl.BlockSpec((tile, D), lambda i: (i, 0))
    whole = pl.BlockSpec(memory_space=pltpu.VMEM)
    router_spec = pl.BlockSpec((D, lanes), lambda i: (0, router_at // lanes))
    return pl.pallas_call(
        functools.partial(moe_kernel, steps, slots, 512),
        grid=(steps,),
        in_specs=[
            row_spec,
            row_spec,
            pl.BlockSpec((tile, lanes), lambda i: (i, 0)),
            router_spec,
            whole,
            whole,
            whole,
        ],
        out_specs=[row_spec, row_spec, whole, whole],
        out_shape=[
            jax.ShapeDtypeStruct((count, D), BF),
            jax.ShapeDtypeStruct((count, D), BF),
            jax.ShapeDtypeStruct(weights.shape, BF),
            jax.ShapeDtypeStruct((D, lanes), BF),
        ],
        scratch_shapes=[
            pltpu.VMEM((D, F), BF),
            pltpu.VMEM((tile, F), F32),
            pltpu.VMEM((tile, units), BF),
            pltpu.VMEM((tile, units), BF),
            pltpu.VMEM((D, tile), BF),
            pltpu.VMEM((D, tile), BF),
            pltpu.VMEM((D, units), F32),
            pltpu.VMEM((D, units), F32),
            pltpu.VMEM((D, lanes), F32),
        ],
        compiler_params=pltpu.CompilerParams(vmem_limit_bytes=60 * 1024 * 1024),
        cost_estimate=pl.CostEstimate(
            flops=12 * count * D * units,
            bytes_accessed=count * D * 8 + D * units * 8,
            transcendentals=count * units,
        ),
    )(rows, cots, member, packed, order, mine, weights)


def fused_kernel(first, owners, slots, wide, tile_cols, *refs):
    if first:
        middle, cots, member, weights, packed, order_ref, mine_ref = refs[:7]
        rows_out, drow_out, moe_out, grads_out, grouter_out = refs[7:12]
        refs = refs[12:]
    else:
        middle, cots, member, weights, packed, order_ref, mine_ref = refs[:7]
        drow_in, moe_in, grouter_in, middle_in = refs[7:11]
        drow_out, layer_out, grads_out, grouter_out = refs[11:15]
        refs = refs[15:]
    (m_s, c_s, b_s, w_s, gup_s, gdn_s, gr_s, hg_s, dpre_s, mt_s, gt_s, router_in, router_s, gate_s) = refs[:14]
    part_d, part_m, local, wsem, tsem = refs[14:19]
    if first:
        gsend, grecv = refs[19:]
    else:
        sib_s, first_s, second_s, ssend, srecv = refs[19:]
    place = Place()
    z = place.z
    count = m_s.shape[0] // 8
    half = count // 2
    lanes = b_s.shape[1]
    share = D // owners
    ins = (middle,)
    bufs = (m_s,)
    sums = (m_s, c_s)
    swap = place.sib - place.e
    mine = (place.e, place.xnb, place.ynb, place.diag)
    if not first:
        mine = (place.diag, place.xnb, place.ynb, place.e)

    def span(e, start=0, size=count):
        return pl.ds(pl.multiple_of(e * count + start, 16), size)

    def remote(sems, a, kind, src, dst, to):
        return pltpu.make_async_remote_copy(
            src_ref=src, dst_ref=dst, send_sem=sems[0].at[a, kind], recv_sem=sems[1].at[a, kind],
            device_id=(z, to), device_id_type=MESH)

    def passing(a, kind):
        buf = bufs[a]
        if kind in (XS, YS, S0):
            src, at = ins[a], span(place.e)
        elif kind == FA:
            at = span(place.xnb, 0, half)
            src = buf.at[at]
        elif kind == FB:
            at = span(place.ynb, half, half)
            src = buf.at[at]
        else:
            at = span(mine[kind - S0])
            src = buf.at[at]
        to = {XS: place.xnb, YS: place.ynb, FA: place.ynb, FB: place.xnb}.get(kind, place.sib)
        return remote((gsend, grecv), a, kind, src, buf.at[at], to)

    def got(a, kind):
        at = {
            XS: lambda: span(place.xnb),
            YS: lambda: span(place.ynb),
            FA: lambda: span(place.diag, 0, half),
            FB: lambda: span(place.diag, half, half),
        }.get(kind, lambda: span(mine[kind - S0] + swap))()
        ref = bufs[a].at[at]
        remote((gsend, grecv), a, kind, ref, ref, place.sib).wait_recv()

    HY0, HY1, HX0, HX1, HX2, HY2 = 4, 5, 6, 7, 8, 9

    def to_sib(a, t):
        return remote((ssend, srecv), a, t, sums[a].at[span(mine[t] + swap)], sib_s.at[a, t], place.sib)

    def hop(a, kind):
        src_e, second, dst, to = {
            HY0: (place.ynb, False, first_s.at[a, 0], place.ynb),
            HY1: (place.diag, False, first_s.at[a, 1], place.ynb),
            HX0: (place.xnb, True, first_s.at[a, 2], place.xnb),
            HX1: (place.diag, True, first_s.at[a, 3], place.xnb),
            HX2: (place.xnb, False, second_s.at[a, 0], place.xnb),
            HY2: (place.ynb, True, second_s.at[a, 1], place.ynb),
        }[kind]
        src = sums[a].at[span(src_e, half if second else 0, half)]
        return remote((ssend, srecv), a, kind, src, dst, to)

    step_rows = 32

    def add(a, e, start, size, terms, keep=None):
        buf = sums[a]

        @pl.loop(0, size // step_rows)
        def _(g):
            here = pl.ds(pl.multiple_of(e * count + start + g * step_rows, 16), step_rows)
            there = pl.ds(pl.multiple_of(g * step_rows, 16), step_rows)
            total = buf[here, :].astype(F32)
            for lead in terms:
                total = total + lead[0][(*lead[1], there, slice(None))].astype(F32)
            if keep is None:
                buf[here, :] = total.astype(BF)
            else:
                own_rows = pl.ds(pl.multiple_of(start + g * step_rows, 16), step_rows)
                if a == 1:
                    total = total + middle_in[own_rows, :]
                keep[own_rows, :] = total.astype(keep.dtype)

    def chip_of(t):
        tx, ty = (t % 2, t // 2) if first else ((3 - t) // 2, (3 - t) % 2)
        chip_x = place.x + tx * (1 - 2 * place.x)
        chip_y = place.y + ty * (1 - 2 * place.y)
        return pl.ds(pl.multiple_of((chip_y * 2 + chip_x) * 2 * count, 16), 2 * count)

    if first:
        own = [
            pltpu.make_async_copy(middle, m_s.at[span(place.e)], local.at[0]),
            pltpu.make_async_copy(cots, c_s, local.at[1]),
        ]
    else:
        own = []
    own.append(pltpu.make_async_copy(member, b_s, local.at[2]))
    for c in own:
        c.start()

    def tile_copies(t):
        at = chip_of(t)
        if first:
            pairs = ((m_s, rows_out), (part_d, drow_out), (part_m, moe_out))
        else:
            pairs = ((middle, m_s), (cots, c_s), (drow_in, part_d), (moe_in, part_m))
        slot = pl.ds(pl.multiple_of((t % 2) * 2 * count, 16), 2 * count)
        return [
            pltpu.make_async_copy(
                src.at[at], dst.at[slot if dst is part_d or dst is part_m else at], tsem.at[t, i]
            )
            for i, (src, dst) in enumerate(pairs)
        ]

    if not first:
        for t in range(4):
            for c in tile_copies(t)[:2]:
                c.start()
    router_copy = pltpu.make_async_copy(packed.at[:, pl.ds(wide, lanes)], router_in, local.at[3])
    router_copy.start()

    @pl.loop(0, slots)
    def _(s):
        for o in range(owners):
            for k in (0, 1):
                pltpu.make_async_copy(
                    weights.at[o, k * slots + s],
                    w_s.at[k, pl.ds(o * share, share), pl.ds(pl.multiple_of(s * F, F), F)],
                    wsem.at[0],
                ).start()

    greet(place, False, owners)
    if first:
        for kind in (XS, YS, S0):
            passing(0, kind).start()
        gr_s[...] = jnp.zeros_like(gr_s)
    else:
        for t in (0, 1):
            for c in tile_copies(t)[2:]:
                c.start()
        gr_s[...] = grouter_in[...]
    gup_s[...] = jnp.zeros_like(gup_s)
    gdn_s[...] = jnp.zeros_like(gdn_s)

    root = math.sqrt(2.0 / math.pi)
    cube = 0.044715
    tile = 2 * count
    units = slots * F
    per = tile_cols // F

    @pl.loop(0, 4)
    def _(t):
        @pl.when(t == 0)
        def _():
            for c in own:
                c.wait()
            router_copy.wait()
            router_s[...] = dot_nn(router_in[...], order_ref[...]).astype(BF)
            if first:
                got(0, S0)
            pltpu.make_async_copy(w_s, w_s, wsem.at[0]).wait()

        if first:

            @pl.when(t == 1)
            def _():
                got(0, XS)
                passing(0, FA).start()
                passing(0, S1).start()
                got(0, YS)
                passing(0, FB).start()
                passing(0, S2).start()
                got(0, S1)

            @pl.when(t == 2)
            def _():
                got(0, FA)
                got(0, FB)
                passing(0, S3).start()
                got(0, S2)

            @pl.when(t == 3)
            def _():
                got(0, S3)

        else:
            for k in range(4):

                @pl.when(t == k)
                def _():
                    for c in tile_copies(k)[:2]:
                        c.wait()

        here = chip_of(t)
        if first:
            tile_copies(t)[0].start()
        mt_s[...] = m_s[here, :].T
        gt_s[...] = c_s[here, :].T
        sig = jax.nn.sigmoid(dot_nn(m_s[here, :], router_s[...]))
        mask = dot_nn(b_s[here, :], mine_ref[...])
        gate_s[...] = sig * mask
        lane = lax.broadcasted_iota(jnp.int32, (1, F), 1)
        d_gate = jnp.zeros(gate_s.shape, F32)
        for c in range(units // tile_cols):
            cols = pl.ds(c * tile_cols, tile_cols)
            pre_all = dot_nn(m_s[here, :], w_s[0, :, cols])
            back_all = dot_nn(c_s[here, :], w_s[1, :, cols])
            for j in range(per):
                slot = c * per + j
                part = slice(j * F, (j + 1) * F)
                pre = pre_all[:, part]
                back = back_all[:, part]
                square = pre * pre
                th = jnp.tanh(root * pre * (1.0 + cube * square))
                halved = 0.5 * (1.0 + th)
                slope = halved + (0.5 * root) * pre * (1.0 - th * th) * (1.0 + (3.0 * cube) * square)
                hidden = (pre * halved).astype(BF).astype(F32)
                gate = gate_s[:, slot : slot + 1]
                d_one = jnp.sum(hidden * back, axis=1, keepdims=True)
                d_gate = d_gate + d_one * (lane == slot).astype(F32)
                where = pl.ds(slot * F, F)
                hg_s[:, where] = (gate * hidden).astype(BF)
                dpre_s[:, where] = (slope * (gate * back)).astype(BF)
        dlog = (d_gate * mask * sig * (1.0 - sig)).astype(BF)
        gr_s[...] += dot_nn(mt_s[...], dot_nt(dlog, order_ref[...]).astype(BF))

        if not first:

            @pl.when(t == 3)
            def _():
                for a in (0, 1):
                    hop(a, HY1).wait_recv()
                    add(a, place.xnb, 0, half, [(first_s, (a, 1))])
                    hop(a, HX2).start()
                    hop(a, HX1).wait_recv()
                    add(a, place.ynb, half, half, [(first_s, (a, 3))])
                    hop(a, HY2).start()

            for k in range(4):

                @pl.when(t == k)
                def _():
                    for c in tile_copies(k)[2:]:
                        c.wait()

        for a, (kept, dst) in enumerate(((part_d, m_s), (part_m, c_s))):
            for n in range(D // 256):
                where = pl.ds(n * 256, 256)
                if a == 0:
                    total = dot_nt(dpre_s[...], w_s[0, where, :]) + dot_nt(dlog, router_s[where, :])
                else:
                    total = dot_nt(hg_s[...], w_s[1, where, :])
                if first:
                    kept[here, where] = total.astype(BF)
                else:
                    there = pl.ds(pl.multiple_of((t % 2) * tile, 16), tile)
                    dst[here, where] = (total + kept[there, where].astype(F32)).astype(BF)
            if first:
                tile_copies(t)[1 + a].start()
            else:
                for k in range(4):

                    @pl.when(t == k)
                    def _():
                        to_sib(a, k).start()
                        if k < 2:
                            tile_copies(k + 2)[2 + a].start()

        def last(a):
            if first:
                return

            for k, kinds in enumerate(((HY1, HX1), (HX0,), (HY0,), ())):

                @pl.when(t == k)
                def _():
                    to_sib(a, k).wait_recv()
                    add(a, mine[k], 0, count, [(sib_s, (a, k))])
                    for kind in kinds:
                        hop(a, kind).start()

        last(0)
        for n in range(D // 256):
            where = pl.ds(n * 256, 256)
            gup_s[where, :] += dot_nn(mt_s[where, :], dpre_s[...])
        last(1)
        for n in range(D // 256):
            where = pl.ds(n * 256, 256)
            gdn_s[where, :] += dot_nn(gt_s[where, :], hg_s[...])

    w_s[0] = gup_s[...].astype(BF)
    w_s[1] = gdn_s[...].astype(BF)

    @pl.loop(0, slots)
    def _(s):
        for o in range(owners):
            for k in (0, 1):
                pltpu.make_async_copy(
                    w_s.at[k, pl.ds(o * share, share), pl.ds(pl.multiple_of(s * F, F), F)],
                    grads_out.at[o, k * slots + s],
                    wsem.at[0],
                ).start()

    grouter_out[...] = gr_s[...].astype(grouter_out.dtype)
    if first:
        for kind in range(8):
            passing(0, kind).wait_send()
        for t in range(4):
            for c in tile_copies(t):
                c.wait()
    else:
        for a, out in ((0, drow_out), (1, layer_out)):
            hop(a, HY0).wait_recv()
            hop(a, HX2).wait_recv()
            add(a, place.e, 0, half, [(first_s, (a, 0)), (second_s, (a, 0))], out)
            hop(a, HX0).wait_recv()
            hop(a, HY2).wait_recv()
            add(a, place.e, half, half, [(first_s, (a, 2)), (second_s, (a, 1))], out)
        for a in (0, 1):
            for t in range(4):
                to_sib(a, t).wait_send()
            for kind in (HY0, HY1, HX0, HX1, HX2, HY2):
                hop(a, kind).wait_send()
    pltpu.make_async_copy(w_s, w_s, wsem.at[0]).wait()


def fused_experts(first, rows, cots, member, weights, packed, wide, order, mine, more, cid):
    owners = weights.shape[0]
    slots = weights.shape[1] // 2
    total = cots.shape[0]
    count = total // 8
    lanes = member.shape[1]
    units = slots * F
    tile = 2 * count
    hbm = pl.BlockSpec(memory_space=pl.ANY)
    vmem = pl.BlockSpec(memory_space=pltpu.VMEM)
    dma = pltpu.SemaphoreType.DMA
    shape = jax.ShapeDtypeStruct
    scratch = [
        pltpu.VMEM((total, D), BF),
        pltpu.VMEM((total, D), BF),
        pltpu.VMEM((total, lanes), BF),
        pltpu.VMEM((2, D, units), BF),
        pltpu.VMEM((D, units), F32),
        pltpu.VMEM((D, units), F32),
        pltpu.VMEM((D, lanes), F32),
        pltpu.VMEM((tile, units), BF),
        pltpu.VMEM((tile, units), BF),
        pltpu.VMEM((D, tile), BF),
        pltpu.VMEM((D, tile), BF),
        pltpu.VMEM((D, lanes), BF),
        pltpu.VMEM((D, F), BF),
        pltpu.VMEM((tile, F), F32),
        pltpu.VMEM((total if first else 2 * tile, D), BF),
        pltpu.VMEM((total if first else 2 * tile, D), BF),
        dma((4,)),
        dma((1,)),
        dma((4, 4)),
    ]
    if first:
        out_specs = [hbm, hbm, hbm, hbm, vmem]
        out_shape = [shape((total, D), BF)] * 3
        out_shape += [shape(weights.shape, BF), shape((D, lanes), F32)]
        in_specs = [hbm] * 5 + [vmem] * 2
        scratch += [dma((1, 8)), dma((1, 8))]
    else:
        out_specs = [vmem, vmem, hbm, vmem]
        out_shape = [shape((count, D), F32), shape((count, D), BF)]
        out_shape += [shape(weights.shape, BF), shape((D, lanes), BF)]
        in_specs = [hbm] * 5 + [vmem] * 2 + [hbm, hbm, vmem, vmem]
        scratch += [
            pltpu.VMEM((2, 4, count, D), BF),
            pltpu.VMEM((2, 4, count // 2, D), BF),
            pltpu.VMEM((2, 2, count // 2, D), BF),
            dma((2, 10)),
            dma((2, 10)),
        ]
    return pl.pallas_call(
        functools.partial(fused_kernel, first, owners, slots, wide, 256),
        in_specs=in_specs,
        out_specs=out_specs,
        out_shape=out_shape,
        scratch_shapes=scratch,
        compiler_params=pltpu.CompilerParams(
            collective_id=cid, has_side_effects=True, vmem_limit_bytes=64 * 1024 * 1024 - 65536
        ),
        cost_estimate=pl.CostEstimate(
            flops=12 * total * D * units,
            bytes_accessed=D * units * 8 + total * D * 8,
            transcendentals=total * units,
        ),
    )(rows, cots, member, weights, packed, order, mine, *more)


def forward_kernel(
    wide,
    lanes,
    lengths_ref,
    x_ref,
    choice_ref,
    packed_ref,
    heads_all_ref,
    qk_ref,
    vals_ref,
    sig_ref,
    mask_ref,
    vlow_ref,
    prob_ref,
    attended_ref,
    mixed_ref,
    middle_ref,
    mlow_ref,
    w_ref,
    heads_ref,
    wsem,
):
    cuts = (pl.ds(wide + lanes, 128), pl.ds(0, QK), pl.ds(QK, VAL))
    coming = [
        pltpu.make_async_copy(packed_ref.at[:, c], w_ref.at[:, c], wsem.at[i])
        for i, c in enumerate(cuts)
    ]
    coming.append(pltpu.make_async_copy(heads_all_ref, heads_ref, wsem.at[3]))
    for c in coming:
        c.start()
    count = x_ref.shape[0]
    seq = count // MB
    xf = x_ref[...].astype(F32)
    centred = xf - jnp.mean(xf, axis=1, keepdims=True)
    variance = jnp.mean(centred * centred, axis=1, keepdims=True)
    coming[0].wait()
    gain_row = w_ref[:, pl.ds(wide + lanes, 128)].astype(F32).T[SEL : SEL + 1, :]
    normed = (centred * lax.rsqrt(variance + epsilon) * gain_row).astype(BF)
    coming[1].wait()
    for n in range(QK // 512):
        cols = pl.ds(n * 512, 512)
        qk_ref[:, cols] = dot_nn(normed, w_ref[:, cols]).astype(BF)
    sig = jax.nn.sigmoid(dot_nn(x_ref[...], w_ref[:, pl.ds(wide + lanes, 128)]))
    row = lax.broadcasted_iota(jnp.int32, (count, 128), 0)
    lane = lax.broadcasted_iota(jnp.int32, (count, 128), 1)
    live = (row < lengths_ref[0, 0]).astype(F32)
    for b in range(1, MB):
        live = jnp.where(row < b * seq, live, (row < b * seq + lengths_ref[b, 0]).astype(F32))
    mask = jnp.zeros((count, 128), F32)
    top = choice_ref.shape[1] // H
    for v in range(H * top):
        picked = choice_ref[:, v : v + 1] + NV * (v // top)
        mask = mask + (picked == lane).astype(F32) + (picked + H * NV == lane).astype(F32) * live
    sig_ref[...] = sig
    mask_ref[...] = mask
    gates = sig * mask
    coming[2].wait()
    for h in range(H):
        vals = dot_nn(x_ref[...], w_ref[:, pl.ds(QK + h * NV * HD, NV * HD)])
        vals_ref[:, pl.ds(h * NV * HD, NV * HD)] = vals.astype(BF)
        total = gates[:, h * NV : h * NV + 1] * vals[:, :HD]
        for e in range(1, NV):
            at = h * NV + e
            total = total + gates[:, at : at + 1] * vals[:, e * HD : (e + 1) * HD]
        vlow_ref[:, pl.ds(h * HD, HD)] = total.astype(BF)
    at_i = lax.broadcasted_iota(jnp.int32, (seq, seq), 0)
    at_j = lax.broadcasted_iota(jnp.int32, (seq, seq), 1)
    for b in range(MB):
        allowed = (at_j <= at_i) & (at_j < lengths_ref[b, 0])
        here = pl.ds(b * seq, seq)
        for h in range(H):
            queries = qk_ref[here, pl.ds(h * HD, HD)]
            keys_all = qk_ref[here, pl.ds((H + h) * HD, HD)]
            scores = jnp.where(allowed, dot_nt(queries, keys_all) * HD ** (-0.5), -1e30)
            expo = jnp.exp(scores - jnp.max(scores, axis=1, keepdims=True))
            prob = expo / jnp.sum(expo, axis=1, keepdims=True)
            prob_ref[b * H + h] = prob
            attended_ref[here, pl.ds(h * HD, HD)] = dot_nn(
                prob.astype(BF), vlow_ref[here, pl.ds(h * HD, HD)]
            )
    for h in range(H):
        attended = attended_ref[:, pl.ds(h * HD, HD)]
        for e in range(NV):
            at = h * NV + e
            gate = gates[:, H * NV + at : H * NV + at + 1]
            mixed_ref[:, pl.ds(at * HD, HD)] = (gate * attended).astype(BF)
    coming[3].wait()
    for n in range(D // 512):
        cols = pl.ds(n * 512, 512)
        middle = x_ref[:, cols].astype(F32) + dot_nn(mixed_ref[...], heads_ref[:, cols])
        middle_ref[:, cols] = middle
        mlow_ref[:, cols] = middle.astype(BF)


def forward(lengths, tokens, choice, packed, heads, wide, lanes):
    count = tokens.shape[0]
    seq = count // MB
    vmem = pl.BlockSpec(memory_space=pltpu.VMEM)
    shape = jax.ShapeDtypeStruct
    return pl.pallas_call(
        functools.partial(forward_kernel, wide, lanes),
        in_specs=[pl.BlockSpec(memory_space=pltpu.SMEM)]
        + [vmem] * 2
        + [pl.BlockSpec(memory_space=pl.ANY)] * 2,
        out_specs=[vmem] * 10,
        scratch_shapes=[
            pltpu.VMEM(packed.shape, BF),
            pltpu.VMEM(heads.shape, BF),
            pltpu.SemaphoreType.DMA((4,)),
        ],
        out_shape=[
            shape((count, QK), BF),
            shape((count, VAL), BF),
            shape((count, 128), F32),
            shape((count, 128), F32),
            shape((count, H * HD), BF),
            shape((MB * H, seq, seq), F32),
            shape((count, H * HD), F32),
            shape((count, VAL), BF),
            shape((count, D), F32),
            shape((count, D), BF),
        ],
        compiler_params=pltpu.CompilerParams(vmem_limit_bytes=56 * 1024 * 1024),
        cost_estimate=pl.CostEstimate(
            flops=2 * count * D * (wide + VAL),
            bytes_accessed=(wide + VAL) * D * 2 + count * D * 20,
            transcendentals=count * seq * H,
        ),
    )(lengths, tokens, choice, packed, heads)


def backward_kernel(wide, lanes, steps, *refs):
    (
        x_ref,
        cots_ref,
        drow_ref,
        qk_ref,
        vals_ref,
        sig_ref,
        mask_ref,
        vlow_ref,
        prob_ref,
        attended_ref,
        mixed_ref,
        grouter_ref,
        packed_ref,
        heads_all_ref,
        _,
        dx_ref,
    ) = refs[:16]
    dvals_s, dqk_s, w_ref, heads_ref, wsem = refs[16:21]
    put_w, put_h, event = steps(refs[21:])
    coming = [
        pltpu.make_async_copy(src, dst, wsem.at[i])
        for i, (src, dst) in enumerate(((heads_all_ref, heads_ref), (packed_ref, w_ref)))
    ]
    for c in coming:
        c.start()
    count = x_ref.shape[0]
    seq = count // MB
    d_branch = (cots_ref[...].astype(F32) + drow_ref[...]).astype(BF)
    width = NV * HD
    for h in range(H):
        where = pl.ds(h * width, width)
        put_h(h, dot_tn(mixed_ref[:, where], d_branch).astype(BF))
    event("heads")
    for c in coming:
        c.wait()
    mask = mask_ref[...]
    sig = sig_ref[...]
    gates = sig * mask
    lane = lax.broadcasted_iota(jnp.int32, (1, 128), 1)
    d_gates = jnp.zeros((count, 128), F32)
    for h in range(H):
        where = pl.ds(h * width, width)
        d_mixed = dot_nt(d_branch, heads_ref[where, :])
        attended = attended_ref[:, pl.ds(h * HD, HD)]
        total = jnp.zeros((count, HD), F32)
        for e in range(NV):
            at = H * NV + h * NV + e
            part = d_mixed[:, e * HD : (e + 1) * HD]
            total = total + gates[:, at : at + 1] * part
            d_one = jnp.sum(part * attended, axis=1, keepdims=True)
            d_gates = d_gates + d_one * (lane == at).astype(F32)
        d_attended = total.astype(BF)
        d_values = []
        for b in range(MB):
            here = pl.ds(b * seq, seq)
            rows = slice(b * seq, (b + 1) * seq)
            prob = prob_ref[b * H + h]
            values = vlow_ref[here, pl.ds(h * HD, HD)]
            d_prob = dot_nt(d_attended[rows], values)
            d_scores = (
                prob * (d_prob - jnp.sum(prob * d_prob, axis=1, keepdims=True))
            ).astype(BF)
            d_values.append(dot_tn(prob.astype(BF), d_attended[rows]).astype(BF).astype(F32))
            queries = qk_ref[here, pl.ds(h * HD, HD)]
            keys_all = qk_ref[here, pl.ds((H + h) * HD, HD)]
            dqk_s[here, pl.ds(h * HD, HD)] = (dot_nn(d_scores, keys_all) * HD ** (-0.5)).astype(BF)
            dqk_s[here, pl.ds((H + h) * HD, HD)] = (
                dot_tn(d_scores, queries) * HD ** (-0.5)
            ).astype(BF)
        d_value = jnp.concatenate(d_values, axis=0)
        for e in range(NV):
            at = h * NV + e
            cols = pl.ds(at * HD, HD)
            d_one = jnp.sum(d_value * vals_ref[:, cols].astype(F32), axis=1, keepdims=True)
            d_gates = d_gates + d_one * (lane == at).astype(F32)
            dvals_s[:, cols] = (gates[:, at : at + 1] * d_value).astype(BF)
        event(h)
    d_select = (d_gates * mask * sig * (1.0 - sig)).astype(BF)
    x_t = x_ref[...].T
    for n in range(VAL // 512):
        put_w(QK + n * 512, dot_nn(x_t, dvals_s[:, pl.ds(n * 512, 512)]).astype(BF))
    event("values")
    xf = x_ref[...].astype(F32)
    centred = xf - jnp.mean(xf, axis=1, keepdims=True)
    variance = jnp.mean(centred * centred, axis=1, keepdims=True)
    rstd = lax.rsqrt(variance + epsilon)
    unit = centred * rstd
    gain_row = w_ref[:, pl.ds(wide + lanes, 128)].astype(F32).T[SEL : SEL + 1, :]
    normed_t = (unit * gain_row).astype(BF).T
    for n in range(QK // 512):
        put_w(n * 512, dot_nn(normed_t, dqk_s[:, pl.ds(n * 512, 512)]).astype(BF))
    d_normed = dot_nt(dqk_s[...], w_ref[:, pl.ds(0, QK)])
    grad_gain = jnp.sum(d_normed * unit, axis=0, keepdims=True)
    small = dot_tn(d_select, x_ref[...])
    which = lax.broadcasted_iota(jnp.int32, (128, 1), 0)
    put_w(wide + lanes, jnp.where(which == SEL, grad_gain, small).T.astype(BF))
    put_w(wide, grouter_ref[...])
    event("rest")
    scaled = d_normed * gain_row
    dx_ref[...] = (
        cots_ref[...].astype(F32)
        + drow_ref[...]
        + (
            scaled
            - jnp.mean(scaled, axis=1, keepdims=True)
            - unit * jnp.mean(scaled * unit, axis=1, keepdims=True)
        )
        * rstd
    )
    for n in range(D // 256):
        rows = pl.ds(n * 256, 256)
        dx_ref[:, rows] += dot_nt(dvals_s[...], w_ref[rows, pl.ds(QK, VAL)]) + dot_nt(
            d_select, w_ref[rows, pl.ds(wide + lanes, 128)]
        )
    event("end")


def plain_steps(wide, refs):
    gw_ref, gheads_ref = refs

    def put_w(start, value):
        gw_ref[:, pl.ds(start, value.shape[1])] = value

    def put_h(h, value):
        gheads_ref[pl.ds(h * value.shape[0], value.shape[0]), :] = value

    def nothing(*_):
        pass

    return put_w, put_h, nothing


def backward(tokens, cots, drow, saved, grouter, packed, heads, ahead, wide, lanes, owners, cid):
    count = tokens.shape[0]
    vmem = pl.BlockSpec(memory_space=pltpu.VMEM)
    shape = jax.ShapeDtypeStruct
    scratch = [
        pltpu.VMEM((count, VAL), BF),
        pltpu.VMEM((count, QK), BF),
        pltpu.VMEM(packed.shape, BF),
        pltpu.VMEM(heads.shape, BF),
        pltpu.SemaphoreType.DMA((2,)),
    ]
    grads = (packed.shape, heads.shape)
    summed = ((D, VAL), heads.shape, (D, packed.shape[1] - VAL))
    if cid is None:
        kernel = lambda *refs: backward_kernel(
            wide, lanes, functools.partial(plain_steps, wide), *refs[:16], *refs[18:23], *refs[16:18]
        )
        out_shape = [shape((count, D), F32)] + [shape(g, BF) for g in grads]
        more = {}
    else:
        kernel = lambda *refs: backward_kernel(
            wide,
            lanes,
            functools.partial(summing_steps, owners),
            *refs[:16],
            *refs[19:24],
            *refs[16:19],
            *refs[24:],
        )
        more_scratch, sums = scatter_space(summed, owners)
        scratch += more_scratch
        out_shape = [shape((count, D), F32)] + sums
        more = dict(collective_id=cid, has_side_effects=True)
    return pl.pallas_call(
        kernel,
        in_specs=[vmem] * 12 + [pl.BlockSpec(memory_space=pl.ANY)] * 3,
        out_specs=[vmem] * len(out_shape),
        out_shape=out_shape,
        scratch_shapes=scratch,
        compiler_params=pltpu.CompilerParams(vmem_limit_bytes=64 * 1024 * 1024 - 65536, **more),
        cost_estimate=pl.CostEstimate(
            flops=4 * count * D * (wide + VAL),
            bytes_accessed=(wide + VAL) * D * 4 + count * D * 30,
            transcendentals=0,
        ),
    )(tokens, cots, drow, *saved, grouter, packed, heads, ahead)


def update_kernel(lanes, rates, values_ref, heads_sum_ref, rest_ref, first_ref, second_ref, *refs):
    results, ins = refs[:2], refs[2:23]
    kept, outs = refs[23:25], refs[25:]
    for src, dst in zip(results, kept):
        dst[...] = src[...]

    def step(i, at, gradient):
        new = update_weight(*(ref[at] for ref in ins[3 * i : 3 * i + 3]), gradient, rates[i])
        for ref, value in zip(outs[4 * i : 4 * i + 4], new):
            ref[at] = value

    everything = (slice(None), slice(None))
    step(0, (slice(None), pl.ds(0, QK)), rest_ref[:, pl.ds(0, QK)])
    step(0, (slice(None), pl.ds(QK, VAL)), values_ref[...])
    step(1, everything, rest_ref[:, pl.ds(QK + lanes, SEL)])
    step(2, everything, rest_ref[:, pl.ds(QK, ins[6].shape[1])])
    step(3, everything, heads_sum_ref[...])
    which = (lax.broadcasted_iota(jnp.int32, (8, 128), 1) == SEL).astype(F32)
    gain_rows = lax.dot_general(
        which,
        rest_ref[:, pl.ds(QK + lanes, 128)],
        (((1,), (1,)), ((), ())),
        precision=lax.Precision.HIGHEST,
        preferred_element_type=F32,
    )
    step(6, everything, gain_rows[:1, :])
    start = 0
    for ref in (first_ref, second_ref):
        part = ref.shape[0] // 2

        @pl.loop(0, part)
        def _(s):
            for k in (0, 1):
                step(4 + k, start + s, ref[k * part + s].astype(F32))

        start += part


def update_all(sums, sums_a, sums_b, results, weights, rates, lanes):
    vmem = pl.BlockSpec(memory_space=pltpu.VMEM)
    shapes = [jax.ShapeDtypeStruct(a.shape, a.dtype) for a in results]
    for i in range(7):
        shapes += [jax.ShapeDtypeStruct(weights[3 * i].shape, t) for t in (F32, F32, F32, BF)]
    return pl.pallas_call(
        functools.partial(update_kernel, lanes, rates),
        in_specs=[vmem] * 28,
        out_specs=[vmem] * 30,
        out_shape=shapes,
        compiler_params=pltpu.CompilerParams(vmem_limit_bytes=60 * 1024 * 1024),
    )(*sums, sums_a, sums_b, *results, *weights)


def body(
    tokens,
    cotangent,
    lengths,
    routes,
    head_choice,
    placement,
    gain_master,
    gain_moment,
    gain_average,
    qkv_master,
    qkv_moment,
    qkv_average,
    select_master,
    select_moment,
    select_average,
    router_master,
    router_moment,
    router_average,
    heads_out_master,
    heads_out_moment,
    heads_out_average,
    up_master,
    up_moment,
    up_average,
    down_master,
    down_moment,
    down_average,
):
    both = ("dp", "expert")
    owners = lax.axis_size("dp")
    group = lax.axis_size("expert")
    own_kernels = group == 8
    experts = placement.shape[0]
    slots = up_master.shape[0]
    units = slots * F
    seq = tokens.shape[1]
    count = MB * seq
    share = up_master.shape[1]
    mine = lax.axis_index("expert")
    lanes = -(-experts // 128) * 128

    own_rows = qkv_master.shape[0]
    wide = QK + VAL
    packed = jnp.concatenate(
        [
            qkv_master.astype(BF),
            router_master.astype(BF),
            jnp.zeros((own_rows, lanes - experts), BF),
            select_master.astype(BF),
            gain_master.astype(BF)[:, None],
            jnp.zeros((own_rows, 127 - SEL), BF),
        ],
        axis=1,
    )
    heads_low = heads_out_master.astype(BF)

    part = slots // 2

    def fetch(own):
        low = jnp.concatenate([up_master[own].astype(BF), down_master[own].astype(BF)], axis=0)
        return lax.all_gather(low, "dp", axis=0, tiled=False)

    weights = (fetch(slice(0, part)), fetch(slice(part, slots)))

    flat_tokens = tokens.reshape(count, D)
    flat_cots = cotangent.reshape(count, D)
    live = (jnp.arange(seq, dtype=jnp.int32)[None, :] < lengths).astype(F32).reshape(count)
    lane_ids = jnp.arange(lanes, dtype=jnp.int32)
    named = jnp.sum(
        (routes.reshape(count, TOPK)[..., None] == lane_ids).astype(F32), axis=1
    ) * live[:, None]
    padded = jnp.pad(placement, (0, lanes - experts), constant_values=-1)
    perm = (padded[:, None] == lane_ids[None, :]).astype(BF)
    member = dot_nn(named.astype(BF), perm).astype(BF)
    own_lane = jnp.arange(F, dtype=jnp.int32)[None, :]

    def selects(start, number):
        slot = mine * slots + start
        inside = own_lane < number
        return (
            (((padded[:, None] - slot) == own_lane) & inside & (padded[:, None] >= 0)).astype(BF),
            (((lane_ids[:, None] - slot) == own_lane) & inside).astype(BF),
        )

    if own_kernels:
        packed_all, heads, cots_all, member_all = gather(
            (packed, heads_low, flat_cots, member),
            (True, True, False, False),
            (own_rows // 2, 48, count // 2, count // 2),
            owners,
            group,
            0,
        )
    else:
        packed_all = lax.all_gather(packed, both, axis=0, tiled=True)
        heads = lax.all_gather(heads_low, both, axis=0, tiled=True)
        cots_all, member_all = (
            lax.all_gather(a, "expert", axis=0, tiled=True) for a in (flat_cots, member)
        )
    choice = head_choice.reshape(count, -1)
    *saved, middle, middle_low = forward(lengths, flat_tokens, choice, packed_all, heads, wide, lanes)
    if own_kernels:
        rows_all, drow_part, moe_part, grads_a, router_part = fused_experts(
            True, middle_low, cots_all, member_all, weights[0], packed_all, wide, *selects(0, part), (), 1
        )
        d_from_rows, mixed, grads_b, grad_router = fused_experts(
            False,
            rows_all,
            cots_all,
            member_all,
            weights[1],
            packed_all,
            wide,
            *selects(part, slots - part),
            (drow_part, moe_part, router_part, middle),
            2,
        )
    else:
        rows_all = lax.all_gather(middle_low, "expert", axis=0, tiled=True)
        side = jnp.concatenate([w.reshape(owners, 2, -1, share, F) for w in weights], axis=2)
        side = side.transpose(0, 1, 3, 2, 4)
        moe_part, drow_part, expert_grads, grad_router = moe(
            rows_all,
            cots_all,
            member_all,
            packed_all,
            wide,
            *selects(0, slots),
            side.reshape(owners, 2, share, units),
        )
        expert_grads = expert_grads.reshape(owners, 2, share, slots, F).transpose(0, 1, 3, 2, 4)
        grads_a, grads_b = expert_grads[:, :, :part], expert_grads[:, :, part:]
        d_from_rows, moe_sum = (
            lax.psum_scatter(a, "expert", scatter_dimension=0, tiled=True).astype(F32)
            for a in (drow_part, moe_part)
        )
        mixed = (middle + moe_sum).astype(BF)
    sums_a, sums_b = (
        lax.psum_scatter(
            g.reshape(-1, share, F), "dp", scatter_dimension=0, tiled=True
        )
        for g in (grads_a, grads_b)
    )
    d_tokens, *grads = backward(
        flat_tokens,
        flat_cots,
        d_from_rows,
        saved,
        grad_router,
        packed_all,
        heads,
        sums_a,
        wide,
        lanes,
        owners,
        3 if own_kernels else None,
    )
    if own_kernels:
        sums = tuple(total.reshape(-1, total.shape[2]) for total in grads)
    else:
        packed_sum, heads_sum = (
            lax.psum_scatter(g, both, scatter_dimension=0, tiled=True).astype(F32) for g in grads
        )
        rest_sum = jnp.concatenate([packed_sum[:, :QK], packed_sum[:, wide:]], axis=1)
        sums = (packed_sum[:, QK:wide], heads_sum, rest_sum)
    rates = step_rates(count * owners * group, experts)
    gain = tuple(a[None] for a in (gain_master, gain_moment, gain_average))
    mixed, d_tokens, *new = update_all(
        sums,
        sums_a,
        sums_b,
        (mixed, d_tokens),
        (
            qkv_master,
            qkv_moment,
            qkv_average,
            select_master,
            select_moment,
            select_average,
            router_master,
            router_moment,
            router_average,
            heads_out_master,
            heads_out_moment,
            heads_out_average,
            up_master,
            up_moment,
            up_average,
            down_master,
            down_moment,
            down_average,
            *gain,
        ),
        rates[1:] + rates[:1],
        lanes,
    )
    gain_new = tuple(a.reshape(gain_master.shape) for a in new[24:])
    return (mixed.reshape(tokens.shape), d_tokens.reshape(tokens.shape), *gain_new, *new[:24])


def solution(mesh):
    rows = P(None, ("dp", "expert"), None)
    flat = P(("dp", "expert"))
    dense = P(("dp", "expert"), None)
    expert = P("expert", "dp", None)
    in_specs = (
        rows,
        rows,
        P(None, ("dp", "expert")),
        rows,
        P(None, ("dp", "expert"), None, None),
        P(),
        *((flat,) * 3),
        *((dense,) * 12),
        *((expert,) * 6),
    )
    out_specs = (rows, rows, *((flat,) * 4), *((dense,) * 16), *((expert,) * 8))
    return jax.shard_map(body, mesh=mesh, in_specs=in_specs, out_specs=out_specs, check_vma=False)
```

```python
import functools
import math

import jax
import jax.numpy as jnp
from jax import lax
from jax.experimental import pallas as pl
from jax.experimental.pallas import tpu as pltpu
from jax.sharding import PartitionSpec as P

D = 1024
H = 4
HD = 128
NV = 5
F = 128
TOPK = 16
MB = 2
QK = 2 * H * HD
VAL = H * NV * HD
SEL = 2 * H * NV

momentum_decay = 0.9
average_decay = 0.5
rate_factor = 0.4
epsilon = 1e-05
BF = jnp.bfloat16
F32 = jnp.float32


def step_rates(total_tokens, experts):
    root_tokens = math.sqrt(total_tokens)
    expert_share = math.sqrt(TOPK / experts)
    spread_list = (
        0.3,
        D ** (-0.5),
        (2 * D) ** (-0.5),
        (9 * D) ** (-0.5),
        0.5,
        D ** (-0.5),
        (4 * F) ** (-0.5),
    )
    gradient_list = (1.0, 1.0, 3.0, 2.0 * expert_share, 0.1, 0.5 * expert_share, 0.4 * expert_share)
    return tuple(
        rate_factor * spread_value / (gradient_value * root_tokens)
        for spread_value, gradient_value in zip(spread_list, gradient_list)
    )


def update_weight(master, moment, average, gradient, step_size):
    new_moment = momentum_decay * moment + gradient
    new_weight = master - step_size * (gradient + momentum_decay * new_moment)
    new_average = average_decay * average + (1.0 - average_decay) * new_weight
    return (new_moment, new_average, new_weight, new_weight.astype(BF))


def dot_nt(a, b):
    return lax.dot_general(a, b, (((1,), (1,)), ((), ())), preferred_element_type=F32)


def dot_tn(a, b):
    return lax.dot_general(a, b, (((0,), (0,)), ((), ())), preferred_element_type=F32)


def dot_nn(a, b):
    return jnp.dot(a, b, preferred_element_type=F32)


MESH = pl.DeviceIdType.MESH


class Place:
    def __init__(self):
        self.z = lax.axis_index("dp")
        self.e = lax.axis_index("expert")
        core = self.e % 2
        x = (self.e // 2) % 2
        y = self.e // 4
        self.sib = self.e + 1 - 2 * core
        self.xnb = self.e + 2 - 4 * x
        self.ynb = self.e + 4 - 8 * y
        self.diag = self.xnb + 4 - 8 * y
        self.core, self.x, self.y = core, x, y


def greet(place, line, owners):
    barrier = pltpu.get_barrier_semaphore()
    z = place.z
    for e in (place.sib, place.xnb, place.ynb):
        pl.semaphore_signal(barrier, inc=1, device_id=(z, e), device_id_type=MESH)
    peers = 3
    if line:

        @pl.when(z > 0)
        def _():
            pl.semaphore_signal(barrier, inc=1, device_id=(z - 1, place.e), device_id_type=MESH)

        @pl.when(z < owners - 1)
        def _():
            pl.semaphore_signal(barrier, inc=1, device_id=(z + 1, place.e), device_id_type=MESH)

        peers = peers + (z + owners - 1) // owners + (2 * owners - 2 - z) // owners
    pl.semaphore_wait(barrier, peers)


XS, YS, FA, FB, S0, S1, S2, S3, UP, DOWN = range(10)

def gather_kernel(owners, group, lines, halves, *refs):
    n = len(lines)
    ins, outs, (send, recv, own) = refs[:n], refs[n : 2 * n], refs[2 * n :]
    place = Place()
    z = place.z
    copies_own = []
    for i in range(n):
        rows = ins[i].shape[0]
        slot = (z * group + place.e) if lines[i] else place.e
        cp = pltpu.make_async_copy(ins[i], outs[i].at[pl.ds(slot * rows, rows)], own.at[i])
        cp.start()
        copies_own.append(cp)
    greet(place, any(lines), owners)

    def block(i, rel, e, part=None):
        rows = ins[i].shape[0]
        slot = ((z + rel) * group + e) if lines[i] else e
        start, size = (0, rows) if part is None else part
        return outs[i].at[pl.ds(slot * rows + start, size)]

    def source(i, rel, part=None):
        if rel == 0:
            return ins[i] if part is None else ins[i].at[pl.ds(*part)]
        return block(i, rel, place.e, part)

    def sem(rel):
        return rel + owners - 1

    def go(i, rel, kind, src, dst, to_e, dz=0):
        return pltpu.make_async_remote_copy(
            src_ref=src, dst_ref=dst, send_sem=send.at[i, sem(rel), kind],
            recv_sem=recv.at[i, sem(rel - dz), min(kind, UP)],
            device_id=(z + dz, to_e), device_id_type=MESH)

    def parts(i):
        rows = ins[i].shape[0]
        return (0, halves[i]), (halves[i], rows - halves[i])

    def valid(rel):
        return (z + rel >= 0) & (z + rel < owners)

    def copies(i, rel):
        first, second = parts(i)
        e, xn, yn, dg, sb = place.e, place.xnb, place.ynb, place.diag, place.sib
        return {
            XS: lambda: go(i, rel, XS, source(i, rel), block(i, rel, e), xn),
            YS: lambda: go(i, rel, YS, source(i, rel), block(i, rel, e), yn),
            FA: lambda: go(i, rel, FA, block(i, rel, xn, first), block(i, rel, xn, first), yn),
            FB: lambda: go(i, rel, FB, block(i, rel, yn, second), block(i, rel, yn, second), xn),
            S0: lambda: go(i, rel, S0, source(i, rel), block(i, rel, e), sb),
            S1: lambda: go(i, rel, S1, block(i, rel, xn), block(i, rel, xn), sb),
            S2: lambda: go(i, rel, S2, block(i, rel, yn), block(i, rel, yn), sb),
            S3: lambda: go(i, rel, S3, block(i, rel, dg), block(i, rel, dg), sb),
        }

    def got(i, rel, kind, e, part=None):
        ref = block(i, rel, e, part)
        pltpu.make_async_remote_copy(
            src_ref=ref, dst_ref=ref, send_sem=send.at[i, sem(rel), min(kind, UP)], recv_sem=recv.at[i, sem(rel), min(kind, UP)],
            device_id=(z, place.sib), device_id_type=MESH).wait_recv()

    def stage_z(rel):
        @pl.when(valid(rel))
        def _():
            for i in range(n):
                if rel != 0 and not lines[i]:
                    continue
                if rel != 0:
                    got(i, rel, UP, place.e)
                if lines[i] and rel <= 0 and rel > 1 - owners:
                    @pl.when(z < owners - 1)
                    def _():
                        go(i, rel, UP, source(i, rel), block(i, rel, place.e), place.e, 1).start()
                if lines[i] and rel >= 0 and rel < owners - 1:
                    @pl.when(z > 0)
                    def _():
                        go(i, rel, DOWN, source(i, rel), block(i, rel, place.e), place.e, -1).start()
                c = copies(i, rel)
                c[XS]().start()
                c[YS]().start()
                c[S0]().start()

    def each(rel, fn):
        @pl.when(valid(rel))
        def _():
            for i in range(n):
                if rel == 0 or lines[i]:
                    fn(i, rel, copies(i, rel))

    def xy(i, rel, c):
        got(i, rel, XS, place.xnb)
        c[FA]().start()
        c[S1]().start()
        got(i, rel, YS, place.ynb)
        c[FB]().start()
        c[S2]().start()

    def dg(i, rel, c):
        first, second = parts(i)
        got(i, rel, FA, place.diag, first)
        got(i, rel, FB, place.diag, second)
        c[S3]().start()

    def end(i, rel, c):
        for k, e in ((S0, place.sib),):
            got(i, rel, S0, place.sib)
        got(i, rel, S1, place.xnb + place.sib - place.e)
        got(i, rel, S2, place.ynb + place.sib - place.e)
        got(i, rel, S3, place.diag + place.sib - place.e)
        for k in (XS, YS, FA, FB, S0, S1, S2, S3):
            c[k]().wait_send()
        if lines[i] and rel <= 0 and rel > 1 - owners:
            @pl.when(z < owners - 1)
            def _():
                go(i, rel, UP, source(i, rel), block(i, rel, place.e), place.e, 1).wait_send()
        if lines[i] and rel >= 0 and rel < owners - 1:
            @pl.when(z > 0)
            def _():
                go(i, rel, DOWN, source(i, rel), block(i, rel, place.e), place.e, -1).wait_send()

    rels = [0] + [s * d for d in range(1, owners) for s in (-1, 1)]
    waves = [[0]] + [[-d, d] for d in range(1, owners)]
    for w in range(owners + 3):
        if w < owners:
            for r in waves[w]:
                stage_z(r)
        if 0 <= w - 1 < owners:
            for r in waves[w - 1]:
                each(r, xy)
        if 0 <= w - 2 < owners:
            for r in waves[w - 2]:
                each(r, dg)
    for cp in copies_own:
        cp.wait()
    for r in rels:
        each(r, end)


def gather(arrays, lines, halves, owners, group, cid):
    outs = [jax.ShapeDtypeStruct((a.shape[0] * (owners if l else 1) * group,) + a.shape[1:], a.dtype) for a, l in zip(arrays, lines)]
    n = len(arrays)
    any_spec = pl.BlockSpec(memory_space=pl.ANY)
    return pl.pallas_call(
        functools.partial(gather_kernel, owners, group, lines, halves),
        out_shape=outs, in_specs=[any_spec] * n, out_specs=[any_spec] * n,
        scratch_shapes=[pltpu.SemaphoreType.DMA((n, 2 * owners - 1, 10)), pltpu.SemaphoreType.DMA((n, 2 * owners - 1, 9)), pltpu.SemaphoreType.DMA((n,))],
        compiler_params=pltpu.CompilerParams(collective_id=cid, has_side_effects=True),
    )(*arrays)


G = 16
(LOAD, SIB, Y0, Y1, X0, X1, X2, Y2, UP, DOWN) = range(10)


def summing_steps(owners, refs):
    outs, scratch = refs[:3], refs[3:]
    send, recv = scratch[18:]
    place = Place()
    z = place.z
    chips = {k: e // 2 for k, e in (("me", place.e), ("xn", place.xnb), ("yn", place.ynb), ("dg", place.diag))}

    class Item:
        def __init__(self, i, rel):
            self.i, self.rel = i, rel
            self.own, self.sib, self.first, self.second, self.up, self.down = scratch[6 * i : 6 * i + 6]
            groups = self.own.shape[3]
            self.groups, self.half = groups, (groups + 1) // 2
            self.at = z + rel
            self.slot = rel + owners - 1
            self.valid = (z + rel >= 0) & (z + rel < owners)

        def piece(self, ref, *lead):
            return ref.at[lead]

        def rows(self, second):
            return pl.ds(self.half, self.groups - self.half) if second else pl.ds(0, self.half)

        def copy(self, kind, src, dst, to, dz=0):
            there = self.slot - dz
            return pltpu.make_async_remote_copy(
                src_ref=src, dst_ref=dst,
                send_sem=send.at[self.i, self.slot, kind], recv_sem=recv.at[self.i, there, kind],
                device_id=(z + dz, to), device_id_type=MESH)

        def to_sib(self):
            return self.copy(SIB, self.own.at[self.at, slice(None), 1 - place.core],
                             self.sib.at[self.at], place.sib)

        def hop1(self, axis, other):
            second = axis == 1
            to = place.xnb if axis else place.ynb
            whose = chips["dg"] if other else chips["xn" if axis else "yn"]
            size = self.groups - self.half if second else self.half
            return self.copy((X0, X1)[other] if axis else (Y0, Y1)[other],
                             self.own.at[self.at, whose, place.core, self.rows(second)],
                             self.piece(self.first, self.at, axis, other, pl.ds(0, size)), to)

        def hop2(self, second):
            to = place.ynb if second else place.xnb
            whose = chips["yn" if second else "xn"]
            size = self.groups - self.half if second else self.half
            return self.copy(Y2 if second else X2,
                             self.own.at[self.at, whose, place.core, self.rows(second)],
                             self.piece(self.second, self.at, int(second), pl.ds(0, size)), to)

        def along(self, up):
            return self.copy(UP if up else DOWN, self.own.at[self.at, chips["me"], place.core],
                             (self.up if up else self.down).at[self.at], place.e, 1 if up else -1)

        def arrive_along(self, up):
            buf = (self.up if up else self.down).at[self.at]
            pltpu.make_async_remote_copy(
                src_ref=buf, dst_ref=buf, send_sem=send.at[self.i, self.slot, UP if up else DOWN],
                recv_sem=recv.at[self.i, self.slot, UP if up else DOWN],
                device_id=(z, place.sib), device_id_type=MESH).wait_recv()

        def add(self, whose, start, count, terms, keep=None):
            own, at, core = self.own, self.at, place.core

            @pl.loop(0, count)
            def _(g):
                total = own[at, whose, core, start + g].astype(F32)
                for ref, lead in terms:
                    total = total + ref[(*lead, g)].astype(F32)
                if keep is None:
                    own[at, whose, core, start + g] = total.astype(BF)
                else:
                    keep[start + g] = total

        def begin(self):
            self.to_sib().start()

        def stage1(self):
            self.to_sib().wait_recv()

            @pl.loop(0, 4)
            def _(chip):
                self.add(chip, 0, self.groups, [(self.sib, (self.at, chip))])
            for axis in (0, 1):
                for other in (1, 0):
                    self.hop1(axis, other).start()

        def stage2(self):
            self.hop1(0, 1).wait_recv()
            self.add(chips["xn"], 0, self.half, [(self.first, (self.at, 0, 1))])
            self.hop2(False).start()
            self.hop1(1, 1).wait_recv()
            self.add(chips["yn"], self.half, self.groups - self.half, [(self.first, (self.at, 1, 1))])
            self.hop2(True).start()

        def stage3(self):
            for axis in (0, 1):
                self.hop1(axis, 0).wait_recv()
                self.hop2(axis == 1).wait_recv()
            out = outs[self.i]
            rel = self.rel
            last = None if rel != 0 else out
            for half in (0, 1):
                start = self.half if half else 0
                size = self.groups - self.half if half else self.half
                self.add(chips["me"], start, size, [(self.first, (self.at, half, 0)), (self.second, (self.at, half))], last)
            for up in (True, False):
                if (rel >= 0) if up else (rel <= 0):
                    @pl.when((z > 0) if up else (z < owners - 1))
                    def _():
                        self.arrive_along(up)
                        buf = self.up if up else self.down

                        @pl.loop(0, self.groups)
                        def _(g):
                            more = buf[self.at, g].astype(F32)
                            if rel == 0:
                                out[g] += more
                            else:
                                where = (self.at, chips["me"], place.core, g)
                                self.own[where] = (self.own[where].astype(F32) + more).astype(BF)
            if rel != 0:
                self.along(rel > 0).start()

        def end(self):
            self.to_sib().wait_send()
            for axis in (0, 1):
                for other in (0, 1):
                    self.hop1(axis, other).wait_send()
                self.hop2(axis == 1).wait_send()
            if self.rel != 0:
                self.along(self.rel > 0).wait_send()

    values, heads, rest = (
        [Item(i, rel) for d in range(owners - 1, 0, -1) for rel in (d, -d)] + [Item(i, 0)]
        for i in range(3)
    )

    def run(items, name):
        for item in items:
            if item.rel != 0:
                pl.when(item.valid)(getattr(item, name))
            else:
                getattr(item, name)()

    def put(i, where, value):
        shape = scratch[6 * i].shape
        scratch[6 * i][where] = value.reshape(*shape[len(shape) - 6 + (where[0] is not Ellipsis) : 5], value.shape[1])

    def put_w(start, value):
        i = 0 if QK <= start < QK + VAL else 2
        at = start if start < QK else start - (QK if i == 0 else VAL)
        put(i, (Ellipsis, pl.ds(at, value.shape[1])), value)

    def put_h(h, value):
        put(1, (h,), value)

    plan = {
        "heads": ((heads, "begin"),),
        1: ((heads, "stage1"),),
        "values": ((values, "begin"), (heads, "stage2")),
        "rest": ((rest, "begin"), (values, "stage1")),
        "end": ((rest, "stage1"),),
    }

    def wave(items, w):
        return items[2 * w : 2 * w + 2] if 0 <= w < owners else []

    def event(name):
        if name == "heads":
            greet(place, True, owners)
        for items, stage in plan.get(name, ()):
            run(items, stage)
        if name == "end":
            for w in range(owners + 1):
                run(wave(heads, w), "stage3")
                run(wave(values, w), "stage2")
                run(wave(rest, w), "stage2")
                run(wave(values, w - 1), "stage3")
                run(wave(rest, w - 1), "stage3")
            run(heads + values + rest, "end")

    return put_w, put_h, event


def scatter_space(grads, owners):
    scratch, outs = [], []
    for rows, wide in grads:
        groups = rows // (owners * 8 * G)
        half = (groups + 1) // 2
        scratch += [
            pltpu.VMEM((owners, 4, 2, groups, G, wide), BF),
            pltpu.VMEM((owners, 4, groups, G, wide), BF),
            pltpu.VMEM((owners, 2, 2, half, G, wide), BF),
            pltpu.VMEM((owners, 2, half, G, wide), BF),
            pltpu.VMEM((owners, groups, G, wide), BF),
            pltpu.VMEM((owners, groups, G, wide), BF),
        ]
        outs.append(jax.ShapeDtypeStruct((groups, G, wide), F32))
    scratch += [pltpu.SemaphoreType.DMA((3, 2 * owners - 1, 10))] * 2
    return scratch, outs


def moe_kernel(
    steps,
    slots,
    chunk,
    m_ref,
    g_ref,
    member_ref,
    router_ref,
    order_ref,
    mine_ref,
    weights_ref,
    moe_ref,
    drow_ref,
    grads_ref,
    grouter_ref,
    router_s,
    gate_s,
    hg_s,
    dpre_s,
    mt_s,
    gt_s,
    gup_s,
    gdn_s,
    gr_s,
):
    step = pl.program_id(0)
    owners, _, share, units = weights_ref.shape
    per = chunk // F

    @pl.when(step == 0)
    def _():
        gup_s[...] = jnp.zeros_like(gup_s)
        gdn_s[...] = jnp.zeros_like(gdn_s)
        gr_s[...] = jnp.zeros_like(gr_s)
        router_s[...] = dot_nn(router_ref[...], order_ref[...]).astype(BF)

    mt_s[...] = m_ref[...].T
    gt_s[...] = g_ref[...].T
    sig = jax.nn.sigmoid(dot_nn(m_ref[...], router_s[...]))
    mask = dot_nn(member_ref[...], mine_ref[...])
    gate_s[...] = sig * mask
    root = math.sqrt(2.0 / math.pi)
    cube = 0.044715
    lane = lax.broadcasted_iota(jnp.int32, (1, F), 1)
    d_gate = jnp.zeros(gate_s.shape, F32)
    for c in range(units // chunk):
        cols = pl.ds(c * chunk, chunk)
        pre_all = dot_nn(m_ref[:, :share], weights_ref[0, 0, :, cols])
        back_all = dot_nn(g_ref[:, :share], weights_ref[0, 1, :, cols])
        for o in range(1, owners):
            part = pl.ds(o * share, share)
            pre_all += dot_nn(m_ref[:, part], weights_ref[o, 0, :, cols])
            back_all += dot_nn(g_ref[:, part], weights_ref[o, 1, :, cols])
        for j in range(per):
            slot = c * per + j
            part = slice(j * F, (j + 1) * F)
            pre = pre_all[:, part]
            back = back_all[:, part]
            square = pre * pre
            th = jnp.tanh(root * pre * (1.0 + cube * square))
            half = 0.5 * (1.0 + th)
            slope = half + (0.5 * root) * pre * (1.0 - th * th) * (1.0 + (3.0 * cube) * square)
            hidden = (pre * half).astype(BF).astype(F32)
            gate = gate_s[:, slot : slot + 1]
            d_one = jnp.sum(hidden * back, axis=1, keepdims=True)
            d_gate = d_gate + d_one * (lane == slot).astype(F32)
            where = pl.ds(slot * F, F)
            hg_s[:, where] = (gate * hidden).astype(BF)
            dpre_s[:, where] = (slope * (gate * back)).astype(BF)
    dlog = (d_gate * mask * sig * (1.0 - sig)).astype(BF)
    gr_s[...] += dot_nn(mt_s[...], dot_nt(dlog, order_ref[...]).astype(BF))
    for o in range(owners):
        where = pl.ds(o * share, share)
        moe_ref[:, where] = dot_nt(hg_s[...], weights_ref[o, 1]).astype(BF)
        drow_ref[:, where] = (
            dot_nt(dpre_s[...], weights_ref[o, 0]) + dot_nt(dlog, router_s[where, :])
        ).astype(BF)
        gup_s[where, :] += dot_nn(mt_s[where, :], dpre_s[...])
        gdn_s[where, :] += dot_nn(gt_s[where, :], hg_s[...])

    @pl.when(step == steps - 1)
    def _():
        for o in range(owners):
            grads_ref[o, 0] = gup_s[pl.ds(o * share, share), :].astype(BF)
            grads_ref[o, 1] = gdn_s[pl.ds(o * share, share), :].astype(BF)
        grouter_ref[...] = gr_s[...].astype(BF)


def moe(rows, cots, member, packed, router_at, order, mine, weights):
    count = rows.shape[0]
    tile = 512
    owners, _, share, units = weights.shape
    slots = units // F
    steps = count // tile
    lanes = member.shape[1]
    row_spec = pl.BlockSpec((tile, D), lambda i: (i, 0))
    whole = pl.BlockSpec(memory_space=pltpu.VMEM)
    router_spec = pl.BlockSpec((D, lanes), lambda i: (0, router_at // lanes))
    return pl.pallas_call(
        functools.partial(moe_kernel, steps, slots, 512),
        grid=(steps,),
        in_specs=[
            row_spec,
            row_spec,
            pl.BlockSpec((tile, lanes), lambda i: (i, 0)),
            router_spec,
            whole,
            whole,
            whole,
        ],
        out_specs=[row_spec, row_spec, whole, whole],
        out_shape=[
            jax.ShapeDtypeStruct((count, D), BF),
            jax.ShapeDtypeStruct((count, D), BF),
            jax.ShapeDtypeStruct(weights.shape, BF),
            jax.ShapeDtypeStruct((D, lanes), BF),
        ],
        scratch_shapes=[
            pltpu.VMEM((D, F), BF),
            pltpu.VMEM((tile, F), F32),
            pltpu.VMEM((tile, units), BF),
            pltpu.VMEM((tile, units), BF),
            pltpu.VMEM((D, tile), BF),
            pltpu.VMEM((D, tile), BF),
            pltpu.VMEM((D, units), F32),
            pltpu.VMEM((D, units), F32),
            pltpu.VMEM((D, lanes), F32),
        ],
        compiler_params=pltpu.CompilerParams(vmem_limit_bytes=60 * 1024 * 1024),
        cost_estimate=pl.CostEstimate(
            flops=12 * count * D * units,
            bytes_accessed=count * D * 8 + D * units * 8,
            transcendentals=count * units,
        ),
    )(rows, cots, member, packed, order, mine, weights)


def fused_kernel(first, owners, slots, wide, tile_cols, *refs):
    if first:
        middle, cots, member, weights, packed, order_ref, mine_ref = refs[:7]
        rows_out, drow_out, moe_out, grads_out, grouter_out = refs[7:12]
        refs = refs[12:]
    else:
        middle, cots, member, weights, packed, order_ref, mine_ref = refs[:7]
        drow_in, moe_in, grouter_in, middle_in = refs[7:11]
        drow_out, layer_out, grads_out, grouter_out = refs[11:15]
        refs = refs[15:]
    (m_s, c_s, b_s, w_s, gup_s, gdn_s, gr_s, hg_s, dpre_s, mt_s, gt_s, router_in, router_s, gate_s) = refs[:14]
    part_d, part_m, local, wsem, tsem = refs[14:19]
    if first:
        gsend, grecv = refs[19:]
    else:
        sib_s, first_s, second_s, ssend, srecv = refs[19:]
    place = Place()
    z = place.z
    count = m_s.shape[0] // 8
    half = count // 2
    lanes = b_s.shape[1]
    share = D // owners
    ins = (middle,)
    bufs = (m_s,)
    sums = (m_s, c_s)
    swap = place.sib - place.e
    mine = (place.e, place.xnb, place.ynb, place.diag)
    if not first:
        mine = (place.diag, place.xnb, place.ynb, place.e)

    def span(e, start=0, size=count):
        return pl.ds(pl.multiple_of(e * count + start, 16), size)

    def remote(sems, a, kind, src, dst, to):
        return pltpu.make_async_remote_copy(
            src_ref=src, dst_ref=dst, send_sem=sems[0].at[a, kind], recv_sem=sems[1].at[a, kind],
            device_id=(z, to), device_id_type=MESH)

    def passing(a, kind):
        buf = bufs[a]
        if kind in (XS, YS, S0):
            src, at = ins[a], span(place.e)
        elif kind == FA:
            at = span(place.xnb, 0, half)
            src = buf.at[at]
        elif kind == FB:
            at = span(place.ynb, half, half)
            src = buf.at[at]
        else:
            at = span(mine[kind - S0])
            src = buf.at[at]
        to = {XS: place.xnb, YS: place.ynb, FA: place.ynb, FB: place.xnb}.get(kind, place.sib)
        return remote((gsend, grecv), a, kind, src, buf.at[at], to)

    def got(a, kind):
        at = {
            XS: lambda: span(place.xnb),
            YS: lambda: span(place.ynb),
            FA: lambda: span(place.diag, 0, half),
            FB: lambda: span(place.diag, half, half),
        }.get(kind, lambda: span(mine[kind - S0] + swap))()
        ref = bufs[a].at[at]
        remote((gsend, grecv), a, kind, ref, ref, place.sib).wait_recv()

    HY0, HY1, HX0, HX1, HX2, HY2 = 4, 5, 6, 7, 8, 9

    def to_sib(a, t):
        return remote((ssend, srecv), a, t, sums[a].at[span(mine[t] + swap)], sib_s.at[a, t], place.sib)

    def hop(a, kind):
        src_e, second, dst, to = {
            HY0: (place.ynb, False, first_s.at[a, 0], place.ynb),
            HY1: (place.diag, False, first_s.at[a, 1], place.ynb),
            HX0: (place.xnb, True, first_s.at[a, 2], place.xnb),
            HX1: (place.diag, True, first_s.at[a, 3], place.xnb),
            HX2: (place.xnb, False, second_s.at[a, 0], place.xnb),
            HY2: (place.ynb, True, second_s.at[a, 1], place.ynb),
        }[kind]
        src = sums[a].at[span(src_e, half if second else 0, half)]
        return remote((ssend, srecv), a, kind, src, dst, to)

    step_rows = 96

    def add(a, e, start, size, terms, keep=None):
        buf = sums[a]

        @pl.loop(0, size // step_rows)
        def _(g):
            here = pl.ds(pl.multiple_of(e * count + start + g * step_rows, 16), step_rows)
            there = pl.ds(pl.multiple_of(g * step_rows, 16), step_rows)
            total = buf[here, :].astype(F32)
            for lead in terms:
                total = total + lead[0][(*lead[1], there, slice(None))].astype(F32)
            if keep is None:
                buf[here, :] = total.astype(BF)
            else:
                own_rows = pl.ds(pl.multiple_of(start + g * step_rows, 16), step_rows)
                if a == 1:
                    total = total + middle_in[own_rows, :]
                keep[own_rows, :] = total.astype(keep.dtype)

    def chip_of(t):
        tx, ty = (t % 2, t // 2) if first else ((3 - t) // 2, (3 - t) % 2)
        chip_x = place.x + tx * (1 - 2 * place.x)
        chip_y = place.y + ty * (1 - 2 * place.y)
        return pl.ds(pl.multiple_of((chip_y * 2 + chip_x) * 2 * count, 16), 2 * count)

    if first:
        own = [
            pltpu.make_async_copy(middle, m_s.at[span(place.e)], local.at[0]),
            pltpu.make_async_copy(cots, c_s, local.at[1]),
        ]
    else:
        own = []
    own.append(pltpu.make_async_copy(member, b_s, local.at[2]))
    for c in own:
        c.start()

    def tile_copies(t):
        at = chip_of(t)
        if first:
            pairs = ((m_s, rows_out), (part_d, drow_out), (part_m, moe_out))
        else:
            pairs = ((middle, m_s), (cots, c_s), (drow_in, part_d), (moe_in, part_m))
        slot = pl.ds(pl.multiple_of((t % 2) * 2 * count, 16), 2 * count)
        return [
            pltpu.make_async_copy(
                src.at[at], dst.at[slot if dst is part_d or dst is part_m else at], tsem.at[t, i]
            )
            for i, (src, dst) in enumerate(pairs)
        ]

    if not first:
        for t in range(4):
            for c in tile_copies(t)[:2]:
                c.start()
    router_copy = pltpu.make_async_copy(packed.at[:, pl.ds(wide, lanes)], router_in, local.at[3])
    router_copy.start()

    @pl.loop(0, slots)
    def _(s):
        for o in range(owners):
            for k in (0, 1):
                pltpu.make_async_copy(
                    weights.at[o, k * slots + s],
                    w_s.at[k, pl.ds(o * share, share), pl.ds(pl.multiple_of(s * F, F), F)],
                    wsem.at[0],
                ).start()

    greet(place, False, owners)
    if first:
        for kind in (XS, YS, S0):
            passing(0, kind).start()
        gr_s[...] = jnp.zeros_like(gr_s)
    else:
        for t in (0, 1):
            for c in tile_copies(t)[2:]:
                c.start()
        gr_s[...] = grouter_in[...]
    gup_s[...] = jnp.zeros_like(gup_s)
    gdn_s[...] = jnp.zeros_like(gdn_s)

    root = math.sqrt(2.0 / math.pi)
    cube = 0.044715
    tile = 2 * count
    units = slots * F
    per = tile_cols // F

    @pl.loop(0, 4)
    def _(t):
        @pl.when(t == 0)
        def _():
            for c in own:
                c.wait()
            router_copy.wait()
            router_s[...] = dot_nn(router_in[...], order_ref[...]).astype(BF)
            if first:
                got(0, S0)
            pltpu.make_async_copy(w_s, w_s, wsem.at[0]).wait()

        if first:

            @pl.when(t == 1)
            def _():
                got(0, XS)
                passing(0, FA).start()
                passing(0, S1).start()
                got(0, YS)
                passing(0, FB).start()
                passing(0, S2).start()
                got(0, S1)

            @pl.when(t == 2)
            def _():
                got(0, FA)
                got(0, FB)
                passing(0, S3).start()
                got(0, S2)

            @pl.when(t == 3)
            def _():
                got(0, S3)

        else:
            for k in range(4):

                @pl.when(t == k)
                def _():
                    for c in tile_copies(k)[:2]:
                        c.wait()

        here = chip_of(t)
        if first:
            tile_copies(t)[0].start()
        mt_s[...] = m_s[here, :].T
        gt_s[...] = c_s[here, :].T
        sig = jax.nn.sigmoid(dot_nn(m_s[here, :], router_s[...]))
        mask = dot_nn(b_s[here, :], mine_ref[...])
        gate_s[...] = sig * mask
        lane = lax.broadcasted_iota(jnp.int32, (1, F), 1)
        d_gate = jnp.zeros(gate_s.shape, F32)
        for c in range(units // tile_cols):
            cols = pl.ds(c * tile_cols, tile_cols)
            pre_all = dot_nn(m_s[here, :], w_s[0, :, cols])
            back_all = dot_nn(c_s[here, :], w_s[1, :, cols])
            for j in range(per):
                slot = c * per + j
                part = slice(j * F, (j + 1) * F)
                pre = pre_all[:, part]
                back = back_all[:, part]
                square = pre * pre
                th = jnp.tanh(root * pre * (1.0 + cube * square))
                halved = 0.5 * (1.0 + th)
                slope = halved + (0.5 * root) * pre * (1.0 - th * th) * (1.0 + (3.0 * cube) * square)
                hidden = (pre * halved).astype(BF).astype(F32)
                gate = gate_s[:, slot : slot + 1]
                d_one = jnp.sum(hidden * back, axis=1, keepdims=True)
                d_gate = d_gate + d_one * (lane == slot).astype(F32)
                where = pl.ds(slot * F, F)
                hg_s[:, where] = (gate * hidden).astype(BF)
                dpre_s[:, where] = (slope * (gate * back)).astype(BF)
        dlog = (d_gate * mask * sig * (1.0 - sig)).astype(BF)
        gr_s[...] += dot_nn(mt_s[...], dot_nt(dlog, order_ref[...]).astype(BF))

        if not first:

            @pl.when(t == 3)
            def _():
                for a in (0, 1):
                    hop(a, HY1).wait_recv()
                    add(a, place.xnb, 0, half, [(first_s, (a, 1))])
                    hop(a, HX2).start()
                    hop(a, HX1).wait_recv()
                    add(a, place.ynb, half, half, [(first_s, (a, 3))])
                    hop(a, HY2).start()

            for k in range(4):

                @pl.when(t == k)
                def _():
                    for c in tile_copies(k)[2:]:
                        c.wait()

        for a, (kept, dst) in enumerate(((part_d, m_s), (part_m, c_s))):
            for n in range(D // 256):
                where = pl.ds(n * 256, 256)
                if a == 0:
                    total = dot_nt(dpre_s[...], w_s[0, where, :]) + dot_nt(dlog, router_s[where, :])
                else:
                    total = dot_nt(hg_s[...], w_s[1, where, :])
                if first:
                    kept[here, where] = total.astype(BF)
                else:
                    there = pl.ds(pl.multiple_of((t % 2) * tile, 16), tile)
                    dst[here, where] = (total + kept[there, where].astype(F32)).astype(BF)
            if first:
                tile_copies(t)[1 + a].start()
            else:
                for k in range(4):

                    @pl.when(t == k)
                    def _():
                        to_sib(a, k).start()
                        if k < 2:
                            tile_copies(k + 2)[2 + a].start()

        def last(a):
            if first:
                return

            for k, kinds in enumerate(((HY1, HX1), (HX0,), (HY0,), ())):

                @pl.when(t == k)
                def _():
                    to_sib(a, k).wait_recv()
                    add(a, mine[k], 0, count, [(sib_s, (a, k))])
                    for kind in kinds:
                        hop(a, kind).start()

        last(0)
        for n in range(D // 256):
            where = pl.ds(n * 256, 256)
            gup_s[where, :] += dot_nn(mt_s[where, :], dpre_s[...])
        last(1)
        for n in range(D // 256):
            where = pl.ds(n * 256, 256)
            gdn_s[where, :] += dot_nn(gt_s[where, :], hg_s[...])

    w_s[0] = gup_s[...].astype(BF)
    w_s[1] = gdn_s[...].astype(BF)

    @pl.loop(0, slots)
    def _(s):
        for o in range(owners):
            for k in (0, 1):
                pltpu.make_async_copy(
                    w_s.at[k, pl.ds(o * share, share), pl.ds(pl.multiple_of(s * F, F), F)],
                    grads_out.at[o, k * slots + s],
                    wsem.at[0],
                ).start()

    grouter_out[...] = gr_s[...].astype(grouter_out.dtype)
    if first:
        for kind in range(8):
            passing(0, kind).wait_send()
        for t in range(4):
            for c in tile_copies(t):
                c.wait()
    else:
        for a, out in ((0, drow_out), (1, layer_out)):
            hop(a, HY0).wait_recv()
            hop(a, HX2).wait_recv()
            add(a, place.e, 0, half, [(first_s, (a, 0)), (second_s, (a, 0))], out)
            hop(a, HX0).wait_recv()
            hop(a, HY2).wait_recv()
            add(a, place.e, half, half, [(first_s, (a, 2)), (second_s, (a, 1))], out)
        for a in (0, 1):
            for t in range(4):
                to_sib(a, t).wait_send()
            for kind in (HY0, HY1, HX0, HX1, HX2, HY2):
                hop(a, kind).wait_send()
    pltpu.make_async_copy(w_s, w_s, wsem.at[0]).wait()


def fused_experts(first, rows, cots, member, weights, packed, wide, order, mine, more, cid):
    owners = weights.shape[0]
    slots = weights.shape[1] // 2
    total = cots.shape[0]
    count = total // 8
    lanes = member.shape[1]
    units = slots * F
    tile = 2 * count
    hbm = pl.BlockSpec(memory_space=pl.ANY)
    vmem = pl.BlockSpec(memory_space=pltpu.VMEM)
    dma = pltpu.SemaphoreType.DMA
    shape = jax.ShapeDtypeStruct
    scratch = [
        pltpu.VMEM((total, D), BF),
        pltpu.VMEM((total, D), BF),
        pltpu.VMEM((total, lanes), BF),
        pltpu.VMEM((2, D, units), BF),
        pltpu.VMEM((D, units), F32),
        pltpu.VMEM((D, units), F32),
        pltpu.VMEM((D, lanes), F32),
        pltpu.VMEM((tile, units), BF),
        pltpu.VMEM((tile, units), BF),
        pltpu.VMEM((D, tile), BF),
        pltpu.VMEM((D, tile), BF),
        pltpu.VMEM((D, lanes), BF),
        pltpu.VMEM((D, F), BF),
        pltpu.VMEM((tile, F), F32),
        pltpu.VMEM((total if first else 2 * tile, D), BF),
        pltpu.VMEM((total if first else 2 * tile, D), BF),
        dma((4,)),
        dma((1,)),
        dma((4, 4)),
    ]
    if first:
        out_specs = [hbm, hbm, hbm, hbm, vmem]
        out_shape = [shape((total, D), BF)] * 3
        out_shape += [shape(weights.shape, BF), shape((D, lanes), F32)]
        in_specs = [hbm] * 5 + [vmem] * 2
        scratch += [dma((1, 8)), dma((1, 8))]
    else:
        out_specs = [vmem, vmem, hbm, vmem]
        out_shape = [shape((count, D), F32), shape((count, D), BF)]
        out_shape += [shape(weights.shape, BF), shape((D, lanes), BF)]
        in_specs = [hbm] * 5 + [vmem] * 2 + [hbm, hbm, vmem, vmem]
        scratch += [
            pltpu.VMEM((2, 4, count, D), BF),
            pltpu.VMEM((2, 4, count // 2, D), BF),
            pltpu.VMEM((2, 2, count // 2, D), BF),
            dma((2, 10)),
            dma((2, 10)),
        ]
    return pl.pallas_call(
        functools.partial(fused_kernel, first, owners, slots, wide, 256),
        in_specs=in_specs,
        out_specs=out_specs,
        out_shape=out_shape,
        scratch_shapes=scratch,
        compiler_params=pltpu.CompilerParams(
            collective_id=cid, has_side_effects=True, vmem_limit_bytes=64 * 1024 * 1024 - 65536
        ),
        cost_estimate=pl.CostEstimate(
            flops=12 * total * D * units,
            bytes_accessed=D * units * 8 + total * D * 8,
            transcendentals=total * units,
        ),
    )(rows, cots, member, weights, packed, order, mine, *more)


def forward_kernel(
    wide,
    lanes,
    lengths_ref,
    x_ref,
    choice_ref,
    packed_ref,
    heads_all_ref,
    qk_ref,
    vals_ref,
    sig_ref,
    mask_ref,
    vlow_ref,
    prob_ref,
    attended_ref,
    mixed_ref,
    middle_ref,
    mlow_ref,
    w_ref,
    heads_ref,
    wsem,
):
    cuts = (pl.ds(wide + lanes, 128), pl.ds(0, QK), pl.ds(QK, VAL))
    coming = [
        pltpu.make_async_copy(packed_ref.at[:, c], w_ref.at[:, c], wsem.at[i])
        for i, c in enumerate(cuts)
    ]
    coming.append(pltpu.make_async_copy(heads_all_ref, heads_ref, wsem.at[3]))
    for c in coming:
        c.start()
    count = x_ref.shape[0]
    seq = count // MB
    xf = x_ref[...].astype(F32)
    centred = xf - jnp.mean(xf, axis=1, keepdims=True)
    variance = jnp.mean(centred * centred, axis=1, keepdims=True)
    coming[0].wait()
    gain_row = w_ref[:, pl.ds(wide + lanes, 128)].astype(F32).T[SEL : SEL + 1, :]
    normed = (centred * lax.rsqrt(variance + epsilon) * gain_row).astype(BF)
    coming[1].wait()
    for n in range(QK // 512):
        cols = pl.ds(n * 512, 512)
        qk_ref[:, cols] = dot_nn(normed, w_ref[:, cols]).astype(BF)
    sig = jax.nn.sigmoid(dot_nn(x_ref[...], w_ref[:, pl.ds(wide + lanes, 128)]))
    row = lax.broadcasted_iota(jnp.int32, (count, 128), 0)
    lane = lax.broadcasted_iota(jnp.int32, (count, 128), 1)
    live = (row < lengths_ref[0, 0]).astype(F32)
    for b in range(1, MB):
        live = jnp.where(row < b * seq, live, (row < b * seq + lengths_ref[b, 0]).astype(F32))
    mask = jnp.zeros((count, 128), F32)
    top = choice_ref.shape[1] // H
    for v in range(H * top):
        picked = choice_ref[:, v : v + 1] + NV * (v // top)
        mask = mask + (picked == lane).astype(F32) + (picked + H * NV == lane).astype(F32) * live
    sig_ref[...] = sig
    mask_ref[...] = mask
    gates = sig * mask
    coming[2].wait()
    for h in range(H):
        vals = dot_nn(x_ref[...], w_ref[:, pl.ds(QK + h * NV * HD, NV * HD)])
        vals_ref[:, pl.ds(h * NV * HD, NV * HD)] = vals.astype(BF)
        total = gates[:, h * NV : h * NV + 1] * vals[:, :HD]
        for e in range(1, NV):
            at = h * NV + e
            total = total + gates[:, at : at + 1] * vals[:, e * HD : (e + 1) * HD]
        vlow_ref[:, pl.ds(h * HD, HD)] = total.astype(BF)
    at_i = lax.broadcasted_iota(jnp.int32, (seq, seq), 0)
    at_j = lax.broadcasted_iota(jnp.int32, (seq, seq), 1)
    for b in range(MB):
        allowed = (at_j <= at_i) & (at_j < lengths_ref[b, 0])
        here = pl.ds(b * seq, seq)
        for h in range(H):
            queries = qk_ref[here, pl.ds(h * HD, HD)]
            keys_all = qk_ref[here, pl.ds((H + h) * HD, HD)]
            scores = jnp.where(allowed, dot_nt(queries, keys_all) * HD ** (-0.5), -1e30)
            expo = jnp.exp(scores - jnp.max(scores, axis=1, keepdims=True))
            prob = expo / jnp.sum(expo, axis=1, keepdims=True)
            prob_ref[b * H + h] = prob
            attended_ref[here, pl.ds(h * HD, HD)] = dot_nn(
                prob.astype(BF), vlow_ref[here, pl.ds(h * HD, HD)]
            )
    for h in range(H):
        attended = attended_ref[:, pl.ds(h * HD, HD)]
        for e in range(NV):
            at = h * NV + e
            gate = gates[:, H * NV + at : H * NV + at + 1]
            mixed_ref[:, pl.ds(at * HD, HD)] = (gate * attended).astype(BF)
    coming[3].wait()
    for n in range(D // 512):
        cols = pl.ds(n * 512, 512)
        middle = x_ref[:, cols].astype(F32) + dot_nn(mixed_ref[...], heads_ref[:, cols])
        middle_ref[:, cols] = middle
        mlow_ref[:, cols] = middle.astype(BF)


def forward(lengths, tokens, choice, packed, heads, wide, lanes):
    count = tokens.shape[0]
    seq = count // MB
    vmem = pl.BlockSpec(memory_space=pltpu.VMEM)
    shape = jax.ShapeDtypeStruct
    return pl.pallas_call(
        functools.partial(forward_kernel, wide, lanes),
        in_specs=[pl.BlockSpec(memory_space=pltpu.SMEM)]
        + [vmem] * 2
        + [pl.BlockSpec(memory_space=pl.ANY)] * 2,
        out_specs=[vmem] * 10,
        scratch_shapes=[
            pltpu.VMEM(packed.shape, BF),
            pltpu.VMEM(heads.shape, BF),
            pltpu.SemaphoreType.DMA((4,)),
        ],
        out_shape=[
            shape((count, QK), BF),
            shape((count, VAL), BF),
            shape((count, 128), F32),
            shape((count, 128), F32),
            shape((count, H * HD), BF),
            shape((MB * H, seq, seq), F32),
            shape((count, H * HD), F32),
            shape((count, VAL), BF),
            shape((count, D), F32),
            shape((count, D), BF),
        ],
        compiler_params=pltpu.CompilerParams(vmem_limit_bytes=56 * 1024 * 1024),
        cost_estimate=pl.CostEstimate(
            flops=2 * count * D * (wide + VAL),
            bytes_accessed=(wide + VAL) * D * 2 + count * D * 20,
            transcendentals=count * seq * H,
        ),
    )(lengths, tokens, choice, packed, heads)


def backward_kernel(wide, lanes, steps, *refs):
    (
        x_ref,
        cots_ref,
        drow_ref,
        qk_ref,
        vals_ref,
        sig_ref,
        mask_ref,
        vlow_ref,
        prob_ref,
        attended_ref,
        mixed_ref,
        grouter_ref,
        packed_ref,
        heads_all_ref,
        _,
        dx_ref,
    ) = refs[:16]
    dvals_s, dqk_s, w_ref, heads_ref, wsem = refs[16:21]
    put_w, put_h, event = steps(refs[21:])
    coming = [
        pltpu.make_async_copy(src, dst, wsem.at[i])
        for i, (src, dst) in enumerate(((heads_all_ref, heads_ref), (packed_ref, w_ref)))
    ]
    for c in coming:
        c.start()
    count = x_ref.shape[0]
    seq = count // MB
    d_branch = (cots_ref[...].astype(F32) + drow_ref[...]).astype(BF)
    width = NV * HD
    for h in range(H):
        where = pl.ds(h * width, width)
        put_h(h, dot_tn(mixed_ref[:, where], d_branch).astype(BF))
    event("heads")
    for c in coming:
        c.wait()
    mask = mask_ref[...]
    sig = sig_ref[...]
    gates = sig * mask
    lane = lax.broadcasted_iota(jnp.int32, (1, 128), 1)
    d_gates = jnp.zeros((count, 128), F32)
    for h in range(H):
        where = pl.ds(h * width, width)
        d_mixed = dot_nt(d_branch, heads_ref[where, :])
        attended = attended_ref[:, pl.ds(h * HD, HD)]
        total = jnp.zeros((count, HD), F32)
        for e in range(NV):
            at = H * NV + h * NV + e
            part = d_mixed[:, e * HD : (e + 1) * HD]
            total = total + gates[:, at : at + 1] * part
            d_one = jnp.sum(part * attended, axis=1, keepdims=True)
            d_gates = d_gates + d_one * (lane == at).astype(F32)
        d_attended = total.astype(BF)
        d_values = []
        for b in range(MB):
            here = pl.ds(b * seq, seq)
            rows = slice(b * seq, (b + 1) * seq)
            prob = prob_ref[b * H + h]
            values = vlow_ref[here, pl.ds(h * HD, HD)]
            d_prob = dot_nt(d_attended[rows], values)
            d_scores = (
                prob * (d_prob - jnp.sum(prob * d_prob, axis=1, keepdims=True))
            ).astype(BF)
            d_values.append(dot_tn(prob.astype(BF), d_attended[rows]).astype(BF).astype(F32))
            queries = qk_ref[here, pl.ds(h * HD, HD)]
            keys_all = qk_ref[here, pl.ds((H + h) * HD, HD)]
            dqk_s[here, pl.ds(h * HD, HD)] = (dot_nn(d_scores, keys_all) * HD ** (-0.5)).astype(BF)
            dqk_s[here, pl.ds((H + h) * HD, HD)] = (
                dot_tn(d_scores, queries) * HD ** (-0.5)
            ).astype(BF)
        d_value = jnp.concatenate(d_values, axis=0)
        for e in range(NV):
            at = h * NV + e
            cols = pl.ds(at * HD, HD)
            d_one = jnp.sum(d_value * vals_ref[:, cols].astype(F32), axis=1, keepdims=True)
            d_gates = d_gates + d_one * (lane == at).astype(F32)
            dvals_s[:, cols] = (gates[:, at : at + 1] * d_value).astype(BF)
        event(h)
    d_select = (d_gates * mask * sig * (1.0 - sig)).astype(BF)
    x_t = x_ref[...].T
    for n in range(VAL // 512):
        put_w(QK + n * 512, dot_nn(x_t, dvals_s[:, pl.ds(n * 512, 512)]).astype(BF))
    event("values")
    xf = x_ref[...].astype(F32)
    centred = xf - jnp.mean(xf, axis=1, keepdims=True)
    variance = jnp.mean(centred * centred, axis=1, keepdims=True)
    rstd = lax.rsqrt(variance + epsilon)
    unit = centred * rstd
    gain_row = w_ref[:, pl.ds(wide + lanes, 128)].astype(F32).T[SEL : SEL + 1, :]
    normed_t = (unit * gain_row).astype(BF).T
    for n in range(QK // 512):
        put_w(n * 512, dot_nn(normed_t, dqk_s[:, pl.ds(n * 512, 512)]).astype(BF))
    d_normed = dot_nt(dqk_s[...], w_ref[:, pl.ds(0, QK)])
    grad_gain = jnp.sum(d_normed * unit, axis=0, keepdims=True)
    small = dot_tn(d_select, x_ref[...])
    which = lax.broadcasted_iota(jnp.int32, (128, 1), 0)
    put_w(wide + lanes, jnp.where(which == SEL, grad_gain, small).T.astype(BF))
    put_w(wide, grouter_ref[...])
    event("rest")
    scaled = d_normed * gain_row
    dx_ref[...] = (
        cots_ref[...].astype(F32)
        + drow_ref[...]
        + (
            scaled
            - jnp.mean(scaled, axis=1, keepdims=True)
            - unit * jnp.mean(scaled * unit, axis=1, keepdims=True)
        )
        * rstd
    )
    for n in range(D // 256):
        rows = pl.ds(n * 256, 256)
        dx_ref[:, rows] += dot_nt(dvals_s[...], w_ref[rows, pl.ds(QK, VAL)]) + dot_nt(
            d_select, w_ref[rows, pl.ds(wide + lanes, 128)]
        )
    event("end")


def plain_steps(wide, refs):
    gw_ref, gheads_ref = refs

    def put_w(start, value):
        gw_ref[:, pl.ds(start, value.shape[1])] = value

    def put_h(h, value):
        gheads_ref[pl.ds(h * value.shape[0], value.shape[0]), :] = value

    def nothing(*_):
        pass

    return put_w, put_h, nothing


def backward(tokens, cots, drow, saved, grouter, packed, heads, ahead, wide, lanes, owners, cid):
    count = tokens.shape[0]
    vmem = pl.BlockSpec(memory_space=pltpu.VMEM)
    shape = jax.ShapeDtypeStruct
    scratch = [
        pltpu.VMEM((count, VAL), BF),
        pltpu.VMEM((count, QK), BF),
        pltpu.VMEM(packed.shape, BF),
        pltpu.VMEM(heads.shape, BF),
        pltpu.SemaphoreType.DMA((2,)),
    ]
    grads = (packed.shape, heads.shape)
    summed = ((D, VAL), heads.shape, (D, packed.shape[1] - VAL))
    if cid is None:
        kernel = lambda *refs: backward_kernel(
            wide, lanes, functools.partial(plain_steps, wide), *refs[:16], *refs[18:23], *refs[16:18]
        )
        out_shape = [shape((count, D), F32)] + [shape(g, BF) for g in grads]
        more = {}
    else:
        kernel = lambda *refs: backward_kernel(
            wide,
            lanes,
            functools.partial(summing_steps, owners),
            *refs[:16],
            *refs[19:24],
            *refs[16:19],
            *refs[24:],
        )
        more_scratch, sums = scatter_space(summed, owners)
        scratch += more_scratch
        out_shape = [shape((count, D), F32)] + sums
        more = dict(collective_id=cid, has_side_effects=True)
    return pl.pallas_call(
        kernel,
        in_specs=[vmem] * 12 + [pl.BlockSpec(memory_space=pl.ANY)] * 3,
        out_specs=[vmem] * len(out_shape),
        out_shape=out_shape,
        scratch_shapes=scratch,
        compiler_params=pltpu.CompilerParams(vmem_limit_bytes=64 * 1024 * 1024 - 65536, **more),
        cost_estimate=pl.CostEstimate(
            flops=4 * count * D * (wide + VAL),
            bytes_accessed=(wide + VAL) * D * 4 + count * D * 30,
            transcendentals=0,
        ),
    )(tokens, cots, drow, *saved, grouter, packed, heads, ahead)


def update_kernel(lanes, rates, values_ref, heads_sum_ref, rest_ref, first_ref, second_ref, *refs):
    results, ins = refs[:2], refs[2:23]
    kept, outs = refs[23:25], refs[25:]
    for src, dst in zip(results, kept):
        dst[...] = src[...]

    def step(i, at, gradient):
        new = update_weight(*(ref[at] for ref in ins[3 * i : 3 * i + 3]), gradient, rates[i])
        for ref, value in zip(outs[4 * i : 4 * i + 4], new):
            ref[at] = value

    everything = (slice(None), slice(None))
    step(0, (slice(None), pl.ds(0, QK)), rest_ref[:, pl.ds(0, QK)])
    step(0, (slice(None), pl.ds(QK, VAL)), values_ref[...])
    step(1, everything, rest_ref[:, pl.ds(QK + lanes, SEL)])
    step(2, everything, rest_ref[:, pl.ds(QK, ins[6].shape[1])])
    step(3, everything, heads_sum_ref[...])
    which = (lax.broadcasted_iota(jnp.int32, (8, 128), 1) == SEL).astype(F32)
    gain_rows = lax.dot_general(
        which,
        rest_ref[:, pl.ds(QK + lanes, 128)],
        (((1,), (1,)), ((), ())),
        precision=lax.Precision.HIGHEST,
        preferred_element_type=F32,
    )
    step(6, everything, gain_rows[:1, :])
    start = 0
    for ref in (first_ref, second_ref):
        part = ref.shape[0] // 2

        @pl.loop(0, part)
        def _(s):
            for k in (0, 1):
                step(4 + k, start + s, ref[k * part + s].astype(F32))

        start += part


def update_all(sums, sums_a, sums_b, results, weights, rates, lanes):
    vmem = pl.BlockSpec(memory_space=pltpu.VMEM)
    shapes = [jax.ShapeDtypeStruct(a.shape, a.dtype) for a in results]
    for i in range(7):
        shapes += [jax.ShapeDtypeStruct(weights[3 * i].shape, t) for t in (F32, F32, F32, BF)]
    return pl.pallas_call(
        functools.partial(update_kernel, lanes, rates),
        in_specs=[vmem] * 28,
        out_specs=[vmem] * 30,
        out_shape=shapes,
        compiler_params=pltpu.CompilerParams(vmem_limit_bytes=60 * 1024 * 1024),
    )(*sums, sums_a, sums_b, *results, *weights)


def body(
    tokens,
    cotangent,
    lengths,
    routes,
    head_choice,
    placement,
    gain_master,
    gain_moment,
    gain_average,
    qkv_master,
    qkv_moment,
    qkv_average,
    select_master,
    select_moment,
    select_average,
    router_master,
    router_moment,
    router_average,
    heads_out_master,
    heads_out_moment,
    heads_out_average,
    up_master,
    up_moment,
    up_average,
    down_master,
    down_moment,
    down_average,
):
    both = ("dp", "expert")
    owners = lax.axis_size("dp")
    group = lax.axis_size("expert")
    own_kernels = group == 8
    experts = placement.shape[0]
    slots = up_master.shape[0]
    units = slots * F
    seq = tokens.shape[1]
    count = MB * seq
    share = up_master.shape[1]
    mine = lax.axis_index("expert")
    lanes = -(-experts // 128) * 128

    own_rows = qkv_master.shape[0]
    wide = QK + VAL
    packed = jnp.concatenate(
        [
            qkv_master.astype(BF),
            router_master.astype(BF),
            jnp.zeros((own_rows, lanes - experts), BF),
            select_master.astype(BF),
            gain_master.astype(BF)[:, None],
            jnp.zeros((own_rows, 127 - SEL), BF),
        ],
        axis=1,
    )
    heads_low = heads_out_master.astype(BF)

    part = slots // 2

    def fetch(own):
        low = jnp.concatenate([up_master[own].astype(BF), down_master[own].astype(BF)], axis=0)
        return lax.all_gather(low, "dp", axis=0, tiled=False)

    weights = (fetch(slice(0, part)), fetch(slice(part, slots)))

    flat_tokens = tokens.reshape(count, D)
    flat_cots = cotangent.reshape(count, D)
    live = (jnp.arange(seq, dtype=jnp.int32)[None, :] < lengths).astype(F32).reshape(count)
    lane_ids = jnp.arange(lanes, dtype=jnp.int32)
    named = jnp.sum(
        (routes.reshape(count, TOPK)[..., None] == lane_ids).astype(F32), axis=1
    ) * live[:, None]
    padded = jnp.pad(placement, (0, lanes - experts), constant_values=-1)
    perm = (padded[:, None] == lane_ids[None, :]).astype(BF)
    member = dot_nn(named.astype(BF), perm).astype(BF)
    own_lane = jnp.arange(F, dtype=jnp.int32)[None, :]

    def selects(start, number):
        slot = mine * slots + start
        inside = own_lane < number
        return (
            (((padded[:, None] - slot) == own_lane) & inside & (padded[:, None] >= 0)).astype(BF),
            (((lane_ids[:, None] - slot) == own_lane) & inside).astype(BF),
        )

    if own_kernels:
        packed_all, heads, cots_all, member_all = gather(
            (packed, heads_low, flat_cots, member),
            (True, True, False, False),
            (own_rows // 2, 48, count // 2, count // 2),
            owners,
            group,
            0,
        )
    else:
        packed_all = lax.all_gather(packed, both, axis=0, tiled=True)
        heads = lax.all_gather(heads_low, both, axis=0, tiled=True)
        cots_all, member_all = (
            lax.all_gather(a, "expert", axis=0, tiled=True) for a in (flat_cots, member)
        )
    choice = head_choice.reshape(count, -1)
    *saved, middle, middle_low = forward(lengths, flat_tokens, choice, packed_all, heads, wide, lanes)
    if own_kernels:
        rows_all, drow_part, moe_part, grads_a, router_part = fused_experts(
            True, middle_low, cots_all, member_all, weights[0], packed_all, wide, *selects(0, part), (), 1
        )
        d_from_rows, mixed, grads_b, grad_router = fused_experts(
            False,
            rows_all,
            cots_all,
            member_all,
            weights[1],
            packed_all,
            wide,
            *selects(part, slots - part),
            (drow_part, moe_part, router_part, middle),
            2,
        )
    else:
        rows_all = lax.all_gather(middle_low, "expert", axis=0, tiled=True)
        side = jnp.concatenate([w.reshape(owners, 2, -1, share, F) for w in weights], axis=2)
        side = side.transpose(0, 1, 3, 2, 4)
        moe_part, drow_part, expert_grads, grad_router = moe(
            rows_all,
            cots_all,
            member_all,
            packed_all,
            wide,
            *selects(0, slots),
            side.reshape(owners, 2, share, units),
        )
        expert_grads = expert_grads.reshape(owners, 2, share, slots, F).transpose(0, 1, 3, 2, 4)
        grads_a, grads_b = expert_grads[:, :, :part], expert_grads[:, :, part:]
        d_from_rows, moe_sum = (
            lax.psum_scatter(a, "expert", scatter_dimension=0, tiled=True).astype(F32)
            for a in (drow_part, moe_part)
        )
        mixed = (middle + moe_sum).astype(BF)
    sums_a, sums_b = (
        lax.psum_scatter(
            g.reshape(-1, share, F), "dp", scatter_dimension=0, tiled=True
        )
        for g in (grads_a, grads_b)
    )
    d_tokens, *grads = backward(
        flat_tokens,
        flat_cots,
        d_from_rows,
        saved,
        grad_router,
        packed_all,
        heads,
        sums_a,
        wide,
        lanes,
        owners,
        3 if own_kernels else None,
    )
    if own_kernels:
        sums = tuple(total.reshape(-1, total.shape[2]) for total in grads)
    else:
        packed_sum, heads_sum = (
            lax.psum_scatter(g, both, scatter_dimension=0, tiled=True).astype(F32) for g in grads
        )
        rest_sum = jnp.concatenate([packed_sum[:, :QK], packed_sum[:, wide:]], axis=1)
        sums = (packed_sum[:, QK:wide], heads_sum, rest_sum)
    rates = step_rates(count * owners * group, experts)
    gain = tuple(a[None] for a in (gain_master, gain_moment, gain_average))
    mixed, d_tokens, *new = update_all(
        sums,
        sums_a,
        sums_b,
        (mixed, d_tokens),
        (
            qkv_master,
            qkv_moment,
            qkv_average,
            select_master,
            select_moment,
            select_average,
            router_master,
            router_moment,
            router_average,
            heads_out_master,
            heads_out_moment,
            heads_out_average,
            up_master,
            up_moment,
            up_average,
            down_master,
            down_moment,
            down_average,
            *gain,
        ),
        rates[1:] + rates[:1],
        lanes,
    )
    gain_new = tuple(a.reshape(gain_master.shape) for a in new[24:])
    return (mixed.reshape(tokens.shape), d_tokens.reshape(tokens.shape), *gain_new, *new[:24])


def solution(mesh):
    rows = P(None, ("dp", "expert"), None)
    flat = P(("dp", "expert"))
    dense = P(("dp", "expert"), None)
    expert = P("expert", "dp", None)
    in_specs = (
        rows,
        rows,
        P(None, ("dp", "expert")),
        rows,
        P(None, ("dp", "expert"), None, None),
        P(),
        *((flat,) * 3),
        *((dense,) * 12),
        *((expert,) * 6),
    )
    out_specs = (rows, rows, *((flat,) * 4), *((dense,) * 16), *((expert,) * 8))
    return jax.shard_map(body, mesh=mesh, in_specs=in_specs, out_specs=out_specs, check_vma=False)
```
